32 devices in a mesh: dp: 8 (over z, y), seq: 4 (over x, core).
Axes of the slice: x: 2, y: 2, z: 4, core: 2. Of those that a mesh axis runs over, the one named last changes fastest.
Arguments:
- tokens: bfloat16 [8, 64, 64, 320], P('dp', 'seq'), may hold values from -6 to 6
- buckets: int32 [8], P('dp'), may hold values from 0 to 1, as said below
- cotangent: bfloat16 [8, 4, 8, 128, 320], P(None, 'seq', 'dp'), may hold values from -8 to 8
- query_weight: float32 [320, 320], P('dp', 'seq'), may hold values from -0.3125 to 0.3125
- reduce_weight: float32 [1280, 320], P('dp', 'seq'), may hold values from -0.15625 to 0.15625
- memory_weight: float32 [320, 640], P('dp', 'seq'), may hold values from -0.3125 to 0.3125
- output_weight: float32 [320, 320], P('dp', 'seq'), may hold values from -2.5 to 2.5
- expand_weight: float32 [320, 1280], P('dp', 'seq'), may hold values from -0.3125 to 0.3125
- contract_weight: float32 [1280, 320], P('dp', 'seq'), may hold values from -0.15625 to 0.15625
- norm_gains: float32 [3, 320], P(None, 'dp'), may hold values from 0.3 to 2.7
- biases: float32 [8, 320], P(None, 'dp'), may hold values from -1 to 1
- hidden_params: float32 [11, 1280], P(None, 'dp'), may hold values from -1.6 to 1.6
- moment_query: float32 [320, 320], P('dp', 'seq'), may hold values from -0.00048828125 to 0.00048828125
- moment_reduce: float32 [1280, 320], P('dp', 'seq'), may hold values from -0.00048828125 to 0.00048828125
- moment_memory: float32 [320, 640], P('dp', 'seq'), may hold values from -0.00048828125 to 0.00048828125
- moment_output: float32 [320, 320], P('dp', 'seq'), may hold values from -0.00048828125 to 0.00048828125
- moment_expand: float32 [320, 1280], P('dp', 'seq'), may hold values from -0.00048828125 to 0.00048828125
- moment_contract: float32 [1280, 320], P('dp', 'seq'), may hold values from -0.00048828125 to 0.00048828125
- moment_gains: float32 [3, 320], P(None, 'dp'), may hold values from -0.00048828125 to 0.00048828125
- moment_biases: float32 [8, 320], P(None, 'dp'), may hold values from -0.0029296875 to 0.0029296875
- moment_hidden: float32 [11, 1280], P(None, 'dp'), may hold values from -0.00048828125 to 0.00048828125
- square_query: float32 [320, 320], P('dp', 'seq'), may hold values from 3.1763285e-08 to 1.268116e-07
- square_reduce: float32 [1280, 320], P('dp', 'seq'), may hold values from 3.1763285e-08 to 1.268116e-07
- square_memory: float32 [320, 640], P('dp', 'seq'), may hold values from 3.1763285e-08 to 1.268116e-07
- square_output: float32 [320, 320], P('dp', 'seq'), may hold values from 3.1763285e-08 to 1.268116e-07
- square_expand: float32 [320, 1280], P('dp', 'seq'), may hold values from 3.1763285e-08 to 1.268116e-07
- square_contract: float32 [1280, 320], P('dp', 'seq'), may hold values from 3.1763285e-08 to 1.268116e-07
- square_gains: float32 [3, 320], P(None, 'dp'), may hold values from 3.1763285e-08 to 1.268116e-07
- square_biases: float32 [8, 320], P(None, 'dp'), may hold values from 9.661836e-07 to 3.804348e-06
- square_hidden: float32 [11, 1280], P(None, 'dp'), may hold values from 3.1763285e-08 to 1.268116e-07
Outputs:
- block_output: bfloat16 [8, 4, 8, 128, 320], P(None, 'seq', 'dp')
- token_grad: bfloat16 [8, 64, 64, 320], P('dp', 'seq')
- global_norm: float32 [], replicated
- updated_query: float32 [320, 320], P('dp', 'seq')
- updated_reduce: float32 [1280, 320], P('dp', 'seq')
- updated_memory: float32 [320, 640], P('dp', 'seq')
- updated_output: float32 [320, 320], P('dp', 'seq')
- updated_expand: float32 [320, 1280], P('dp', 'seq')
- updated_contract: float32 [1280, 320], P('dp', 'seq')
- updated_gains: float32 [3, 320], P(None, 'dp')
- updated_biases: float32 [8, 320], P(None, 'dp')
- updated_hidden: float32 [11, 1280], P(None, 'dp')
- momentum_query: float32 [320, 320], P('dp', 'seq')
- momentum_reduce: float32 [1280, 320], P('dp', 'seq')
- momentum_memory: float32 [320, 640], P('dp', 'seq')
- momentum_output: float32 [320, 320], P('dp', 'seq')
- momentum_expand: float32 [320, 1280], P('dp', 'seq')
- momentum_contract: float32 [1280, 320], P('dp', 'seq')
- momentum_gains: float32 [3, 320], P(None, 'dp')
- momentum_biases: float32 [8, 320], P(None, 'dp')
- momentum_hidden: float32 [11, 1280], P(None, 'dp')
- squares_query: float32 [320, 320], P('dp', 'seq')
- squares_reduce: float32 [1280, 320], P('dp', 'seq')
- squares_memory: float32 [320, 640], P('dp', 'seq')
- squares_output: float32 [320, 320], P('dp', 'seq')
- squares_expand: float32 [320, 1280], P('dp', 'seq')
- squares_contract: float32 [1280, 320], P('dp', 'seq')
- squares_gains: float32 [3, 320], P(None, 'dp')
- squares_biases: float32 [8, 320], P(None, 'dp')
- squares_hidden: float32 [11, 1280], P(None, 'dp')
The draws below stay inside these ranges and needn't reach their ends.
Inputs may be any that keep to these rules, and one draw needn't show every extreme that they name: `buckets`: 0 marks a canvas holding one scene of 64 x 64 tokens, 1 a canvas holding four scenes, one in each quadrant; both values occur in every draw.
All inputs are finite; a program needn't handle non-finite values.
Results may differ from the reference program's by a relative error of at most 0.023.
Values may be sent and summed in bfloat16 or wider, within the bound.
A program may use at most 128 MiB of HBM per device.

```python
import math
import jax
import jax.numpy as jnp
from jax import lax

D = 320
HEADS = 5
HEAD = 64
FF = 1280
SIDE = 64
STEP = 10
CANVASES = 8
PIECE = 128
OUT_FAN = 5
PARAMS = 1656000
N_DP = 8
N_SEQ = 4


def draw_buckets(key, part):
    key = jax.random.fold_in(key, 11)
    first_key, second_key = jax.random.split(key)
    labels = jax.random.randint(first_key, (CANVASES,), 0, 2, dtype=jnp.int32)
    chosen = jax.random.randint(second_key, (), 0, CANVASES, dtype=jnp.int32)
    spots = jnp.arange(CANVASES, dtype=jnp.int32)
    labels = jnp.where(spots == chosen, 0, labels)
    labels = jnp.where(spots == (chosen + 1) % CANVASES, 1, labels)
    return labels


def draw_cotangent(key, part):
    key = jax.random.fold_in(key, 12)
    bands = SIDE * SIDE // (CANVASES * PIECE)
    shape = (CANVASES, bands, CANVASES, PIECE, D)
    across = jnp.arange(D, dtype=jnp.float32) / (D - 1)
    scales = 0.6 * 3.0 ** across
    samples = jnp.clip(jax.random.normal(key, shape, jnp.float32), -4.0, 4.0)
    return (samples * scales).astype(jnp.bfloat16)


def draw_norm_gains(key, part):
    key = jax.random.fold_in(key, 13)
    across = jnp.arange(D, dtype=jnp.float32) / (D - 1)
    scales = 0.6 * 3.0 ** across
    noise = jnp.clip(0.06 * jax.random.normal(key, (3, D), jnp.float32), -0.2, 0.2)
    return scales * (1.0 + noise)


def level_of(rng, shape, shards, least, top_value):
    def one(axis_at, blocks):
        steps = jax.random.uniform(jax.random.fold_in(jax.random.fold_in(rng, 6), axis_at), (blocks,), jnp.float32, least / len(shards), top_value / len(shards))
        return jnp.repeat(jnp.exp(steps), shape[axis_at] // blocks).reshape((-1,) + (1,) * (len(shape) - axis_at - 1))

    factor_of = one(*shards[0])
    for cut in shards[1:]:
        factor_of = factor_of * one(*cut)
    return factor_of


def scatter_about(stream_key, dims, scale, bound, cuts=(), kind=jnp.bfloat16):
    drawn = jax.random.normal(stream_key, dims, jnp.float32) * scale
    if len(cuts) > 0:
        drawn = level_of(stream_key, dims, cuts, -0.22, 0.18) * drawn
    return jnp.clip(drawn, min=-bound, max=bound).astype(kind)


def setup_inputs(seed: int = 0) -> dict:
    splits = jax.random.split(jax.random.key(seed), 31)
    tokens = scatter_about(splits[0], (CANVASES, SIDE, SIDE, D), 1.0, 6.0, ((0, 8), (1, 4)))
    buckets = draw_buckets(jax.random.fold_in(splits[30], 71), 0)
    cotangent = draw_cotangent(jax.random.fold_in(splits[30], 71), 0)
    query_weight = scatter_about(splits[3], (D, D), D ** -0.5, 0.3125, ((0, 8), (1, 4)), jnp.float32)
    reduce_weight = scatter_about(splits[4], (4 * D, D), (4 * D) ** -0.5, 0.15625, ((0, 8), (1, 4)), jnp.float32)
    memory_weight = scatter_about(splits[5], (D, 2 * D), D ** -0.5, 0.3125, ((0, 8), (1, 4)), jnp.float32)
    output_weight = scatter_about(splits[6], (D, D), OUT_FAN ** -0.5, 2.5, ((0, 8), (1, 4)), jnp.float32)
    expand_weight = scatter_about(splits[7], (D, FF), D ** -0.5, 0.3125, ((0, 8), (1, 4)), jnp.float32)
    contract_weight = scatter_about(splits[8], (FF, D), FF ** -0.5, 0.15625, ((0, 8), (1, 4)), jnp.float32)
    norm_gains = draw_norm_gains(jax.random.fold_in(splits[30], 71), 0)
    biases = scatter_about(splits[10], (8, D), 0.2, 1.0, ((1, 8),), jnp.float32)
    hidden_params = scatter_about(splits[11], (11, FF), 0.33, 1.6, ((1, 8),), jnp.float32)
    moment_query = scatter_about(splits[12], (D, D), (0.111 * PARAMS ** -0.5), 0.00048828125, ((0, 8), (1, 4)), jnp.float32)
    moment_reduce = scatter_about(splits[13], (4 * D, D), (0.111 * PARAMS ** -0.5), 0.00048828125, ((0, 8), (1, 4)), jnp.float32)
    moment_memory = scatter_about(splits[14], (D, 2 * D), (0.111 * PARAMS ** -0.5), 0.00048828125, ((0, 8), (1, 4)), jnp.float32)
    moment_output = scatter_about(splits[15], (D, D), (0.111 * PARAMS ** -0.5), 0.00048828125, ((0, 8), (1, 4)), jnp.float32)
    moment_expand = scatter_about(splits[16], (D, FF), (0.111 * PARAMS ** -0.5), 0.00048828125, ((0, 8), (1, 4)), jnp.float32)
    moment_contract = scatter_about(splits[17], (FF, D), (0.111 * PARAMS ** -0.5), 0.00048828125, ((0, 8), (1, 4)), jnp.float32)
    moment_gains = scatter_about(splits[18], (3, D), (0.111 * PARAMS ** -0.5), 0.00048828125, ((1, 8),), jnp.float32)
    moment_biases = scatter_about(splits[19], (8, D), (0.61 * PARAMS ** -0.5), 0.0029296875, ((1, 8),), jnp.float32)
    moment_hidden = scatter_about(splits[20], (11, FF), (0.111 * PARAMS ** -0.5), 0.00048828125, ((1, 8),), jnp.float32)
    square_query = jnp.clip(jnp.exp(math.log(1.268115994434993e-07) - 1.3843914 * jax.random.uniform(splits[21], (D, D), jnp.float32) ** level_of(splits[21], (D, D), ((0, 8), (1, 4)), -0.2, 0.2)), 3.1763285335273395e-08, 1.268115994434993e-07)
    square_reduce = jnp.clip(jnp.exp(math.log(1.268115994434993e-07) - 1.3843914 * jax.random.uniform(splits[22], (4 * D, D), jnp.float32) ** level_of(splits[22], (4 * D, D), ((0, 8), (1, 4)), -0.2, 0.2)), 3.1763285335273395e-08, 1.268115994434993e-07)
    square_memory = jnp.clip(jnp.exp(math.log(1.268115994434993e-07) - 1.3843914 * jax.random.uniform(splits[23], (D, 2 * D), jnp.float32) ** level_of(splits[23], (D, 2 * D), ((0, 8), (1, 4)), -0.2, 0.2)), 3.1763285335273395e-08, 1.268115994434993e-07)
    square_output = jnp.clip(jnp.exp(math.log(1.268115994434993e-07) - 1.3843914 * jax.random.uniform(splits[24], (D, D), jnp.float32) ** level_of(splits[24], (D, D), ((0, 8), (1, 4)), -0.2, 0.2)), 3.1763285335273395e-08, 1.268115994434993e-07)
    square_expand = jnp.clip(jnp.exp(math.log(1.268115994434993e-07) - 1.3843914 * jax.random.uniform(splits[25], (D, FF), jnp.float32) ** level_of(splits[25], (D, FF), ((0, 8), (1, 4)), -0.2, 0.2)), 3.1763285335273395e-08, 1.268115994434993e-07)
    square_contract = jnp.clip(jnp.exp(math.log(1.268115994434993e-07) - 1.3843914 * jax.random.uniform(splits[26], (FF, D), jnp.float32) ** level_of(splits[26], (FF, D), ((0, 8), (1, 4)), -0.2, 0.2)), 3.1763285335273395e-08, 1.268115994434993e-07)
    square_gains = jnp.clip(jnp.exp(math.log(1.268115994434993e-07) - 1.3843914 * jax.random.uniform(splits[27], (3, D), jnp.float32) ** level_of(splits[27], (3, D), ((1, 8),), -0.2, 0.2)), 3.1763285335273395e-08, 1.268115994434993e-07)
    square_biases = jnp.clip(jnp.exp(math.log(3.8043478980398504e-06) - 1.370546 * jax.random.uniform(splits[28], (8, D), jnp.float32) ** level_of(splits[28], (8, D), ((1, 8),), -0.2, 0.2)), 9.661836202212726e-07, 3.8043478980398504e-06)
    square_hidden = jnp.clip(jnp.exp(math.log(1.268115994434993e-07) - 1.3843914 * jax.random.uniform(splits[29], (11, FF), jnp.float32) ** level_of(splits[29], (11, FF), ((1, 8),), -0.2, 0.2)), 3.1763285335273395e-08, 1.268115994434993e-07)
    return dict(tokens=tokens, buckets=buckets, cotangent=cotangent, query_weight=query_weight, reduce_weight=reduce_weight, memory_weight=memory_weight, output_weight=output_weight, expand_weight=expand_weight, contract_weight=contract_weight, norm_gains=norm_gains, biases=biases, hidden_params=hidden_params, moment_query=moment_query, moment_reduce=moment_reduce, moment_memory=moment_memory, moment_output=moment_output, moment_expand=moment_expand, moment_contract=moment_contract, moment_gains=moment_gains, moment_biases=moment_biases, moment_hidden=moment_hidden, square_query=square_query, square_reduce=square_reduce, square_memory=square_memory, square_output=square_output, square_expand=square_expand, square_contract=square_contract, square_gains=square_gains, square_biases=square_biases, square_hidden=square_hidden)


HIGHEST = lax.Precision.HIGHEST
NORM_EPS = 1e-06
MAX_NORM = 1.0
BETA_ONE = 0.9
BETA_TWO = 0.95
ADAM_EPS = 1e-08
DECAY_RATE = 0.01
VECTOR_RATE = 0.3
GAIN_RATE = 0.8
MASKED = -1e+30

@jax.custom_vjp
def low(v):
    return lax.optimization_barrier(v.astype(jnp.bfloat16)).astype(jnp.float32)

@jax.custom_vjp
def low_back(v):
    return v

def low_keep(v):
    return (low(v), None)

def low_pass(kept, grad):
    return (grad,)

def back_keep(v):
    return (v, None)

def back_low(kept, grad):
    return (low(grad),)
low.defvjp(low_keep, low_pass)
low_back.defvjp(back_keep, back_low)

def layer_norm(values, scale_row, offset_row):
    average = lax.optimization_barrier(jnp.mean(values, axis=-1, keepdims=True))
    centered = values - average
    spread = lax.optimization_barrier(jnp.mean(centered * centered, axis=-1, keepdims=True))
    return centered * lax.rsqrt(spread + NORM_EPS) * scale_row + offset_row

def gelu_exact(values):
    return jax.nn.gelu(values, approximate=False)

def scene_ids(bucket_id, row_ids, col_ids, side):
    half = side // 2
    quarter = (row_ids >= half).astype(jnp.int32) * 2 + (col_ids >= half).astype(jnp.int32)
    return quarter * bucket_id

def padded_ids(bucket_id, first_row, band_rows, side):
    row_ids = first_row + jnp.arange(band_rows + 2, dtype=jnp.int32) - 1
    col_ids = jnp.arange(side + 2, dtype=jnp.int32) - 1
    inside = (row_ids[:, None] >= 0) & (row_ids[:, None] < side) & (col_ids[None, :] >= 0) & (col_ids[None, :] < side)
    return jnp.where(inside, scene_ids(bucket_id, row_ids[:, None], col_ids[None, :], side), -1)

def neighbor_masks(ids_pad, band_rows, side):
    center = ids_pad[1:1 + band_rows, 1:1 + side]
    masks = []
    for row_step in range(3):
        for col_step in range(3):
            masks.append((ids_pad[row_step:row_step + band_rows, col_step:col_step + side] == center).astype(jnp.float32))
    return masks

def canvas_forward(inputs, bucket_id, params):
    query_matrix, reduce_matrix, memory_matrix, output_matrix, expand_matrix, contract_matrix, gain_rows, shift_rows, hidden_rows = params
    side = inputs.shape[0]
    width = inputs.shape[2]
    normed_in = low(layer_norm(inputs, gain_rows[0], shift_rows[0]))
    queries = low(low_back(jnp.dot(normed_in, query_matrix, precision=HIGHEST) + shift_rows[1]))
    patches = normed_in.reshape(side // 2, 2, side // 2, 2, width).transpose(0, 2, 1, 3, 4).reshape(side // 2, side // 2, 4 * width)
    reduced = low_back(jnp.dot(patches, reduce_matrix, precision=HIGHEST) + shift_rows[2])
    memory_in = low(layer_norm(reduced, gain_rows[1], shift_rows[3]))
    value_shift = jnp.concatenate([jnp.zeros((width,), jnp.float32), shift_rows[4]])
    memory = low(low_back(jnp.dot(memory_in, memory_matrix, precision=HIGHEST) + value_shift))
    keys = memory[..., :width].reshape(-1, HEADS, HEAD)
    values = memory[..., width:].reshape(-1, HEADS, HEAD)
    query_heads = queries.reshape(-1, HEADS, HEAD)
    places = jnp.arange(side, dtype=jnp.int32)
    query_ids = scene_ids(bucket_id, places[:, None], places[None, :], side).reshape(-1)
    key_cells = jnp.arange(side // 2, dtype=jnp.int32)
    key_ids = scene_ids(bucket_id, key_cells[:, None], key_cells[None, :], side // 2).reshape(-1)
    same_scene = query_ids[:, None] == key_ids[None, :]
    scores = jnp.einsum('qhe,khe->hqk', query_heads, keys, precision=HIGHEST) * HEAD ** (-0.5)
    scores = low_back(jnp.where(same_scene[None], scores, MASKED))
    largest = lax.optimization_barrier(jnp.max(scores, axis=-1, keepdims=True))
    powers = jnp.exp(scores - largest)
    probs = low(powers / lax.optimization_barrier(jnp.sum(powers, axis=-1, keepdims=True)))
    attended = jnp.einsum('hqk,khe->qhe', probs, values, precision=HIGHEST).reshape(side, side, width)
    attended = low(low_back(attended))
    branch = low_back(jnp.dot(attended, output_matrix, precision=HIGHEST) + shift_rows[5])
    middle = inputs + branch
    normed_mid = low(layer_norm(middle, gain_rows[2], shift_rows[6]))
    expanded = low(low_back(jnp.dot(normed_mid, expand_matrix, precision=HIGHEST) + hidden_rows[9]))
    masks = neighbor_masks(padded_ids(bucket_id, jnp.int32(0), side, side), side, side)
    padded = jnp.pad(expanded, ((1, 1), (1, 1), (0, 0)))
    total = jnp.zeros(expanded.shape, jnp.float32) + hidden_rows[10]
    for tap_index in range(9):
        row_step = tap_index // 3
        col_step = tap_index % 3
        total = total + hidden_rows[tap_index] * padded[row_step:row_step + side, col_step:col_step + side] * masks[tap_index][:, :, None]
    activated = low(gelu_exact(low_back(total)))
    return middle + jnp.dot(activated, contract_matrix, precision=HIGHEST) + shift_rows[7]

def adam_step(weight_now, first_now, second_now, clipped, step_rate, decay_rate):
    first_new = BETA_ONE * first_now + (1.0 - BETA_ONE) * clipped
    second_new = BETA_TWO * second_now + (1.0 - BETA_TWO) * clipped * clipped
    direction = first_new / (1.0 - BETA_ONE ** STEP) / (jnp.sqrt(second_new / (1.0 - BETA_TWO ** STEP)) + ADAM_EPS)
    return (weight_now - step_rate * (direction + decay_rate * weight_now), first_new, second_new)

def reference(tokens, buckets, cotangent, query_weight, reduce_weight, memory_weight, output_weight, expand_weight, contract_weight, norm_gains, biases, hidden_params, moment_query, moment_reduce, moment_memory, moment_output, moment_expand, moment_contract, moment_gains, moment_biases, moment_hidden, square_query, square_reduce, square_memory, square_output, square_expand, square_contract, square_gains, square_biases, square_hidden):
    weights = (query_weight, reduce_weight, memory_weight, output_weight, expand_weight, contract_weight, norm_gains, biases, hidden_params)
    firsts = (moment_query, moment_reduce, moment_memory, moment_output, moment_expand, moment_contract, moment_gains, moment_biases, moment_hidden)
    seconds = (square_query, square_reduce, square_memory, square_output, square_expand, square_contract, square_gains, square_biases, square_hidden)
    inputs = tokens.astype(jnp.float32)

    def forward(values_in, params):
        rounded = tuple((low(element) for element in params))

        def one_canvas(canvas_pair):
            return canvas_forward(canvas_pair[0], canvas_pair[1], rounded)
        return lax.map(jax.checkpoint(one_canvas), (values_in, buckets))
    outputs, pullback = jax.vjp(forward, inputs, weights)
    block_output = outputs.astype(jnp.bfloat16).reshape(CANVASES, N_SEQ, N_DP, PIECE, D)
    incoming = cotangent.astype(jnp.float32).reshape(CANVASES, SIDE, SIDE, D)
    token_slope, gradients = pullback(incoming)
    token_grad = token_slope.astype(jnp.bfloat16)
    total_squares = sum((jnp.sum(element * element) for element in gradients))
    global_norm = jnp.sqrt(total_squares)
    clip_factor = jnp.minimum(1.0, MAX_NORM / (global_norm + 1e-06))
    step_rates = (D ** (-0.5), (4 * D) ** (-0.5), D ** (-0.5), OUT_FAN ** (-0.5), D ** (-0.5), FF ** (-0.5), GAIN_RATE, VECTOR_RATE, VECTOR_RATE)
    decays = (DECAY_RATE,) * 6 + (0.0,) * 3
    results = [adam_step(weights[index], firsts[index], seconds[index], clip_factor * gradients[index], step_rates[index], decays[index]) for index in range(9)]
    updated = [entry[0] for entry in results]
    momenta = [entry[1] for entry in results]
    squares = [entry[2] for entry in results]
    return (block_output, token_grad, global_norm, updated[0], updated[1], updated[2], updated[3], updated[4], updated[5], updated[6], updated[7], updated[8], momenta[0], momenta[1], momenta[2], momenta[3], momenta[4], momenta[5], momenta[6], momenta[7], momenta[8], squares[0], squares[1], squares[2], squares[3], squares[4], squares[5], squares[6], squares[7], squares[8])
```

```python
import functools

import jax
import jax.numpy as jnp
from jax import lax
from jax.experimental import pallas as pl
from jax.experimental.pallas import tpu as pltpu
from jax.sharding import PartitionSpec as P

D = 320
HEADS = 5
HEAD = 64
FF = 1280
STEP = 10
OUT_FAN = 5

NORM_EPS = 1e-06
MAX_NORM = 1.0
BETA_ONE = 0.9
BETA_TWO = 0.95
ADAM_EPS = 1e-08
DECAY_RATE = 0.01
VECTOR_RATE = 0.3
GAIN_RATE = 0.8
MASKED = -1e30

BF = jnp.bfloat16
F32 = jnp.float32
MESH = pl.DeviceIdType.MESH
QC = 256
VMEM_LIMIT = 63 * 1024 * 1024


def nn(a, b):
    return lax.dot_general(a, b, (((1,), (0,)), ((), ())), preferred_element_type=F32)


def nt(a, b):
    return lax.dot_general(a, b, (((1,), (1,)), ((), ())), preferred_element_type=F32)


def up(n, m):
    return (n + m - 1) // m * m


def norm_parts(v):
    centered = v - jnp.mean(v, axis=-1, keepdims=True)
    rstd = lax.rsqrt(jnp.mean(centered * centered, axis=-1, keepdims=True) + NORM_EPS)
    return centered * rstd, rstd


def norm_back(v, gain, e):
    vhat, rstd = norm_parts(v)
    u = e * gain
    dv = rstd * (
        u
        - jnp.mean(u, axis=-1, keepdims=True)
        - vhat * jnp.mean(u * vhat, axis=-1, keepdims=True)
    )
    return dv, jnp.sum(e * vhat, axis=0, keepdims=True), jnp.sum(e, axis=0, keepdims=True)


def colsum(v):
    return jnp.sum(v, axis=0, keepdims=True)


def rows(start, size):
    return pl.ds(pl.multiple_of(start, 16), size)


def block_kernel(
    n,
    side,
    band,
    bucket_ref,
    tok_ref,
    cot_ref,
    wq_ref,
    wr_ref,
    wm_ref,
    wo_ref,
    w1_ref,
    w2_ref,
    gains_ref,
    biases_ref,
    hidden_ref,
    out_ref,
    tgrad_ref,
    own_ref,
    x_s,
    fq,
    fr,
    fm,
    fo,
    f1,
    f2,
    fg,
    fb,
    fh,
    gvec,
    g0,
    g1,
    vp,
    hp,
    wqt,
    wqp,
    wot,
    wop,
    wmt,
    wrt,
    w1t,
    w2t,
    a3,
    abf,
    pat,
    red_s,
    memin,
    kv,
    kvt,
    kmask,
    qmask,
    qnat,
    qt,
    prob,
    att_t,
    att_n,
    rtot,
    delta,
    mid,
    bn,
    bn_t,
    hidp,
    hidh,
    act,
    gp,
    out_t,
    dy_in,
    dy_t,
    dy,
    dzh,
    datn,
    gkv,
    rk1,
    rk2,
    dq_t,
    hg,
    vg,
    rf1,
    rf2,
    rf3,
    rt1,
    rt2,
    rt3,
    rm1,
    rm2,
    rm3,
    sv,
    rv1,
    rv2,
    rv3,
    nrm,
    nrs,
    maskl,
    maskr,
    loc,
    vg_s,
    vg_r,
    ga_s,
    ga_r,
    gb_s,
    gb_r,
    gx_s,
    gx_r,
    co_s,
    co_r,
    ou_s,
    ou_r,
    kv_s,
    kv_r,
    ha_s,
    ha_r,
    dk_s,
    dk_r,
    rs_s,
    rs_r,
    rd_s,
    rd_r,
    nd_s,
    nd_r,
    ns_s,
    ns_r,
):
    me = lax.axis_index("dp")
    j = lax.axis_index("seq")
    j1 = j + 1 - 2 * lax.rem(j, 2)
    j2 = lax.rem(j + 2, 4)
    j3 = 3 - j
    tokens = band * side
    chunks = tokens // QC
    rb = wq_ref.shape[0]
    piece = tokens // n
    keys = kv.shape[2]
    turned = cot_ref.shape[1] == D

    def remote(src, dst, ss, rs, dp, seq):
        return pltpu.make_async_remote_copy(
            src_ref=src,
            dst_ref=dst,
            send_sem=ss,
            recv_sem=rs,
            device_id=(dp, seq),
            device_id_type=MESH,
        )

    def peers(body):
        def step(k, carry):
            body(k, lax.rem(me + k, n), lax.rem(me + n - k, n))
            return carry

        lax.fori_loop(1, n, step, 0)

    loads = [
        pltpu.make_async_copy(src, dst, loc.at[at])
        for at, (src, dst) in enumerate(
            (
                (gains_ref, fg),
                (biases_ref, fb),
                (hidden_ref, fh),
                (wr_ref, fr),
                (wm_ref, fm),
                (wq_ref, fq),
                (wo_ref, fo),
                (w1_ref, f1),
                (w2_ref, f2),
                (tok_ref, x_s),
            )
        )
    ]
    for copy in loads:
        copy.start()
    own_cot = pltpu.make_async_copy(cot_ref.at[me], dy_in.at[me], loc.at[10])
    own_cot.start()

    barrier = pltpu.get_barrier_semaphore()

    def greet(k, peer, source):
        pl.semaphore_signal(barrier, inc=1, device_id=(peer, j), device_id_type=MESH)

    peers(greet)
    for other in (j1, j2, j3):
        pl.semaphore_signal(barrier, inc=1, device_id=(me, other), device_id_type=MESH)

    for copy in loads[:3]:
        copy.wait()
    vl = gvec.shape[2]
    hidden16 = jnp.concatenate([fh[...], jnp.zeros((5, 4 * rb), F32)], axis=0)
    small16 = jnp.concatenate([fg[...], fb[...], jnp.zeros((5, rb), F32)], axis=0)
    gvec[me] = jnp.concatenate(
        [hidden16, small16, jnp.zeros((16, vl - 5 * rb), F32)], axis=1
    ).astype(BF)
    for copy in loads[3:7]:
        copy.wait()
    width0 = up(8 * rb, 128)
    wm_t = fm[...].T
    g0[j, me, :, 0:width0] = jnp.concatenate(
        [
            fr[...].T,
            wm_t[0:80],
            wm_t[80:160],
            fq[...].T,
            fo[...].T,
            jnp.zeros((80, width0 - 8 * rb), F32),
        ],
        axis=1,
    ).astype(BF)

    first_block = g0.at[:, :, :, 0:width0]
    tl = up(6 * rb, 128)
    ml = up(2 * rb, 128)
    st = g0.at[:, :, :, 0:tl]
    sm = g0.at[:, :, :, tl : tl + ml]
    pl.semaphore_wait(barrier, n - 1 + 3)

    def send_vec(k, peer, source):
        remote(gvec.at[me], gvec.at[me], vg_s.at[k], vg_r.at[k], peer, j).start()

    def wait_vec(k, peer, source):
        d = remote(gvec.at[source], gvec.at[source], vg_s.at[k], vg_r.at[k], peer, j)
        d.wait_send()
        d.wait_recv()

    def send_g0(k, peer, source):
        remote(first_block.at[j, me], first_block.at[j, me], ga_s.at[k], ga_r.at[k], peer, j).start()

    def wait_g0(k, peer, source):
        d = remote(first_block.at[j, source], first_block.at[j, source], ga_s.at[k], ga_r.at[k], peer, j)
        d.wait_send()
        d.wait_recv()

    def send_g1(k, peer, source):
        remote(g1.at[j, me], g1.at[j, me], gb_s.at[k], gb_r.at[k], peer, j).start()

    def wait_g1(k, peer, source):
        d = remote(g1.at[j, source], g1.at[j, source], gb_s.at[k], gb_r.at[k], peer, j)
        d.wait_send()
        d.wait_recv()

    def seq_gather(g, at):
        def copy(slot, t, other):
            return remote(g.at[slot], g.at[slot], gx_s.at[at, t], gx_r.at[at, t], me, other)

        def first():
            copy(j, 0, j2).start()
            copy(j, 1, j1).start()

        def second():
            copy(j2, 0, j2).wait_recv()
            copy(j2, 2, j1).start()

        def third():
            copy(j, 0, j2).wait_send()
            copy(j, 1, j1).wait_send()
            copy(j1, 1, j1).wait_recv()
            copy(j2, 2, j1).wait_send()
            copy(j3, 2, j1).wait_recv()

        return first, second, third

    peers(send_vec)
    peers(send_g0)

    for copy in loads[7:9]:
        copy.wait()
    w1_t = f1[...].T
    g1[j, me] = jnp.concatenate(
        [f2[...].T]
        + [w1_t[80 * v : 80 * v + 80] for v in range(4)]
        + [jnp.zeros((80, g1.shape[3] - 8 * rb), F32)],
        axis=1,
    ).astype(BF)

    peers(wait_vec)
    hp[...] = jnp.concatenate([gvec[i, :, 0 : 4 * rb] for i in range(n)], axis=1).astype(F32)
    vp[...] = jnp.concatenate(
        [gvec[i, :, 4 * rb : 5 * rb] for i in range(n)], axis=1
    ).astype(F32)

    def gain(k):
        return vp[k : k + 1, :]

    def shift(k):
        return vp[3 + k : 4 + k, :]

    loads[9].wait()

    def norm_one(c, carry):
        at = rows(c * QC, QC)
        vhat, _ = norm_parts(x_s[at, :].astype(F32))
        low = (vhat * gain(0) + shift(0)).astype(BF)
        abf[at, :] = low
        wide = jnp.concatenate([low.astype(F32), jnp.zeros((QC, 64), F32)], axis=1)
        for t in range(3):
            a3[t, at, :] = wide[:, 128 * t : 128 * t + 128]
        return carry

    lax.fori_loop(0, chunks, norm_one, 0)
    half = side // 2
    for dd in range(4):
        for i in range(band // 2):
            start = (2 * i + dd // 2) * side + dd % 2
            cut = jnp.concatenate(
                [a3[t, pl.ds(start, half, stride=2), :] for t in range(3)], axis=1
            )
            pat[dd, i * half : (i + 1) * half, :] = cut[:, 0:D].astype(BF)

    bucket = bucket_ref[0]
    k_row = lax.broadcasted_iota(jnp.int32, (4 * keys, 128), 0)
    k_lane = lax.broadcasted_iota(jnp.int32, (4 * keys, 128), 1)
    k_id = (lax.div(k_row, half) >= half // 2).astype(jnp.int32) * 2 + (
        lax.rem(k_row, half) >= half // 2
    ).astype(jnp.int32)
    off = (k_id != k_lane).astype(jnp.int32) * bucket * (k_lane < 4).astype(jnp.int32)
    kmask[...] = (off.astype(F32) * MASKED).astype(BF)
    q_row = lax.broadcasted_iota(jnp.int32, (128, QC), 0)
    q_at = lax.broadcasted_iota(jnp.int32, (128, QC), 1)
    for c in range(chunks):
        place = q_at + c * QC
        q_id = (lax.div(place, side) + j * band >= half).astype(jnp.int32) * 2 + (
            lax.rem(place, side) >= half
        ).astype(jnp.int32)
        qmask[c] = (q_id == q_row).astype(F32).astype(BF)
    col = lax.broadcasted_iota(jnp.int32, (side, 128), 0)
    maskl[...] = ((col > 0).astype(jnp.int32) * (1 - bucket * (col == half).astype(jnp.int32))).astype(F32)
    maskr[...] = (
        (col < side - 1).astype(jnp.int32) * (1 - bucket * (col == half - 1).astype(jnp.int32))
    ).astype(F32)
    top_ok = (
        (j > 0).astype(jnp.int32) * (1 - bucket * (j * band == half).astype(jnp.int32))
    ).astype(F32)
    low_ok = (
        (j < 3).astype(jnp.int32) * (1 - bucket * ((j + 1) * band == half).astype(jnp.int32))
    ).astype(F32)

    first0, second0, third0 = seq_gather(first_block, 0)
    first1, second1, third1 = seq_gather(g1, 1)
    peers(wait_g0)
    first0()
    peers(send_g1)

    def send_cot(k, peer, source):
        remote(cot_ref.at[peer], dy_in.at[me], co_s.at[k], co_r.at[k], peer, j).start()

    def wait_cot(k, peer, source):
        d = remote(cot_ref.at[peer], dy_in.at[source], co_s.at[k], co_r.at[k], peer, j)
        d.wait_send()
        d.wait_recv()

    peers(send_cot)
    second0()
    third0()

    for s in range(4):
        span = slice(80 * s, 80 * s + 80)

        def lanes(lo, hi, over):
            return jnp.concatenate([g0[s, i, :, lo:hi] for i in over], axis=1)

        for dd in range(4):
            wrt[dd, span, :] = lanes(0, 4 * rb, range(dd * n // 4, (dd + 1) * n // 4))
        for v in range(2):
            wop[160 * s + 80 * v : 160 * s + 80 * v + 80, :] = lanes(
                (4 + v) * rb, (5 + v) * rb, range(n)
            )
        wqt[span, :] = lanes(6 * rb, 7 * rb, range(n))
        wot[span, :] = lanes(7 * rb, 8 * rb, range(n))
    for h in range(HEADS):
        head = slice(HEAD * h, HEAD * h + HEAD)
        wmt[128 * h : 128 * h + 64, :] = wop[head, :]
        wmt[128 * h + 64 : 128 * h + 128, :] = wop[D + HEAD * h : D + HEAD * h + HEAD, :]
        wqp[128 * h : 128 * h + 64, :] = wqt[head, :]
        wqp[128 * h + 64 : 128 * h + 128, :] = jnp.zeros((64, D), BF)

    red = shift(2) + nt(pat[0], wrt[0])
    for dd in range(1, 4):
        red = red + nt(pat[dd], wrt[dd])
    red_s[...] = red
    vhat, _ = norm_parts(red)
    low = (vhat * gain(1) + shift(3)).astype(BF)
    memin[...] = low
    zero64 = jnp.zeros((1, HEAD), F32)
    value_shift = jnp.concatenate(
        [
            part
            for h in range(HEADS)
            for part in (zero64, shift(4)[:, HEAD * h : HEAD * h + HEAD])
        ],
        axis=1,
    )
    memory = (nt(low, wmt[...]) + value_shift).astype(BF)
    for h in range(HEADS):
        kv[h, j] = memory[:, 128 * h : 128 * h + 128]

    def kv_copy(h, slot, t, other):
        return remote(
            kv.at[h, slot], kv.at[h, slot], kv_s.at[h, t], kv_r.at[h, t], me, other
        )

    def kv_send(h, carry):
        kv_copy(h, j, 0, j2).start()
        kv_copy(h, j, 1, j1).start()
        return carry

    lax.fori_loop(0, HEADS, kv_send, 0)

    query_shift = jnp.concatenate(
        [
            part
            for h in range(HEADS)
            for part in (shift(1)[:, HEAD * h : HEAD * h + HEAD], zero64)
        ],
        axis=1,
    )

    def queries(c, carry):
        at = rows(c * QC, QC)
        q = (nt(abf[at, :], wqp[...]) + query_shift).astype(BF) * jnp.asarray(HEAD**-0.5, BF)
        for h in range(HEADS):
            tile = q[:, 128 * h : 128 * h + 128]
            qnat[h, at, :] = tile
            qt[h, c] = tile.T
        return carry

    lax.fori_loop(0, chunks, queries, 0)
    wop_full = wot[...].T
    for h in range(HEADS):
        wop[128 * h : 128 * h + 64, :] = jnp.zeros((64, D), BF)
        wop[128 * h + 64 : 128 * h + 128, :] = wop_full[HEAD * h : HEAD * h + HEAD, :]

    def kv_forward(h, carry):
        kv_copy(h, j2, 0, j2).wait_recv()
        kv_copy(h, j2, 2, j1).start()
        return carry

    lax.fori_loop(0, HEADS, kv_forward, 0)
    peers(wait_g1)
    first1()

    ones = jnp.ones((16, 4 * keys), BF)

    def attend(h, carry):
        kv_copy(h, j, 0, j2).wait_send()
        kv_copy(h, j, 1, j1).wait_send()
        kv_copy(h, j2, 2, j1).wait_send()
        kv_copy(h, j1, 1, j1).wait_recv()
        kv_copy(h, j3, 2, j1).wait_recv()
        tile = kv[h].reshape(4 * keys, 128)
        kvt[h] = tile.T

        def chunk(c, inner):
            left = jnp.concatenate([kv[h].reshape(4 * keys, 128), kmask[...]], axis=1)
            right = jnp.concatenate([qt[h, c], qmask[c]], axis=0)
            scores = nn(left, right)
            largest = jnp.max(scores, axis=0, keepdims=True)
            powers = jnp.exp(scores - largest).astype(BF)
            prob[h, c] = powers
            values = jnp.concatenate([kvt[h, 64:128, :], ones], axis=0)
            got = nn(values, powers)
            scale = 1.0 / got[64:65, :]
            rtot[h, c] = scale
            att_t[c, rows(h * HEAD, HEAD), :] = (got[0:64, :] * scale).astype(BF)
            return inner

        lax.fori_loop(0, chunks, chunk, 0)
        return carry

    lax.fori_loop(0, HEADS, attend, 0)
    second1()

    def middle(c, carry):
        at = rows(c * QC, QC)
        att = att_t[c].T
        att_n[at, :] = att
        value = x_s[at, :].astype(F32) + nt(att, wot[...]) + shift(5)
        mid[at, :] = value
        vhat, _ = norm_parts(value)
        low = (vhat * gain(2) + shift(6)).astype(BF)
        bn[at, :] = low
        bn_t[:, pl.ds(pl.multiple_of(c * QC, QC), QC)] = low.T
        return carry

    lax.fori_loop(0, chunks, middle, 0)

    third1()
    for s in range(4):
        w2t[80 * s : 80 * s + 80, :] = jnp.concatenate(
            [g1[s, i, :, 0 : 4 * rb] for i in range(n)], axis=1
        )
        for v in range(4):
            at = 320 * s + 80 * v
            w1t[at : at + 80, :] = jnp.concatenate(
                [g1[s, i, :, (4 + v) * rb : (5 + v) * rb] for i in range(n)], axis=1
            )

    edge = tokens - side

    def hidden_of(value):
        return (nt(value, w1t[...]) + hp[9:10, :]).astype(BF)

    ends = hidden_of(jnp.concatenate([bn[0:side, :], bn[edge:tokens, :]], axis=0))
    hidp[side : 2 * side, :] = ends[0:side]
    hidp[tokens : tokens + side, :] = ends[side : 2 * side]
    above = lax.rem(j + 3, 4)
    below = lax.rem(j + 1, 4)

    def rim(buf, halo, at):
        return (
            remote(buf.at[pl.ds(side, side)], halo.at[1], ha_s.at[at], ha_r.at[at], me, above),
            remote(
                buf.at[pl.ds(tokens, side)], halo.at[0], ha_s.at[at + 1], ha_r.at[at + 1], me, below
            ),
        )

    def rim_send(buf, halo, at):
        for copy in rim(buf, halo, at):
            copy.start()

    def rim_wait(buf, halo, at):
        for copy in rim(buf, halo, at):
            copy.wait_send()
            copy.wait_recv()
        buf[0:side, :] = (halo[0].astype(F32) * top_ok).astype(BF)
        buf[tokens + side : tokens + 2 * side, :] = (halo[1].astype(F32) * low_ok).astype(BF)

    rim_send(hidp, hidh, 0)

    def inner_hidden(c, carry):
        start = side + c * 2 * side
        hidp[rows(start + side, 2 * side), :] = hidden_of(bn[rows(start, 2 * side), :])
        return carry

    lax.fori_loop(0, (tokens - 2 * side) // (2 * side), inner_hidden, 0)
    rim_wait(hidp, hidh, 0)

    def taps_of(lanes):
        return [hp[k : k + 1, lanes] for k in range(9)]

    def conv_tile(t, carry):
        lanes = pl.ds(pl.multiple_of(t * 128, 128), 128)
        taps = taps_of(lanes)
        base = hp[10:11, lanes]

        def row(r, inner):
            around = [hidp[rows((r + a) * side, side), lanes].astype(F32) for a in range(3)]
            parts = [
                taps[b] * around[0] + taps[3 + b] * around[1] + taps[6 + b] * around[2]
                for b in range(3)
            ]
            z = (
                base
                + parts[1]
                + maskl[...] * pltpu.roll(parts[0], 1, 0)
                + maskr[...] * pltpu.roll(parts[2], side - 1, 0)
            )
            cdf = 0.5 + 0.5 * lax.erf(z * (0.5**0.5))
            pdf = jnp.exp(z * z * -0.5) * 0.3989422804014327
            act[rows((r + 1) * side, side), lanes] = (z * cdf).astype(BF)
            gp[rows(r * side, side), lanes] = (cdf + z * pdf).astype(BF)
            return inner

        lax.fori_loop(0, band, row, 0)
        return carry

    lax.fori_loop(0, FF // 128, conv_tile, 0)

    def out_piece(at, d):
        value = (
            mid[rows(d * piece, piece), :]
            + nt(act[rows(side + d * piece, piece), :], w2t[...])
            + shift(7)
        )
        out_t[at] = (value.T if turned else value).astype(BF)

    def send_out(k, peer, source):
        out_piece(k, peer)
        remote(out_t.at[k], out_ref.at[me], ou_s.at[k], ou_r.at[k], peer, j).start()

    def wait_out(k, peer, source):
        d = remote(out_t.at[k], out_ref.at[source], ou_s.at[k], ou_r.at[k], peer, j)
        d.wait_send()
        d.wait_recv()

    peers(send_out)
    out_piece(0, me)
    own_out = pltpu.make_async_copy(out_t.at[0], out_ref.at[me], loc.at[11])
    own_out.start()

    own_cot.wait()
    peers(wait_cot)
    for i in range(n):
        if turned:
            dy_t[:, i * piece : (i + 1) * piece] = dy_in[i]
            dy[i * piece : (i + 1) * piece, :] = dy_in[i].T
        else:
            dy[i * piece : (i + 1) * piece, :] = dy_in[i]
    if not turned:
        dy_t[...] = dy[...].T
    vg[...] = jnp.zeros(vg.shape, F32)
    vg[10:11, :] = colsum(dy[...].astype(F32))

    sf = g1
    per = 640 // (4 * rb)
    for b in range(2):
        value = nn(dy_t[...], act[side : side + tokens, 640 * b : 640 * b + 640]).astype(BF)
        for ii in range(per):
            sf[:, b * per + ii, :, 0 : 4 * rb] = value[:, 4 * rb * ii : 4 * rb * (ii + 1)].reshape(
                4, 80, 4 * rb
            )

    def slope_of(at):
        return nn(dy[at, :], w2t[...])

    dz = act
    for at in (0, edge):
        dz[side + at : 2 * side + at, :] = (
            slope_of(slice(at, at + side)) * gp[at : at + side, :].astype(F32)
        ).astype(BF)
    rim_send(dz, dzh, 2)

    def inner_slope(c, carry):
        at = rows(side + c * 2 * side, 2 * side)
        dz[rows(2 * side + c * 2 * side, 2 * side), :] = (
            slope_of(at) * gp[at, :].astype(F32)
        ).astype(BF)
        return carry

    lax.fori_loop(0, (tokens - 2 * side) // (2 * side), inner_slope, 0)
    rim_wait(dz, dzh, 2)

    dhid = gp

    def fold(v):
        return jnp.sum(v.reshape(side // 8, 8, 128), axis=0)

    def back_tile(t, carry):
        lanes = pl.ds(pl.multiple_of(t * 128, 128), 128)
        taps = taps_of(lanes)

        def row(r, sums):
            around = [dz[rows((r + a) * side, side), lanes].astype(F32) for a in range(3)]
            parts = [
                taps[b] * around[2] + taps[3 + b] * around[1] + taps[6 + b] * around[0]
                for b in range(3)
            ]
            low = (
                parts[1]
                + maskr[...] * pltpu.roll(parts[0], side - 1, 0)
                + maskl[...] * pltpu.roll(parts[2], 1, 0)
            ).astype(BF)
            dhid[rows(r * side, side), lanes] = low
            here = around[1]
            moved = [
                maskr[...] * pltpu.roll(here, side - 1, 0),
                here,
                maskl[...] * pltpu.roll(here, 1, 0),
            ]
            found = []
            for a in range(3):
                source = hidp[rows((r + a) * side, side), lanes].astype(F32)
                for b in range(3):
                    found.append(fold(moved[b] * source))
            found.append(fold(low.astype(F32)))
            found.append(fold(here))
            return tuple(s + f for s, f in zip(sums, found))

        sums = lax.fori_loop(0, band, row, tuple(jnp.zeros((8, 128), F32) for _ in range(11)))
        hg[:, lanes] = jnp.concatenate(
            [colsum(s) for s in sums] + [jnp.zeros((5, 128), F32)], axis=0
        )
        return carry

    lax.fori_loop(0, FF // 128, back_tile, 0)

    for b in range(2):
        value = nn(bn_t[...], dhid[:, 640 * b : 640 * b + 640]).T.astype(BF)
        value = value.reshape(2, 4, 80, D)
        for i in range(n):
            sf[2 * b : 2 * b + 2, i, :, 4 * rb : 8 * rb] = jnp.concatenate(
                [value[:, v, :, rb * i : rb * i + rb] for v in range(4)], axis=2
            )

    def scatter(at, s, r1, r2, r3):
        core = [
            remote(s.at[slot], r1.at[t], rs_s.at[at, t], rs_r.at[at, t], me, j1)
            for t, slot in enumerate((j1, j3))
        ]
        over_x = remote(s.at[j2], r2, rs_s.at[at, 2], rs_r.at[at, 2], me, j2)

        def one():
            for copy in core:
                copy.start()

        def two():
            for copy in core:
                copy.wait_send()
                copy.wait_recv()

            def add(i, carry):
                s[j, i] = (s[j, i].astype(F32) + r1[0, i].astype(F32)).astype(BF)
                s[j2, i] = (s[j2, i].astype(F32) + r1[1, i].astype(F32)).astype(BF)
                return carry

            lax.fori_loop(0, n, add, 0)
            over_x.start()

        def dp_copy(k, peer):
            return remote(s.at[j, peer], r3.at[k], rd_s.at[at, k], rd_r.at[at, k], peer, j)

        def three():
            over_x.wait_send()
            over_x.wait_recv()

            def add(i, carry):
                s[j, i] = (s[j, i].astype(F32) + r2[i].astype(F32)).astype(BF)
                return carry

            lax.fori_loop(0, n, add, 0)
            peers(lambda k, peer, source: dp_copy(k, peer).start())

        def four():
            def land(k, peer, source):
                d = dp_copy(k, peer)
                d.wait_send()
                d.wait_recv()

            peers(land)
            return lax.fori_loop(
                1, n, lambda k, total: total + r3[k].astype(F32), s[j, me].astype(F32)
            )

        return one, two, three, four

    f_one, f_two, f_three, f_four = scatter(0, sf, rf1, rf2, rf3)
    f_one()

    zero_row = jnp.zeros((1, D), F32)

    dbr = bn
    dbr_t = dy_t

    def back_middle(c, carry):
        at = rows(c * QC, QC)
        value, in_gain, in_shift = norm_back(mid[at, :], gain(2), nn(dhid[at, :], w1t[...]))
        value = value + dy[at, :].astype(F32)
        mid[at, :] = value
        low = value.astype(BF)
        dbr[at, :] = low
        dbr_t[:, pl.ds(pl.multiple_of(c * QC, QC), QC)] = low.T
        spread = nt(wop[...], low)
        for h in range(HEADS):
            tile = spread[128 * h : 128 * h + 128, :] * rtot[h, c]
            tile_low = tile.astype(BF)
            qt[h, c] = tile_low
            datn[h, at, :] = tile_low.T
            delta[h, c] = colsum(
                tile_low[64:128, :].astype(F32)
                * att_t[c, HEAD * h : HEAD * h + HEAD, :].astype(F32)
            )
        return (carry[0] + in_gain, carry[1] + in_shift, carry[2] + colsum(low.astype(F32)))

    sums = lax.fori_loop(0, chunks, back_middle, (zero_row, zero_row, zero_row))
    vg[2:3, :] = sums[0]
    vg[9:10, :] = sums[1]
    vg[8:9, :] = sums[2]
    f_two()
    value = nn(dbr_t[...], att_n[...]).astype(BF)
    for i in range(n):
        sm[:, i, :, rb : 2 * rb] = value[:, rb * i : rb * i + rb].reshape(4, 80, rb)

    def dkv(h, slot):
        return act.at[rows(slot * keys, keys), 128 * h : 128 * h + 128]

    def dk_core(h):
        return [
            remote(dkv(h, slot), rk1.at[h, t], dk_s.at[h, t], dk_r.at[h, t], me, j1)
            for t, slot in enumerate((j1, j3))
        ]

    def dk_x(h):
        return remote(dkv(h, j2), rk2.at[h], dk_s.at[h, 2], dk_r.at[h, 2], me, j2)

    def dk_two(h):
        for copy in dk_core(h):
            copy.wait_send()
            copy.wait_recv()
        for t, slot in enumerate((j, j2)):
            part = dkv(h, slot)
            part[...] = (part[...].astype(F32) + rk1[h, t].astype(F32)).astype(BF)
        dk_x(h).start()

    def dk_three(h):
        over_x = dk_x(h)
        over_x.wait_send()
        over_x.wait_recv()
        qnat[h, 0:keys, :] = (dkv(h, j)[...].astype(F32) + rk2[h].astype(F32)).astype(BF)

    def back_head(h):
        gkv[...] = jnp.zeros(gkv.shape, F32)

        def chunk(c, inner):
            at = rows(c * QC, QC)
            tile = kv[h].reshape(4 * keys, 128)
            powers = prob[h, c]
            slopes = nn(tile, qt[h, c]) - delta[h, c]
            ds = (powers.astype(F32) * slopes).astype(BF)
            gkv[...] += nn(
                jnp.concatenate([ds, powers], axis=1),
                jnp.concatenate([qnat[h, at, :], datn[h, at, :]], axis=0),
            )
            dq_t[c, rows(h * HEAD, HEAD), :] = (
                nn(kvt[h, 0:64, :], ds) * HEAD**-0.5
            ).astype(BF)
            return inner

        lax.fori_loop(0, chunks, chunk, 0)
        act[0 : 4 * keys, 128 * h : 128 * h + 128] = gkv[...].astype(BF)
        for copy in dk_core(h):
            copy.start()

    for h in range(HEADS):
        back_head(h)
        if h >= 1:
            dk_two(h - 1)
        if h >= 2:
            dk_three(h - 2)
        if h == 1:
            f_three()

    dq = att_n

    def flip(c, total):
        low = dq_t[c].T
        dq[rows(c * QC, QC), :] = low
        return total + colsum(low.astype(F32))

    vg[4:5, :] = lax.fori_loop(0, chunks, flip, zero_row)
    dk_two(HEADS - 1)
    value = nn(dq_t[0], abf[0:QC, :])
    for c in range(1, chunks):
        value = value + nn(dq_t[c], abf[QC * c : QC * c + QC, :])
    value = value.astype(BF)
    for i in range(n):
        sm[:, i, :, 0:rb] = value[:, rb * i : rb * i + rb].reshape(4, 80, rb)
    m_one, m_two, m_three, m_four = scatter(1, sm, rm1, rm2, rm3)
    m_one()
    dk_three(HEADS - 2)
    dk_three(HEADS - 1)

    dm = jnp.concatenate([qnat[h, 0:keys, :] for h in range(HEADS)], axis=1)
    dm_sum = colsum(dm.astype(F32))
    vg[7:8, :] = jnp.concatenate(
        [dm_sum[:, 128 * h + 64 : 128 * h + 128] for h in range(HEADS)], axis=1
    )
    dv, in_gain, in_shift = norm_back(red_s[...], gain(1), nn(dm, wmt[...]))
    vg[1:2, :] = in_gain
    vg[6:7, :] = in_shift
    dred = dv.astype(BF)
    vg[5:6, :] = colsum(dred.astype(F32))
    dred_t = dred.T
    for dd in range(4):
        value = nn(dred_t, pat[dd]).astype(BF)
        count = n // 4
        for ii in range(count):
            st[:, dd * count + ii, :, 0 : 4 * rb] = value[
                :, 4 * rb * ii : 4 * rb * (ii + 1)
            ].reshape(4, 80, 4 * rb)
    value = nn(dm.T, memin[...]).astype(BF)
    value = jnp.concatenate(
        [value[128 * h : 128 * h + 64] for h in range(HEADS)]
        + [value[128 * h + 64 : 128 * h + 128] for h in range(HEADS)],
        axis=0,
    ).reshape(4, 2, 80, D)
    for i in range(n):
        st[:, i, :, 4 * rb : 6 * rb] = jnp.concatenate(
            [value[:, v, :, rb * i : rb * i + rb] for v in range(2)], axis=2
        )
    t_one, t_two, t_three, t_four = scatter(2, st, rt1, rt2, rt3)
    t_one()
    m_two()

    for dd in range(4):
        back = nn(dred, wrt[dd])
        back = jnp.concatenate([back, jnp.zeros((keys, 64), F32)], axis=1)
        for i in range(band // 2):
            start = (2 * i + dd // 2) * side + dd % 2
            for t in range(3):
                a3[t, pl.ds(start, half, stride=2), :] = back[
                    i * half : (i + 1) * half, 128 * t : 128 * t + 128
                ]
    t_two()

    def back_first(c, carry):
        at = rows(c * QC, QC)
        e = nn(dq[at, :], wqt[...]) + jnp.concatenate([a3[t, at, :] for t in range(3)], axis=1)[:, 0:D]
        value, in_gain, in_shift = norm_back(x_s[at, :].astype(F32), gain(0), e)
        bn[at, :] = (mid[at, :] + value).astype(BF)
        return (carry[0] + in_gain, carry[1] + in_shift)

    sums = lax.fori_loop(0, chunks, back_first, (zero_row, zero_row))
    token_out = pltpu.make_async_copy(bn, tgrad_ref, loc.at[12])
    token_out.start()
    vg[0:1, :] = sums[0]
    vg[3:4, :] = sums[1]
    for i in range(n):
        sv[i, :, 0 : 4 * rb] = hg[:, 4 * rb * i : 4 * rb * (i + 1)].astype(BF)
        sv[i, :, 4 * rb : 5 * rb] = vg[:, rb * i : rb * i + rb].astype(BF)

    v_core = remote(sv, rv1, rs_s.at[3, 0], rs_r.at[3, 0], me, j1)
    v_core.start()
    m_three()
    v_core.wait_send()
    v_core.wait_recv()
    sv[...] = (sv[...].astype(F32) + rv1[...].astype(F32)).astype(BF)
    v_x = remote(sv, rv2, rs_s.at[3, 1], rs_r.at[3, 1], me, j2)
    v_x.start()
    t_three()
    v_x.wait_send()
    v_x.wait_recv()
    sv[...] = (sv[...].astype(F32) + rv2[...].astype(F32)).astype(BF)

    def v_copy(k, peer):
        return remote(sv.at[peer], rv3.at[k], rd_s.at[3, k], rd_r.at[3, k], peer, j)

    peers(lambda k, peer, source: v_copy(k, peer).start())

    own_f = f_four()
    own_ref[0:80, tl + ml : tl + ml + own_f.shape[1]] = own_f
    squares = jnp.sum(own_f[:, 0 : 8 * rb] * own_f[:, 0 : 8 * rb])
    own_m = m_four()
    own_ref[0:80, tl : tl + ml] = own_m
    squares += jnp.sum(own_m[:, 0 : 2 * rb] * own_m[:, 0 : 2 * rb])

    def land_vec(k, peer, source):
        d = v_copy(k, peer)
        d.wait_send()
        d.wait_recv()

    peers(land_vec)
    own_v = lax.fori_loop(
        1, n, lambda k, total: total + rv3[k].astype(F32), sv[me].astype(F32)
    )
    own_ref[80:96, 0:vl] = own_v
    first_band = (j == 0).astype(jnp.int32).astype(F32)
    vec_squares = jnp.sum(own_v[0:11, 0 : 5 * rb] * own_v[0:11, 0 : 5 * rb])
    own_t = t_four()
    own_ref[0:80, 0:tl] = own_t
    squares += jnp.sum(own_t[:, 0 : 6 * rb] * own_t[:, 0 : 6 * rb])
    squares += first_band * vec_squares

    nrm[me] = jnp.full((8, 128), squares, F32)

    def send_norm(k, peer, source):
        remote(nrm.at[me], nrm.at[me], nd_s.at[k], nd_r.at[k], peer, j).start()

    def wait_norm(k, peer, source):
        d = remote(nrm.at[source], nrm.at[source], nd_s.at[k], nd_r.at[k], peer, j)
        d.wait_send()
        d.wait_recv()

    peers(send_norm)
    peers(wait_norm)
    nrs[j] = lax.fori_loop(1, n, lambda k, total: total + nrm[k], nrm[0])
    for t, other in enumerate((j1, j2, j3)):
        remote(nrs.at[j], nrs.at[j], ns_s.at[t], ns_r.at[t], me, other).start()
    for t, other in enumerate((j1, j2, j3)):
        d = remote(nrs.at[other], nrs.at[other], ns_s.at[t], ns_r.at[t], me, other)
        d.wait_send()
        d.wait_recv()
    own_ref[80:88, vl : vl + 128] = nrs[0] + nrs[1] + nrs[2] + nrs[3]

    peers(wait_out)
    own_out.wait()
    token_out.wait()


def update_kernel(rb, vl, tl, ml, rates, decays, own_ref, outt_ref, tg_ref, *refs):
    weights, firsts, seconds = refs[0:9], refs[9:18], refs[18:27]
    out_ref, tok_ref, norm_ref = refs[27:30]
    news = refs[30:57]
    sems = refs[57]
    copies = [
        pltpu.make_async_copy(outt_ref, out_ref, sems.at[0]),
        pltpu.make_async_copy(tg_ref, tok_ref, sems.at[1]),
    ]
    for copy in copies:
        copy.start()
    total = own_ref[80:81, vl : vl + 128]
    norm = jnp.sqrt(total)
    norm_ref[...] = norm
    clip = jnp.minimum(1.0, MAX_NORM / (norm + 1e-06))[:, 0:1]
    turned_t = own_ref[0:80, 0:tl].T
    turned_m = own_ref[0:80, tl : tl + ml].T
    turned_f = own_ref[0:80, tl + ml :].T
    grads = (
        turned_m[0:rb],
        turned_t[0 : 4 * rb],
        jnp.concatenate([turned_t[(4 + v) * rb : (5 + v) * rb] for v in range(2)], axis=1),
        turned_m[rb : 2 * rb],
        jnp.concatenate([turned_f[(4 + v) * rb : (5 + v) * rb] for v in range(4)], axis=1),
        turned_f[0 : 4 * rb],
        own_ref[80:83, 4 * rb : 5 * rb],
        own_ref[83:91, 4 * rb : 5 * rb],
        own_ref[80:91, 0 : 4 * rb],
    )
    for at in range(9):
        clipped = clip * grads[at]
        weight = weights[at][...]
        first = BETA_ONE * firsts[at][...] + (1.0 - BETA_ONE) * clipped
        second = BETA_TWO * seconds[at][...] + (1.0 - BETA_TWO) * clipped * clipped
        direction = (
            first
            / (1.0 - BETA_ONE**STEP)
            / (jnp.sqrt(second / (1.0 - BETA_TWO**STEP)) + ADAM_EPS)
        )
        news[at][...] = weight - rates[at] * (direction + decays[at] * weight)
        news[9 + at][...] = first
        news[18 + at][...] = second
    for copy in copies:
        copy.wait()


def on_device(n, *args):
    tokens, buckets, cotangent = args[0:3]
    weights, firsts, seconds = args[3:12], args[12:21], args[21:30]
    band, side, width = tokens.shape[1:4]
    count = band * side
    keys = count // 4
    rb = weights[0].shape[0]
    piece = cotangent.shape[3]
    chunks = count // QC
    wide = up(8 * rb, 128)
    tl = up(6 * rb, 128)
    ml = up(2 * rb, 128)
    vl = up(5 * rb, 128)
    total = tl + ml + wide
    turned = piece % 128 == 0
    block = (n, D, piece) if turned else (n, piece, D)
    vm = pltpu.VMEM
    dma = pltpu.SemaphoreType.DMA
    scratch = [
        vm((count, D), BF),
        *[vm(weights[at].shape, F32) for at in (0, 1, 2, 3, 4, 5, 6, 7, 8)],
        vm((n, 16, vl), BF),
        vm((4, n, 80, max(wide, tl + ml)), BF),
        vm((4, n, 80, wide), BF),
        vm((16, D), F32),
        vm((16, FF), F32),
        vm((D, D), BF),
        vm((2 * D, D), BF),
        vm((D, D), BF),
        vm((2 * D, D), BF),
        vm((2 * D, D), BF),
        vm((4, D, D), BF),
        vm((FF, D), BF),
        vm((D, FF), BF),
        vm((3, count, 128), F32),
        vm((count, D), BF),
        vm((4, keys, D), BF),
        vm((keys, D), F32),
        vm((keys, D), BF),
        vm((HEADS, 4, keys, 128), BF),
        vm((HEADS, 128, count), BF),
        vm((count, 128), BF),
        vm((chunks, 128, QC), BF),
        vm((HEADS, count, 128), BF),
        vm((HEADS, chunks, 128, QC), BF),
        vm((HEADS, chunks, count, QC), BF),
        vm((chunks, D, QC), BF),
        vm((count, D), BF),
        vm((HEADS, chunks, 1, QC), F32),
        vm((HEADS, chunks, 1, QC), F32),
        vm((count, D), F32),
        vm((count, D), BF),
        vm((D, count), BF),
        vm((count + 2 * side, FF), BF),
        vm((2, side, FF), BF),
        vm((count + 2 * side, FF), BF),
        vm((count, FF), BF),
        vm(block, BF),
        vm(block, BF),
        vm((D, count), BF),
        vm((count, D), BF),
        vm((2, side, FF), BF),
        vm((HEADS, count, 128), BF),
        vm((count, 128), F32),
        vm((HEADS, 2, keys, 128), BF),
        vm((HEADS, keys, 128), BF),
        vm((chunks, D, QC), BF),
        vm((16, FF), F32),
        vm((16, D), F32),
        vm((2, n, 80, wide), BF),
        vm((n, 80, wide), BF),
        vm((n, 80, wide), BF),
        vm((2, n, 80, tl), BF),
        vm((n, 80, tl), BF),
        vm((n, 80, tl), BF),
        vm((2, n, 80, ml), BF),
        vm((n, 80, ml), BF),
        vm((n, 80, ml), BF),
        vm((n, 16, vl), BF),
        vm((n, 16, vl), BF),
        vm((n, 16, vl), BF),
        vm((n, 16, vl), BF),
        vm((n, 8, 128), F32),
        vm((4, 8, 128), F32),
        vm((side, 128), F32),
        vm((side, 128), F32),
        dma((13,)),
        *[dma((n,)) for _ in range(6)],
        dma((2, 3)),
        dma((2, 3)),
        *[dma((n,)) for _ in range(4)],
        dma((HEADS, 3)),
        dma((HEADS, 3)),
        dma((4,)),
        dma((4,)),
        dma((HEADS, 3)),
        dma((HEADS, 3)),
        dma((4, 3)),
        dma((4, 3)),
        dma((4, n)),
        dma((4, n)),
        dma((n,)),
        dma((n,)),
        dma((3,)),
        dma((3,)),
    ]
    anywhere = pl.BlockSpec(memory_space=pl.ANY)
    in_vmem = pl.BlockSpec(memory_space=pltpu.VMEM)
    out_t, token_grad, own = pl.pallas_call(
        functools.partial(block_kernel, n, side, band),
        out_shape=(
            jax.ShapeDtypeStruct(block, BF),
            jax.ShapeDtypeStruct((count, D), BF),
            jax.ShapeDtypeStruct((96, total), F32),
        ),
        in_specs=[pl.BlockSpec(memory_space=pltpu.SMEM)] + [anywhere] * 11,
        out_specs=(anywhere, anywhere, in_vmem),
        scratch_shapes=scratch,
        compiler_params=pltpu.CompilerParams(
            collective_id=0, has_side_effects=True, vmem_limit_bytes=VMEM_LIMIT
        ),
    )(
        buckets,
        tokens.reshape(count, width),
        jnp.swapaxes(cotangent, 3, 4).reshape(block) if turned else cotangent.reshape(block),
        *weights,
    )
    rates = (
        D ** (-0.5),
        (4 * D) ** (-0.5),
        D ** (-0.5),
        OUT_FAN ** (-0.5),
        D ** (-0.5),
        FF ** (-0.5),
        GAIN_RATE,
        VECTOR_RATE,
        VECTOR_RATE,
    )
    decays = (DECAY_RATE,) * 6 + (0.0,) * 3
    shapes = tuple(jax.ShapeDtypeStruct(w.shape, F32) for w in weights)
    results = pl.pallas_call(
        functools.partial(update_kernel, rb, vl, tl, ml, rates, decays),
        out_shape=(
            jax.ShapeDtypeStruct(block, BF),
            jax.ShapeDtypeStruct((count, D), BF),
            jax.ShapeDtypeStruct((1, 128), F32),
        )
        + shapes * 3,
        in_specs=[in_vmem, anywhere, anywhere] + [in_vmem] * 27,
        out_specs=(anywhere, anywhere) + (in_vmem,) * 28,
        scratch_shapes=[dma((2,))],
    )(own, out_t, token_grad, *weights, *firsts, *seconds)
    if turned:
        block_output = jnp.swapaxes(results[0].reshape(n, 1, 1, width, piece), 3, 4)
    else:
        block_output = results[0].reshape(n, 1, 1, piece, width)
    return (
        block_output,
        results[1].reshape(1, band, side, width),
        results[2][0, 0],
        *results[3:],
    )


def solution(mesh):
    matrix = (P("dp", "seq"),) * 6 + (P(None, "dp"),) * 3
    return jax.shard_map(
        functools.partial(on_device, mesh.shape["dp"]),
        mesh=mesh,
        in_specs=(
            P("dp", "seq", None, None),
            P("dp"),
            P(None, "seq", "dp", None, None),
            *(matrix * 3),
        ),
        out_specs=(
            P(None, "seq", "dp", None, None),
            P("dp", "seq", None, None),
            P(),
            *(matrix * 3),
        ),
        check_vma=False,
    )
```

```python
import functools

import jax
import jax.numpy as jnp
from jax import lax
from jax.experimental import pallas as pl
from jax.experimental.pallas import tpu as pltpu
from jax.sharding import PartitionSpec as P

D = 320
HEADS = 5
HEAD = 64
FF = 1280
STEP = 10
OUT_FAN = 5

NORM_EPS = 1e-06
MAX_NORM = 1.0
BETA_ONE = 0.9
BETA_TWO = 0.95
ADAM_EPS = 1e-08
DECAY_RATE = 0.01
VECTOR_RATE = 0.3
GAIN_RATE = 0.8
MASKED = -1e30

BF = jnp.bfloat16
F32 = jnp.float32
MESH = pl.DeviceIdType.MESH
QC = 256
CUT = 48
VMEM_LIMIT = 63 * 1024 * 1024


def nn(a, b):
    return lax.dot_general(a, b, (((1,), (0,)), ((), ())), preferred_element_type=F32)


def nt(a, b):
    return lax.dot_general(a, b, (((1,), (1,)), ((), ())), preferred_element_type=F32)


def up(n, m):
    return (n + m - 1) // m * m


def norm_parts(v):
    centered = v - jnp.mean(v, axis=-1, keepdims=True)
    rstd = lax.rsqrt(jnp.mean(centered * centered, axis=-1, keepdims=True) + NORM_EPS)
    return centered * rstd, rstd


def norm_back(v, gain, e):
    vhat, rstd = norm_parts(v)
    u = e * gain
    dv = rstd * (
        u
        - jnp.mean(u, axis=-1, keepdims=True)
        - vhat * jnp.mean(u * vhat, axis=-1, keepdims=True)
    )
    return dv, jnp.sum(e * vhat, axis=0, keepdims=True), jnp.sum(e, axis=0, keepdims=True)


def colsum(v):
    return jnp.sum(v, axis=0, keepdims=True)


def rows(start, size):
    return pl.ds(pl.multiple_of(start, 16), size)


def block_kernel(
    n,
    side,
    band,
    qa,
    bucket_ref,
    tok_ref,
    cot_ref,
    wq_ref,
    wr_ref,
    wm_ref,
    wo_ref,
    w1_ref,
    w2_ref,
    gains_ref,
    biases_ref,
    hidden_ref,
    out_ref,
    tgrad_ref,
    own_ref,
    x_s,
    fq,
    fr,
    fm,
    fo,
    f1,
    f2,
    fg,
    fb,
    fh,
    gvec,
    gt,
    gm,
    gf,
    vp,
    hp,
    wqt,
    wqp,
    wot,
    wop,
    wmt,
    wrt,
    w1t,
    w2t,
    a3,
    abf,
    pat,
    red_s,
    memin,
    kv,
    kvt,
    kmask,
    qmask,
    qnat,
    qt,
    prob,
    att_t,
    att_n,
    rtot,
    delta,
    mid,
    bn,
    bn_t,
    hidp,
    hidh,
    act,
    gp,
    out_t,
    dy_in,
    dy_t,
    dy,
    dzh,
    datn,
    rk1,
    rk2,
    dq_t,
    hg,
    vg,
    rf1,
    rf4,
    rf5,
    rt1,
    rt2,
    rt3,
    rt4,
    rt5,
    rm1,
    rm2,
    rm3,
    sv,
    rv1,
    rv2,
    rv3,
    nrm,
    nrs,
    maskl,
    maskr,
    loc,
    vg_s,
    vg_r,
    gd_s,
    gd_r,
    gx_s,
    gx_r,
    co_s,
    co_r,
    ou_s,
    ou_r,
    kv_s,
    kv_r,
    ha_s,
    ha_r,
    dk_s,
    dk_r,
    rs_s,
    rs_r,
    rd_s,
    rd_r,
    nd_s,
    nd_r,
    ns_s,
    ns_r,
):
    me = lax.axis_index("dp")
    j = lax.axis_index("seq")
    j1 = j + 1 - 2 * lax.rem(j, 2)
    j2 = lax.rem(j + 2, 4)
    j3 = 3 - j
    tokens = band * side
    chunks = tokens // QC
    rb = wq_ref.shape[0]
    piece = tokens // n
    keys = kv.shape[2]
    turned = cot_ref.shape[1] == D
    tl = gt.shape[3]
    fl = gf.shape[3]
    vl = gvec.shape[2]

    def remote(src, dst, ss, rs, dp, seq):
        return pltpu.make_async_remote_copy(
            src_ref=src,
            dst_ref=dst,
            send_sem=ss,
            recv_sem=rs,
            device_id=(dp, seq),
            device_id_type=MESH,
        )

    def both(copy):
        copy.wait_send()
        copy.wait_recv()

    def peers(body):
        def step(k, carry):
            body(k, lax.rem(me + k, n), lax.rem(me + n - k, n))
            return carry

        lax.fori_loop(1, n, step, 0)

    loads = [
        pltpu.make_async_copy(src, dst, loc.at[at])
        for at, (src, dst) in enumerate(
            (
                (gains_ref, fg),
                (biases_ref, fb),
                (hidden_ref, fh),
                (wr_ref, fr),
                (wm_ref, fm),
                (wq_ref, fq),
                (wo_ref, fo),
                (w1_ref, f1),
                (w2_ref, f2),
                (tok_ref, x_s),
            )
        )
    ]
    for copy in loads:
        copy.start()
    own_cot = pltpu.make_async_copy(cot_ref.at[me], dy_in.at[me], loc.at[10])
    own_cot.start()

    barrier = pltpu.get_barrier_semaphore()

    def greet(k, peer, source):
        pl.semaphore_signal(barrier, inc=1, device_id=(peer, j), device_id_type=MESH)

    peers(greet)
    for other in (j1, j2, j3):
        pl.semaphore_signal(barrier, inc=1, device_id=(me, other), device_id_type=MESH)

    for copy in loads[:5]:
        copy.wait()
    hidden16 = jnp.concatenate([fh[...], jnp.zeros((5, 4 * rb), F32)], axis=0)
    small16 = jnp.concatenate([fg[...], fb[...], jnp.zeros((5, rb), F32)], axis=0)
    gvec[me] = jnp.concatenate(
        [hidden16, small16, jnp.zeros((16, vl - 5 * rb), F32)], axis=1
    ).astype(BF)
    wm_t = fm[...].T
    gt[j, me] = jnp.concatenate(
        [fr[...].T, wm_t[0:80], wm_t[80:160], jnp.zeros((80, tl - 6 * rb), F32)], axis=1
    ).astype(BF)

    def send_vec(k, peer, source):
        remote(gvec.at[me], gvec.at[me], vg_s.at[k], vg_r.at[k], peer, j).start()

    def wait_vec(k, peer, source):
        both(remote(gvec.at[source], gvec.at[source], vg_s.at[k], vg_r.at[k], peer, j))

    def to_peers(at, piece_of, slot):
        def start():
            def body(k, peer, source):
                remote(
                    piece_of(slot, me), piece_of(slot, me), gd_s.at[at, k], gd_r.at[at, k], peer, j
                ).start()

            peers(body)

        def wait():
            def body(k, peer, source):
                ref = piece_of(slot, source)
                both(remote(ref, ref, gd_s.at[at, k], gd_r.at[at, k], peer, j))

            peers(body)

        return start, wait

    def swap(at, t, mine, theirs, other):
        def start():
            remote(mine, mine, gx_s.at[at, t], gx_r.at[at, t], me, other).start()

        def wait():
            remote(mine, mine, gx_s.at[at, t], gx_r.at[at, t], me, other).wait_send()
            remote(theirs, theirs, gx_s.at[at, t], gx_r.at[at, t], me, other).wait_recv()

        return start, wait

    def t_low(slot, i):
        return gt.at[slot, i, 0:CUT]

    def t_high(slot, i):
        return gt.at[slot, i, CUT:80]

    def whole_m(slot, i):
        return gm.at[slot, i]

    def whole_f(slot, i):
        return gf.at[slot, i]

    t_dp, t_dp_wait = to_peers(0, t_low, j)
    t_dpa, t_dpa_wait = to_peers(1, t_high, j)
    t_dpb, t_dpb_wait = to_peers(2, t_high, j2)
    m_dp, m_dp_wait = to_peers(3, whole_m, j)
    f_dpa, f_dpa_wait = to_peers(4, whole_f, j)
    f_dpb, f_dpb_wait = to_peers(5, whole_f, j2)
    t_x, t_x_wait = swap(0, 0, gt.at[j, :, 0:CUT], gt.at[j2, :, 0:CUT], j2)
    t_x0, t_x0_wait = swap(0, 1, t_high(j, me), t_high(j2, me), j2)
    t_ca, t_ca_wait = swap(0, 2, gt.at[j], gt.at[j1], j1)
    t_cb, t_cb_wait = swap(0, 3, gt.at[j2], gt.at[j3], j1)
    m_x, m_x_wait = swap(1, 0, gm.at[j], gm.at[j2], j2)
    m_ca, m_ca_wait = swap(1, 2, gm.at[j], gm.at[j1], j1)
    m_cb, m_cb_wait = swap(1, 3, gm.at[j2], gm.at[j3], j1)
    f_x0, f_x0_wait = swap(2, 1, gf.at[j, me], gf.at[j2, me], j2)
    f_ca, f_ca_wait = swap(2, 2, gf.at[j], gf.at[j1], j1)
    f_cb, f_cb_wait = swap(2, 3, gf.at[j2], gf.at[j3], j1)

    pl.semaphore_wait(barrier, n - 1 + 3)
    t_x0()
    peers(send_vec)
    t_dp()

    for copy in loads[5:9]:
        copy.wait()
    wq_t = fq[...].T
    gm[j, me] = jnp.concatenate(
        [
            wq_t[0:32],
            wq_t[32:64],
            jnp.concatenate([wq_t[64:80], jnp.zeros((16, rb), F32)], axis=0),
            jnp.zeros((32, 128 - 3 * rb), F32),
        ],
        axis=1,
    ).astype(BF)
    w1_t = f1[...].T
    gf[j, me] = jnp.concatenate(
        [f2[...].T]
        + [w1_t[80 * v : 80 * v + 80] for v in range(4)]
        + [fo[...].T, jnp.zeros((80, fl - 9 * rb), F32)],
        axis=1,
    ).astype(BF)
    f_x0()
    t_x0_wait()
    t_dpa()
    t_dpb()
    m_dp()

    peers(wait_vec)
    hp[...] = jnp.concatenate([gvec[i, :, 0 : 4 * rb] for i in range(n)], axis=1).astype(F32)
    vp[...] = jnp.concatenate(
        [gvec[i, :, 4 * rb : 5 * rb] for i in range(n)], axis=1
    ).astype(F32)

    def gain(k):
        return vp[k : k + 1, :]

    def shift(k):
        return vp[3 + k : 4 + k, :]

    loads[9].wait()

    def norm_one(c, carry):
        at = rows(c * QC, QC)
        vhat, _ = norm_parts(x_s[at, :].astype(F32))
        low = (vhat * gain(0) + shift(0)).astype(BF)
        abf[at, :] = low
        wide = jnp.concatenate([low.astype(F32), jnp.zeros((QC, 64), F32)], axis=1)
        for t in range(3):
            a3[t, at, :] = wide[:, 128 * t : 128 * t + 128]
        return carry

    lax.fori_loop(0, chunks, norm_one, 0)
    half = side // 2
    for dd in range(4):
        for i in range(band // 2):
            start = (2 * i + dd // 2) * side + dd % 2
            cut = jnp.concatenate(
                [a3[t, pl.ds(start, half, stride=2), :] for t in range(3)], axis=1
            )
            pat[dd, i * half : (i + 1) * half, :] = cut[:, 0:D].astype(BF)

    bucket = bucket_ref[0]
    k_row = lax.broadcasted_iota(jnp.int32, (4 * keys, 128), 0)
    k_lane = lax.broadcasted_iota(jnp.int32, (4 * keys, 128), 1)
    k_id = (lax.div(k_row, half) >= half // 2).astype(jnp.int32) * 2 + (
        lax.rem(k_row, half) >= half // 2
    ).astype(jnp.int32)
    off = (k_id != k_lane).astype(jnp.int32) * bucket * (k_lane < 4).astype(jnp.int32)
    kmask[...] = (off.astype(F32) * MASKED).astype(BF)
    q_row = lax.broadcasted_iota(jnp.int32, (128, tokens), 0)
    place = lax.broadcasted_iota(jnp.int32, (128, tokens), 1)
    q_id = (lax.div(place, side) + j * band >= half).astype(jnp.int32) * 2 + (
        lax.rem(place, side) >= half
    ).astype(jnp.int32)
    qmask[...] = (q_id == q_row).astype(F32).astype(BF)
    col = lax.broadcasted_iota(jnp.int32, (side, 128), 0)
    maskl[...] = (
        (col > 0).astype(jnp.int32) * (1 - bucket * (col == half).astype(jnp.int32))
    ).astype(F32)
    maskr[...] = (
        (col < side - 1).astype(jnp.int32) * (1 - bucket * (col == half - 1).astype(jnp.int32))
    ).astype(F32)
    top_ok = (
        (j > 0).astype(jnp.int32) * (1 - bucket * (j * band == half).astype(jnp.int32))
    ).astype(F32)
    low_ok = (
        (j < 3).astype(jnp.int32) * (1 - bucket * ((j + 1) * band == half).astype(jnp.int32))
    ).astype(F32)

    t_dp_wait()
    t_x()
    t_dpa_wait()
    t_dpb_wait()
    m_dp_wait()
    m_x()
    f_x0_wait()
    f_dpa()
    f_dpb()
    t_x_wait()
    t_ca()
    t_cb()
    m_x_wait()
    m_ca()
    m_cb()
    t_ca_wait()
    t_cb_wait()

    for s in range(4):
        span = slice(80 * s, 80 * s + 80)

        def lanes(lo, hi, over):
            return jnp.concatenate([gt[s, i, :, lo:hi] for i in over], axis=1)

        for dd in range(4):
            wrt[dd, span, :] = lanes(0, 4 * rb, range(dd * n // 4, (dd + 1) * n // 4))
        for v in range(2):
            wop[160 * s + 80 * v : 160 * s + 80 * v + 80, :] = lanes(
                (4 + v) * rb, (5 + v) * rb, range(n)
            )
    for h in range(HEADS):
        wmt[128 * h : 128 * h + 64, :] = wop[HEAD * h : HEAD * h + HEAD, :]
        wmt[128 * h + 64 : 128 * h + 128, :] = wop[D + HEAD * h : D + HEAD * h + HEAD, :]

    red = shift(2) + nt(pat[0], wrt[0])
    for dd in range(1, 4):
        red = red + nt(pat[dd], wrt[dd])
    red_s[...] = red
    vhat, _ = norm_parts(red)
    low = (vhat * gain(1) + shift(3)).astype(BF)
    memin[...] = low
    zero64 = jnp.zeros((1, HEAD), F32)
    value_shift = jnp.concatenate(
        [
            part
            for h in range(HEADS)
            for part in (zero64, shift(4)[:, HEAD * h : HEAD * h + HEAD])
        ],
        axis=1,
    )
    memory = (nt(low, wmt[...]) + value_shift).astype(BF)
    for h in range(HEADS):
        kv[h, j] = memory[:, 128 * h : 128 * h + 128]

    def kv_copy(h, slot, t, other):
        return remote(
            kv.at[h, slot], kv.at[h, slot], kv_s.at[h, t], kv_r.at[h, t], me, other
        )

    def kv_send(h, carry):
        kv_copy(h, j, 0, j2).start()
        kv_copy(h, j, 1, j1).start()
        return carry

    lax.fori_loop(0, HEADS, kv_send, 0)

    m_ca_wait()
    m_cb_wait()
    for s in range(4):
        at = 80 * s
        wqt[at : at + 32, :] = jnp.concatenate([gm[s, i, :, 0:rb] for i in range(n)], axis=1)
        wqt[at + 32 : at + 64, :] = jnp.concatenate(
            [gm[s, i, :, rb : 2 * rb] for i in range(n)], axis=1
        )
        wqt[at + 64 : at + 80, :] = jnp.concatenate(
            [gm[s, i, 0:16, 2 * rb : 3 * rb] for i in range(n)], axis=1
        )
    for h in range(HEADS):
        wqp[128 * h : 128 * h + 64, :] = wqt[HEAD * h : HEAD * h + HEAD, :]
        wqp[128 * h + 64 : 128 * h + 128, :] = jnp.zeros((64, D), BF)

    query_shift = jnp.concatenate(
        [
            part
            for h in range(HEADS)
            for part in (shift(1)[:, HEAD * h : HEAD * h + HEAD], zero64)
        ],
        axis=1,
    )

    def across(c):
        return pl.ds(pl.multiple_of(c * QC, QC), QC)

    def queries(c, carry):
        at = rows(c * QC, QC)
        q = (nt(abf[at, :], wqp[...]) + query_shift).astype(BF) * jnp.asarray(HEAD**-0.5, BF)
        for h in range(HEADS):
            tile = q[:, 128 * h : 128 * h + 128]
            qnat[h, at, :] = tile
            qt[h, :, across(c)] = tile.T
        return carry

    lax.fori_loop(0, chunks, queries, 0)

    def send_cot(k, peer, source):
        remote(cot_ref.at[peer], dy_in.at[me], co_s.at[k], co_r.at[k], peer, j).start()

    def wait_cot(k, peer, source):
        both(remote(cot_ref.at[peer], dy_in.at[source], co_s.at[k], co_r.at[k], peer, j))

    def kv_forward(h):
        kv_copy(h, j2, 0, j2).wait_recv()
        kv_copy(h, j2, 2, j1).start()

    kv_forward(0)

    def attend(h, carry):
        @pl.when(h < HEADS - 1)
        def _():
            kv_forward(h + 1)

        @pl.when(h == HEADS - 1)
        def _():
            f_dpa_wait()
            f_dpb_wait()
            f_ca()
            f_cb()
            peers(send_cot)

        kv_copy(h, j, 0, j2).wait_send()
        kv_copy(h, j, 1, j1).wait_send()
        kv_copy(h, j2, 2, j1).wait_send()
        kv_copy(h, j1, 1, j1).wait_recv()
        kv_copy(h, j3, 2, j1).wait_recv()
        tile = kv[h].reshape(4 * keys, 128)
        kvt[h] = tile.T
        left = jnp.concatenate([tile, kmask[...]], axis=1)
        values = jnp.concatenate([kvt[h, 64:128, :], jnp.ones((16, 4 * keys), BF)], axis=0)
        for c in range(tokens // qa):
            cut = slice(c * qa, (c + 1) * qa)
            scores = nn(left, jnp.concatenate([qt[h, :, cut], qmask[:, cut]], axis=0))
            largest = jnp.max(scores, axis=0, keepdims=True)
            powers = jnp.exp(scores - largest).astype(BF)
            prob[h, :, cut] = powers
            got = nn(values, powers)
            scale = 1.0 / got[64:65, :]
            rtot[h, :, cut] = scale
            att_t[rows(h * HEAD, HEAD), cut] = (got[0:64, :] * scale).astype(BF)
        return carry

    lax.fori_loop(0, HEADS, attend, 0)

    f_ca_wait()
    f_cb_wait()
    for s in range(4):
        span = slice(80 * s, 80 * s + 80)
        w2t[span, :] = jnp.concatenate([gf[s, i, :, 0 : 4 * rb] for i in range(n)], axis=1)
        for v in range(4):
            at = 320 * s + 80 * v
            w1t[at : at + 80, :] = jnp.concatenate(
                [gf[s, i, :, (4 + v) * rb : (5 + v) * rb] for i in range(n)], axis=1
            )
        wot[span, :] = jnp.concatenate(
            [gf[s, i, :, 8 * rb : 9 * rb] for i in range(n)], axis=1
        )
    wop_full = wot[...].T
    for h in range(HEADS):
        wop[128 * h : 128 * h + 64, :] = jnp.zeros((64, D), BF)
        wop[128 * h + 64 : 128 * h + 128, :] = wop_full[HEAD * h : HEAD * h + HEAD, :]

    def middle(c, carry):
        at = rows(c * QC, QC)
        att = att_t[:, across(c)].T
        att_n[at, :] = att
        value = x_s[at, :].astype(F32) + nt(att, wot[...]) + shift(5)
        mid[at, :] = value
        vhat, _ = norm_parts(value)
        low = (vhat * gain(2) + shift(6)).astype(BF)
        bn[at, :] = low
        bn_t[:, across(c)] = low.T
        return carry

    lax.fori_loop(0, chunks, middle, 0)

    edge = tokens - side

    def hidden_of(value):
        return (nt(value, w1t[...]) + hp[9:10, :]).astype(BF)

    ends = hidden_of(jnp.concatenate([bn[0:side, :], bn[edge:tokens, :]], axis=0))
    hidp[side : 2 * side, :] = ends[0:side]
    hidp[tokens : tokens + side, :] = ends[side : 2 * side]
    above = lax.rem(j + 3, 4)
    below = lax.rem(j + 1, 4)

    def rim(buf, halo, at):
        return (
            remote(buf.at[pl.ds(side, side)], halo.at[1], ha_s.at[at], ha_r.at[at], me, above),
            remote(
                buf.at[pl.ds(tokens, side)], halo.at[0], ha_s.at[at + 1], ha_r.at[at + 1], me, below
            ),
        )

    def rim_send(buf, halo, at):
        for copy in rim(buf, halo, at):
            copy.start()

    def rim_wait(buf, halo, at):
        for copy in rim(buf, halo, at):
            both(copy)
        buf[0:side, :] = (halo[0].astype(F32) * top_ok).astype(BF)
        buf[tokens + side : tokens + 2 * side, :] = (halo[1].astype(F32) * low_ok).astype(BF)

    rim_send(hidp, hidh, 0)

    def inner_hidden(c, carry):
        start = side + c * 2 * side
        hidp[rows(start + side, 2 * side), :] = hidden_of(bn[rows(start, 2 * side), :])
        return carry

    lax.fori_loop(0, (tokens - 2 * side) // (2 * side), inner_hidden, 0)

    def tile_at(t):
        return pl.ds(pl.multiple_of(t * 128, 128), 128)

    def taps_of(lanes):
        return [hp[k : k + 1, lanes] for k in range(9)]

    def conv_over(lo, hi, step):
        def conv_tile(t, carry):
            lanes = tile_at(t)
            taps = taps_of(lanes)
            base = hp[10:11, lanes]

            def row(at, inner):
                r = lo + at * step
                around = [hidp[rows((r + a) * side, side), lanes].astype(F32) for a in range(3)]
                parts = [
                    taps[b] * around[0] + taps[3 + b] * around[1] + taps[6 + b] * around[2]
                    for b in range(3)
                ]
                z = (
                    base
                    + parts[1]
                    + maskl[...] * pltpu.roll(parts[0], 1, 0)
                    + maskr[...] * pltpu.roll(parts[2], side - 1, 0)
                )
                cdf = 0.5 + 0.5 * lax.erf(z * (0.5**0.5))
                pdf = jnp.exp(z * z * -0.5) * 0.3989422804014327
                act[rows((r + 1) * side, side), lanes] = (z * cdf).astype(BF)
                gp[rows(r * side, side), lanes] = (cdf + z * pdf).astype(BF)
                return inner

            lax.fori_loop(0, (hi - lo) // step, row, 0)
            return carry

        lax.fori_loop(0, FF // 128, conv_tile, 0)

    conv_over(1, band - 1, 1)
    rim_wait(hidp, hidh, 0)
    conv_over(0, 2 * (band - 1), band - 1)

    def out_chunk(c, carry):
        at = rows(c * QC, QC)
        value = mid[at, :] + nt(act[rows(side + c * QC, QC), :], w2t[...]) + shift(7)
        for p in range(QC // piece):
            part = value[p * piece : (p + 1) * piece, :]
            out_t[c * (QC // piece) + p] = (part.T if turned else part).astype(BF)
        return carry

    lax.fori_loop(0, chunks, out_chunk, 0)

    def send_out(k, peer, source):
        remote(out_t.at[peer], out_ref.at[me], ou_s.at[k], ou_r.at[k], peer, j).start()

    def wait_out(k, peer, source):
        both(remote(out_t.at[peer], out_ref.at[source], ou_s.at[k], ou_r.at[k], peer, j))

    peers(send_out)
    own_out = pltpu.make_async_copy(out_t.at[me], out_ref.at[me], loc.at[11])
    own_out.start()

    own_cot.wait()
    peers(wait_cot)
    for i in range(n):
        if turned:
            dy_t[:, i * piece : (i + 1) * piece] = dy_in[i]
            dy[i * piece : (i + 1) * piece, :] = dy_in[i].T
        else:
            dy[i * piece : (i + 1) * piece, :] = dy_in[i]
    if not turned:
        dy_t[...] = dy[...].T
    vg[...] = jnp.zeros(vg.shape, F32)
    vg[10:11, :] = colsum(dy[...].astype(F32))

    per = 640 // (4 * rb)
    for b in range(2):
        value = nn(dy_t[...], act[side : side + tokens, 640 * b : 640 * b + 640]).astype(BF)
        for ii in range(per):
            gf[:, b * per + ii, :, 0 : 4 * rb] = value[:, 4 * rb * ii : 4 * rb * (ii + 1)].reshape(
                4, 80, 4 * rb
            )

    def slope_of(at):
        return nn(dy[at, :], w2t[...])

    dz = act
    for at in (0, edge):
        dz[side + at : 2 * side + at, :] = (
            slope_of(slice(at, at + side)) * gp[at : at + side, :].astype(F32)
        ).astype(BF)
    rim_send(dz, dzh, 2)

    def inner_slope(c, carry):
        at = rows(side + c * 2 * side, 2 * side)
        dz[rows(2 * side + c * 2 * side, 2 * side), :] = (
            slope_of(at) * gp[at, :].astype(F32)
        ).astype(BF)
        return carry

    lax.fori_loop(0, (tokens - 2 * side) // (2 * side), inner_slope, 0)

    dhid = gp

    def fold(v):
        return jnp.sum(v.reshape(side // 8, 8, 128), axis=0)

    def back_over(lo, hi, step, first):
        def back_tile(t, carry):
            lanes = tile_at(t)
            taps = taps_of(lanes)

            def row(at, sums):
                r = lo + at * step
                around = [dz[rows((r + a) * side, side), lanes].astype(F32) for a in range(3)]
                parts = [
                    taps[b] * around[2] + taps[3 + b] * around[1] + taps[6 + b] * around[0]
                    for b in range(3)
                ]
                low = (
                    parts[1]
                    + maskr[...] * pltpu.roll(parts[0], side - 1, 0)
                    + maskl[...] * pltpu.roll(parts[2], 1, 0)
                ).astype(BF)
                dhid[rows(r * side, side), lanes] = low
                here = around[1]
                moved = [
                    maskr[...] * pltpu.roll(here, side - 1, 0),
                    here,
                    maskl[...] * pltpu.roll(here, 1, 0),
                ]
                found = []
                for a in range(3):
                    source = hidp[rows((r + a) * side, side), lanes].astype(F32)
                    for b in range(3):
                        found.append(fold(moved[b] * source))
                found.append(fold(low.astype(F32)))
                found.append(fold(here))
                return tuple(s + f for s, f in zip(sums, found))

            sums = lax.fori_loop(
                0, (hi - lo) // step, row, tuple(jnp.zeros((8, 128), F32) for _ in range(11))
            )
            found = jnp.concatenate([colsum(s) for s in sums] + [jnp.zeros((5, 128), F32)], axis=0)
            hg[:, lanes] = found if first else hg[:, lanes] + found
            return carry

        lax.fori_loop(0, FF // 128, back_tile, 0)

    back_over(1, band - 1, 1, True)
    rim_wait(dz, dzh, 2)
    back_over(0, 2 * (band - 1), band - 1, False)

    for b in range(2):
        value = nn(bn_t[...], dhid[:, 640 * b : 640 * b + 640]).T.astype(BF)
        value = value.reshape(2, 4, 80, D)
        for i in range(n):
            gf[2 * b : 2 * b + 2, i, :, 4 * rb : 8 * rb] = jnp.concatenate(
                [value[:, v, :, rb * i : rb * i + rb] for v in range(4)], axis=2
            )

    def scatter(at, s, cut, r1, r2, r3, r4, r5, own):
        high = s.shape[2]

        def core():
            return [
                remote(s.at[slot], r1.at[t], rs_s.at[at, t], rs_r.at[at, t], me, j1)
                for t, slot in enumerate((j1, j3))
            ]

        def over_x():
            return remote(
                s.at[j2, :, 0:cut], r2, rs_s.at[at, 2], rs_r.at[at, 2], me, j2
            )

        def high_x():
            return remote(
                s.at[j2, me, cut:high], r5, rs_s.at[at, 3], rs_r.at[at, 3], me, j2
            )

        def low_dp(k, peer):
            return remote(
                s.at[j, peer, 0:cut], r3.at[k], rd_s.at[3 * at, k], rd_r.at[3 * at, k], peer, j
            )

        def high_dp(k, peer, t, slot):
            return remote(
                s.at[slot, peer, cut:high],
                r4.at[t, k],
                rd_s.at[3 * at + 1 + t, k],
                rd_r.at[3 * at + 1 + t, k],
                peer,
                j,
            )

        def one():
            for copy in core():
                copy.start()

        def two():
            for copy in core():
                both(copy)

            def add(i, carry):
                s[j, i] = (s[j, i].astype(F32) + r1[0, i].astype(F32)).astype(BF)
                s[j2, i] = (s[j2, i].astype(F32) + r1[1, i].astype(F32)).astype(BF)
                return carry

            lax.fori_loop(0, n, add, 0)
            if cut > 0:
                over_x().start()
            if cut < high:

                def send(k, peer, source):
                    high_dp(k, peer, 0, j).start()
                    high_dp(k, peer, 1, j2).start()

                peers(send)

        def low_three():
            both(over_x())

            def add(i, carry):
                s[j, i, 0:cut] = (s[j, i, 0:cut].astype(F32) + r2[i].astype(F32)).astype(BF)
                return carry

            lax.fori_loop(0, n, add, 0)
            peers(lambda k, peer, source: low_dp(k, peer).start())

        def high_three():
            def land(k, peer, source):
                both(high_dp(k, peer, 0, j))
                both(high_dp(k, peer, 1, j2))

            peers(land)
            for t, slot in enumerate((j, j2)):
                total = lax.fori_loop(
                    1,
                    n,
                    lambda k, v: v + r4[t, k].astype(F32),
                    s[slot, me, cut:high].astype(F32),
                )
                if t == 0:
                    own[cut:high, :] = total
                else:
                    s[j2, me, cut:high] = total.astype(BF)
            high_x().start()

        def low_four():
            def land(k, peer, source):
                both(low_dp(k, peer))

            peers(land)
            own[0:cut, :] = lax.fori_loop(
                1, n, lambda k, v: v + r3[k].astype(F32), s[j, me, 0:cut].astype(F32)
            )

        def high_four():
            both(high_x())
            own[cut:high, :] = own[cut:high, :] + r5[...].astype(F32)

        return one, two, low_three, high_three, low_four, high_four

    own_t = own_ref.at[0:80, 0:tl]
    own_f = own_ref.at[0:80, tl : tl + fl]
    own_m = own_ref.at[96:128, 0:128]
    f_one, f_two, _, f_three, _, f_four = scatter(
        0, gf, 0, rf1, None, None, rf4, rf5, own_f
    )
    m_one, m_two, m_three, _, m_four, _ = scatter(1, gm, 32, rm1, rm2, rm3, None, None, own_m)
    t_one, t_two, t_low_three, t_high_three, t_low_four, t_high_four = scatter(
        2, gt, CUT, rt1, rt2, rt3, rt4, rt5, own_t
    )

    zero_row = jnp.zeros((1, D), F32)
    dbr = bn
    dbr_t = dy_t

    def back_middle(c, carry):
        at = rows(c * QC, QC)
        value, in_gain, in_shift = norm_back(mid[at, :], gain(2), nn(dhid[at, :], w1t[...]))
        value = value + dy[at, :].astype(F32)
        mid[at, :] = value
        low = value.astype(BF)
        dbr[at, :] = low
        dbr_t[:, across(c)] = low.T
        spread = nt(wop[...], low)
        for h in range(HEADS):
            tile = spread[128 * h : 128 * h + 128, :] * rtot[h, :, across(c)]
            tile_low = tile.astype(BF)
            qt[h, :, across(c)] = tile_low
            datn[h, at, :] = tile_low.T
            delta[h, :, across(c)] = colsum(
                tile_low[64:128, :].astype(F32)
                * att_t[HEAD * h : HEAD * h + HEAD, across(c)].astype(F32)
            )
        return (carry[0] + in_gain, carry[1] + in_shift, carry[2] + colsum(low.astype(F32)))

    sums = lax.fori_loop(0, chunks, back_middle, (zero_row, zero_row, zero_row))
    vg[2:3, :] = sums[0]
    vg[9:10, :] = sums[1]
    vg[8:9, :] = sums[2]
    value = nn(dbr_t[...], att_n[...]).astype(BF)
    for i in range(n):
        gf[:, i, :, 8 * rb : 9 * rb] = value[:, rb * i : rb * i + rb].reshape(4, 80, rb)
    f_one()

    def dkv(h, slot):
        return act.at[rows(slot * keys, keys), tile_at(h)]

    def dk_core(h):
        return [
            remote(dkv(h, slot), rk1.at[h, t], dk_s.at[h, t], dk_r.at[h, t], me, j1)
            for t, slot in enumerate((j1, j3))
        ]

    def dk_x(h):
        return remote(dkv(h, j2), rk2.at[h], dk_s.at[h, 2], dk_r.at[h, 2], me, j2)

    def dk_two(h):
        for copy in dk_core(h):
            both(copy)
        for t, slot in enumerate((j, j2)):
            part = dkv(h, slot)
            part[...] = (part[...].astype(F32) + rk1[h, t].astype(F32)).astype(BF)
        dk_x(h).start()

    def dk_three(h):
        both(dk_x(h))
        qnat[h, 0:keys, :] = (dkv(h, j)[...].astype(F32) + rk2[h].astype(F32)).astype(BF)

    def back_head(h, carry):
        tile = kv[h].reshape(4 * keys, 128)
        total = None
        for c in range(tokens // qa):
            cut = slice(c * qa, (c + 1) * qa)
            powers = prob[h, :, cut]
            slopes = nn(tile, qt[h, :, cut]) - delta[h, :, cut]
            ds = (powers.astype(F32) * slopes).astype(BF)
            part = nn(ds, qnat[h, cut, :]) + nn(powers, datn[h, cut, :])
            prob[h, :, cut] = ds
            total = part if total is None else total + part
        act[0 : 4 * keys, tile_at(h)] = total.astype(BF)
        for copy in dk_core(h):
            copy.start()

        @pl.when(h == 1)
        def _():
            f_two()

        @pl.when(h >= 1)
        def _():
            dk_two(h - 1)

        @pl.when(h >= 2)
        def _():
            dk_three(h - 2)

        return carry

    lax.fori_loop(0, HEADS, back_head, 0)

    def back_query(h, carry):
        for c in range(tokens // qa):
            cut = slice(c * qa, (c + 1) * qa)
            dq_t[rows(h * HEAD, HEAD), cut] = (
                nn(kvt[h, 0:64, :], prob[h, :, cut]) * HEAD**-0.5
            ).astype(BF)
        return carry

    lax.fori_loop(0, 2, back_query, 0)
    dk_two(HEADS - 1)
    dk_three(HEADS - 2)
    lax.fori_loop(2, HEADS, back_query, 0)
    dk_three(HEADS - 1)

    dm = jnp.concatenate([qnat[h, 0:keys, :] for h in range(HEADS)], axis=1)
    dm_sum = colsum(dm.astype(F32))
    vg[7:8, :] = jnp.concatenate(
        [dm_sum[:, 128 * h + 64 : 128 * h + 128] for h in range(HEADS)], axis=1
    )
    dv, in_gain, in_shift = norm_back(red_s[...], gain(1), nn(dm, wmt[...]))
    vg[1:2, :] = in_gain
    vg[6:7, :] = in_shift
    dred = dv.astype(BF)
    vg[5:6, :] = colsum(dred.astype(F32))
    dred_t = dred.T
    for dd in range(4):
        value = nn(dred_t, pat[dd]).astype(BF)
        count = n // 4
        for ii in range(count):
            gt[:, dd * count + ii, :, 0 : 4 * rb] = value[
                :, 4 * rb * ii : 4 * rb * (ii + 1)
            ].reshape(4, 80, 4 * rb)
    value = nn(dm.T, memin[...]).astype(BF)
    value = jnp.concatenate(
        [value[128 * h : 128 * h + 64] for h in range(HEADS)]
        + [value[128 * h + 64 : 128 * h + 128] for h in range(HEADS)],
        axis=0,
    ).reshape(4, 2, 80, D)
    for i in range(n):
        gt[:, i, :, 4 * rb : 6 * rb] = jnp.concatenate(
            [value[:, v, :, rb * i : rb * i + rb] for v in range(2)], axis=2
        )
    t_one()

    dq = att_n

    def flip(c, total):
        low = dq_t[:, across(c)].T
        dq[rows(c * QC, QC), :] = low
        return total + colsum(low.astype(F32))

    vg[4:5, :] = lax.fori_loop(0, chunks, flip, zero_row)
    value = nn(dq_t[...], abf[...]).astype(BF)
    for i in range(n):
        part = value[:, rb * i : rb * i + rb].reshape(4, 80, rb)
        gm[:, i, :, 0 : 3 * rb] = jnp.concatenate(
            [
                part[:, 0:32],
                part[:, 32:64],
                jnp.concatenate([part[:, 64:80], jnp.zeros((4, 16, rb), BF)], axis=1),
            ],
            axis=2,
        )
    m_one()
    t_two()

    for dd in range(4):
        back = nn(dred, wrt[dd])
        back = jnp.concatenate([back, jnp.zeros((keys, 64), F32)], axis=1)
        for i in range(band // 2):
            start = (2 * i + dd // 2) * side + dd % 2
            for t in range(3):
                a3[t, pl.ds(start, half, stride=2), :] = back[
                    i * half : (i + 1) * half, 128 * t : 128 * t + 128
                ]
    m_two()

    def back_first(c, carry):
        at = rows(c * QC, QC)
        e = nn(dq[at, :], wqt[...]) + jnp.concatenate([a3[t, at, :] for t in range(3)], axis=1)[:, 0:D]
        value, in_gain, in_shift = norm_back(x_s[at, :].astype(F32), gain(0), e)
        bn[at, :] = (mid[at, :] + value).astype(BF)
        return (carry[0] + in_gain, carry[1] + in_shift)

    sums = lax.fori_loop(0, chunks, back_first, (zero_row, zero_row))
    token_out = pltpu.make_async_copy(bn, tgrad_ref, loc.at[12])
    token_out.start()
    vg[0:1, :] = sums[0]
    vg[3:4, :] = sums[1]
    for i in range(n):
        sv[i, :, 0 : 4 * rb] = hg[:, 4 * rb * i : 4 * rb * (i + 1)].astype(BF)
        sv[i, :, 4 * rb : 5 * rb] = vg[:, rb * i : rb * i + rb].astype(BF)

    def v_swap(t, to, other):
        return remote(sv, to, rs_s.at[3, t], rs_r.at[3, t], me, other)

    v_swap(0, rv1, j1).start()
    f_three()
    both(v_swap(0, rv1, j1))
    sv[...] = (sv[...].astype(F32) + rv1[...].astype(F32)).astype(BF)
    v_swap(1, rv2, j2).start()
    m_three()
    both(v_swap(1, rv2, j2))
    sv[...] = (sv[...].astype(F32) + rv2[...].astype(F32)).astype(BF)

    def v_copy(k, peer):
        return remote(sv.at[peer], rv3.at[k], rd_s.at[9, k], rd_r.at[9, k], peer, j)

    peers(lambda k, peer, source: v_copy(k, peer).start())
    t_low_three()
    t_high_three()
    f_four()
    squares = jnp.sum(own_f[:, 0 : 9 * rb] * own_f[:, 0 : 9 * rb])
    m_four()
    squares += jnp.sum(own_m[:, 0 : 2 * rb] * own_m[:, 0 : 2 * rb])
    squares += jnp.sum(own_m[0:16, 2 * rb : 3 * rb] * own_m[0:16, 2 * rb : 3 * rb])

    def land_vec(k, peer, source):
        both(v_copy(k, peer))

    peers(land_vec)
    own_v = lax.fori_loop(
        1, n, lambda k, total: total + rv3[k].astype(F32), sv[me].astype(F32)
    )
    own_ref[80:96, 0:vl] = own_v
    first_band = (j == 0).astype(jnp.int32).astype(F32)
    squares += first_band * jnp.sum(own_v[0:11, 0 : 5 * rb] * own_v[0:11, 0 : 5 * rb])
    t_high_four()
    t_low_four()
    squares += jnp.sum(own_t[:, 0 : 6 * rb] * own_t[:, 0 : 6 * rb])

    nrm[me] = jnp.full((8, 128), squares, F32)

    def send_norm(k, peer, source):
        remote(nrm.at[me], nrm.at[me], nd_s.at[k], nd_r.at[k], peer, j).start()

    def wait_norm(k, peer, source):
        both(remote(nrm.at[source], nrm.at[source], nd_s.at[k], nd_r.at[k], peer, j))

    peers(send_norm)
    peers(wait_norm)
    nrs[j] = lax.fori_loop(1, n, lambda k, total: total + nrm[k], nrm[0])
    for t, other in enumerate((j1, j2, j3)):
        remote(nrs.at[j], nrs.at[j], ns_s.at[t], ns_r.at[t], me, other).start()
    for t, other in enumerate((j1, j2, j3)):
        both(remote(nrs.at[other], nrs.at[other], ns_s.at[t], ns_r.at[t], me, other))
    own_ref[80:88, vl : vl + 128] = nrs[0] + nrs[1] + nrs[2] + nrs[3]

    peers(wait_out)
    own_out.wait()
    token_out.wait()


def update_kernel(rb, vl, tl, rates, decays, *refs):
    own_hbm, outt_hbm, tg_hbm = refs[0:3]
    in_hbm = refs[3:30]
    out_hbm, tok_hbm, norm_hbm = refs[30:33]
    new_hbm = refs[33:60]
    own_ref, out_v, tok_v, norm_v = refs[60:64]
    in_v, new_v = refs[64:91], refs[91:118]
    in_sem, out_sem = refs[118:120]
    loads = [
        pltpu.make_async_copy(src, dst, in_sem.at[at])
        for at, (src, dst) in enumerate(
            [(own_hbm, own_ref), *zip(in_hbm, in_v), (outt_hbm, out_v), (tg_hbm, tok_v)]
        )
    ]
    for load in loads:
        load.start()
    stores = [
        pltpu.make_async_copy(src, dst, out_sem.at[at])
        for at, (src, dst) in enumerate(
            [*zip(new_v, new_hbm), (out_v, out_hbm), (tok_v, tok_hbm), (norm_v, norm_hbm)]
        )
    ]
    loads[0].wait()
    total = own_ref[80:81, vl : vl + 128]
    norm = jnp.sqrt(total)
    norm_v[...] = norm
    stores[29].start()
    clip = jnp.minimum(1.0, MAX_NORM / (norm + 1e-06))[:, 0:1]
    turned_t = own_ref[0:80, 0:tl].T
    turned_f = own_ref[0:80, tl:].T
    turned_q = jnp.concatenate(
        [
            own_ref[96:128, 0:rb],
            own_ref[96:128, rb : 2 * rb],
            own_ref[96:112, 2 * rb : 3 * rb],
        ],
        axis=0,
    ).T
    grads = (
        turned_q,
        turned_t[0 : 4 * rb],
        jnp.concatenate([turned_t[(4 + v) * rb : (5 + v) * rb] for v in range(2)], axis=1),
        turned_f[8 * rb : 9 * rb],
        jnp.concatenate([turned_f[(4 + v) * rb : (5 + v) * rb] for v in range(4)], axis=1),
        turned_f[0 : 4 * rb],
        own_ref[80:83, 4 * rb : 5 * rb],
        own_ref[83:91, 4 * rb : 5 * rb],
        own_ref[80:91, 0 : 4 * rb],
    )
    for at in range(9):
        for part in range(3):
            loads[1 + at + 9 * part].wait()
        clipped = clip * grads[at]
        weight = in_v[at][...]
        first = BETA_ONE * in_v[9 + at][...] + (1.0 - BETA_ONE) * clipped
        second = BETA_TWO * in_v[18 + at][...] + (1.0 - BETA_TWO) * clipped * clipped
        direction = (
            first
            / (1.0 - BETA_ONE**STEP)
            / (jnp.sqrt(second / (1.0 - BETA_TWO**STEP)) + ADAM_EPS)
        )
        new_v[at][...] = weight - rates[at] * (direction + decays[at] * weight)
        new_v[9 + at][...] = first
        new_v[18 + at][...] = second
        for part in range(3):
            stores[at + 9 * part].start()
    for at in (28, 29):
        loads[at].wait()
        stores[at - 1].start()
    for store in stores:
        store.wait()


def on_device(n, *args):
    tokens, buckets, cotangent = args[0:3]
    weights, firsts, seconds = args[3:12], args[12:21], args[21:30]
    band, side, width = tokens.shape[1:4]
    count = band * side
    keys = count // 4
    rb = weights[0].shape[0]
    piece = cotangent.shape[3]
    wide = up(9 * rb, 128)
    tl = up(6 * rb, 128)
    vl = up(5 * rb, 128)
    total = tl + wide
    qa = count if n <= 8 else QC
    turned = piece % 128 == 0
    block = (n, D, piece) if turned else (n, piece, D)
    vm = pltpu.VMEM
    dma = pltpu.SemaphoreType.DMA
    scratch = [
        vm((count, D), BF),
        *[vm(weights[at].shape, F32) for at in range(9)],
        vm((n, 16, vl), BF),
        vm((4, n, 80, tl), BF),
        vm((4, n, 32, 128), BF),
        vm((4, n, 80, wide), BF),
        vm((16, D), F32),
        vm((16, FF), F32),
        vm((D, D), BF),
        vm((2 * D, D), BF),
        vm((D, D), BF),
        vm((2 * D, D), BF),
        vm((2 * D, D), BF),
        vm((4, D, D), BF),
        vm((FF, D), BF),
        vm((D, FF), BF),
        vm((3, count, 128), F32),
        vm((count, D), BF),
        vm((4, keys, D), BF),
        vm((keys, D), F32),
        vm((keys, D), BF),
        vm((HEADS, 4, keys, 128), BF),
        vm((HEADS, 128, 4 * keys), BF),
        vm((4 * keys, 128), BF),
        vm((128, count), BF),
        vm((HEADS, count, 128), BF),
        vm((HEADS, 128, count), BF),
        vm((HEADS, 4 * keys, count), BF),
        vm((D, count), BF),
        vm((count, D), BF),
        vm((HEADS, 1, count), F32),
        vm((HEADS, 1, count), F32),
        vm((count, D), F32),
        vm((count, D), BF),
        vm((D, count), BF),
        vm((count + 2 * side, FF), BF),
        vm((2, side, FF), BF),
        vm((count + 2 * side, FF), BF),
        vm((count, FF), BF),
        vm(block, BF),
        vm(block, BF),
        vm((D, count), BF),
        vm((count, D), BF),
        vm((2, side, FF), BF),
        vm((HEADS, count, 128), BF),
        vm((HEADS, 2, keys, 128), BF),
        vm((HEADS, keys, 128), BF),
        vm((D, count), BF),
        vm((16, FF), F32),
        vm((16, D), F32),
        vm((2, n, 80, wide), BF),
        vm((2, n, 80, wide), BF),
        vm((80, wide), BF),
        vm((2, n, 80, tl), BF),
        vm((n, CUT, tl), BF),
        vm((n, CUT, tl), BF),
        vm((2, n, 80 - CUT, tl), BF),
        vm((80 - CUT, tl), BF),
        vm((2, n, 32, 128), BF),
        vm((n, 32, 128), BF),
        vm((n, 32, 128), BF),
        vm((n, 16, vl), BF),
        vm((n, 16, vl), BF),
        vm((n, 16, vl), BF),
        vm((n, 16, vl), BF),
        vm((n, 8, 128), F32),
        vm((4, 8, 128), F32),
        vm((side, 128), F32),
        vm((side, 128), F32),
        dma((13,)),
        *[dma((n,)) for _ in range(2)],
        *[dma((6, n)) for _ in range(2)],
        *[dma((3, 4)) for _ in range(2)],
        *[dma((n,)) for _ in range(4)],
        *[dma((HEADS, 3)) for _ in range(2)],
        *[dma((4,)) for _ in range(2)],
        *[dma((HEADS, 3)) for _ in range(2)],
        *[dma((4, 4)) for _ in range(2)],
        *[dma((10, n)) for _ in range(2)],
        *[dma((n,)) for _ in range(2)],
        *[dma((3,)) for _ in range(2)],
    ]
    anywhere = pl.BlockSpec(memory_space=pl.ANY)
    in_vmem = pl.BlockSpec(memory_space=pltpu.VMEM)
    out_t, token_grad, own = pl.pallas_call(
        functools.partial(block_kernel, n, side, band, qa),
        out_shape=(
            jax.ShapeDtypeStruct(block, BF),
            jax.ShapeDtypeStruct((count, D), BF),
            jax.ShapeDtypeStruct((128, total), F32),
        ),
        in_specs=[pl.BlockSpec(memory_space=pltpu.SMEM)] + [anywhere] * 11,
        out_specs=(anywhere, anywhere, in_vmem),
        scratch_shapes=scratch,
        compiler_params=pltpu.CompilerParams(
            collective_id=0, has_side_effects=True, vmem_limit_bytes=VMEM_LIMIT
        ),
    )(
        buckets,
        tokens.reshape(count, width),
        jnp.swapaxes(cotangent, 3, 4).reshape(block) if turned else cotangent.reshape(block),
        *weights,
    )
    rates = (
        D ** (-0.5),
        (4 * D) ** (-0.5),
        D ** (-0.5),
        OUT_FAN ** (-0.5),
        D ** (-0.5),
        FF ** (-0.5),
        GAIN_RATE,
        VECTOR_RATE,
        VECTOR_RATE,
    )
    decays = (DECAY_RATE,) * 6 + (0.0,) * 3
    shapes = tuple(jax.ShapeDtypeStruct(w.shape, F32) for w in weights)
    results = pl.pallas_call(
        functools.partial(update_kernel, rb, vl, tl, rates, decays),
        out_shape=(
            jax.ShapeDtypeStruct(block, BF),
            jax.ShapeDtypeStruct((count, D), BF),
            jax.ShapeDtypeStruct((1, 128), F32),
        )
        + shapes * 3,
        in_specs=[anywhere] * 30,
        out_specs=(anywhere,) * 30,
        scratch_shapes=[
            vm((128, total), F32),
            vm(block, BF),
            vm((count, D), BF),
            vm((1, 128), F32),
            *[vm(w.shape, F32) for w in weights * 6],
            dma((30,)),
            dma((30,)),
        ],
    )(own, out_t, token_grad, *weights, *firsts, *seconds)
    if turned:
        block_output = jnp.swapaxes(results[0].reshape(n, 1, 1, width, piece), 3, 4)
    else:
        block_output = results[0].reshape(n, 1, 1, piece, width)
    return (
        block_output,
        results[1].reshape(1, band, side, width),
        results[2][0, 0],
        *results[3:],
    )


def solution(mesh):
    matrix = (P("dp", "seq"),) * 6 + (P(None, "dp"),) * 3
    return jax.shard_map(
        functools.partial(on_device, mesh.shape["dp"]),
        mesh=mesh,
        in_specs=(
            P("dp", "seq", None, None),
            P("dp"),
            P(None, "seq", "dp", None, None),
            *(matrix * 3),
        ),
        out_specs=(
            P(None, "seq", "dp", None, None),
            P("dp", "seq", None, None),
            P(),
            *(matrix * 3),
        ),
        check_vma=False,
    )
```

```python
import functools

import jax
import jax.numpy as jnp
from jax import lax
from jax.experimental import pallas as pl
from jax.experimental.pallas import tpu as pltpu
from jax.sharding import PartitionSpec as P

D = 320
HEADS = 5
HEAD = 64
FF = 1280
STEP = 10
OUT_FAN = 5

NORM_EPS = 1e-06
MAX_NORM = 1.0
BETA_ONE = 0.9
BETA_TWO = 0.95
ADAM_EPS = 1e-08
DECAY_RATE = 0.01
VECTOR_RATE = 0.3
GAIN_RATE = 0.8
MASKED = -1e30

BF = jnp.bfloat16
F32 = jnp.float32
MESH = pl.DeviceIdType.MESH
QC = 512
CUT = 48
VMEM_LIMIT = 63 * 1024 * 1024


def nn(a, b):
    return lax.dot_general(a, b, (((1,), (0,)), ((), ())), preferred_element_type=F32)


def nt(a, b):
    return lax.dot_general(a, b, (((1,), (1,)), ((), ())), preferred_element_type=F32)


def up(n, m):
    return (n + m - 1) // m * m


def norm_parts(v):
    centered = v - jnp.mean(v, axis=-1, keepdims=True)
    rstd = lax.rsqrt(jnp.mean(centered * centered, axis=-1, keepdims=True) + NORM_EPS)
    return centered * rstd, rstd


def norm_back(v, gain, e):
    vhat, rstd = norm_parts(v)
    u = e * gain
    dv = rstd * (
        u
        - jnp.mean(u, axis=-1, keepdims=True)
        - vhat * jnp.mean(u * vhat, axis=-1, keepdims=True)
    )
    return dv, jnp.sum(e * vhat, axis=0, keepdims=True), jnp.sum(e, axis=0, keepdims=True)


def colsum(v):
    return jnp.sum(v, axis=0, keepdims=True)


def rows(start, size):
    return pl.ds(pl.multiple_of(start, 16), size)


def block_kernel(
    n,
    side,
    band,
    qa,
    bucket_ref,
    tok_ref,
    cot_ref,
    wq_ref,
    wr_ref,
    wm_ref,
    wo_ref,
    w1_ref,
    w2_ref,
    gains_ref,
    biases_ref,
    hidden_ref,
    out_ref,
    tgrad_ref,
    own_ref,
    norm_ref,
    x_s,
    fq,
    fr,
    fm,
    fo,
    f1,
    f2,
    fg,
    fb,
    fh,
    gvec,
    gt,
    gm,
    gf,
    vp,
    hp,
    wqt,
    wot,
    wop,
    wmt,
    wrt,
    w1t,
    w2t,
    a3,
    abf,
    pat,
    red_s,
    memin,
    kv,
    kvt,
    qnat,
    qt,
    prob,
    att_t,
    att_n,
    rtot,
    delta,
    mid,
    bn,
    hidp,
    hidh,
    act,
    gp,
    out_t,
    dy_in,
    dy_t,
    dy,
    dzh,
    datn,
    rk1,
    rk2,
    hg,
    vg,
    own_s,
    sb,
    ra0,
    ra1,
    ra2,
    ra3,
    ra4,
    ra5,
    ra6,
    rb0,
    rb1,
    rb2,
    rb3,
    rb4,
    rb5,
    rb6,
    rt0,
    rt1,
    rt2,
    rt3,
    rt4,
    rt5,
    rt6,
    rm0,
    rm1,
    rm2,
    rm3,
    rm4,
    rm5,
    rm6,
    sv,
    rv1,
    rv2,
    nrm,
    shift_f,
    shift_b,
    shift_m,
    loc,
    gd_s,
    gd_r,
    gx_s,
    gx_r,
    co_s,
    co_r,
    ou_s,
    ou_r,
    kv_s,
    kv_r,
    ha_s,
    ha_r,
    dk_s,
    dk_r,
    rs_s,
    rs_r,
    nd_s,
    nd_r,
):
    me = lax.axis_index("dp")
    j = lax.axis_index("seq")
    y0 = lax.rem(me, 2)
    y1 = 1 - y0
    z0 = lax.div(me, 2)
    beside = me + 1 - 2 * y0
    zn = n // 2
    here = y0 * zn + z0

    def place_of(i):
        return i % 2 * zn + i // 2

    def spot(i):
        return lax.rem(i, 2) * zn + lax.div(i, 2)

    j1 = j + 1 - 2 * lax.rem(j, 2)
    j2 = lax.rem(j + 2, 4)
    j3 = 3 - j
    tokens = band * side
    chunks = tokens // QC
    rb = wq_ref.shape[0]
    piece = tokens // n
    keys = kv.shape[2]
    turned = cot_ref.shape[1] == D
    tl = gt.shape[3]
    fl = gf.shape[3]
    vl = gvec.shape[2]
    al = up(4 * rb, 128)
    bl = sb.shape[3]

    def remote(src, dst, ss, rs, dp, seq):
        return pltpu.make_async_remote_copy(
            src_ref=src,
            dst_ref=dst,
            send_sem=ss,
            recv_sem=rs,
            device_id=(dp, seq),
            device_id_type=MESH,
        )

    def both(copy):
        copy.wait_send()
        copy.wait_recv()

    def peers(body):
        def step(k, carry):
            body(k, lax.rem(me + k, n), lax.rem(me + n - k, n))
            return carry

        lax.fori_loop(1, n, step, 0)

    def z_peers(body):
        def step(k, carry):
            body(k, lax.rem(me + 2 * k, n), lax.rem(z0 + k, zn), lax.rem(z0 + zn - k, zn))
            return carry

        lax.fori_loop(1, zn, step, 0)

    loads = [
        pltpu.make_async_copy(src, dst, loc.at[at])
        for at, (src, dst) in enumerate(
            (
                (gains_ref, fg),
                (biases_ref, fb),
                (hidden_ref, fh),
                (wr_ref, fr),
                (wm_ref, fm),
                (wq_ref, fq),
                (wo_ref, fo),
                (w1_ref, f1),
                (w2_ref, f2),
                (tok_ref, x_s),
            )
        )
    ]
    for copy in loads:
        copy.start()
    def incoming(i):
        return dy_in.at[i] if turned else dy.at[rows(i * piece, piece)]

    own_cot = pltpu.make_async_copy(cot_ref.at[me], incoming(me), loc.at[10])
    own_cot.start()

    barrier = pltpu.get_barrier_semaphore()

    def greet(k, carry):
        to = lax.rem(4 * me + j + k, 4 * n)
        pl.semaphore_signal(
            barrier, inc=1, device_id=(lax.div(to, 4), lax.rem(to, 4)), device_id_type=MESH
        )
        return carry

    lax.fori_loop(1, 4 * n, greet, 0)

    for copy in loads[:5]:
        copy.wait()
    hidden16 = jnp.concatenate([fh[...], jnp.zeros((5, 4 * rb), F32)], axis=0)
    small16 = jnp.concatenate([fg[...], fb[...], jnp.zeros((5, rb), F32)], axis=0)
    gvec[here] = jnp.concatenate(
        [hidden16, small16, jnp.zeros((16, vl - 5 * rb), F32)], axis=1
    ).astype(BF)
    wm_t = fm[...].T
    gt[j, here] = jnp.concatenate(
        [fr[...].T, wm_t[0:80], wm_t[80:160], jnp.zeros((80, tl - 6 * rb), F32)], axis=1
    ).astype(BF)

    def group(at, one_of, all_but_one, each):
        def start():
            def send(peer):
                ref = one_of(here)
                remote(ref, ref, gd_s.at[at], gd_r.at[at], peer, j).start()

            each(send)

        def wait():
            both(remote(all_but_one, all_but_one, gd_s.at[at], gd_r.at[at], beside, j))

        return start, wait

    def each_peer(send):
        peers(lambda k, peer, source: send(peer))

    def each_z(send):
        z_peers(lambda k, peer, to, source: send(peer))

    def over_dp(at, buf, rows_of):
        return group(
            at, lambda i: buf.at[i, rows_of], buf.at[pl.ds(0, n - 1), rows_of], each_peer
        )

    def over_z(at, buf, rows_of):
        return group(
            at, lambda i: buf.at[i, rows_of], buf.at[pl.ds(0, zn - 1), rows_of], each_z
        )

    def swap(at, mine, theirs, dp, seq):
        def start():
            remote(mine, mine, gx_s.at[at], gx_r.at[at], dp, seq).start()

        def wait():
            remote(mine, mine, gx_s.at[at], gx_r.at[at], dp, seq).wait_send()
            remote(theirs, theirs, gx_s.at[at], gx_r.at[at], dp, seq).wait_recv()

        return start, wait

    def over_y(at, buf, rows_of):
        mine = buf.at[pl.ds(y0 * zn, zn), rows_of]
        theirs = buf.at[pl.ds(y1 * zn, zn), rows_of]
        return swap(at, mine, theirs, beside, j)

    lower = slice(0, CUT)
    upper = slice(CUT, 80)
    every = slice(0, 16)
    v_dp, v_dp_wait = over_dp(0, gvec, every)
    t_dp, t_dp_wait = over_dp(1, gt.at[j], lower)
    t_x, t_x_wait = swap(0, gt.at[j, :, lower], gt.at[j2, :, lower], me, j2)
    t_x0, t_x0_wait = swap(1, gt.at[j, here, upper], gt.at[j2, here, upper], me, j2)
    t_za, t_za_wait = over_z(2, gt.at[j], upper)
    t_zb, t_zb_wait = over_z(3, gt.at[j2], upper)
    t_ya, t_ya_wait = over_y(2, gt.at[j], upper)
    t_yb, t_yb_wait = over_y(3, gt.at[j2], upper)
    t_ca, t_ca_wait = swap(4, gt.at[j], gt.at[j1], me, j1)
    t_cb, t_cb_wait = swap(5, gt.at[j2], gt.at[j3], me, j1)
    m_dp, m_dp_wait = over_dp(4, gm.at[j], slice(0, 32))
    m_x, m_x_wait = swap(6, gm.at[j], gm.at[j2], me, j2)
    m_ca, m_ca_wait = swap(7, gm.at[j], gm.at[j1], me, j1)
    m_cb, m_cb_wait = swap(8, gm.at[j2], gm.at[j3], me, j1)
    f_x0, f_x0_wait = swap(9, gf.at[j, here], gf.at[j2, here], me, j2)
    fl_za, fl_za_wait = over_z(5, gf.at[j], lower)
    fl_zb, fl_zb_wait = over_z(6, gf.at[j2], lower)
    fh_za, fh_za_wait = over_z(7, gf.at[j], upper)
    fh_zb, fh_zb_wait = over_z(8, gf.at[j2], upper)
    fl_ya, fl_ya_wait = over_y(10, gf.at[j], lower)
    fl_yb, fl_yb_wait = over_y(11, gf.at[j2], lower)
    fh_ya, fh_ya_wait = over_y(12, gf.at[j], upper)
    fh_yb, fh_yb_wait = over_y(13, gf.at[j2], upper)
    f_ca, f_ca_wait = swap(14, gf.at[j], gf.at[j1], me, j1)
    f_cb, f_cb_wait = swap(15, gf.at[j2], gf.at[j3], me, j1)

    pl.semaphore_wait(barrier, 4 * n - 1)
    t_x0()
    v_dp()
    t_dp()

    for copy in loads[5:9]:
        copy.wait()
    wq_t = fq[...].T
    gm[j, here] = jnp.concatenate(
        [
            wq_t[0:32],
            wq_t[32:64],
            jnp.concatenate([wq_t[64:80], jnp.zeros((16, rb), F32)], axis=0),
            jnp.zeros((32, 128 - 3 * rb), F32),
        ],
        axis=1,
    ).astype(BF)
    w1_t = f1[...].T
    gf[j, here] = jnp.concatenate(
        [f2[...].T]
        + [w1_t[80 * v : 80 * v + 80] for v in range(4)]
        + [fo[...].T, jnp.zeros((80, fl - 9 * rb), F32)],
        axis=1,
    ).astype(BF)
    f_x0()
    t_x0_wait()
    t_za()
    t_zb()
    m_dp()

    v_dp_wait()
    hp[...] = jnp.concatenate([gvec[place_of(i), :, 0 : 4 * rb] for i in range(n)], axis=1).astype(F32)
    vp[...] = jnp.concatenate(
        [gvec[place_of(i), :, 4 * rb : 5 * rb] for i in range(n)], axis=1
    ).astype(F32)

    def gain(k):
        return vp[k : k + 1, :]

    def shift(k):
        return vp[3 + k : 4 + k, :]

    loads[9].wait()

    def norm_one(c, carry):
        at = rows(c * QC, QC)
        vhat, _ = norm_parts(x_s[at, :].astype(F32))
        low = (vhat * gain(0) + shift(0)).astype(BF)
        abf[at, :] = low
        wide = jnp.concatenate([low.astype(F32), jnp.zeros((QC, 64), F32)], axis=1)
        for t in range(3):
            a3[t, at, :] = wide[:, 128 * t : 128 * t + 128]
        return carry

    lax.fori_loop(0, chunks, norm_one, 0)
    half = side // 2
    for dd in range(4):
        for i in range(band // 2):
            start = (2 * i + dd // 2) * side + dd % 2
            cut = jnp.concatenate(
                [a3[t, pl.ds(start, half, stride=2), :] for t in range(3)], axis=1
            )
            pat[dd, i * half : (i + 1) * half, :] = cut[:, 0:D].astype(BF)

    bucket = bucket_ref[0]
    k_row = lax.broadcasted_iota(jnp.int32, (4 * keys, 128), 0)
    k_lane = lax.broadcasted_iota(jnp.int32, (4 * keys, 128), 1)
    k_id = (lax.div(k_row, half) >= half // 2).astype(jnp.int32) * 2 + (
        lax.rem(k_row, half) >= half // 2
    ).astype(jnp.int32)
    off = (k_id != k_lane).astype(jnp.int32) * bucket * (k_lane < 4).astype(jnp.int32)
    kmask = datn.at[0]
    qmask = dy_t.at[0:128]
    kmask[...] = (off.astype(F32) * MASKED).astype(BF)
    q_row = lax.broadcasted_iota(jnp.int32, (128, tokens), 0)
    place = lax.broadcasted_iota(jnp.int32, (128, tokens), 1)
    q_id = (lax.div(place, side) + j * band >= half).astype(jnp.int32) * 2 + (
        lax.rem(place, side) >= half
    ).astype(jnp.int32)
    qmask[...] = (q_id == q_row).astype(F32).astype(BF)
    col = lax.broadcasted_iota(jnp.int32, (side, side), 0)
    ok_l = (col > 0).astype(jnp.int32) * (1 - bucket * (col == half).astype(jnp.int32))
    ok_r = (col < side - 1).astype(jnp.int32) * (
        1 - bucket * (col == half - 1).astype(jnp.int32)
    )
    lane = lax.broadcasted_iota(jnp.int32, (side, side), 1)
    from_l = (ok_l * (lane == col - 1).astype(jnp.int32)).astype(F32).astype(BF)
    from_r = (ok_r * (lane == col + 1).astype(jnp.int32)).astype(F32).astype(BF)
    shift_f[...] = jnp.concatenate([from_l, from_r], axis=1)
    shift_b[...] = jnp.concatenate([from_r, from_l], axis=1)
    shift_m[...] = jnp.concatenate([from_r, from_l], axis=0)
    top_ok = (
        (j > 0).astype(jnp.int32) * (1 - bucket * (j * band == half).astype(jnp.int32))
    ).astype(F32)
    low_ok = (
        (j < 3).astype(jnp.int32) * (1 - bucket * ((j + 1) * band == half).astype(jnp.int32))
    ).astype(F32)

    t_dp_wait()
    t_x()
    t_za_wait()
    t_zb_wait()
    t_ya()
    t_yb()
    f_x0_wait()
    fl_za()
    fl_zb()
    fh_za()
    fh_zb()
    t_ya_wait()
    t_yb_wait()
    m_dp_wait()
    m_x()
    t_x_wait()
    t_ca()
    t_cb()
    m_x_wait()
    m_ca()
    m_cb()
    t_ca_wait()
    t_cb_wait()

    for s in range(4):
        span = slice(80 * s, 80 * s + 80)

        def lanes(lo, hi, over):
            return jnp.concatenate([gt[s, place_of(i), :, lo:hi] for i in over], axis=1)

        for dd in range(4):
            wrt[dd, span, :] = lanes(0, 4 * rb, range(dd * n // 4, (dd + 1) * n // 4))
        for v in range(2):
            wop[160 * s + 80 * v : 160 * s + 80 * v + 80, :] = lanes(
                (4 + v) * rb, (5 + v) * rb, range(n)
            )
    for h in range(HEADS):
        wmt[128 * h : 128 * h + 64, :] = wop[HEAD * h : HEAD * h + HEAD, :]
        wmt[128 * h + 64 : 128 * h + 128, :] = wop[D + HEAD * h : D + HEAD * h + HEAD, :]

    red = shift(2) + nt(pat[0], wrt[0])
    for dd in range(1, 4):
        red = red + nt(pat[dd], wrt[dd])
    red_s[...] = red
    vhat, _ = norm_parts(red)
    low = (vhat * gain(1) + shift(3)).astype(BF)
    memin[...] = low
    zero64 = jnp.zeros((1, HEAD), F32)
    value_shift = jnp.concatenate(
        [
            part
            for h in range(HEADS)
            for part in (zero64, shift(4)[:, HEAD * h : HEAD * h + HEAD])
        ],
        axis=1,
    )
    memory = (nt(low, wmt[...]) + value_shift).astype(BF)
    for h in range(HEADS):
        kv[h, j] = memory[:, 128 * h : 128 * h + 128]

    def kv_copy(h, slot, t, other):
        return remote(
            kv.at[h, slot], kv.at[h, slot], kv_s.at[h, t], kv_r.at[h, t], me, other
        )

    def kv_send(h, carry):
        kv_copy(h, j, 0, j2).start()
        kv_copy(h, j, 1, j1).start()
        return carry

    lax.fori_loop(0, HEADS, kv_send, 0)

    fl_za_wait()
    fl_zb_wait()
    fl_ya()
    fl_yb()
    wqp = wop
    m_ca_wait()
    m_cb_wait()
    for s in range(4):
        at = 80 * s
        wqt[at : at + 32, :] = jnp.concatenate([gm[s, place_of(i), :, 0:rb] for i in range(n)], axis=1)
        wqt[at + 32 : at + 64, :] = jnp.concatenate(
            [gm[s, place_of(i), :, rb : 2 * rb] for i in range(n)], axis=1
        )
        wqt[at + 64 : at + 80, :] = jnp.concatenate(
            [gm[s, place_of(i), 0:16, 2 * rb : 3 * rb] for i in range(n)], axis=1
        )
    for h in range(HEADS):
        wqp[128 * h : 128 * h + 64, :] = wqt[HEAD * h : HEAD * h + HEAD, :]
        wqp[128 * h + 64 : 128 * h + 128, :] = jnp.zeros((64, D), BF)

    query_shift = jnp.concatenate(
        [
            part
            for h in range(HEADS)
            for part in (shift(1)[:, HEAD * h : HEAD * h + HEAD], zero64)
        ],
        axis=1,
    )

    def across(c):
        return pl.ds(pl.multiple_of(c * QC, QC), QC)

    def queries(c, carry):
        at = rows(c * QC, QC)
        q = (nt(abf[at, :], wqp[...]) + query_shift).astype(BF) * jnp.asarray(HEAD**-0.5, BF)
        for h in range(HEADS):
            tile = q[:, 128 * h : 128 * h + 128]
            qnat[h, at, :] = tile
            qt[h, :, across(c)] = tile.T
        return carry

    lax.fori_loop(0, chunks, queries, 0)

    def send_cot(k, peer, source):
        remote(cot_ref.at[peer], incoming(me), co_s.at[0], co_r.at[0], peer, j).start()

    def wait_cot():
        part = cot_ref.at[pl.ds(0, n - 1)]
        both(remote(part, part, co_s.at[0], co_r.at[0], beside, j))

    def kv_forward(h):
        kv_copy(h, j2, 0, j2).wait_recv()
        kv_copy(h, j2, 2, j1).start()

    kv_forward(0)

    def attend(h, carry):
        @pl.when(h == 1)
        def _():
            fh_za_wait()
            fh_zb_wait()
            fh_ya()
            fh_yb()

        @pl.when(h == HEADS - 1)
        def _():
            fl_ya_wait()
            fl_yb_wait()
            fh_ya_wait()
            fh_yb_wait()
            f_ca()
            f_cb()
            peers(send_cot)

        kv_copy(h, j, 0, j2).wait_send()
        kv_copy(h, j, 1, j1).wait_send()
        kv_copy(h, j2, 2, j1).wait_send()
        kv_copy(h, j1, 1, j1).wait_recv()
        kv_copy(h, j3, 2, j1).wait_recv()
        tile = kv[h].reshape(4 * keys, 128)
        kvt[h] = tile.T
        left = jnp.concatenate([tile, kmask[...]], axis=1)
        values = jnp.concatenate([kvt[h, 64:128, :], jnp.ones((16, 4 * keys), BF)], axis=0)
        for c in range(tokens // qa):
            cut = slice(c * qa, (c + 1) * qa)
            scores = nn(left, jnp.concatenate([qt[h, :, cut], qmask[:, cut]], axis=0))
            if c == 0:

                @pl.when(h < HEADS - 1)
                def _():
                    kv_forward(h + 1)

            largest = jnp.max(scores, axis=0, keepdims=True)
            powers = jnp.exp(scores - largest).astype(BF)
            prob[h, :, cut] = powers
            got = nn(values, powers)
            scale = 1.0 / got[64:65, :]
            rtot[h, :, cut] = scale
            att_t[rows(h * HEAD, HEAD), cut] = (got[0:64, :] * scale).astype(BF)
        return carry

    lax.fori_loop(0, HEADS, attend, 0)

    f_ca_wait()
    f_cb_wait()
    for s in range(4):
        span = slice(80 * s, 80 * s + 80)
        w2t[span, :] = jnp.concatenate([gf[s, place_of(i), :, 0 : 4 * rb] for i in range(n)], axis=1)
        for v in range(4):
            at = 320 * s + 80 * v
            w1t[at : at + 80, :] = jnp.concatenate(
                [gf[s, place_of(i), :, (4 + v) * rb : (5 + v) * rb] for i in range(n)], axis=1
            )
        wot[span, :] = jnp.concatenate(
            [gf[s, place_of(i), :, 8 * rb : 9 * rb] for i in range(n)], axis=1
        )
    wop_full = wot[...].T
    for h in range(HEADS):
        wop[128 * h : 128 * h + 64, :] = jnp.zeros((64, D), BF)
        wop[128 * h + 64 : 128 * h + 128, :] = wop_full[HEAD * h : HEAD * h + HEAD, :]

    def middle(c, carry):
        at = rows(c * QC, QC)
        att = att_t[:, across(c)].T
        att_n[at, :] = att
        value = x_s[at, :].astype(F32) + nt(att, wot[...]) + shift(5)
        mid[at, :] = value
        vhat, _ = norm_parts(value)
        low = (vhat * gain(2) + shift(6)).astype(BF)
        bn[at, :] = low
        return carry

    lax.fori_loop(0, chunks, middle, 0)

    edge = tokens - side

    def hidden_of(value):
        return (nt(value, w1t[...]) + hp[9:10, :]).astype(BF)

    ends = hidden_of(jnp.concatenate([bn[0:side, :], bn[edge:tokens, :]], axis=0))
    hidp[side : 2 * side, :] = ends[0:side]
    hidp[tokens : tokens + side, :] = ends[side : 2 * side]
    above = lax.rem(j + 3, 4)
    below = lax.rem(j + 1, 4)

    def rim_up(buf, halo, at):
        return remote(buf.at[pl.ds(side, side)], halo.at[1], ha_s.at[at], ha_r.at[at], me, above)

    def rim_down(buf, halo, at):
        return remote(
            buf.at[pl.ds(tokens, side)], halo.at[0], ha_s.at[at + 1], ha_r.at[at + 1], me, below
        )

    def rim_send(buf, halo, at):
        @pl.when(j > 0)
        def _():
            rim_up(buf, halo, at).start()

        @pl.when(j < 3)
        def _():
            rim_down(buf, halo, at).start()

    def rim_wait(buf, halo, at):
        @pl.when(j > 0)
        def _():
            rim_up(buf, halo, at).wait_send()
            rim_down(buf, halo, at).wait_recv()

        @pl.when(j < 3)
        def _():
            rim_down(buf, halo, at).wait_send()
            rim_up(buf, halo, at).wait_recv()

        for t, (to, ok) in enumerate(((0, top_ok), (tokens + side, low_ok))):
            seen = jnp.full((side, FF), ok, F32) > 0.5
            buf[to : to + side, :] = jnp.where(seen, halo[t].astype(F32), 0.0).astype(BF)

    rim_send(hidp, hidh, 0)

    inner = (tokens - 2 * side) // 2

    def inner_hidden(c, carry):
        start = side + c * inner
        hidp[rows(start + side, inner), :] = hidden_of(bn[rows(start, inner), :])
        return carry

    lax.fori_loop(0, 2, inner_hidden, 0)

    def tile_at(t):
        return pl.ds(pl.multiple_of(t * 128, 128), 128)

    def taps_of(lanes):
        return [hp[k : k + 1, lanes] for k in range(9)]

    def conv_over(lo, hi, step, tiles):
        def conv_tile(t, carry):
            lanes = tile_at(t)
            taps = taps_of(lanes)
            base = hp[10:11, lanes]

            def row(at, inner):
                r = lo + at * step
                around = [hidp[rows((r + a) * side, side), lanes].astype(F32) for a in range(3)]
                parts = [
                    taps[b] * around[0] + taps[3 + b] * around[1] + taps[6 + b] * around[2]
                    for b in range(3)
                ]
                moved = jnp.concatenate([parts[0].astype(BF), parts[2].astype(BF)], axis=0)
                z = base + parts[1] + nn(shift_f[...], moved)
                cdf = 0.5 + 0.5 * lax.erf(z * (0.5**0.5))
                pdf = jnp.exp(z * z * -0.5) * 0.3989422804014327
                act[rows((r + 1) * side, side), lanes] = (z * cdf).astype(BF)
                gp[rows(r * side, side), lanes] = (cdf + z * pdf).astype(BF)
                return inner

            lax.fori_loop(0, (hi - lo) // step, row, 0, unroll=True)
            return carry

        lax.fori_loop(0, FF // 128, conv_tile, 0, unroll=tiles)

    conv_over(1, band - 1, 1, 1)
    rim_wait(hidp, hidh, 0)
    conv_over(0, 2 * (band - 1), band - 1, 5)

    def out_chunk(c, carry):
        at = rows(c * QC, QC)
        value = mid[at, :] + nt(act[rows(side + c * QC, QC), :], w2t[...]) + shift(7)
        for p in range(QC // piece):
            part = value[p * piece : (p + 1) * piece, :]
            out_t[c * (QC // piece) + p] = (part.T if turned else part).astype(BF)
        return carry

    lax.fori_loop(0, chunks, out_chunk, 0)

    def send_out(k, peer, source):
        remote(out_t.at[peer], out_ref.at[me], ou_s.at[0], ou_r.at[0], peer, j).start()

    def wait_out():
        part = out_t.at[pl.ds(0, n - 1)]
        both(remote(part, part, ou_s.at[0], ou_r.at[0], beside, j))

    peers(send_out)
    own_out = pltpu.make_async_copy(out_t.at[me], out_ref.at[me], loc.at[11])
    own_out.start()

    own_cot.wait()
    wait_cot()
    for i in range(n):
        if turned:
            dy_t[:, i * piece : (i + 1) * piece] = dy_in[i]
            dy[i * piece : (i + 1) * piece, :] = dy_in[i].T
    if not turned:
        dy_t[...] = dy[...].T
    vg[...] = jnp.zeros(vg.shape, F32)
    vg[10:11, :] = colsum(dy[...].astype(F32))

    def scatter(sems, s, cut, direct, bufs, own):
        top = s.shape[2]
        r1, xl, yl, dl, yh, dh, xh = bufs
        low, high = slice(0, cut), slice(cut, top)
        slots = (j, j2)
        count = n if direct else zn
        mine = pl.ds(y0 * zn, zn)
        theirs = pl.ds(y1 * zn, zn)

        def copy(src, dst, t, dp, seq):
            at = sems[t]
            return remote(src, dst, rs_s.at[at], rs_r.at[at], dp, seq)

        def core():
            return [copy(s.at[slot], r1.at[t], t, me, j1) for t, slot in enumerate((j1, j3))]

        def low_x():
            return copy(s.at[j2, :, low], xl, 2, me, j2)

        def low_y():
            return copy(s.at[j, theirs, low], yl, 3, beside, j)

        def high_y():
            return [
                copy(s.at[slot, theirs, high], yh.at[t], 4 + t, beside, j)
                for t, slot in enumerate(slots)
            ]

        def high_x():
            return copy(s.at[j2, here, high], xh, 6, me, j2)

        def out(slot, rows_of, land, t):
            def send(k, peer, to):
                copy(s.at[slot, to, rows_of], land.at[k], t, peer, j).start()

            if direct:
                peers(lambda k, peer, source: send(k, peer, spot(peer)))
            else:
                z_peers(lambda k, peer, to, source: send(k, peer, y0 * zn + to))

        def landed(slot, rows_of, land, t):
            part = land.at[pl.ds(1, count - 1)]
            both(copy(part, part, t, beside, j))
            return lax.fori_loop(
                1,
                count,
                lambda k, v: v + land[k].astype(F32),
                s[slot, here, rows_of].astype(F32),
            )

        def add(slot, start, rows_of, extra):
            def body(i, carry):
                s[slot, start + i, rows_of] = (
                    s[slot, start + i, rows_of].astype(F32) + extra[i].astype(F32)
                ).astype(BF)
                return carry

            lax.fori_loop(0, extra.shape[0], body, 0)

        def one():
            for c in core():
                c.start()

        def two():
            for c in core():
                both(c)
            for t, slot in enumerate(slots):
                add(slot, 0, slice(0, top), r1.at[t])
            if cut < top:
                if direct:
                    for t, slot in enumerate(slots):
                        out(slot, high, dh.at[t], 4 + t)
                else:
                    for c in high_y():
                        c.start()
            if cut > 0:
                low_x().start()

        def low_three():
            both(low_x())
            add(j, 0, low, xl)
            if direct:
                out(j, low, dl, 3)
            else:
                low_y().start()

        def high_three():
            for c in high_y():
                both(c)
            for t, slot in enumerate(slots):
                add(slot, y0 * zn, high, yh.at[t])
                out(slot, high, dh.at[t], 7 + t)

        def low_four():
            both(low_y())
            add(j, y0 * zn, low, yl)
            out(j, low, dl, 9)

        def high_four():
            first = 4 if direct else 7
            own[high, :] = landed(j, high, dh.at[0], first)
            s[j2, here, high] = landed(j2, high, dh.at[1], first + 1).astype(BF)
            high_x().start()

        def low_five():
            own[low, :] = landed(j, low, dl, 3 if direct else 9)

        def high_five():
            both(high_x())
            own[high, :] = own[high, :] + xh[...].astype(F32)

        return one, two, low_three, low_four, low_five, high_three, high_four, high_five

    own_t = own_s.at[0:80, 0:tl]
    own_a = own_s.at[0:80, tl : tl + al]
    own_b = own_s.at[0:80, tl + al : tl + al + bl]
    own_m = own_s.at[96:128, 0:128]
    a_one, a_two, a_three, a_four, a_five, _, _, _ = scatter(
        (0, 1, 2, 3, 0, 0, 0, 0, 0, 4), gf.at[:, :, :, 0:al], 80, False, (ra0, ra1, ra2, ra3, ra4, ra5, ra6), own_a
    )
    b_one, b_two, _, _, _, b_three, b_four, b_five = scatter(
        (5, 6, 0, 0, 7, 8, 9, 10, 11), sb, 0, False, (rb0, rb1, rb2, rb3, rb4, rb5, rb6), own_b
    )
    m_one, m_two, m_three, _, m_five, _, _, _ = scatter(
        (12, 13, 14, 15), gm, 32, True, (rm0, rm1, rm2, rm3, rm4, rm5, rm6), own_m
    )
    t_one, t_two, tl_three, _, tl_five, _, th_four, th_five = scatter(
        (16, 17, 18, 19, 20, 21, 22), gt, CUT, True, (rt0, rt1, rt2, rt3, rt4, rt5, rt6), own_t
    )

    per = 640 // (4 * rb)
    for b in range(2):
        value = nn(dy_t[...], act[side : side + tokens, 640 * b : 640 * b + 640]).astype(BF)
        for ii in range(per):
            i = b * per + ii
            gf[:, place_of(i), :, 0 : 4 * rb] = value[
                :, 4 * rb * ii : 4 * rb * (ii + 1)
            ].reshape(4, 80, 4 * rb)

    a_one()

    def slope_of(at):
        return nn(dy[at, :], w2t[...])

    dz = act
    for at in (0, edge):
        dz[side + at : 2 * side + at, :] = (
            slope_of(slice(at, at + side)) * gp[at : at + side, :].astype(F32)
        ).astype(BF)
    rim_send(dz, dzh, 2)

    def inner_slope(c, carry):
        at = rows(side + c * inner, inner)
        dz[rows(2 * side + c * inner, inner), :] = (
            slope_of(at) * gp[at, :].astype(F32)
        ).astype(BF)
        return carry

    lax.fori_loop(0, 2, inner_slope, 0)

    a_two()

    dhid = gp

    def fold(v):
        return jnp.sum(v.reshape(side // 8, 8, 128), axis=0)

    def back_over(lo, hi, step, first, tiles):
        def back_tile(t, carry):
            lanes = tile_at(t)
            taps = taps_of(lanes)

            def row(at, sums):
                r = lo + at * step
                around = [dz[rows((r + a) * side, side), lanes].astype(F32) for a in range(3)]
                parts = [
                    taps[b] * around[2] + taps[3 + b] * around[1] + taps[6 + b] * around[0]
                    for b in range(3)
                ]
                both_ways = jnp.concatenate([parts[0].astype(BF), parts[2].astype(BF)], axis=0)
                low = (parts[1] + nn(shift_b[...], both_ways)).astype(BF)
                dhid[rows(r * side, side), lanes] = low
                here = around[1]
                sides = nn(shift_m[...], dz[rows((r + 1) * side, side), lanes])
                moved = [sides[0:side], here, sides[side : 2 * side]]
                found = []
                for a in range(3):
                    source = hidp[rows((r + a) * side, side), lanes].astype(F32)
                    for b in range(3):
                        found.append(fold(moved[b] * source))
                found.append(fold(low.astype(F32)))
                found.append(fold(here))
                return tuple(s + f for s, f in zip(sums, found))

            sums = lax.fori_loop(
                0,
                (hi - lo) // step,
                row,
                tuple(jnp.zeros((8, 128), F32) for _ in range(11)),
                unroll=True,
            )
            found = jnp.concatenate([colsum(s) for s in sums] + [jnp.zeros((5, 128), F32)], axis=0)
            hg[:, lanes] = found if first else hg[:, lanes] + found
            return carry

        lax.fori_loop(0, FF // 128, back_tile, 0, unroll=tiles)

    back_over(1, band - 1, 1, True, 1)
    rim_wait(dz, dzh, 2)
    back_over(0, 2 * (band - 1), band - 1, False, 5)

    a_three()
    bn_t = dy_t
    bn_t[...] = bn[...].T
    for b in range(2):
        value = nn(bn_t[...], dhid[:, 640 * b : 640 * b + 640]).T.astype(BF)
        value = value.reshape(2, 4, 80, D)
        for i in range(n):
            sb[2 * b : 2 * b + 2, place_of(i), :, 0 : 4 * rb] = jnp.concatenate(
                [value[:, v, :, rb * i : rb * i + rb] for v in range(4)], axis=2
            )

    zero_row = jnp.zeros((1, D), F32)
    dbr = bn
    dbr_t = dy_t

    def back_middle(c, carry):
        at = rows(c * QC, QC)
        value, in_gain, in_shift = norm_back(mid[at, :], gain(2), nn(dhid[at, :], w1t[...]))
        value = value + dy[at, :].astype(F32)
        mid[at, :] = value
        low = value.astype(BF)
        dbr[at, :] = low
        dbr_t[:, across(c)] = low.T
        spread = nt(wop[...], low)
        for h in range(HEADS):
            tile = spread[128 * h : 128 * h + 128, :] * rtot[h, :, across(c)]
            tile_low = tile.astype(BF)
            qt[h, :, across(c)] = tile_low
            datn[h, at, :] = tile_low.T
            delta[h, :, across(c)] = colsum(
                tile_low[64:128, :].astype(F32)
                * att_t[HEAD * h : HEAD * h + HEAD, across(c)].astype(F32)
            )
        return (carry[0] + in_gain, carry[1] + in_shift, carry[2] + colsum(low.astype(F32)))

    sums = lax.fori_loop(0, chunks, back_middle, (zero_row, zero_row, zero_row))
    vg[2:3, :] = sums[0]
    vg[9:10, :] = sums[1]
    vg[8:9, :] = sums[2]
    value = nn(dbr_t[...], att_n[...]).astype(BF)
    for i in range(n):
        sb[:, place_of(i), :, 4 * rb : 5 * rb] = value[:, rb * i : rb * i + rb].reshape(
            4, 80, rb
        )
    b_one()
    a_four()

    def dkv(h, slot):
        return act.at[rows(slot * keys, keys), tile_at(h)]

    def dk_core(h):
        return [
            remote(dkv(h, slot), rk1.at[h, t], dk_s.at[h, t], dk_r.at[h, t], me, j1)
            for t, slot in enumerate((j1, j3))
        ]

    def dk_x(h):
        return remote(dkv(h, j2), rk2.at[h], dk_s.at[h, 2], dk_r.at[h, 2], me, j2)

    def dk_two(h):
        for copy in dk_core(h):
            both(copy)
        for t, slot in enumerate((j, j2)):
            part = dkv(h, slot)
            part[...] = (part[...].astype(F32) + rk1[h, t].astype(F32)).astype(BF)
        dk_x(h).start()

    def dk_three(h):
        both(dk_x(h))
        qnat[h, 0:keys, :] = (dkv(h, j)[...].astype(F32) + rk2[h].astype(F32)).astype(BF)

    def back_head(h, carry):
        tile = kv[h].reshape(4 * keys, 128)
        total = None
        for c in range(tokens // qa):
            cut = slice(c * qa, (c + 1) * qa)
            powers = prob[h, :, cut]
            slopes = nn(tile, qt[h, :, cut]) - delta[h, :, cut]
            ds = (powers.astype(F32) * slopes).astype(BF)
            part = nn(ds, qnat[h, cut, :]) + nn(powers, datn[h, cut, :])
            prob[h, :, cut] = ds
            total = part if total is None else total + part
        act[0 : 4 * keys, tile_at(h)] = total.astype(BF)
        for copy in dk_core(h):
            copy.start()

        @pl.when(h == 1)
        def _():
            b_two()

        @pl.when(h >= 1)
        def _():
            dk_two(h - 1)

        return carry

    lax.fori_loop(0, HEADS, back_head, 0)

    dq_t = att_t

    def back_query(h, carry):
        for c in range(tokens // qa):
            cut = slice(c * qa, (c + 1) * qa)
            dq_t[rows(h * HEAD, HEAD), cut] = (
                nn(kvt[h, 0:64, :], prob[h, :, cut]) * HEAD**-0.5
            ).astype(BF)
        return carry

    lax.fori_loop(0, 2, back_query, 0)
    dk_two(HEADS - 1)
    b_three()
    for h in range(HEADS - 2):
        dk_three(h)
    lax.fori_loop(2, HEADS, back_query, 0)
    dq = att_n

    def flip(c, total):
        low = dq_t[:, across(c)].T
        dq[rows(c * QC, QC), :] = low
        return total + colsum(low.astype(F32))

    vg[4:5, :] = lax.fori_loop(0, chunks, flip, zero_row)
    value = nn(dq_t[...], abf[...]).astype(BF)
    for i in range(n):
        part = value[:, rb * i : rb * i + rb].reshape(4, 80, rb)
        gm[:, place_of(i), :, 0 : 3 * rb] = jnp.concatenate(
            [
                part[:, 0:32],
                part[:, 32:64],
                jnp.concatenate([part[:, 64:80], jnp.zeros((4, 16, rb), BF)], axis=1),
            ],
            axis=2,
        )
    dk_three(HEADS - 2)
    dk_three(HEADS - 1)

    dm = jnp.concatenate([qnat[h, 0:keys, :] for h in range(HEADS)], axis=1)
    dm_sum = colsum(dm.astype(F32))
    vg[7:8, :] = jnp.concatenate(
        [dm_sum[:, 128 * h + 64 : 128 * h + 128] for h in range(HEADS)], axis=1
    )
    dv, in_gain, in_shift = norm_back(red_s[...], gain(1), nn(dm, wmt[...]))
    vg[1:2, :] = in_gain
    vg[6:7, :] = in_shift
    dred = dv.astype(BF)
    vg[5:6, :] = colsum(dred.astype(F32))
    dred_t = dred.T
    for dd in range(4):
        value = nn(dred_t, pat[dd]).astype(BF)
        count = n // 4
        for ii in range(count):
            i = dd * count + ii
            gt[:, place_of(i), :, 0 : 4 * rb] = value[
                :, 4 * rb * ii : 4 * rb * (ii + 1)
            ].reshape(4, 80, 4 * rb)
    value = nn(dm.T, memin[...]).astype(BF)
    value = jnp.concatenate(
        [value[128 * h : 128 * h + 64] for h in range(HEADS)]
        + [value[128 * h + 64 : 128 * h + 128] for h in range(HEADS)],
        axis=0,
    ).reshape(4, 2, 80, D)
    for i in range(n):
        gt[:, place_of(i), :, 4 * rb : 6 * rb] = jnp.concatenate(
            [value[:, v, :, rb * i : rb * i + rb] for v in range(2)], axis=2
        )
    t_one()

    m_one()
    t_two()

    for dd in range(4):
        back = nn(dred, wrt[dd])
        back = jnp.concatenate([back, jnp.zeros((keys, 64), F32)], axis=1)
        for i in range(band // 2):
            start = (2 * i + dd // 2) * side + dd % 2
            for t in range(3):
                a3[t, pl.ds(start, half, stride=2), :] = back[
                    i * half : (i + 1) * half, 128 * t : 128 * t + 128
                ]
    m_two()

    def back_first(c, carry):
        at = rows(c * QC, QC)
        e = nn(dq[at, :], wqt[...]) + jnp.concatenate([a3[t, at, :] for t in range(3)], axis=1)[:, 0:D]
        value, in_gain, in_shift = norm_back(x_s[at, :].astype(F32), gain(0), e)
        bn[at, :] = (mid[at, :] + value).astype(BF)
        return (carry[0] + in_gain, carry[1] + in_shift)

    sums = lax.fori_loop(0, chunks, back_first, (zero_row, zero_row))
    token_out = pltpu.make_async_copy(bn, tgrad_ref, loc.at[12])
    token_out.start()
    vg[0:1, :] = sums[0]
    vg[3:4, :] = sums[1]
    for i in range(n):
        sv[place_of(i), :, 0 : 4 * rb] = hg[:, 4 * rb * i : 4 * rb * (i + 1)].astype(BF)
        sv[place_of(i), :, 4 * rb : 5 * rb] = vg[:, rb * i : rb * i + rb].astype(BF)

    def v_out(k, peer, source):
        remote(sv.at[spot(peer)], rv1.at[k], rs_s.at[23], rs_r.at[23], peer, j).start()

    peers(v_out)
    tl_three()
    b_four()
    m_three()
    part = rv1.at[pl.ds(1, n - 1)]
    both(remote(part, part, rs_s.at[23], rs_r.at[23], beside, j))
    rv2[j] = lax.fori_loop(
        1, n, lambda k, total: total + rv1[k].astype(F32), sv[here].astype(F32)
    ).astype(BF)

    def v_seq(t, slot, other):
        ref = rv2.at[slot]
        return remote(ref, ref, rs_s.at[24 + t], rs_r.at[24 + t], me, other)

    for t, other in enumerate((j1, j2, j3)):
        v_seq(t, j, other).start()
    th_four()
    a_five()
    b_five()
    squares = jnp.sum(own_a[:, 0 : 4 * rb] * own_a[:, 0 : 4 * rb])
    squares += jnp.sum(own_b[:, 0 : 5 * rb] * own_b[:, 0 : 5 * rb])
    th_five()
    m_five()
    squares += jnp.sum(own_m[:, 0 : 2 * rb] * own_m[:, 0 : 2 * rb])
    squares += jnp.sum(own_m[0:16, 2 * rb : 3 * rb] * own_m[0:16, 2 * rb : 3 * rb])
    tl_five()
    squares += jnp.sum(own_t[:, 0 : 6 * rb] * own_t[:, 0 : 6 * rb])
    for t, other in enumerate((j1, j2, j3)):
        v_seq(t, other, other).wait_send()
        v_seq(t, other, other).wait_recv()
    own_v = (rv2[0].astype(F32) + rv2[1].astype(F32)) + (rv2[2].astype(F32) + rv2[3].astype(F32))
    own_s[80:96, 0:vl] = own_v
    first_band = (j == 0).astype(jnp.int32).astype(F32)
    squares += first_band * jnp.sum(own_v[0:11, 0 : 5 * rb] * own_v[0:11, 0 : 5 * rb])

    nrm[4 * me + j] = jnp.full((8, 128), squares, F32)
    own_out_copy = pltpu.make_async_copy(own_s, own_ref, loc.at[13])
    own_out_copy.start()

    def send_norm(k, carry):
        mine = 4 * me + j
        to = lax.rem(mine + k, 4 * n)
        remote(
            nrm.at[mine], nrm.at[mine], nd_s.at[0], nd_r.at[0], lax.div(to, 4), lax.rem(to, 4)
        ).start()
        return carry

    lax.fori_loop(1, 4 * n, send_norm, 0)
    part = nrm.at[pl.ds(0, 4 * n - 1)]
    both(remote(part, part, nd_s.at[0], nd_r.at[0], beside, j))
    nrm[4 * n] = lax.fori_loop(1, 4 * n, lambda k, total: total + nrm[k], nrm[0])
    norm_out = pltpu.make_async_copy(nrm.at[4 * n], norm_ref, loc.at[14])
    norm_out.start()

    wait_out()
    own_out.wait()
    token_out.wait()
    own_out_copy.wait()
    norm_out.wait()


def update_kernel(rb, tl, al, rates, decays, *refs):
    own_hbm, total_hbm, outt_hbm, tg_hbm = refs[0:4]
    in_hbm = refs[4:31]
    out_hbm, tok_hbm, norm_hbm = refs[31:34]
    new_hbm = refs[34:61]
    own_ref, total_ref, out_v, tok_v, norm_v = refs[61:66]
    in_v, new_v = refs[66:93], refs[93:120]
    in_sem, out_sem = refs[120:122]
    loads = [
        pltpu.make_async_copy(src, dst, in_sem.at[at])
        for at, (src, dst) in enumerate(
            [
                (own_hbm, own_ref),
                *zip(in_hbm, in_v),
                (outt_hbm, out_v),
                (tg_hbm, tok_v),
                (total_hbm, total_ref),
            ]
        )
    ]
    for load in loads:
        load.start()
    stores = [
        pltpu.make_async_copy(src, dst, out_sem.at[at])
        for at, (src, dst) in enumerate(
            [*zip(new_v, new_hbm), (out_v, out_hbm), (tok_v, tok_hbm), (norm_v, norm_hbm)]
        )
    ]
    loads[0].wait()
    loads[30].wait()
    total = total_ref[0:1, :]
    norm = jnp.sqrt(total)
    norm_v[...] = norm
    stores[29].start()
    clip = jnp.minimum(1.0, MAX_NORM / (norm + 1e-06))[:, 0:1]
    turned_t = own_ref[0:80, 0:tl].T
    turned_a = own_ref[0:80, tl : tl + al].T
    turned_b = own_ref[0:80, tl + al :].T
    turned_q = jnp.concatenate(
        [
            own_ref[96:128, 0:rb],
            own_ref[96:128, rb : 2 * rb],
            own_ref[96:112, 2 * rb : 3 * rb],
        ],
        axis=0,
    ).T
    grads = (
        turned_q,
        turned_t[0 : 4 * rb],
        jnp.concatenate([turned_t[(4 + v) * rb : (5 + v) * rb] for v in range(2)], axis=1),
        turned_b[4 * rb : 5 * rb],
        jnp.concatenate([turned_b[v * rb : (v + 1) * rb] for v in range(4)], axis=1),
        turned_a[0 : 4 * rb],
        own_ref[80:83, 4 * rb : 5 * rb],
        own_ref[83:91, 4 * rb : 5 * rb],
        own_ref[80:91, 0 : 4 * rb],
    )
    for at in range(9):
        for part in range(3):
            loads[1 + at + 9 * part].wait()
        clipped = clip * grads[at]
        weight = in_v[at][...]
        first = BETA_ONE * in_v[9 + at][...] + (1.0 - BETA_ONE) * clipped
        second = BETA_TWO * in_v[18 + at][...] + (1.0 - BETA_TWO) * clipped * clipped
        direction = (
            first
            / (1.0 - BETA_ONE**STEP)
            / (jnp.sqrt(second / (1.0 - BETA_TWO**STEP)) + ADAM_EPS)
        )
        new_v[at][...] = weight - rates[at] * (direction + decays[at] * weight)
        new_v[9 + at][...] = first
        new_v[18 + at][...] = second
        for part in range(3):
            stores[at + 9 * part].start()
    for at in (28, 29):
        loads[at].wait()
        stores[at - 1].start()
    for store in stores:
        store.wait()


def on_device(n, *args):
    tokens, buckets, cotangent = args[0:3]
    weights, firsts, seconds = args[3:12], args[12:21], args[21:30]
    band, side, width = tokens.shape[1:4]
    count = band * side
    keys = count // 4
    rb = weights[0].shape[0]
    piece = cotangent.shape[3]
    wide = up(9 * rb, 128)
    tl = up(6 * rb, 128)
    al = up(4 * rb, 128)
    bl = up(5 * rb, 128)
    h = n // 2
    vl = up(5 * rb, 128)
    total = tl + al + bl
    qa = count if n <= 8 else 256
    turned = piece % 128 == 0
    block = (n, D, piece) if turned else (n, piece, D)
    vm = pltpu.VMEM
    dma = pltpu.SemaphoreType.DMA
    def landing(height, lanes, cut, direct):
        rest = height - cut
        count = n if direct else h
        shapes = (
            (2, n, height, lanes),
            (n, cut, lanes),
            (0 if direct else h, cut, lanes),
            (count, cut, lanes),
            (0 if direct else 2, h, rest, lanes),
            (2, count, rest, lanes),
            (rest, lanes),
        )
        return [vm(shape if 0 not in shape else (8, 128), BF) for shape in shapes]

    scratch = [
        vm((count, D), BF),
        *[vm(weights[at].shape, F32) for at in range(9)],
        vm((n, 16, vl), BF),
        vm((4, n, 80, tl), BF),
        vm((4, n, 32, 128), BF),
        vm((4, n, 80, wide), BF),
        vm((16, D), F32),
        vm((16, FF), F32),
        vm((D, D), BF),
        vm((D, D), BF),
        vm((2 * D, D), BF),
        vm((2 * D, D), BF),
        vm((4, D, D), BF),
        vm((FF, D), BF),
        vm((D, FF), BF),
        vm((3, count, 128), F32),
        vm((count, D), BF),
        vm((4, keys, D), BF),
        vm((keys, D), F32),
        vm((keys, D), BF),
        vm((HEADS, 4, keys, 128), BF),
        vm((HEADS, 128, 4 * keys), BF),
        vm((HEADS, count, 128), BF),
        vm((HEADS, 128, count), BF),
        vm((HEADS, 4 * keys, count), BF),
        vm((D, count), BF),
        vm((count, D), BF),
        vm((HEADS, 1, count), F32),
        vm((HEADS, 1, count), F32),
        vm((count, D), F32),
        vm((count, D), BF),
        vm((count + 2 * side, FF), BF),
        vm((2, side, FF), BF),
        vm((count + 2 * side, FF), BF),
        vm((count, FF), BF),
        vm(block, BF),
        vm(block if turned else (8, 128), BF),
        vm((D, count), BF),
        vm((count, D), BF),
        vm((2, side, FF), BF),
        vm((HEADS, count, 128), BF),
        vm((HEADS, 2, keys, 128), BF),
        vm((HEADS, keys, 128), BF),
        vm((16, FF), F32),
        vm((16, D), F32),
        vm((128, total), F32),
        vm((4, n, 80, bl), BF),
        *landing(80, al, 80, False),
        *landing(80, bl, 0, False),
        *landing(80, tl, CUT, True),
        *landing(32, 128, 32, True),
        vm((n, 16, vl), BF),
        vm((n, 16, vl), BF),
        vm((4, 16, vl), BF),
        vm((4 * n + 1, 8, 128), F32),
        vm((side, 2 * side), BF),
        vm((side, 2 * side), BF),
        vm((2 * side, side), BF),
        dma((15,)),
        *[dma((9,)) for _ in range(2)],
        *[dma((16,)) for _ in range(2)],
        *[dma((1,)) for _ in range(4)],
        *[dma((HEADS, 3)) for _ in range(2)],
        *[dma((4,)) for _ in range(2)],
        *[dma((HEADS, 3)) for _ in range(2)],
        *[dma((27,)) for _ in range(2)],
        *[dma((1,)) for _ in range(2)],
    ]
    anywhere = pl.BlockSpec(memory_space=pl.ANY)
    out_t, token_grad, own, total_squares = pl.pallas_call(
        functools.partial(block_kernel, n, side, band, qa),
        out_shape=(
            jax.ShapeDtypeStruct(block, BF),
            jax.ShapeDtypeStruct((count, D), BF),
            jax.ShapeDtypeStruct((128, total), F32),
            jax.ShapeDtypeStruct((8, 128), F32),
        ),
        in_specs=[pl.BlockSpec(memory_space=pltpu.SMEM)] + [anywhere] * 11,
        out_specs=(anywhere,) * 4,
        scratch_shapes=scratch,
        compiler_params=pltpu.CompilerParams(
            collective_id=0, has_side_effects=True, vmem_limit_bytes=VMEM_LIMIT
        ),
    )(
        buckets,
        tokens.reshape(count, width),
        jnp.swapaxes(cotangent, 3, 4).reshape(block) if turned else cotangent.reshape(block),
        *weights,
    )
    rates = (
        D ** (-0.5),
        (4 * D) ** (-0.5),
        D ** (-0.5),
        OUT_FAN ** (-0.5),
        D ** (-0.5),
        FF ** (-0.5),
        GAIN_RATE,
        VECTOR_RATE,
        VECTOR_RATE,
    )
    decays = (DECAY_RATE,) * 6 + (0.0,) * 3
    shapes = tuple(jax.ShapeDtypeStruct(w.shape, F32) for w in weights)
    results = pl.pallas_call(
        functools.partial(update_kernel, rb, tl, al, rates, decays),
        out_shape=(
            jax.ShapeDtypeStruct(block, BF),
            jax.ShapeDtypeStruct((count, D), BF),
            jax.ShapeDtypeStruct((1, 128), F32),
        )
        + shapes * 3,
        in_specs=[anywhere] * 31,
        out_specs=(anywhere,) * 30,
        scratch_shapes=[
            vm((128, total), F32),
            vm((8, 128), F32),
            vm(block, BF),
            vm((count, D), BF),
            vm((1, 128), F32),
            *[vm(w.shape, F32) for w in weights * 6],
            dma((31,)),
            dma((30,)),
        ],
    )(own, total_squares, out_t, token_grad, *weights, *firsts, *seconds)
    if turned:
        block_output = jnp.swapaxes(results[0].reshape(n, 1, 1, width, piece), 3, 4)
    else:
        block_output = results[0].reshape(n, 1, 1, piece, width)
    return (
        block_output,
        results[1].reshape(1, band, side, width),
        results[2][0, 0],
        *results[3:],
    )


def solution(mesh):
    matrix = (P("dp", "seq"),) * 6 + (P(None, "dp"),) * 3
    return jax.shard_map(
        functools.partial(on_device, mesh.shape["dp"]),
        mesh=mesh,
        in_specs=(
            P("dp", "seq", None, None),
            P("dp"),
            P(None, "seq", "dp", None, None),
            *(matrix * 3),
        ),
        out_specs=(
            P(None, "seq", "dp", None, None),
            P("dp", "seq", None, None),
            P(),
            *(matrix * 3),
        ),
        check_vma=False,
    )
```

```python
import functools

import jax
import jax.numpy as jnp
from jax import lax
from jax.experimental import pallas as pl
from jax.experimental.pallas import tpu as pltpu
from jax.sharding import PartitionSpec as P

D = 320
HEADS = 5
HEAD = 64
FF = 1280
STEP = 10
OUT_FAN = 5

NORM_EPS = 1e-06
MAX_NORM = 1.0
BETA_ONE = 0.9
BETA_TWO = 0.95
ADAM_EPS = 1e-08
DECAY_RATE = 0.01
VECTOR_RATE = 0.3
GAIN_RATE = 0.8
MASKED = -1e30

BF = jnp.bfloat16
F32 = jnp.float32
MESH = pl.DeviceIdType.MESH
QC = 512
CUT = 48
VMEM_LIMIT = 63 * 1024 * 1024


def nn(a, b):
    return lax.dot_general(a, b, (((1,), (0,)), ((), ())), preferred_element_type=F32)


def nt(a, b):
    return lax.dot_general(a, b, (((1,), (1,)), ((), ())), preferred_element_type=F32)


def up(n, m):
    return (n + m - 1) // m * m


def norm_parts(v):
    centered = v - jnp.mean(v, axis=-1, keepdims=True)
    rstd = lax.rsqrt(jnp.mean(centered * centered, axis=-1, keepdims=True) + NORM_EPS)
    return centered * rstd, rstd


def norm_back(v, gain, e):
    vhat, rstd = norm_parts(v)
    u = e * gain
    dv = rstd * (
        u
        - jnp.mean(u, axis=-1, keepdims=True)
        - vhat * jnp.mean(u * vhat, axis=-1, keepdims=True)
    )
    return dv, jnp.sum(e * vhat, axis=0, keepdims=True), jnp.sum(e, axis=0, keepdims=True)


def colsum(v):
    return jnp.sum(v, axis=0, keepdims=True)


def rows(start, size):
    return pl.ds(pl.multiple_of(start, 16), size)


def block_kernel(
    n,
    side,
    band,
    qa,
    bucket_ref,
    tok_ref,
    cot_ref,
    wq_ref,
    wr_ref,
    wm_ref,
    wo_ref,
    w1_ref,
    w2_ref,
    gains_ref,
    biases_ref,
    hidden_ref,
    out_ref,
    tgrad_ref,
    own_ref,
    norm_ref,
    x_s,
    fq,
    fr,
    fm,
    fo,
    f1,
    f2,
    fg,
    fb,
    fh,
    gvec,
    gt,
    gm,
    gf,
    vp,
    hp,
    wqt,
    wot,
    wop,
    wmt,
    wrt,
    w1t,
    w2t,
    a3,
    abf,
    pat,
    memin,
    kv,
    kvt,
    qnat,
    qt,
    prob,
    att_t,
    att_n,
    rtot,
    delta,
    mid,
    bn,
    hidp,
    hidh,
    act,
    gp,
    out_t,
    dy_in,
    dy_t,
    dy,
    dzh,
    datn,
    rk1,
    rk2,
    hg,
    vg,
    own_s,
    sb,
    ra0,
    ra1,
    ra2,
    ra3,
    ra4,
    ra5,
    ra6,
    rb0,
    rb1,
    rb2,
    rb3,
    rb4,
    rb5,
    rb6,
    rt0,
    rt1,
    rt2,
    rt3,
    rt4,
    rt5,
    rt6,
    rm0,
    rm1,
    rm2,
    rm3,
    rm4,
    rm5,
    rm6,
    sv,
    rv1,
    rv2,
    nrm,
    shift_f,
    shift_b,
    shift_m,
    loc,
    gd_s,
    gd_r,
    tl_r,
    th_r,
    gx_s,
    gx_r,
    co_s,
    co_r,
    ou_s,
    ou_r,
    kv_s,
    kv_r,
    ha_s,
    ha_r,
    rs_s,
    rs_r,
    nd_s,
    nd_r,
):
    me = lax.axis_index("dp")
    j = lax.axis_index("seq")
    y0 = lax.rem(me, 2)
    y1 = 1 - y0
    z0 = lax.div(me, 2)
    beside = me + 1 - 2 * y0
    zn = n // 2
    here = y0 * zn + z0

    def place_of(i):
        return i % 2 * zn + i // 2

    def spot(i):
        return lax.rem(i, 2) * zn + lax.div(i, 2)

    j1 = j + 1 - 2 * lax.rem(j, 2)
    j2 = lax.rem(j + 2, 4)
    j3 = 3 - j
    tokens = band * side
    chunks = tokens // QC
    deep = band if qa == tokens else 4
    rb = wq_ref.shape[0]
    piece = tokens // n
    keys = kv.shape[2]
    turned = cot_ref.shape[1] == D
    tl = gt.shape[3]
    fl = gf.shape[3]
    vl = gvec.shape[2]
    al = up(4 * rb, 128)
    bl = sb.shape[3]
    ml = gm.shape[3]
    mo = 128 if ml > 128 else 3 * rb

    def remote(src, dst, ss, rs, dp, seq):
        return pltpu.make_async_remote_copy(
            src_ref=src,
            dst_ref=dst,
            send_sem=ss,
            recv_sem=rs,
            device_id=(dp, seq),
            device_id_type=MESH,
        )

    def both(copy):
        copy.wait_send()
        copy.wait_recv()

    def peers(body):
        def step(k, carry):
            body(k, lax.rem(me + k, n), lax.rem(me + n - k, n))
            return carry

        lax.fori_loop(1, n, step, 0)

    def z_peers(body):
        def step(k, carry):
            body(k, lax.rem(me + 2 * k, n), lax.rem(z0 + k, zn), lax.rem(z0 + zn - k, zn))
            return carry

        lax.fori_loop(1, zn, step, 0)

    loads = [
        pltpu.make_async_copy(src, dst, loc.at[at])
        for at, (src, dst) in enumerate(
            (
                (gains_ref, fg),
                (biases_ref, fb),
                (hidden_ref, fh),
                (wr_ref, fr),
                (wm_ref, fm),
                (wq_ref, fq),
                (wo_ref, fo),
                (w1_ref, f1),
                (w2_ref, f2),
                (tok_ref, x_s),
            )
        )
    ]
    for copy in loads:
        copy.start()
    def incoming(i):
        return dy_in.at[i] if turned else dy.at[rows(i * piece, piece)]

    own_cot = pltpu.make_async_copy(cot_ref.at[me], incoming(me), loc.at[10])
    own_cot.start()

    barrier = pltpu.get_barrier_semaphore()

    def greet(k, carry):
        to = lax.rem(4 * me + j + k, 4 * n)
        pl.semaphore_signal(
            barrier, inc=1, device_id=(lax.div(to, 4), lax.rem(to, 4)), device_id_type=MESH
        )
        return carry

    lax.fori_loop(1, 4 * n, greet, 0)

    for copy in loads[:5]:
        copy.wait()
    hidden16 = jnp.concatenate([fh[...], jnp.zeros((5, 4 * rb), F32)], axis=0)
    small16 = jnp.concatenate([fg[...], fb[...], jnp.zeros((5, rb), F32)], axis=0)
    gvec[here] = jnp.concatenate(
        [hidden16, small16, jnp.zeros((16, vl - 5 * rb), F32)], axis=1
    ).astype(BF)
    wm_t = fm[...].T
    gt[j, here] = jnp.concatenate(
        [fr[...].T, wm_t[0:80], wm_t[80:160], jnp.zeros((80, tl - 6 * rb), F32)], axis=1
    ).astype(BF)

    def group(at, one_of, all_but_one, each):
        def start():
            def send(peer):
                ref = one_of(here)
                remote(ref, ref, gd_s.at[at], gd_r.at[at], peer, j).start()

            each(send)

        def wait():
            both(remote(all_but_one, all_but_one, gd_s.at[at], gd_r.at[at], beside, j))

        return start, wait

    def each_peer(send):
        peers(lambda k, peer, source: send(peer))

    def each_z(send):
        z_peers(lambda k, peer, to, source: send(peer))

    def over_dp(at, buf, rows_of):
        return group(
            at, lambda i: buf.at[i, rows_of], buf.at[pl.ds(0, n - 1), rows_of], each_peer
        )

    def over_z(at, buf, rows_of):
        return group(
            at, lambda i: buf.at[i, rows_of], buf.at[pl.ds(0, zn - 1), rows_of], each_z
        )

    def swap(at, mine, theirs, dp, seq):
        def start():
            remote(mine, mine, gx_s.at[at], gx_r.at[at], dp, seq).start()

        def wait():
            remote(mine, mine, gx_s.at[at], gx_r.at[at], dp, seq).wait_send()
            remote(theirs, theirs, gx_s.at[at], gx_r.at[at], dp, seq).wait_recv()

        return start, wait

    def over_y(at, buf, rows_of):
        mine = buf.at[pl.ds(y0 * zn, zn), rows_of]
        theirs = buf.at[pl.ds(y1 * zn, zn), rows_of]
        return swap(at, mine, theirs, beside, j)

    lower = slice(0, CUT)
    upper = slice(CUT, 80)
    every = slice(0, 16)
    v_dp, v_dp_wait = over_dp(0, gvec, every)

    def t_low(i):
        return gt.at[j, i, lower]

    def t_low_copy(k, i, peer):
        return remote(t_low(i), t_low(i), gd_s.at[1], tl_r.at[k], peer, j)

    def t_low_on(i):
        remote(t_low(i), t_low(i), gx_s.at[0], gx_r.at[0], me, j2).start()

    def t_low_start():
        t_low_on(here)
        peers(lambda k, peer, source: t_low_copy(k, here, peer).start())

    def t_low_forward():
        def body(k, peer, source):
            t_low_copy(k, spot(source), peer).wait_recv()
            t_low_on(spot(source))

        peers(body)

    def t_low_wait():
        part = gt.at[j, pl.ds(0, n - 1), lower]
        remote(part, part, gd_s.at[1], tl_r.at[0], beside, j).wait_send()
        both(remote(gt.at[j, :, lower], gt.at[j2, :, lower], gx_s.at[0], gx_r.at[0], me, j2))

    t_x0, t_x0_wait = swap(1, gt.at[j, here, upper], gt.at[j2, here, upper], me, j2)

    def t_high(slot, t):
        def ref(i):
            return gt.at[slot, i, upper]

        def copy(k, i, peer):
            return remote(ref(i), ref(i), gd_s.at[2 + t], th_r.at[t, k], peer, j)

        def on(i):
            remote(ref(i), ref(i), gx_s.at[2 + t], gx_r.at[2 + t], beside, j).start()

        def start():
            z_peers(lambda k, peer, to, source: copy(k, here, peer).start())
            on(here)

        def forward():
            def body(k, peer, to, source):
                copy(k, y0 * zn + source, peer).wait_recv()
                on(y0 * zn + source)

            z_peers(body)

        def wait():
            part = gt.at[slot, pl.ds(0, zn - 1), upper]
            remote(part, part, gd_s.at[2 + t], th_r.at[t, 0], beside, j).wait_send()
            mine = gt.at[slot, pl.ds(y0 * zn, zn), upper]
            theirs = gt.at[slot, pl.ds(y1 * zn, zn), upper]
            both(remote(mine, theirs, gx_s.at[2 + t], gx_r.at[2 + t], beside, j))

        return start, forward, wait

    t_za, t_za_forward, t_ya_wait = t_high(j, 0)
    t_zb, t_zb_forward, t_yb_wait = t_high(j2, 1)
    t_ca, t_ca_wait = swap(4, gt.at[j], gt.at[j1], me, j1)
    t_cb, t_cb_wait = swap(5, gt.at[j2], gt.at[j3], me, j1)
    wq_block = gm.at[:, :, :, 0:128]
    m_dp, m_dp_wait = over_dp(4, wq_block.at[j], slice(0, 32))
    m_x, m_x_wait = swap(6, wq_block.at[j], wq_block.at[j2], me, j2)
    m_ca, m_ca_wait = swap(7, wq_block.at[j], wq_block.at[j1], me, j1)
    m_cb, m_cb_wait = swap(8, wq_block.at[j2], wq_block.at[j3], me, j1)
    f_x0, f_x0_wait = swap(9, gf.at[j, here], gf.at[j2, here], me, j2)
    fl_za, fl_za_wait = over_z(5, gf.at[j], lower)
    fl_zb, fl_zb_wait = over_z(6, gf.at[j2], lower)
    fh_za, fh_za_wait = over_z(7, gf.at[j], upper)
    fh_zb, fh_zb_wait = over_z(8, gf.at[j2], upper)
    fl_ya, fl_ya_wait = over_y(10, gf.at[j], lower)
    fl_yb, fl_yb_wait = over_y(11, gf.at[j2], lower)
    fh_ya, fh_ya_wait = over_y(12, gf.at[j], upper)
    fh_yb, fh_yb_wait = over_y(13, gf.at[j2], upper)
    f_ca, f_ca_wait = swap(14, gf.at[j], gf.at[j1], me, j1)
    f_cb, f_cb_wait = swap(15, gf.at[j2], gf.at[j3], me, j1)

    pl.semaphore_wait(barrier, 4 * n - 1)
    t_x0()
    t_za()
    t_low_start()

    for copy in loads[5:9]:
        copy.wait()
    wq_t = fq[...].T
    gm[j, here, :, 0:128] = jnp.concatenate(
        [
            wq_t[0:32],
            wq_t[32:64],
            jnp.concatenate([wq_t[64:80], jnp.zeros((16, rb), F32)], axis=0),
            jnp.zeros((32, 128 - 3 * rb), F32),
        ],
        axis=1,
    ).astype(BF)
    w1_t = f1[...].T
    gf[j, here] = jnp.concatenate(
        [f2[...].T]
        + [w1_t[80 * v : 80 * v + 80] for v in range(4)]
        + [fo[...].T, jnp.zeros((80, fl - 9 * rb), F32)],
        axis=1,
    ).astype(BF)
    t_x0_wait()
    t_zb()
    v_dp()
    m_dp()
    f_x0()

    t_low_forward()
    t_za_forward()
    t_zb_forward()
    f_x0_wait()
    fl_za()
    fl_zb()
    v_dp_wait()
    hp[...] = jnp.concatenate([gvec[place_of(i), :, 0 : 4 * rb] for i in range(n)], axis=1).astype(F32)
    vp[...] = jnp.concatenate(
        [gvec[place_of(i), :, 4 * rb : 5 * rb] for i in range(n)], axis=1
    ).astype(F32)

    def gain(k):
        return vp[k : k + 1, :]

    def shift(k):
        return vp[3 + k : 4 + k, :]

    loads[9].wait()

    def norm_one(c, carry):
        at = rows(c * QC, QC)
        vhat, _ = norm_parts(x_s[at, :].astype(F32))
        low = (vhat * gain(0) + shift(0)).astype(BF)
        abf[at, :] = low
        wide = jnp.concatenate([low.astype(F32), jnp.zeros((QC, 64), F32)], axis=1)
        for t in range(3):
            a3[t, at, :] = wide[:, 128 * t : 128 * t + 128]
        return carry

    lax.fori_loop(0, chunks, norm_one, 0)
    half = side // 2
    for dd in range(4):
        for i in range(band // 2):
            start = (2 * i + dd // 2) * side + dd % 2
            cut = jnp.concatenate(
                [a3[t, pl.ds(start, half, stride=2), :] for t in range(3)], axis=1
            )
            pat[dd, i * half : (i + 1) * half, :] = cut[:, 0:D].astype(BF)

    bucket = bucket_ref[0]
    k_row = lax.broadcasted_iota(jnp.int32, (4 * keys, 128), 0)
    k_lane = lax.broadcasted_iota(jnp.int32, (4 * keys, 128), 1)
    k_id = (lax.div(k_row, half) >= half // 2).astype(jnp.int32) * 2 + (
        lax.rem(k_row, half) >= half // 2
    ).astype(jnp.int32)
    off = (k_id != k_lane).astype(jnp.int32) * bucket * (k_lane < 4).astype(jnp.int32)
    kmask = datn.at[0]
    qmask = dy_t.at[0:128]
    kmask[...] = (off.astype(F32) * MASKED).astype(BF)
    q_row = lax.broadcasted_iota(jnp.int32, (128, tokens), 0)
    place = lax.broadcasted_iota(jnp.int32, (128, tokens), 1)
    q_id = (lax.div(place, side) + j * band >= half).astype(jnp.int32) * 2 + (
        lax.rem(place, side) >= half
    ).astype(jnp.int32)
    qmask[...] = (q_id == q_row).astype(F32).astype(BF)
    col = lax.broadcasted_iota(jnp.int32, (side, side), 0)
    ok_l = (col > 0).astype(jnp.int32) * (1 - bucket * (col == half).astype(jnp.int32))
    ok_r = (col < side - 1).astype(jnp.int32) * (
        1 - bucket * (col == half - 1).astype(jnp.int32)
    )
    lane = lax.broadcasted_iota(jnp.int32, (side, side), 1)
    from_l = (ok_l * (lane == col - 1).astype(jnp.int32)).astype(F32).astype(BF)
    from_r = (ok_r * (lane == col + 1).astype(jnp.int32)).astype(F32).astype(BF)
    shift_f[...] = jnp.concatenate([from_l, from_r], axis=1)
    shift_b[...] = jnp.concatenate([from_r, from_l], axis=1)
    shift_m[...] = jnp.concatenate([from_r, from_l], axis=0)
    top_ok = (
        (j > 0).astype(jnp.int32) * (1 - bucket * (j * band == half).astype(jnp.int32))
    ).astype(F32)
    low_ok = (
        (j < 3).astype(jnp.int32) * (1 - bucket * ((j + 1) * band == half).astype(jnp.int32))
    ).astype(F32)

    m_dp_wait()
    m_x()
    t_ya_wait()
    t_yb_wait()
    t_low_wait()
    t_ca()
    t_cb()
    m_x_wait()
    m_ca()
    m_cb()
    t_ca_wait()
    t_cb_wait()

    for s in range(4):
        span = slice(80 * s, 80 * s + 80)

        def lanes(lo, hi, over):
            return jnp.concatenate([gt[s, place_of(i), :, lo:hi] for i in over], axis=1)

        for dd in range(4):
            wrt[dd, span, :] = lanes(0, 4 * rb, range(dd * n // 4, (dd + 1) * n // 4))
        for v in range(2):
            wop[160 * s + 80 * v : 160 * s + 80 * v + 80, :] = lanes(
                (4 + v) * rb, (5 + v) * rb, range(n)
            )
    for h in range(HEADS):
        wmt[128 * h : 128 * h + 64, :] = wop[HEAD * h : HEAD * h + HEAD, :]
        wmt[128 * h + 64 : 128 * h + 128, :] = wop[D + HEAD * h : D + HEAD * h + HEAD, :]

    red = shift(2) + nt(pat[0], wrt[0])
    for dd in range(1, 4):
        red = red + nt(pat[dd], wrt[dd])
    wide_red = jnp.concatenate([red, jnp.zeros((keys, 64), F32)], axis=1)
    for t in range(3):
        a3[t, 0:keys, :] = wide_red[:, 128 * t : 128 * t + 128]
    vhat, _ = norm_parts(red)
    low = (vhat * gain(1) + shift(3)).astype(BF)
    memin[...] = low
    zero64 = jnp.zeros((1, HEAD), F32)
    value_shift = jnp.concatenate(
        [
            part
            for h in range(HEADS)
            for part in (zero64, shift(4)[:, HEAD * h : HEAD * h + HEAD])
        ],
        axis=1,
    )
    memory = (nt(low, wmt[...]) + value_shift).astype(BF)
    for h in range(HEADS):
        kv[h, j] = memory[:, 128 * h : 128 * h + 128]

    def kv_copy(h, slot, t, other):
        return remote(
            kv.at[h, slot], kv.at[h, slot], kv_s.at[h, t], kv_r.at[h, t], me, other
        )

    def kv_send(h, carry):
        kv_copy(h, j, 0, j2).start()
        kv_copy(h, j, 1, j1).start()
        return carry

    lax.fori_loop(0, 2, kv_send, 0)

    wqp = wop
    m_ca_wait()
    m_cb_wait()
    for s in range(4):
        at = 80 * s
        wqt[at : at + 32, :] = jnp.concatenate([gm[s, place_of(i), :, 0:rb] for i in range(n)], axis=1)
        wqt[at + 32 : at + 64, :] = jnp.concatenate(
            [gm[s, place_of(i), :, rb : 2 * rb] for i in range(n)], axis=1
        )
        wqt[at + 64 : at + 80, :] = jnp.concatenate(
            [gm[s, place_of(i), 0:16, 2 * rb : 3 * rb] for i in range(n)], axis=1
        )
    for h in range(HEADS):
        wqp[128 * h : 128 * h + 64, :] = wqt[HEAD * h : HEAD * h + HEAD, :]
        wqp[128 * h + 64 : 128 * h + 128, :] = jnp.zeros((64, D), BF)

    query_shift = jnp.concatenate(
        [
            part
            for h in range(HEADS)
            for part in (shift(1)[:, HEAD * h : HEAD * h + HEAD], zero64)
        ],
        axis=1,
    )

    def across(c):
        return pl.ds(pl.multiple_of(c * QC, QC), QC)

    def queries(c, carry):
        at = rows(c * QC, QC)
        q = (nt(abf[at, :], wqp[...]) + query_shift).astype(BF) * jnp.asarray(HEAD**-0.5, BF)
        for h in range(HEADS):
            tile = q[:, 128 * h : 128 * h + 128]
            qnat[h, at, :] = tile
            qt[h, :, across(c)] = tile.T
        return carry

    lax.fori_loop(0, chunks, queries, 0)
    lax.fori_loop(2, HEADS, kv_send, 0)

    def send_cot(k, peer, source):
        remote(cot_ref.at[peer], incoming(me), co_s.at[0], co_r.at[0], peer, j).start()

    def wait_cot():
        part = cot_ref.at[pl.ds(0, n - 1)]
        both(remote(part, part, co_s.at[0], co_r.at[0], beside, j))

    def kv_forward(h):
        kv_copy(h, j2, 0, j2).wait_recv()
        kv_copy(h, j2, 2, j1).start()

    fl_za_wait()
    fl_zb_wait()
    fl_ya()
    fl_yb()
    fh_za()
    fh_zb()
    kv_forward(0)

    def attend(h, carry):
        @pl.when(h == HEADS - 1)
        def _():
            fl_ya_wait()
            fl_yb_wait()
            fh_ya_wait()
            fh_yb_wait()
            f_ca()
            f_cb()
            peers(send_cot)

        kv_copy(h, j, 0, j2).wait_send()
        kv_copy(h, j, 1, j1).wait_send()
        kv_copy(h, j2, 2, j1).wait_send()
        kv_copy(h, j1, 1, j1).wait_recv()
        kv_copy(h, j3, 2, j1).wait_recv()
        tile = kv[h].reshape(4 * keys, 128)
        kvt[h] = tile.T
        left = jnp.concatenate([tile, kmask[...]], axis=1)
        values = jnp.concatenate([kvt[h, 64:128, :], jnp.ones((16, 4 * keys), BF)], axis=0)
        for c in range(tokens // qa):
            cut = slice(c * qa, (c + 1) * qa)
            scores = nn(left, jnp.concatenate([qt[h, :, cut], qmask[:, cut]], axis=0))
            if c == 0:

                @pl.when(h < HEADS - 1)
                def _():
                    kv_forward(h + 1)

                @pl.when(h == 1)
                def _():
                    fh_za_wait()
                    fh_zb_wait()
                    fh_ya()
                    fh_yb()

            largest = jnp.max(scores, axis=0, keepdims=True)
            powers = jnp.exp(scores - largest).astype(BF)
            prob[h, :, cut] = powers
            got = nn(values, powers)
            scale = 1.0 / got[64:65, :]
            rtot[h, :, cut] = scale
            att_t[rows(h * HEAD, HEAD), cut] = (got[0:64, :] * scale).astype(BF)
        return carry

    lax.fori_loop(0, HEADS, attend, 0)

    f_ca_wait()
    f_cb_wait()
    for s in range(4):
        span = slice(80 * s, 80 * s + 80)
        w2t[span, :] = jnp.concatenate([gf[s, place_of(i), :, 0 : 4 * rb] for i in range(n)], axis=1)
        for v in range(4):
            at = 320 * s + 80 * v
            w1t[at : at + 80, :] = jnp.concatenate(
                [gf[s, place_of(i), :, (4 + v) * rb : (5 + v) * rb] for i in range(n)], axis=1
            )
        wot[span, :] = jnp.concatenate(
            [gf[s, place_of(i), :, 8 * rb : 9 * rb] for i in range(n)], axis=1
        )
    wop_full = wot[...].T
    for h in range(HEADS):
        wop[128 * h : 128 * h + 64, :] = jnp.zeros((64, D), BF)
        wop[128 * h + 64 : 128 * h + 128, :] = wop_full[HEAD * h : HEAD * h + HEAD, :]

    def middle(c, carry):
        at = rows(c * QC, QC)
        att = att_t[:, across(c)].T
        att_n[at, :] = att
        value = x_s[at, :].astype(F32) + nt(att, wot[...]) + shift(5)
        mid[at, :] = value
        vhat, _ = norm_parts(value)
        low = (vhat * gain(2) + shift(6)).astype(BF)
        bn[at, :] = low
        return carry

    lax.fori_loop(0, chunks, middle, 0)

    edge = tokens - side

    def hidden_of(value):
        return (nt(value, w1t[...]) + hp[9:10, :]).astype(BF)

    ends = hidden_of(jnp.concatenate([bn[0:side, :], bn[edge:tokens, :]], axis=0))
    hidp[side : 2 * side, :] = ends[0:side]
    hidp[tokens : tokens + side, :] = ends[side : 2 * side]
    above = lax.rem(j + 3, 4)
    below = lax.rem(j + 1, 4)

    def rim_up(buf, halo, at):
        return remote(buf.at[pl.ds(side, side)], halo.at[1], ha_s.at[at], ha_r.at[at], me, above)

    def rim_down(buf, halo, at):
        return remote(
            buf.at[pl.ds(tokens, side)], halo.at[0], ha_s.at[at + 1], ha_r.at[at + 1], me, below
        )

    def rim_send(buf, halo, at):
        @pl.when(j > 0)
        def _():
            rim_up(buf, halo, at).start()

        @pl.when(j < 3)
        def _():
            rim_down(buf, halo, at).start()

    def rim_wait(buf, halo, at):
        @pl.when(j > 0)
        def _():
            rim_up(buf, halo, at).wait_send()
            rim_down(buf, halo, at).wait_recv()

        @pl.when(j < 3)
        def _():
            rim_down(buf, halo, at).wait_send()
            rim_up(buf, halo, at).wait_recv()

        for t, (to, ok) in enumerate(((0, top_ok), (tokens + side, low_ok))):
            seen = jnp.full((side, FF), ok, F32) > 0.5
            buf[to : to + side, :] = jnp.where(seen, halo[t].astype(F32), 0.0).astype(BF)

    rim_send(hidp, hidh, 0)

    inner = (tokens - 2 * side) // 2

    def inner_hidden(c, carry):
        start = side + c * inner
        hidp[rows(start + side, inner), :] = hidden_of(bn[rows(start, inner), :])
        return carry

    lax.fori_loop(0, 2, inner_hidden, 0)

    def tile_at(t):
        return pl.ds(pl.multiple_of(t * 128, 128), 128)

    def taps_of(lanes):
        return [hp[k : k + 1, lanes] for k in range(9)]

    def conv_over(lo, hi, step, tiles):
        def conv_tile(t, carry):
            lanes = tile_at(t)
            taps = taps_of(lanes)
            base = hp[10:11, lanes]

            def row(at, inner):
                r = lo + at * step
                around = [hidp[rows((r + a) * side, side), lanes].astype(F32) for a in range(3)]
                parts = [
                    taps[b] * around[0] + taps[3 + b] * around[1] + taps[6 + b] * around[2]
                    for b in range(3)
                ]
                moved = jnp.concatenate([parts[0].astype(BF), parts[2].astype(BF)], axis=0)
                z = base + parts[1] + nn(shift_f[...], moved)
                cdf = 0.5 + 0.5 * lax.erf(z * (0.5**0.5))
                pdf = jnp.exp(z * z * -0.5) * 0.3989422804014327
                act[rows((r + 1) * side, side), lanes] = (z * cdf).astype(BF)
                gp[rows(r * side, side), lanes] = (cdf + z * pdf).astype(BF)
                return inner

            lax.fori_loop(0, (hi - lo) // step, row, 0, unroll=True)
            return carry

        lax.fori_loop(0, FF // 128, conv_tile, 0, unroll=tiles)

    conv_over(1, band - 1, 1, 1)
    rim_wait(hidp, hidh, 0)
    conv_over(0, 2 * (band - 1), band - 1, 5)

    def out_chunk(c, carry):
        at = rows(c * QC, QC)
        value = mid[at, :] + nt(act[rows(side + c * QC, QC), :], w2t[...]) + shift(7)
        for p in range(QC // piece):
            part = value[p * piece : (p + 1) * piece, :]
            out_t[c * (QC // piece) + p] = (part.T if turned else part).astype(BF)
        return carry

    lax.fori_loop(0, chunks, out_chunk, 0)

    def send_out(k, peer, source):
        remote(out_t.at[peer], out_ref.at[me], ou_s.at[0], ou_r.at[0], peer, j).start()

    def wait_out():
        part = out_t.at[pl.ds(0, n - 1)]
        both(remote(part, part, ou_s.at[0], ou_r.at[0], beside, j))

    peers(send_out)
    own_out = pltpu.make_async_copy(out_t.at[me], out_ref.at[me], loc.at[11])
    own_out.start()

    own_cot.wait()
    wait_cot()
    for i in range(n):
        if turned:
            dy_t[:, i * piece : (i + 1) * piece] = dy_in[i]
            dy[i * piece : (i + 1) * piece, :] = dy_in[i].T
    if not turned:
        dy_t[...] = dy[...].T
    vg[...] = jnp.zeros(vg.shape, F32)
    vg[10:11, :] = colsum(dy[...].astype(F32))

    def scatter(sems, s, cut, direct, bufs, own):
        top = s.shape[2]
        r1, xl, yl, dl, yh, dh, xh = bufs
        low, high = slice(0, cut), slice(cut, top)
        slots = (j, j2)
        count = n if direct else zn
        mine = pl.ds(y0 * zn, zn)
        theirs = pl.ds(y1 * zn, zn)

        def copy(src, dst, t, dp, seq):
            at = sems[t]
            return remote(src, dst, rs_s.at[at], rs_r.at[at], dp, seq)

        def core():
            return [copy(s.at[slot], r1.at[t], t, me, j1) for t, slot in enumerate((j1, j3))]

        def low_x():
            return copy(s.at[j2, :, low], xl, 2, me, j2)

        def low_y():
            return copy(s.at[j, theirs, low], yl, 3, beside, j)

        def high_y():
            return [
                copy(s.at[slot, theirs, high], yh.at[t], 4 + t, beside, j)
                for t, slot in enumerate(slots)
            ]

        def high_x():
            return copy(s.at[j2, here, high], xh, 6, me, j2)

        def out(slot, rows_of, land, t):
            def send(k, peer, to):
                copy(s.at[slot, to, rows_of], land.at[k], t, peer, j).start()

            if direct:
                peers(lambda k, peer, source: send(k, peer, spot(peer)))
            else:
                z_peers(lambda k, peer, to, source: send(k, peer, y0 * zn + to))

        def landed(slot, rows_of, land, t):
            part = land.at[pl.ds(1, count - 1)]
            both(copy(part, part, t, beside, j))
            return lax.fori_loop(
                1,
                count,
                lambda k, v: v + land[k].astype(F32),
                s[slot, here, rows_of].astype(F32),
            )

        def add(slot, start, rows_of, extra):
            def body(i, carry):
                s[slot, start + i, rows_of] = (
                    s[slot, start + i, rows_of].astype(F32) + extra[i].astype(F32)
                ).astype(BF)
                return carry

            lax.fori_loop(0, extra.shape[0], body, 0)

        def one():
            for c in core():
                c.start()

        def two():
            for c in core():
                both(c)
            for t, slot in enumerate(slots):
                add(slot, 0, slice(0, top), r1.at[t])
            if cut < top:
                if direct:
                    for t, slot in enumerate(slots):
                        out(slot, high, dh.at[t], 4 + t)
                else:
                    for c in high_y():
                        c.start()
            if cut > 0:
                low_x().start()

        def low_three():
            both(low_x())
            add(j, 0, low, xl)
            if direct:
                out(j, low, dl, 3)
            else:
                low_y().start()

        def high_three():
            for c in high_y():
                both(c)
            for t, slot in enumerate(slots):
                add(slot, y0 * zn, high, yh.at[t])
                out(slot, high, dh.at[t], 7 + t)

        def low_four():
            both(low_y())
            add(j, y0 * zn, low, yl)
            out(j, low, dl, 9)

        def high_four():
            first = 4 if direct else 7
            own[high, :] = landed(j, high, dh.at[0], first)
            s[j2, here, high] = landed(j2, high, dh.at[1], first + 1).astype(BF)
            high_x().start()

        def low_five():
            own[low, :] = landed(j, low, dl, 3 if direct else 9)

        def high_five():
            both(high_x())
            own[high, :] = own[high, :] + xh[...].astype(F32)

        return one, two, low_three, low_four, low_five, high_three, high_four, high_five

    own_t = own_s.at[0:80, 0:tl]
    own_a = own_s.at[0:80, tl : tl + al]
    own_b = own_s.at[0:80, tl + al : tl + al + bl]
    own_m = own_s.at[96:128, 0:ml]
    a_one, a_two, a_three, a_four, a_five, _, _, _ = scatter(
        (0, 1, 2, 3, 0, 0, 0, 0, 0, 4), gf.at[:, :, :, 0:al], 80, False, (ra0, ra1, ra2, ra3, ra4, ra5, ra6), own_a
    )
    b_one, b_two, bl_three, bl_four, bl_five, bh_three, bh_four, bh_five = scatter(
        (5, 6, 27, 28, 7, 8, 9, 10, 11, 29), sb, 32, False, (rb0, rb1, rb2, rb3, rb4, rb5, rb6), own_b
    )
    m_one, m_two, m_three, m_four, m_five, _, _, _ = scatter(
        (12, 13, 14, 15, 0, 0, 0, 0, 0, 33), gm, 32, False, (rm0, rm1, rm2, rm3, rm4, rm5, rm6), own_m
    )
    def t_core(t, slot, to, rows_of):
        return remote(
            gt.at[slot, :, rows_of], rt0.at[to, :, rows_of], rs_s.at[16 + t], rs_r.at[16 + t], me, j1
        )

    def t_cores():
        return (
            t_core(0, j3, 1, lower),
            t_core(1, j1, 0, upper),
            t_core(2, j3, 1, upper),
            t_core(3, j1, 0, lower),
        )

    def t_add(slot, start, count, rows_of, extra):
        def body(i, carry):
            gt[slot, start + i, rows_of] = (
                gt[slot, start + i, rows_of].astype(F32) + extra[start + i, rows_of].astype(F32)
            ).astype(BF)
            return carry

        lax.fori_loop(0, count, body, 0)

    def t_half(t):
        part = pl.ds((y1 if t == 0 else y0) * zn, zn)
        return remote(
            gt.at[j2, part, lower], rt1.at[part], rs_s.at[20 + t], rs_r.at[20 + t], me, j2
        )

    def t_dp(slot, i, rows_of, land, sem, k, peer):
        remote(
            gt.at[slot, i, rows_of], land.at[k], rs_s.at[sem], rs_r.at[sem], peer, j
        ).start()

    def t_landed(slot, rows_of, land, sem):
        part = land.at[pl.ds(1, n - 1)]
        both(remote(part, part, rs_s.at[sem], rs_r.at[sem], beside, j))
        return lax.fori_loop(
            1, n, lambda k, v: v + land[k].astype(F32), gt[slot, here, rows_of].astype(F32)
        )

    def t_one():
        for c in t_cores():
            c.start()

    def t_two():
        cores = t_cores()
        both(cores[0])
        t_add(j2, 0, n, lower, rt0.at[1])
        t_half(0).start()
        t_half(1).start()
        both(cores[1])
        both(cores[2])
        for t, slot in enumerate((j, j2)):
            t_add(slot, 0, n, upper, rt0.at[t])
            peers(
                lambda k, peer, source: t_dp(
                    slot, spot(peer), upper, rt5.at[t], 22 + t, k, peer
                )
            )
        both(cores[3])
        t_add(j, 0, n, lower, rt0.at[0])

    def tl_three(t):
        both(t_half(t))
        start = (y1 if t == 0 else y0) * zn

        def body(i, carry):
            at = start + i
            gt[j, at, lower] = (gt[j, at, lower].astype(F32) + rt1[at].astype(F32)).astype(BF)
            return carry

        lax.fori_loop(0, zn, body, 0)

        def send(i, carry):
            k = 2 * i + (1 if t == 0 else 2)
            peer = lax.rem(me + k, n)
            t_dp(j, spot(peer), lower, rt3, 24, k, peer)
            return carry

        lax.fori_loop(0, zn if t == 0 else zn - 1, send, 0)

    def th_x():
        return remote(gt.at[j2, here, upper], rt6, rs_s.at[25], rs_r.at[25], me, j2)

    def th_four():
        own_t[upper, :] = t_landed(j, upper, rt5.at[0], 22)
        gt[j2, here, upper] = t_landed(j2, upper, rt5.at[1], 23).astype(BF)
        th_x().start()

    def tl_five():
        own_t[lower, :] = t_landed(j, lower, rt3, 24)

    def th_five():
        both(th_x())
        own_t[upper, :] = own_t[upper, :] + rt6[...].astype(F32)


    per = 640 // (4 * rb)
    for b in range(2):
        value = nn(dy_t[...], act[side : side + tokens, 640 * b : 640 * b + 640]).astype(BF)
        for ii in range(per):
            i = b * per + ii
            gf[:, place_of(i), :, 0 : 4 * rb] = value[
                :, 4 * rb * ii : 4 * rb * (ii + 1)
            ].reshape(4, 80, 4 * rb)

    a_one()

    def slope_of(at):
        return nn(dy[at, :], w2t[...])

    dz = act
    for at in (0, edge):
        dz[side + at : 2 * side + at, :] = (
            slope_of(slice(at, at + side)) * gp[at : at + side, :].astype(F32)
        ).astype(BF)
    rim_send(dz, dzh, 2)

    def inner_slope(c, carry):
        at = rows(side + c * inner, inner)
        dz[rows(2 * side + c * inner, inner), :] = (
            slope_of(at) * gp[at, :].astype(F32)
        ).astype(BF)
        return carry

    lax.fori_loop(0, 2, inner_slope, 0)

    a_two()

    dhid = gp

    def back_over(lo, hi, step, tiles):
        def back_tile(t, carry):
            lanes = tile_at(t)
            taps = taps_of(lanes)

            def row(at, inner):
                r = lo + at * step
                around = [dz[rows((r + a) * side, side), lanes].astype(F32) for a in range(3)]
                parts = [
                    taps[b] * around[2] + taps[3 + b] * around[1] + taps[6 + b] * around[0]
                    for b in range(3)
                ]
                both_ways = jnp.concatenate([parts[0].astype(BF), parts[2].astype(BF)], axis=0)
                low = (parts[1] + nn(shift_b[...], both_ways)).astype(BF)
                dhid[rows(r * side, side), lanes] = low
                return inner

            lax.fori_loop(0, (hi - lo) // step, row, 0, unroll=True)
            return carry

        lax.fori_loop(0, FF // 128, back_tile, 0, unroll=tiles)

    back_over(1, band - 1, 1, 1)
    rim_wait(dz, dzh, 2)
    back_over(0, 2 * (band - 1), band - 1, 5)

    def fold(v):
        return jnp.sum(v.reshape(-1, 8, 128), axis=0)

    def tap_sums(lo, hi):
        def tile(t, carry):
            lanes = tile_at(t)

            def row(r, sums):
                low = dz[rows((r + 1) * side, side), lanes]
                here_f = low.astype(F32)
                sides = nn(shift_m[...], low)
                moved = [sides[0:side], here_f, sides[side : 2 * side]]
                found = []
                for a in range(3):
                    source = hidp[rows((r + a) * side, side), lanes].astype(F32)
                    for b in range(3):
                        found.append(fold(moved[b] * source))
                found.append(fold(here_f))
                return tuple(s + f for s, f in zip(sums, found))

            sums = lax.fori_loop(
                0, band, row, tuple(jnp.zeros((8, 128), F32) for _ in range(10)), unroll=deep
            )
            hg[:, lanes] = jnp.concatenate(
                [colsum(s) for s in sums[0:9]]
                + [hg[9:10, lanes], colsum(sums[9]), jnp.zeros((5, 128), F32)],
                axis=0,
            )
            return carry

        lax.fori_loop(lo, hi, tile, 0)

    hg[9:10, :] = colsum(dhid[...].astype(F32))
    bn_t = dy_t
    bn_t[...] = bn[...].T
    for b in range(2):
        value = nn(bn_t[...], dhid[:, 640 * b : 640 * b + 640]).T.astype(BF)
        value = value.reshape(2, 4, 80, D)
        for i in range(n):
            sb[2 * b : 2 * b + 2, place_of(i), :, 0 : 4 * rb] = jnp.concatenate(
                [value[:, v, :, rb * i : rb * i + rb] for v in range(4)], axis=2
            )

    b_one()

    zero_row = jnp.zeros((1, D), F32)
    dbr = bn
    dbr_t = dy_t

    def back_middle(c, carry):
        at = rows(c * QC, QC)
        value, in_gain, in_shift = norm_back(mid[at, :], gain(2), nn(dhid[at, :], w1t[...]))
        value = value + dy[at, :].astype(F32)
        mid[at, :] = value
        low = value.astype(BF)
        dbr[at, :] = low
        dbr_t[:, across(c)] = low.T
        spread = nt(wop[...], low)
        for h in range(HEADS):
            tile = spread[128 * h : 128 * h + 128, :] * rtot[h, :, across(c)]
            tile_low = tile.astype(BF)
            qt[h, :, across(c)] = tile_low
            datn[h, at, :] = tile_low.T
            delta[h, :, across(c)] = colsum(
                tile_low[64:128, :].astype(F32)
                * att_t[HEAD * h : HEAD * h + HEAD, across(c)].astype(F32)
            )
        return (carry[0] + in_gain, carry[1] + in_shift, carry[2] + colsum(low.astype(F32)))

    sums = lax.fori_loop(0, chunks, back_middle, (zero_row, zero_row, zero_row))
    vg[2:3, :] = sums[0]
    vg[9:10, :] = sums[1]
    vg[8:9, :] = sums[2]
    a_three()
    b_two()

    def dkv(h, slot):
        return gp.at[rows(slot * keys, keys), tile_at(h)]

    def dk_core(h):
        return [
            remote(dkv(h, slot), rk1.at[h, t], kv_s.at[h, t], kv_r.at[h, t], me, j1)
            for t, slot in enumerate((j1, j3))
        ]

    def dk_x(h):
        return remote(dkv(h, j2), rk2.at[h], kv_s.at[h, 2], kv_r.at[h, 2], me, j2)

    def dk_two(h):
        for copy in dk_core(h):
            both(copy)
        for t, slot in enumerate((j, j2)):
            part = dkv(h, slot)
            part[...] = (part[...].astype(F32) + rk1[h, t].astype(F32)).astype(BF)
        dk_x(h).start()

    def dk_three(h):
        both(dk_x(h))
        qnat[h, 0:keys, :] = (dkv(h, j)[...].astype(F32) + rk2[h].astype(F32)).astype(BF)

    def back_head(h, carry):
        tile = kv[h].reshape(4 * keys, 128)
        total = None
        for c in range(tokens // qa):
            cut = slice(c * qa, (c + 1) * qa)
            powers = prob[h, :, cut]
            slopes = nn(tile, qt[h, :, cut]) - delta[h, :, cut]
            ds = (powers.astype(F32) * slopes).astype(BF)
            part = nn(ds, qnat[h, cut, :]) + nn(powers, datn[h, cut, :])
            prob[h, :, cut] = ds
            total = part if total is None else total + part
        gp[0 : 4 * keys, tile_at(h)] = total.astype(BF)
        for copy in dk_core(h):
            copy.start()

        @pl.when(h == 2)
        def _():
            a_four()

        @pl.when(h == 3)
        def _():
            bl_three()

        @pl.when(h == 4)
        def _():
            bh_three()

        @pl.when(h >= 1)
        def _():
            dk_two(h - 1)

        return carry

    lax.fori_loop(0, HEADS, back_head, 0)

    dq_t = att_t

    def back_query(h, carry):
        for c in range(tokens // qa):
            cut = slice(c * qa, (c + 1) * qa)
            dq_t[rows(h * HEAD, HEAD), cut] = (
                nn(kvt[h, 0:64, :], prob[h, :, cut]) * HEAD**-0.5
            ).astype(BF)
        return carry

    lax.fori_loop(0, 2, back_query, 0)
    dk_two(HEADS - 1)
    lax.fori_loop(2, HEADS, back_query, 0)
    bl_four()

    dq = dy

    def flip(c, total):
        low = dq_t[:, across(c)].T
        dq[rows(c * QC, QC), :] = low
        return total + colsum(low.astype(F32))

    vg[4:5, :] = lax.fori_loop(0, chunks, flip, zero_row)
    value = nn(dq_t[...], abf[...]).astype(BF)
    other = nn(dbr_t[...], att_n[...]).astype(BF)

    def folded(v, i):
        part = v[:, rb * i : rb * i + rb].reshape(4, 80, rb)
        return [
            part[:, 0:32],
            part[:, 32:64],
            jnp.concatenate([part[:, 64:80], jnp.zeros((4, 16, rb), BF)], axis=1),
        ]

    for i in range(n):
        gm[:, place_of(i), :, 0 : 3 * rb] = jnp.concatenate(folded(value, i), axis=2)
        gm[:, place_of(i), :, mo : mo + 3 * rb] = jnp.concatenate(folded(other, i), axis=2)
    m_one()
    tap_sums(0, FF // 256)
    m_two()
    for h in range(HEADS):
        dk_three(h)

    dm = jnp.concatenate([qnat[h, 0:keys, :] for h in range(HEADS)], axis=1)
    dm_sum = colsum(dm.astype(F32))
    vg[7:8, :] = jnp.concatenate(
        [dm_sum[:, 128 * h + 64 : 128 * h + 128] for h in range(HEADS)], axis=1
    )
    kept = jnp.concatenate([a3[t, 0:keys, :] for t in range(3)], axis=1)[:, 0:D]
    dv, in_gain, in_shift = norm_back(kept, gain(1), nn(dm, wmt[...]))
    vg[1:2, :] = in_gain
    vg[6:7, :] = in_shift
    dred = dv.astype(BF)
    vg[5:6, :] = colsum(dred.astype(F32))
    dred_t = dred.T
    for dd in range(4):
        value = nn(dred_t, pat[dd]).astype(BF)
        count = n // 4
        for ii in range(count):
            i = dd * count + ii
            gt[:, place_of(i), :, 0 : 4 * rb] = value[
                :, 4 * rb * ii : 4 * rb * (ii + 1)
            ].reshape(4, 80, 4 * rb)
    value = nn(dm.T, memin[...]).astype(BF)
    value = jnp.concatenate(
        [value[128 * h : 128 * h + 64] for h in range(HEADS)]
        + [value[128 * h + 64 : 128 * h + 128] for h in range(HEADS)],
        axis=0,
    ).reshape(4, 2, 80, D)
    for i in range(n):
        gt[:, place_of(i), :, 4 * rb : 6 * rb] = jnp.concatenate(
            [value[:, v, :, rb * i : rb * i + rb] for v in range(2)], axis=2
        )
    t_one()

    t_two()

    for dd in range(4):
        back = nn(dred, wrt[dd])
        back = jnp.concatenate([back, jnp.zeros((keys, 64), F32)], axis=1)
        for i in range(band // 2):
            start = (2 * i + dd // 2) * side + dd % 2
            for t in range(3):
                a3[t, pl.ds(start, half, stride=2), :] = back[
                    i * half : (i + 1) * half, 128 * t : 128 * t + 128
                ]

    def back_first(c, carry):
        at = rows(c * QC, QC)
        e = nn(dq[at, :], wqt[...]) + jnp.concatenate([a3[t, at, :] for t in range(3)], axis=1)[:, 0:D]
        value, in_gain, in_shift = norm_back(x_s[at, :].astype(F32), gain(0), e)
        bn[at, :] = (mid[at, :] + value).astype(BF)
        return (carry[0] + in_gain, carry[1] + in_shift)

    sums = lax.fori_loop(0, chunks, back_first, (zero_row, zero_row))
    token_out = pltpu.make_async_copy(bn, tgrad_ref, loc.at[12])
    token_out.start()
    vg[0:1, :] = sums[0]
    vg[3:4, :] = sums[1]
    m_three()
    tap_sums(FF // 256, FF // 128)
    for i in range(n):
        sv[place_of(i), :, 0 : 4 * rb] = hg[:, 4 * rb * i : 4 * rb * (i + 1)].astype(BF)
        sv[place_of(i), :, 4 * rb : 5 * rb] = vg[:, rb * i : rb * i + rb].astype(BF)

    def v_out(k, peer, source):
        remote(sv.at[spot(peer)], rv1.at[k], rs_s.at[26], rs_r.at[26], peer, j).start()

    peers(v_out)
    tl_three(0)
    tl_three(1)
    bh_four()
    m_four()
    part = rv1.at[pl.ds(1, n - 1)]
    both(remote(part, part, rs_s.at[26], rs_r.at[26], beside, j))
    rv2[j] = lax.fori_loop(
        1, n, lambda k, total: total + rv1[k].astype(F32), sv[here].astype(F32)
    ).astype(BF)

    def v_seq(t, slot, other):
        ref = rv2.at[slot]
        return remote(ref, ref, rs_s.at[30 + t], rs_r.at[30 + t], me, other)

    for t, other in enumerate((j1, j2, j3)):
        v_seq(t, j, other).start()
    th_four()
    a_five()
    bl_five()
    bh_five()
    squares = jnp.sum(own_a[:, 0 : 4 * rb] * own_a[:, 0 : 4 * rb])
    squares += jnp.sum(own_b[:, 0 : 4 * rb] * own_b[:, 0 : 4 * rb])
    th_five()
    m_five()
    for at in (0, mo):
        full = own_m[:, at : at + 2 * rb]
        rest = own_m[0:16, at + 2 * rb : at + 3 * rb]
        squares += jnp.sum(full * full) + jnp.sum(rest * rest)
    tl_five()
    squares += jnp.sum(own_t[:, 0 : 6 * rb] * own_t[:, 0 : 6 * rb])
    for t, other in enumerate((j1, j2, j3)):
        v_seq(t, other, other).wait_send()
        v_seq(t, other, other).wait_recv()
    own_v = (rv2[0].astype(F32) + rv2[1].astype(F32)) + (rv2[2].astype(F32) + rv2[3].astype(F32))
    own_s[80:96, 0:vl] = own_v
    first_band = (j == 0).astype(jnp.int32).astype(F32)
    squares += first_band * jnp.sum(own_v[0:11, 0 : 5 * rb] * own_v[0:11, 0 : 5 * rb])

    nrm[4 * me + j] = jnp.full((1, 128), squares, F32)
    own_out_copy = pltpu.make_async_copy(own_s, own_ref, loc.at[13])
    own_out_copy.start()

    def send_norm(k, carry):
        mine = 4 * me + j
        to = lax.rem(mine + k, 4 * n)
        remote(
            nrm.at[mine], nrm.at[mine], nd_s.at[0], nd_r.at[0], lax.div(to, 4), lax.rem(to, 4)
        ).start()
        return carry

    lax.fori_loop(1, 4 * n, send_norm, 0)
    part = nrm.at[pl.ds(0, 4 * n - 1)]
    both(remote(part, part, nd_s.at[0], nd_r.at[0], beside, j))
    nrm[4 * n] = lax.fori_loop(1, 4 * n, lambda k, total: total + nrm[k], nrm[0])
    norm_out = pltpu.make_async_copy(nrm.at[4 * n], norm_ref, loc.at[14])
    norm_out.start()

    wait_out()
    own_out.wait()
    token_out.wait()
    own_out_copy.wait()
    norm_out.wait()


def update_kernel(rb, tl, al, mo, rates, decays, *refs):
    own_hbm, total_hbm, outt_hbm, tg_hbm = refs[0:4]
    in_hbm = refs[4:31]
    out_hbm, tok_hbm, norm_hbm = refs[31:34]
    new_hbm = refs[34:61]
    own_ref, total_ref, out_v, tok_v, norm_v = refs[61:66]
    in_v, new_v = refs[66:75], refs[75:84]
    in_sem, out_sem = refs[84:86]
    own_load, total_load, out_load, tok_load = [
        pltpu.make_async_copy(src, dst, in_sem.at[9 + at])
        for at, (src, dst) in enumerate(
            ((own_hbm, own_ref), (total_hbm, total_ref), (outt_hbm, out_v), (tg_hbm, tok_v))
        )
    ]
    own_load.start()
    total_load.start()
    for at in range(9):
        for part in range(3):
            pltpu.make_async_copy(in_hbm[at + 9 * part], in_v[at].at[part], in_sem.at[at]).start()
    out_load.start()
    tok_load.start()
    norm_store, out_store, tok_store = [
        pltpu.make_async_copy(src, dst, out_sem.at[9 + at])
        for at, (src, dst) in enumerate(((norm_v, norm_hbm), (out_v, out_hbm), (tok_v, tok_hbm)))
    ]
    own_load.wait()
    total_load.wait()
    total = total_ref[...]
    norm = jnp.sqrt(total)
    norm_v[...] = norm
    norm_store.start()
    clip = jnp.minimum(1.0, MAX_NORM / (norm + 1e-06))[:, 0:1]
    turned_t = own_ref[0:80, 0:tl].T
    turned_a = own_ref[0:80, tl : tl + al].T
    turned_b = own_ref[0:80, tl + al :].T
    turned_q, turned_o = [
        jnp.concatenate(
            [
                own_ref[96:128, at : at + rb],
                own_ref[96:128, at + rb : at + 2 * rb],
                own_ref[96:112, at + 2 * rb : at + 3 * rb],
            ],
            axis=0,
        ).T
        for at in (0, mo)
    ]
    grads = (
        turned_q,
        turned_t[0 : 4 * rb],
        jnp.concatenate([turned_t[(4 + v) * rb : (5 + v) * rb] for v in range(2)], axis=1),
        turned_o,
        jnp.concatenate([turned_b[v * rb : (v + 1) * rb] for v in range(4)], axis=1),
        turned_a[0 : 4 * rb],
        own_ref[80:83, 4 * rb : 5 * rb],
        own_ref[83:91, 4 * rb : 5 * rb],
        own_ref[80:91, 0 : 4 * rb],
    )
    for at in range(9):
        pltpu.make_async_copy(in_v[at], in_v[at], in_sem.at[at]).wait()
        clipped = clip * grads[at]
        weight = in_v[at][0]
        first = BETA_ONE * in_v[at][1] + (1.0 - BETA_ONE) * clipped
        second = BETA_TWO * in_v[at][2] + (1.0 - BETA_TWO) * clipped * clipped
        direction = (
            first
            / (1.0 - BETA_ONE**STEP)
            / (jnp.sqrt(second / (1.0 - BETA_TWO**STEP)) + ADAM_EPS)
        )
        new_v[at][0] = weight - rates[at] * (direction + decays[at] * weight)
        new_v[at][1] = first
        new_v[at][2] = second
        for part in range(3):
            pltpu.make_async_copy(
                new_v[at].at[part], new_hbm[at + 9 * part], out_sem.at[at]
            ).start()
    out_load.wait()
    out_store.start()
    tok_load.wait()
    tok_store.start()
    for at in range(9):
        pltpu.make_async_copy(new_v[at], new_v[at], out_sem.at[at]).wait()
    for store in (norm_store, out_store, tok_store):
        store.wait()


def on_device(n, *args):
    tokens, buckets, cotangent = args[0:3]
    weights, firsts, seconds = args[3:12], args[12:21], args[21:30]
    band, side, width = tokens.shape[1:4]
    count = band * side
    keys = count // 4
    rb = weights[0].shape[0]
    piece = cotangent.shape[3]
    wide = up(9 * rb, 128)
    tl = up(6 * rb, 128)
    al = up(4 * rb, 128)
    bl = up(4 * rb, 128)
    ml = up(6 * rb, 128)
    h = n // 2
    vl = up(5 * rb, 128)
    total = tl + al + bl
    qa = count if n <= 8 else 128
    turned = piece % 128 == 0
    block = (n, D, piece) if turned else (n, piece, D)
    vm = pltpu.VMEM
    dma = pltpu.SemaphoreType.DMA
    def landing(height, lanes, cut, direct):
        rest = height - cut
        count = n if direct else h
        shapes = (
            (2, n, height, lanes),
            (n, cut, lanes),
            (0 if direct else h, cut, lanes),
            (count, cut, lanes),
            (0 if direct else 2, h, rest, lanes),
            (2, count, rest, lanes),
            (rest, lanes),
        )
        return [vm(shape if 0 not in shape else (8, 128), BF) for shape in shapes]

    scratch = [
        vm((count, D), BF),
        *[vm(weights[at].shape, F32) for at in range(9)],
        vm((n, 16, vl), BF),
        vm((4, n, 80, tl), BF),
        vm((4, n, 32, ml), BF),
        vm((4, n, 80, wide), BF),
        vm((16, D), F32),
        vm((16, FF), F32),
        vm((D, D), BF),
        vm((D, D), BF),
        vm((2 * D, D), BF),
        vm((2 * D, D), BF),
        vm((4, D, D), BF),
        vm((FF, D), BF),
        vm((D, FF), BF),
        vm((3, count, 128), F32),
        vm((count, D), BF),
        vm((4, keys, D), BF),
        vm((keys, D), BF),
        vm((HEADS, 4, keys, 128), BF),
        vm((HEADS, 128, 4 * keys), BF),
        vm((HEADS, count, 128), BF),
        vm((HEADS, 128, count), BF),
        vm((HEADS, 4 * keys, count), BF),
        vm((D, count), BF),
        vm((count, D), BF),
        vm((HEADS, 1, count), F32),
        vm((HEADS, 1, count), F32),
        vm((count, D), F32),
        vm((count, D), BF),
        vm((count + 2 * side, FF), BF),
        vm((2, side, FF), BF),
        vm((count + 2 * side, FF), BF),
        vm((count, FF), BF),
        vm(block, BF),
        vm(block if turned else (8, 128), BF),
        vm((D, count), BF),
        vm((count, D), BF),
        vm((2, side, FF), BF),
        vm((HEADS, count, 128), BF),
        vm((HEADS, 2, keys, 128), BF),
        vm((HEADS, keys, 128), BF),
        vm((16, FF), F32),
        vm((16, D), F32),
        vm((128, total), F32),
        vm((4, n, 80, bl), BF),
        *landing(80, al, 80, False),
        *landing(80, bl, 32, False),
        *landing(80, tl, CUT, True),
        *landing(32, ml, 32, False),
        vm((n, 16, vl), BF),
        vm((n, 16, vl), BF),
        vm((4, 16, vl), BF),
        vm((4 * n + 1, 1, 128), F32),
        vm((side, 2 * side), BF),
        vm((side, 2 * side), BF),
        vm((2 * side, side), BF),
        dma((15,)),
        *[dma((9,)) for _ in range(2)],
        dma((n,)),
        dma((2, h)),
        *[dma((16,)) for _ in range(2)],
        *[dma((1,)) for _ in range(4)],
        *[dma((HEADS, 3)) for _ in range(2)],
        *[dma((4,)) for _ in range(2)],
        *[dma((34,)) for _ in range(2)],
        *[dma((1,)) for _ in range(2)],
    ]
    anywhere = pl.BlockSpec(memory_space=pl.ANY)
    out_t, token_grad, own, total_squares = pl.pallas_call(
        functools.partial(block_kernel, n, side, band, qa),
        out_shape=(
            jax.ShapeDtypeStruct(block, BF),
            jax.ShapeDtypeStruct((count, D), BF),
            jax.ShapeDtypeStruct((128, total), F32),
            jax.ShapeDtypeStruct((1, 128), F32),
        ),
        in_specs=[pl.BlockSpec(memory_space=pltpu.SMEM)] + [anywhere] * 11,
        out_specs=(anywhere,) * 4,
        scratch_shapes=scratch,
        compiler_params=pltpu.CompilerParams(
            collective_id=0, has_side_effects=True, vmem_limit_bytes=VMEM_LIMIT
        ),
    )(
        buckets,
        tokens.reshape(count, width),
        jnp.swapaxes(cotangent, 3, 4).reshape(block) if turned else cotangent.reshape(block),
        *weights,
    )
    rates = (
        D ** (-0.5),
        (4 * D) ** (-0.5),
        D ** (-0.5),
        OUT_FAN ** (-0.5),
        D ** (-0.5),
        FF ** (-0.5),
        GAIN_RATE,
        VECTOR_RATE,
        VECTOR_RATE,
    )
    decays = (DECAY_RATE,) * 6 + (0.0,) * 3
    shapes = tuple(jax.ShapeDtypeStruct(w.shape, F32) for w in weights)
    results = pl.pallas_call(
        functools.partial(
            update_kernel, rb, tl, al, 128 if ml > 128 else 3 * rb, rates, decays
        ),
        out_shape=(
            jax.ShapeDtypeStruct(block, BF),
            jax.ShapeDtypeStruct((count, D), BF),
            jax.ShapeDtypeStruct((1, 128), F32),
        )
        + shapes * 3,
        in_specs=[anywhere] * 31,
        out_specs=(anywhere,) * 30,
        scratch_shapes=[
            vm((128, total), F32),
            vm((1, 128), F32),
            vm(block, BF),
            vm((count, D), BF),
            vm((1, 128), F32),
            *[vm((3, *w.shape), F32) for w in weights * 2],
            dma((13,)),
            dma((12,)),
        ],
    )(own, total_squares, out_t, token_grad, *weights, *firsts, *seconds)
    if turned:
        block_output = jnp.swapaxes(results[0].reshape(n, 1, 1, width, piece), 3, 4)
    else:
        block_output = results[0].reshape(n, 1, 1, piece, width)
    return (
        block_output,
        results[1].reshape(1, band, side, width),
        results[2][0, 0],
        *results[3:],
    )


def solution(mesh):
    matrix = (P("dp", "seq"),) * 6 + (P(None, "dp"),) * 3
    return jax.shard_map(
        functools.partial(on_device, mesh.shape["dp"]),
        mesh=mesh,
        in_specs=(
            P("dp", "seq", None, None),
            P("dp"),
            P(None, "seq", "dp", None, None),
            *(matrix * 3),
        ),
        out_specs=(
            P(None, "seq", "dp", None, None),
            P("dp", "seq", None, None),
            P(),
            *(matrix * 3),
        ),
        check_vma=False,
    )
```

```python
import functools

import jax
import jax.numpy as jnp
from jax import lax
from jax.experimental import pallas as pl
from jax.experimental.pallas import tpu as pltpu
from jax.sharding import PartitionSpec as P

D = 320
HEADS = 5
HEAD = 64
FF = 1280
STEP = 10
OUT_FAN = 5

NORM_EPS = 1e-06
MAX_NORM = 1.0
BETA_ONE = 0.9
BETA_TWO = 0.95
ADAM_EPS = 1e-08
DECAY_RATE = 0.01
VECTOR_RATE = 0.3
GAIN_RATE = 0.8
MASKED = -1e30

BF = jnp.bfloat16
F32 = jnp.float32
MESH = pl.DeviceIdType.MESH
QC = 512
GATHER_CUT = 32
CUT = 48
VMEM_LIMIT = 63 * 1024 * 1024


def nn(a, b):
    return lax.dot_general(a, b, (((1,), (0,)), ((), ())), preferred_element_type=F32)


def nt(a, b):
    return lax.dot_general(a, b, (((1,), (1,)), ((), ())), preferred_element_type=F32)


def up(n, m):
    return (n + m - 1) // m * m


def norm_parts(v):
    centered = v - jnp.mean(v, axis=-1, keepdims=True)
    rstd = lax.rsqrt(jnp.mean(centered * centered, axis=-1, keepdims=True) + NORM_EPS)
    return centered * rstd, rstd


def norm_back(v, gain, e):
    vhat, rstd = norm_parts(v)
    u = e * gain
    dv = rstd * (
        u
        - jnp.mean(u, axis=-1, keepdims=True)
        - vhat * jnp.mean(u * vhat, axis=-1, keepdims=True)
    )
    return dv, jnp.sum(e * vhat, axis=0, keepdims=True), jnp.sum(e, axis=0, keepdims=True)


def colsum(v):
    return jnp.sum(v, axis=0, keepdims=True)


def rows(start, size):
    return pl.ds(pl.multiple_of(start, 16), size)


def block_kernel(
    n,
    side,
    band,
    qa,
    bucket_ref,
    tok_ref,
    cot_ref,
    wq_ref,
    wr_ref,
    wm_ref,
    wo_ref,
    w1_ref,
    w2_ref,
    gains_ref,
    biases_ref,
    hidden_ref,
    out_ref,
    tgrad_ref,
    own_ref,
    norm_ref,
    x_s,
    fq,
    fr,
    fm,
    fo,
    f1,
    f2,
    fg,
    fb,
    fh,
    gvec,
    gt,
    gm,
    gf,
    vp,
    hp,
    wqt,
    wot,
    wop,
    wmt,
    wrt,
    w1t,
    w2t,
    a3,
    abf,
    pat,
    memin,
    kv,
    kvt,
    qnat,
    qt,
    prob,
    att_t,
    att_n,
    rtot,
    delta,
    mid,
    bn,
    hidp,
    hidh,
    act,
    gp,
    out_t,
    dy_in,
    dy_t,
    dy,
    dzh,
    datn,
    rk1,
    rk2,
    hg,
    vg,
    own_s,
    sb,
    ra0,
    ra1,
    ra2,
    ra3,
    ra4,
    ra5,
    ra6,
    rb0,
    rb1,
    rb2,
    rb3,
    rb4,
    rb5,
    rb6,
    rt0,
    rt1,
    rt2,
    rt3,
    rt4,
    rt5,
    rt6,
    rm0,
    rm1,
    rm2,
    rm3,
    rm4,
    rm5,
    rm6,
    sv,
    rv1,
    rv2,
    nrm,
    shift_f,
    shift_b,
    shift_m,
    loc,
    tl_r,
    th_r,
    gx_s,
    gx_r,
    co_s,
    co_r,
    ou_s,
    ou_r,
    kv_s,
    kv_r,
    ha_s,
    ha_r,
    nd_s,
    nd_r,
):
    me = lax.axis_index("dp")
    j = lax.axis_index("seq")
    y0 = lax.rem(me, 2)
    y1 = 1 - y0
    z0 = lax.div(me, 2)
    beside = me + 1 - 2 * y0
    zn = n // 2
    here = y0 * zn + z0

    def place_of(i):
        return i % 2 * zn + i // 2

    def spot(i):
        return lax.rem(i, 2) * zn + lax.div(i, 2)

    j1 = j + 1 - 2 * lax.rem(j, 2)
    j2 = lax.rem(j + 2, 4)
    j3 = 3 - j
    tokens = band * side
    chunks = tokens // QC
    deep = band if qa == tokens else 4
    rb = wq_ref.shape[0]
    piece = tokens // n
    keys = kv.shape[2]
    turned = cot_ref.shape[1] == D
    tl = gt.shape[3]
    fl = gf.shape[3]
    vl = gvec.shape[2]
    al = up(4 * rb, 128)
    bl = sb.shape[3]
    ml = gm.shape[3]
    mo = 128 if ml > 128 else 3 * rb

    def remote(src, dst, ss, rs, dp, seq):
        return pltpu.make_async_remote_copy(
            src_ref=src,
            dst_ref=dst,
            send_sem=ss,
            recv_sem=rs,
            device_id=(dp, seq),
            device_id_type=MESH,
        )

    def both(copy):
        copy.wait_send()
        copy.wait_recv()

    def peers(body):
        def step(k, carry):
            body(k, lax.rem(me + k, n), lax.rem(me + n - k, n))
            return carry

        lax.fori_loop(1, n, step, 0)

    def z_peers(body):
        def step(k, carry):
            body(k, lax.rem(me + 2 * k, n), lax.rem(z0 + k, zn), lax.rem(z0 + zn - k, zn))
            return carry

        lax.fori_loop(1, zn, step, 0)

    loads = [
        pltpu.make_async_copy(src, dst, loc.at[at])
        for at, (src, dst) in enumerate(
            (
                (gains_ref, fg),
                (biases_ref, fb),
                (hidden_ref, fh),
                (wr_ref, fr),
                (wm_ref, fm),
                (wq_ref, fq),
                (wo_ref, fo),
                (w1_ref, f1),
                (w2_ref, f2),
                (tok_ref, x_s),
            )
        )
    ]
    for copy in loads:
        copy.start()
    def incoming(i):
        return dy_in.at[i] if turned else dy.at[rows(i * piece, piece)]

    own_cot = pltpu.make_async_copy(cot_ref.at[me], incoming(me), loc.at[10])
    own_cot.start()

    barrier = pltpu.get_barrier_semaphore()

    def greet(k, carry):
        to = lax.rem(4 * me + j + k, 4 * n)
        pl.semaphore_signal(
            barrier, inc=1, device_id=(lax.div(to, 4), lax.rem(to, 4)), device_id_type=MESH
        )
        return carry

    lax.fori_loop(1, 4 * n, greet, 0)

    for copy in loads[:5]:
        copy.wait()
    hidden16 = jnp.concatenate([fh[...], jnp.zeros((5, 4 * rb), F32)], axis=0)
    small16 = jnp.concatenate([fg[...], fb[...], jnp.zeros((5, rb), F32)], axis=0)
    gvec[here] = jnp.concatenate(
        [hidden16, small16, jnp.zeros((16, vl - 5 * rb), F32)], axis=1
    ).astype(BF)
    wm_t = fm[...].T
    gt[j, here] = jnp.concatenate(
        [fr[...].T, wm_t[0:80], wm_t[80:160], jnp.zeros((80, tl - 6 * rb), F32)], axis=1
    ).astype(BF)

    def group(at, one_of, all_but_one, each):
        def start():
            def send(peer):
                ref = one_of(here)
                remote(ref, ref, gx_s.at[14 + at], gx_r.at[14 + at], peer, j).start()

            each(send)

        def wait():
            both(remote(all_but_one, all_but_one, gx_s.at[14 + at], gx_r.at[14 + at], beside, j))

        return start, wait

    def each_peer(send):
        peers(lambda k, peer, source: send(peer))

    def each_z(send):
        z_peers(lambda k, peer, to, source: send(peer))

    def over_dp(at, buf, rows_of):
        return group(
            at, lambda i: buf.at[i, rows_of], buf.at[pl.ds(0, n - 1), rows_of], each_peer
        )

    def over_z(at, buf, rows_of):
        return group(
            at, lambda i: buf.at[i, rows_of], buf.at[pl.ds(0, zn - 1), rows_of], each_z
        )

    def swap(at, mine, theirs, dp, seq):
        def start():
            remote(mine, mine, gx_s.at[at], gx_r.at[at], dp, seq).start()

        def wait():
            remote(mine, mine, gx_s.at[at], gx_r.at[at], dp, seq).wait_send()
            remote(theirs, theirs, gx_s.at[at], gx_r.at[at], dp, seq).wait_recv()

        return start, wait

    def over_y(at, buf, rows_of):
        mine = buf.at[pl.ds(y0 * zn, zn), rows_of]
        theirs = buf.at[pl.ds(y1 * zn, zn), rows_of]
        return swap(at, mine, theirs, beside, j)

    lower = slice(0, GATHER_CUT)
    upper = slice(GATHER_CUT, 80)
    every = slice(0, 16)
    v_dp, v_dp_wait = over_dp(0, gvec, every)

    def t_low(i):
        return gt.at[j, i, lower]

    def t_low_copy(k, i, peer):
        return remote(t_low(i), t_low(i), gx_s.at[15], tl_r.at[k], peer, j)

    def t_low_on(i):
        remote(t_low(i), t_low(i), gx_s.at[0], gx_r.at[0], me, j2).start()

    def t_low_start():
        t_low_on(here)
        peers(lambda k, peer, source: t_low_copy(k, here, peer).start())

    def t_low_forward():
        def body(k, peer, source):
            t_low_copy(k, spot(source), peer).wait_recv()
            t_low_on(spot(source))

        peers(body)

    def t_low_wait():
        part = gt.at[j, pl.ds(0, n - 1), lower]
        remote(part, part, gx_s.at[15], tl_r.at[0], beside, j).wait_send()
        both(remote(gt.at[j, :, lower], gt.at[j2, :, lower], gx_s.at[0], gx_r.at[0], me, j2))

    t_x0, t_x0_wait = swap(1, gt.at[j, here, upper], gt.at[j2, here, upper], me, j2)

    def t_high(slot, t):
        def ref(i):
            return gt.at[slot, i, upper]

        def copy(k, i, peer):
            return remote(ref(i), ref(i), gx_s.at[16 + t], th_r.at[t, k], peer, j)

        def on(i):
            remote(ref(i), ref(i), gx_s.at[2 + t], gx_r.at[2 + t], beside, j).start()

        def start():
            z_peers(lambda k, peer, to, source: copy(k, here, peer).start())
            on(here)

        def forward():
            def body(k, peer, to, source):
                copy(k, y0 * zn + source, peer).wait_recv()
                on(y0 * zn + source)

            z_peers(body)

        def wait():
            part = gt.at[slot, pl.ds(0, zn - 1), upper]
            remote(part, part, gx_s.at[16 + t], th_r.at[t, 0], beside, j).wait_send()
            mine = gt.at[slot, pl.ds(y0 * zn, zn), upper]
            theirs = gt.at[slot, pl.ds(y1 * zn, zn), upper]
            both(remote(mine, theirs, gx_s.at[2 + t], gx_r.at[2 + t], beside, j))

        return start, forward, wait

    t_za, t_za_forward, t_ya_wait = t_high(j, 0)
    t_zb, t_zb_forward, t_yb_wait = t_high(j2, 1)
    t_ca, t_ca_wait = swap(4, gt.at[j], gt.at[j1], me, j1)
    t_cb, t_cb_wait = swap(5, gt.at[j2], gt.at[j3], me, j1)
    wq_block = gm.at[:, :, :, 0:128]
    m_dp, m_dp_wait = over_dp(4, wq_block.at[j], slice(0, 32))
    m_x, m_x_wait = swap(6, wq_block.at[j], wq_block.at[j2], me, j2)
    m_ca, m_ca_wait = swap(7, wq_block.at[j], wq_block.at[j1], me, j1)
    m_cb, m_cb_wait = swap(8, wq_block.at[j2], wq_block.at[j3], me, j1)
    f_x0, f_x0_wait = swap(9, gf.at[j, here], gf.at[j2, here], me, j2)
    fl_za, fl_za_wait = over_z(5, gf.at[j], lower)
    fl_zb, fl_zb_wait = over_z(6, gf.at[j2], lower)
    fh_a, fh_a_wait = over_dp(7, gf.at[j], upper)
    fh_b, fh_b_wait = over_dp(8, gf.at[j2], upper)
    fl_ya, fl_ya_wait = over_y(10, gf.at[j], lower)
    fl_yb, fl_yb_wait = over_y(11, gf.at[j2], lower)
    fl_ca, fl_ca_wait = swap(12, gf.at[j, :, lower], gf.at[j1, :, lower], me, j1)
    fl_cb, fl_cb_wait = swap(13, gf.at[j2, :, lower], gf.at[j3, :, lower], me, j1)
    fh_ca, fh_ca_wait = swap(34, gf.at[j, :, upper], gf.at[j1, :, upper], me, j1)
    fh_cb, fh_cb_wait = swap(35, gf.at[j2, :, upper], gf.at[j3, :, upper], me, j1)

    pl.semaphore_wait(barrier, 4 * n - 1)
    t_x0()
    t_za()
    t_low_start()

    for copy in loads[5:9]:
        copy.wait()
    wq_t = fq[...].T
    gm[j, here, :, 0:128] = jnp.concatenate(
        [
            wq_t[0:32],
            wq_t[32:64],
            jnp.concatenate([wq_t[64:80], jnp.zeros((16, rb), F32)], axis=0),
            jnp.zeros((32, 128 - 3 * rb), F32),
        ],
        axis=1,
    ).astype(BF)
    w1_t = f1[...].T
    gf[j, here] = jnp.concatenate(
        [f2[...].T]
        + [w1_t[80 * v : 80 * v + 80] for v in range(4)]
        + [fo[...].T, jnp.zeros((80, fl - 9 * rb), F32)],
        axis=1,
    ).astype(BF)
    t_x0_wait()
    t_zb()
    v_dp()

    t_low_forward()
    m_dp()
    f_x0()
    t_za_forward()
    t_zb_forward()
    f_x0_wait()
    fl_za()
    fl_zb()
    v_dp_wait()
    hp[...] = jnp.concatenate([gvec[place_of(i), :, 0 : 4 * rb] for i in range(n)], axis=1).astype(F32)
    vp[...] = jnp.concatenate(
        [gvec[place_of(i), :, 4 * rb : 5 * rb] for i in range(n)], axis=1
    ).astype(F32)

    def gain(k):
        return vp[k : k + 1, :]

    def shift(k):
        return vp[3 + k : 4 + k, :]

    loads[9].wait()

    def norm_one(c, carry):
        at = rows(c * QC, QC)
        vhat, _ = norm_parts(x_s[at, :].astype(F32))
        low = (vhat * gain(0) + shift(0)).astype(BF)
        abf[at, :] = low
        wide = jnp.concatenate([low.astype(F32), jnp.zeros((QC, 64), F32)], axis=1)
        for t in range(3):
            a3[t, at, :] = wide[:, 128 * t : 128 * t + 128]
        return carry

    lax.fori_loop(0, chunks, norm_one, 0)
    half = side // 2
    for dd in range(4):
        for i in range(band // 2):
            start = (2 * i + dd // 2) * side + dd % 2
            cut = jnp.concatenate(
                [a3[t, pl.ds(start, half, stride=2), :] for t in range(3)], axis=1
            )
            pat[dd, i * half : (i + 1) * half, :] = cut[:, 0:D].astype(BF)

    bucket = bucket_ref[0]
    k_row = lax.broadcasted_iota(jnp.int32, (4 * keys, 128), 0)
    k_lane = lax.broadcasted_iota(jnp.int32, (4 * keys, 128), 1)
    k_id = (lax.div(k_row, half) >= half // 2).astype(jnp.int32) * 2 + (
        lax.rem(k_row, half) >= half // 2
    ).astype(jnp.int32)
    off = (k_id != k_lane).astype(jnp.int32) * bucket * (k_lane < 4).astype(jnp.int32)
    kmask = datn.at[0]
    qmask = dy_t.at[0:128]
    kmask[...] = (off.astype(F32) * MASKED).astype(BF)
    q_row = lax.broadcasted_iota(jnp.int32, (128, tokens), 0)
    place = lax.broadcasted_iota(jnp.int32, (128, tokens), 1)
    q_id = (lax.div(place, side) + j * band >= half).astype(jnp.int32) * 2 + (
        lax.rem(place, side) >= half
    ).astype(jnp.int32)
    qmask[...] = (q_id == q_row).astype(F32).astype(BF)
    col = lax.broadcasted_iota(jnp.int32, (side, side), 0)
    ok_l = (col > 0).astype(jnp.int32) * (1 - bucket * (col == half).astype(jnp.int32))
    ok_r = (col < side - 1).astype(jnp.int32) * (
        1 - bucket * (col == half - 1).astype(jnp.int32)
    )
    lane = lax.broadcasted_iota(jnp.int32, (side, side), 1)
    from_l = (ok_l * (lane == col - 1).astype(jnp.int32)).astype(F32).astype(BF)
    from_r = (ok_r * (lane == col + 1).astype(jnp.int32)).astype(F32).astype(BF)
    shift_f[...] = jnp.concatenate([from_l, from_r], axis=1)
    shift_b[...] = jnp.concatenate([from_r, from_l], axis=1)
    shift_m[...] = jnp.concatenate([from_r, from_l], axis=0)
    top_ok = (
        (j > 0).astype(jnp.int32) * (1 - bucket * (j * band == half).astype(jnp.int32))
    ).astype(F32)
    low_ok = (
        (j < 3).astype(jnp.int32) * (1 - bucket * ((j + 1) * band == half).astype(jnp.int32))
    ).astype(F32)

    t_ya_wait()
    t_yb_wait()
    t_low_wait()
    t_ca()
    t_cb()
    m_dp_wait()
    m_x()
    t_ca_wait()
    t_cb_wait()

    fh_a()
    fh_b()

    for s in range(4):
        span = slice(80 * s, 80 * s + 80)

        def lanes(lo, hi, over):
            return jnp.concatenate([gt[s, place_of(i), :, lo:hi] for i in over], axis=1)

        for dd in range(4):
            wrt[dd, span, :] = lanes(0, 4 * rb, range(dd * n // 4, (dd + 1) * n // 4))
        for v in range(2):
            wop[160 * s + 80 * v : 160 * s + 80 * v + 80, :] = lanes(
                (4 + v) * rb, (5 + v) * rb, range(n)
            )
    for h in range(HEADS):
        wmt[128 * h : 128 * h + 64, :] = wop[HEAD * h : HEAD * h + HEAD, :]
        wmt[128 * h + 64 : 128 * h + 128, :] = wop[D + HEAD * h : D + HEAD * h + HEAD, :]

    red = shift(2) + nt(pat[0], wrt[0])
    for dd in range(1, 4):
        red = red + nt(pat[dd], wrt[dd])
    wide_red = jnp.concatenate([red, jnp.zeros((keys, 64), F32)], axis=1)
    for t in range(3):
        a3[t, 0:keys, :] = wide_red[:, 128 * t : 128 * t + 128]
    vhat, _ = norm_parts(red)
    low = (vhat * gain(1) + shift(3)).astype(BF)
    memin[...] = low
    zero64 = jnp.zeros((1, HEAD), F32)
    value_shift = jnp.concatenate(
        [
            part
            for h in range(HEADS)
            for part in (zero64, shift(4)[:, HEAD * h : HEAD * h + HEAD])
        ],
        axis=1,
    )
    memory = (nt(low, wmt[...]) + value_shift).astype(BF)
    for h in range(HEADS):
        kv[h, j] = memory[:, 128 * h : 128 * h + 128]

    def kv_copy(h, slot, t, other):
        return remote(
            kv.at[h, slot], kv.at[h, slot], kv_s.at[h, t], kv_r.at[h, t], me, other
        )

    def kv_send(h, carry):
        kv_copy(h, j, 0, j2).start()
        kv_copy(h, j, 1, j1).start()
        return carry

    lax.fori_loop(0, 2, kv_send, 0)

    m_x_wait()
    m_ca()
    m_cb()
    wqp = wop
    m_ca_wait()
    m_cb_wait()
    for s in range(4):
        at = 80 * s
        wqt[at : at + 32, :] = jnp.concatenate([gm[s, place_of(i), :, 0:rb] for i in range(n)], axis=1)
        wqt[at + 32 : at + 64, :] = jnp.concatenate(
            [gm[s, place_of(i), :, rb : 2 * rb] for i in range(n)], axis=1
        )
        wqt[at + 64 : at + 80, :] = jnp.concatenate(
            [gm[s, place_of(i), 0:16, 2 * rb : 3 * rb] for i in range(n)], axis=1
        )
    for h in range(HEADS):
        wqp[128 * h : 128 * h + 64, :] = wqt[HEAD * h : HEAD * h + HEAD, :]
        wqp[128 * h + 64 : 128 * h + 128, :] = jnp.zeros((64, D), BF)

    query_shift = jnp.concatenate(
        [
            part
            for h in range(HEADS)
            for part in (shift(1)[:, HEAD * h : HEAD * h + HEAD], zero64)
        ],
        axis=1,
    )

    def across(c):
        return pl.ds(pl.multiple_of(c * QC, QC), QC)

    def queries(c, carry):
        at = rows(c * QC, QC)
        q = (nt(abf[at, :], wqp[...]) + query_shift).astype(BF) * jnp.asarray(HEAD**-0.5, BF)
        for h in range(HEADS):
            tile = q[:, 128 * h : 128 * h + 128]
            qnat[h, at, :] = tile
            qt[h, :, across(c)] = tile.T
        return carry

    lax.fori_loop(0, chunks, queries, 0)
    lax.fori_loop(2, HEADS, kv_send, 0)

    def send_cot(k, peer, source):
        remote(cot_ref.at[peer], incoming(me), co_s.at[0], co_r.at[0], peer, j).start()

    def wait_cot():
        part = cot_ref.at[pl.ds(0, n - 1)]
        both(remote(part, part, co_s.at[0], co_r.at[0], beside, j))

    def kv_forward(h):
        kv_copy(h, j2, 0, j2).wait_recv()
        kv_copy(h, j2, 2, j1).start()

    fl_za_wait()
    fl_zb_wait()
    fl_ya()
    fl_yb()
    kv_forward(0)

    def attend(h, carry):
        kv_copy(h, j, 0, j2).wait_send()
        kv_copy(h, j, 1, j1).wait_send()
        kv_copy(h, j2, 2, j1).wait_send()
        kv_copy(h, j1, 1, j1).wait_recv()
        kv_copy(h, j3, 2, j1).wait_recv()
        tile = kv[h].reshape(4 * keys, 128)
        kvt[h] = tile.T
        left = jnp.concatenate([tile, kmask[...]], axis=1)
        values = jnp.concatenate([kvt[h, 64:128, :], jnp.ones((16, 4 * keys), BF)], axis=0)
        for c in range(tokens // qa):
            cut = slice(c * qa, (c + 1) * qa)
            scores = nn(left, jnp.concatenate([qt[h, :, cut], qmask[:, cut]], axis=0))
            if c == 0:

                @pl.when(h < HEADS - 1)
                def _():
                    kv_forward(h + 1)

                @pl.when(h == HEADS - 2)
                def _():
                    fl_ya_wait()
                    fl_yb_wait()
                    fl_ca()
                    fl_cb()

                @pl.when(h == HEADS - 1)
                def _():
                    fh_a_wait()
                    fh_b_wait()
                    fh_ca()
                    fh_cb()
                    peers(send_cot)

            largest = jnp.max(scores, axis=0, keepdims=True)
            powers = jnp.exp(scores - largest).astype(BF)
            prob[h, :, cut] = powers
            got = nn(values, powers)
            scale = 1.0 / got[64:65, :]
            rtot[h, :, cut] = scale
            att_t[rows(h * HEAD, HEAD), cut] = (got[0:64, :] * scale).astype(BF)
        return carry

    lax.fori_loop(0, HEADS, attend, 0)

    fl_ca_wait()
    fl_cb_wait()

    def unpack_rows(part, lo, hi):
        for s in range(4):
            span = slice(80 * s + lo, 80 * s + hi)

            def lanes(at, width):
                return jnp.concatenate(
                    [gf[s, place_of(i), part, at : at + width] for i in range(n)], axis=1
                )

            w2t[span, :] = lanes(0, 4 * rb)
            for v in range(4):
                at = 320 * s + 80 * v
                w1t[at + lo : at + hi, :] = lanes((4 + v) * rb, rb)
            wot[span, :] = lanes(8 * rb, rb)

    unpack_rows(lower, 0, GATHER_CUT)
    fh_ca_wait()
    fh_cb_wait()
    unpack_rows(upper, GATHER_CUT, 80)
    wop_full = wot[...].T
    for h in range(HEADS):
        wop[128 * h : 128 * h + 64, :] = jnp.zeros((64, D), BF)
        wop[128 * h + 64 : 128 * h + 128, :] = wop_full[HEAD * h : HEAD * h + HEAD, :]

    def middle(c, carry):
        at = rows(c * QC, QC)
        att = att_t[:, across(c)].T
        att_n[at, :] = att
        value = x_s[at, :].astype(F32) + nt(att, wot[...]) + shift(5)
        mid[at, :] = value
        vhat, _ = norm_parts(value)
        low = (vhat * gain(2) + shift(6)).astype(BF)
        bn[at, :] = low
        return carry

    lax.fori_loop(0, chunks, middle, 0)

    edge = tokens - side

    def hidden_of(value):
        return (nt(value, w1t[...]) + hp[9:10, :]).astype(BF)

    ends = hidden_of(jnp.concatenate([bn[0:side, :], bn[edge:tokens, :]], axis=0))
    hidp[side : 2 * side, :] = ends[0:side]
    hidp[tokens : tokens + side, :] = ends[side : 2 * side]
    above = lax.rem(j + 3, 4)
    below = lax.rem(j + 1, 4)

    def rim_up(buf, halo, at):
        return remote(buf.at[pl.ds(side, side)], halo.at[1], ha_s.at[at], ha_r.at[at], me, above)

    def rim_down(buf, halo, at):
        return remote(
            buf.at[pl.ds(tokens, side)], halo.at[0], ha_s.at[at + 1], ha_r.at[at + 1], me, below
        )

    def rim_send(buf, halo, at):
        @pl.when(j > 0)
        def _():
            rim_up(buf, halo, at).start()

        @pl.when(j < 3)
        def _():
            rim_down(buf, halo, at).start()

    def rim_wait(buf, halo, at):
        @pl.when(j > 0)
        def _():
            rim_up(buf, halo, at).wait_send()
            rim_down(buf, halo, at).wait_recv()

        @pl.when(j < 3)
        def _():
            rim_down(buf, halo, at).wait_send()
            rim_up(buf, halo, at).wait_recv()

        for t, (to, ok) in enumerate(((0, top_ok), (tokens + side, low_ok))):
            seen = jnp.full((side, FF), ok, F32) > 0.5
            buf[to : to + side, :] = jnp.where(seen, halo[t].astype(F32), 0.0).astype(BF)

    rim_send(hidp, hidh, 0)

    inner = (tokens - 2 * side) // 2

    def inner_hidden(c, carry):
        start = side + c * inner
        hidp[rows(start + side, inner), :] = hidden_of(bn[rows(start, inner), :])
        return carry

    lax.fori_loop(0, 2, inner_hidden, 0)

    def tile_at(t):
        return pl.ds(pl.multiple_of(t * 128, 128), 128)

    def taps_of(lanes):
        return [hp[k : k + 1, lanes] for k in range(9)]

    def conv_over(lo, hi, step, tiles):
        def conv_tile(t, carry):
            lanes = tile_at(t)
            taps = taps_of(lanes)
            base = hp[10:11, lanes]

            def row(at, inner):
                r = lo + at * step
                around = [hidp[rows((r + a) * side, side), lanes].astype(F32) for a in range(3)]
                parts = [
                    taps[b] * around[0] + taps[3 + b] * around[1] + taps[6 + b] * around[2]
                    for b in range(3)
                ]
                moved = jnp.concatenate([parts[0].astype(BF), parts[2].astype(BF)], axis=0)
                z = base + parts[1] + nn(shift_f[...], moved)
                root = z * (0.5**0.5)
                cdf = 0.5 + 0.5 * lax.erf(root)
                slope = (z * 0.3989422804014327) * jnp.exp2(root * root * -1.4426950408889634)
                act[rows((r + 1) * side, side), lanes] = (z * cdf).astype(BF)
                gp[rows(r * side, side), lanes] = (cdf + slope).astype(BF)
                return inner

            lax.fori_loop(0, (hi - lo) // step, row, 0, unroll=True)
            return carry

        lax.fori_loop(0, FF // 128, conv_tile, 0, unroll=tiles)

    conv_over(1, band - 1, 1, 1)
    rim_wait(hidp, hidh, 0)
    conv_over(0, 2 * (band - 1), band - 1, 5)

    def out_chunk(c, carry):
        at = rows(c * QC, QC)
        value = mid[at, :] + nt(act[rows(side + c * QC, QC), :], w2t[...]) + shift(7)
        for p in range(QC // piece):
            part = value[p * piece : (p + 1) * piece, :]
            out_t[c * (QC // piece) + p] = (part.T if turned else part).astype(BF)
        return carry

    lax.fori_loop(0, chunks, out_chunk, 0)

    def send_out(k, peer, source):
        remote(out_t.at[peer], out_ref.at[me], ou_s.at[0], ou_r.at[0], peer, j).start()

    def wait_out():
        part = out_t.at[pl.ds(0, n - 1)]
        both(remote(part, part, ou_s.at[0], ou_r.at[0], beside, j))

    peers(send_out)
    own_out = pltpu.make_async_copy(out_t.at[me], out_ref.at[me], loc.at[11])
    own_out.start()

    own_cot.wait()
    wait_cot()
    for i in range(n):
        if turned:
            dy_t[:, i * piece : (i + 1) * piece] = dy_in[i]
            dy[i * piece : (i + 1) * piece, :] = dy_in[i].T
    if not turned:
        dy_t[...] = dy[...].T
    vg[...] = jnp.zeros(vg.shape, F32)
    vg[10:11, :] = colsum(dy[...].astype(F32))

    def scatter(sems, s, cut, direct, bufs, own):
        top = s.shape[2]
        r1, xl, yl, dl, yh, dh, xh = bufs
        low, high = slice(0, cut), slice(cut, top)
        slots = (j, j2)
        count = n if direct else zn
        mine = pl.ds(y0 * zn, zn)
        theirs = pl.ds(y1 * zn, zn)

        def copy(src, dst, t, dp, seq):
            at = sems[t]
            return remote(src, dst, gx_s.at[at], gx_r.at[at], dp, seq)

        def core():
            return [copy(s.at[slot], r1.at[t], t, me, j1) for t, slot in enumerate((j1, j3))]

        def low_x():
            return copy(s.at[j2, :, low], xl, 2, me, j2)

        def low_y():
            return copy(s.at[j, theirs, low], yl, 3, beside, j)

        def high_y():
            return [
                copy(s.at[slot, theirs, high], yh.at[t], 4 + t, beside, j)
                for t, slot in enumerate(slots)
            ]

        def high_x():
            return copy(s.at[j2, here, high], xh, 6, me, j2)

        def out(slot, rows_of, land, t):
            def send(k, peer, to):
                copy(s.at[slot, to, rows_of], land.at[k], t, peer, j).start()

            if direct:
                peers(lambda k, peer, source: send(k, peer, spot(peer)))
            else:
                z_peers(lambda k, peer, to, source: send(k, peer, y0 * zn + to))

        def landed(slot, rows_of, land, t):
            part = land.at[pl.ds(1, count - 1)]
            both(copy(part, part, t, beside, j))
            return lax.fori_loop(
                1,
                count,
                lambda k, v: v + land[k].astype(F32),
                s[slot, here, rows_of].astype(F32),
            )

        def add(slot, start, rows_of, extra):
            def body(i, carry):
                s[slot, start + i, rows_of] = (
                    s[slot, start + i, rows_of].astype(F32) + extra[i].astype(F32)
                ).astype(BF)
                return carry

            lax.fori_loop(0, extra.shape[0], body, 0)

        def one():
            for c in core():
                c.start()

        def two():
            for c in core():
                both(c)
            for t, slot in enumerate(slots):
                add(slot, 0, slice(0, top), r1.at[t])
            if cut < top:
                if direct:
                    for t, slot in enumerate(slots):
                        out(slot, high, dh.at[t], 4 + t)
                else:
                    for c in high_y():
                        c.start()
            if cut > 0:
                low_x().start()

        def low_three():
            both(low_x())
            add(j, 0, low, xl)
            if direct:
                out(j, low, dl, 3)
            else:
                low_y().start()

        def high_three():
            for c in high_y():
                both(c)
            for t, slot in enumerate(slots):
                add(slot, y0 * zn, high, yh.at[t])
                out(slot, high, dh.at[t], 7 + t)

        def low_four():
            both(low_y())
            add(j, y0 * zn, low, yl)
            out(j, low, dl, 9)

        def high_four():
            first = 4 if direct else 7
            own[high, :] = landed(j, high, dh.at[0], first)
            s[j2, here, high] = landed(j2, high, dh.at[1], first + 1).astype(BF)
            high_x().start()

        def low_five():
            own[low, :] = landed(j, low, dl, 3 if direct else 9)

        def high_five():
            both(high_x())
            own[high, :] = own[high, :] + xh[...].astype(F32)

        return one, two, low_three, low_four, low_five, high_three, high_four, high_five

    own_t = own_s.at[0:80, 0:tl]
    own_a = own_s.at[0:80, tl : tl + al]
    own_b = own_s.at[0:80, tl + al : tl + al + bl]
    own_m = own_s.at[96:128, 0:ml]
    a_one, a_two, a_three, a_four, a_five, _, _, _ = scatter(
        (0, 1, 2, 3, 0, 0, 0, 0, 0, 4), gf.at[:, :, :, 0:al], 80, False, (ra0, ra1, ra2, ra3, ra4, ra5, ra6), own_a
    )
    b_one, b_two, bl_three, bl_four, bl_five, bh_three, bh_four, bh_five = scatter(
        (5, 6, 27, 28, 7, 8, 9, 10, 11, 29), sb, 32, False, (rb0, rb1, rb2, rb3, rb4, rb5, rb6), own_b
    )
    m_one, m_two, m_three, m_four, m_five, _, _, _ = scatter(
        (12, 13, 14, 15, 0, 0, 0, 0, 0, 33), gm, 32, False, (rm0, rm1, rm2, rm3, rm4, rm5, rm6), own_m
    )
    below_cut = slice(0, CUT)
    above_cut = slice(CUT, 80)

    def t_core(t, slot, to, rows_of):
        return remote(
            gt.at[slot, :, rows_of], rt0.at[to, :, rows_of], gx_s.at[16 + t], gx_r.at[16 + t], me, j1
        )

    def t_cores():
        return (
            t_core(0, j3, 1, below_cut),
            t_core(1, j1, 0, above_cut),
            t_core(2, j3, 1, above_cut),
            t_core(3, j1, 0, below_cut),
        )

    def t_add(slot, start, count, rows_of, extra):
        def body(i, carry):
            gt[slot, start + i, rows_of] = (
                gt[slot, start + i, rows_of].astype(F32) + extra[start + i, rows_of].astype(F32)
            ).astype(BF)
            return carry

        lax.fori_loop(0, count, body, 0)

    def t_half(t):
        part = pl.ds((y1 if t == 0 else y0) * zn, zn)
        return remote(
            gt.at[j2, part, below_cut], rt1.at[part], gx_s.at[20 + t], gx_r.at[20 + t], me, j2
        )

    def t_dp(slot, i, rows_of, land, sem, k, peer):
        remote(
            gt.at[slot, i, rows_of], land.at[k], gx_s.at[sem], gx_r.at[sem], peer, j
        ).start()

    def t_landed(slot, rows_of, land, sem):
        part = land.at[pl.ds(1, n - 1)]
        both(remote(part, part, gx_s.at[sem], gx_r.at[sem], beside, j))
        return lax.fori_loop(
            1, n, lambda k, v: v + land[k].astype(F32), gt[slot, here, rows_of].astype(F32)
        )

    def t_one():
        for c in t_cores():
            c.start()

    def t_two():
        cores = t_cores()
        both(cores[0])
        t_add(j2, 0, n, below_cut, rt0.at[1])
        t_half(0).start()
        t_half(1).start()
        both(cores[1])
        both(cores[2])
        for t, slot in enumerate((j, j2)):
            t_add(slot, 0, n, above_cut, rt0.at[t])
            peers(
                lambda k, peer, source: t_dp(
                    slot, spot(peer), above_cut, rt5.at[t], 22 + t, k, peer
                )
            )
        both(cores[3])
        t_add(j, 0, n, below_cut, rt0.at[0])

    def tl_three(t):
        both(t_half(t))
        start = (y1 if t == 0 else y0) * zn

        def body(i, carry):
            at = start + i
            gt[j, at, below_cut] = (gt[j, at, below_cut].astype(F32) + rt1[at].astype(F32)).astype(BF)
            return carry

        lax.fori_loop(0, zn, body, 0)

        def send(i, carry):
            k = 2 * i + (1 if t == 0 else 2)
            peer = lax.rem(me + k, n)
            t_dp(j, spot(peer), below_cut, rt3, 24, k, peer)
            return carry

        lax.fori_loop(0, zn if t == 0 else zn - 1, send, 0)

    def th_x():
        return remote(gt.at[j2, here, above_cut], rt6, gx_s.at[25], gx_r.at[25], me, j2)

    def th_four():
        own_t[above_cut, :] = t_landed(j, above_cut, rt5.at[0], 22)
        gt[j2, here, above_cut] = t_landed(j2, above_cut, rt5.at[1], 23).astype(BF)
        th_x().start()

    def tl_five():
        own_t[below_cut, :] = t_landed(j, below_cut, rt3, 24)

    def th_five():
        both(th_x())
        own_t[above_cut, :] = own_t[above_cut, :] + rt6[...].astype(F32)


    per = 640 // (4 * rb)
    for b in range(2):
        value = nn(dy_t[...], act[side : side + tokens, 640 * b : 640 * b + 640]).astype(BF)
        for ii in range(per):
            i = b * per + ii
            gf[:, place_of(i), :, 0 : 4 * rb] = value[
                :, 4 * rb * ii : 4 * rb * (ii + 1)
            ].reshape(4, 80, 4 * rb)

    a_one()

    def slope_of(at):
        return nn(dy[at, :], w2t[...])

    dz = act
    for at in (0, edge):
        dz[side + at : 2 * side + at, :] = (
            slope_of(slice(at, at + side)) * gp[at : at + side, :].astype(F32)
        ).astype(BF)
    rim_send(dz, dzh, 2)

    def inner_slope(c, carry):
        at = rows(side + c * inner, inner)
        dz[rows(2 * side + c * inner, inner), :] = (
            slope_of(at) * gp[at, :].astype(F32)
        ).astype(BF)
        return carry

    lax.fori_loop(0, 2, inner_slope, 0)

    a_two()

    dhid = gp

    def back_over(lo, hi, step, tiles):
        def back_tile(t, carry):
            lanes = tile_at(t)
            taps = taps_of(lanes)

            def row(at, inner):
                r = lo + at * step
                around = [dz[rows((r + a) * side, side), lanes].astype(F32) for a in range(3)]
                parts = [
                    taps[b] * around[2] + taps[3 + b] * around[1] + taps[6 + b] * around[0]
                    for b in range(3)
                ]
                both_ways = jnp.concatenate([parts[0].astype(BF), parts[2].astype(BF)], axis=0)
                low = (parts[1] + nn(shift_b[...], both_ways)).astype(BF)
                dhid[rows(r * side, side), lanes] = low
                return inner

            lax.fori_loop(0, (hi - lo) // step, row, 0, unroll=True)
            return carry

        lax.fori_loop(0, FF // 128, back_tile, 0, unroll=tiles)

    back_over(1, band - 1, 1, 1)
    rim_wait(dz, dzh, 2)
    back_over(0, 2 * (band - 1), band - 1, 5)

    def fold(v):
        return jnp.sum(v.reshape(-1, 8, 128), axis=0)

    def tap_sums(lo, hi):
        def tile(t, carry):
            lanes = tile_at(t)

            def row(r, sums):
                low = dz[rows((r + 1) * side, side), lanes]
                here_f = low.astype(F32)
                sides = nn(shift_m[...], low)
                moved = [sides[0:side], here_f, sides[side : 2 * side]]
                found = []
                for a in range(3):
                    source = hidp[rows((r + a) * side, side), lanes].astype(F32)
                    for b in range(3):
                        found.append(fold(moved[b] * source))
                found.append(fold(here_f))
                return tuple(s + f for s, f in zip(sums, found))

            sums = lax.fori_loop(
                0, band, row, tuple(jnp.zeros((8, 128), F32) for _ in range(10)), unroll=deep
            )
            hg[:, lanes] = jnp.concatenate(
                [colsum(s) for s in sums[0:9]]
                + [hg[9:10, lanes], colsum(sums[9]), jnp.zeros((5, 128), F32)],
                axis=0,
            )
            return carry

        lax.fori_loop(lo, hi, tile, 0)

    bn_t = jnp.concatenate([bn[...].T, jnp.ones((16, tokens), BF)], axis=0)
    for b in range(2):
        found = nn(bn_t, dhid[:, 640 * b : 640 * b + 640])
        hg[9:10, 640 * b : 640 * b + 640] = found[D : D + 1]
        value = found[0:D].T.astype(BF).reshape(2, 4, 80, D)
        for i in range(n):
            sb[2 * b : 2 * b + 2, place_of(i), :, 0 : 4 * rb] = jnp.concatenate(
                [value[:, v, :, rb * i : rb * i + rb] for v in range(4)], axis=2
            )

    b_one()

    zero_row = jnp.zeros((1, D), F32)
    dbr = bn
    dbr_t = dy_t

    def back_middle(c, carry):
        at = rows(c * QC, QC)
        value, in_gain, in_shift = norm_back(mid[at, :], gain(2), nn(dhid[at, :], w1t[...]))
        value = value + dy[at, :].astype(F32)
        mid[at, :] = value
        low = value.astype(BF)
        dbr[at, :] = low
        dbr_t[:, across(c)] = low.T
        spread = nt(wop[...], low)
        for h in range(HEADS):
            tile = spread[128 * h : 128 * h + 128, :] * rtot[h, :, across(c)]
            tile_low = tile.astype(BF)
            qt[h, :, across(c)] = tile_low
            datn[h, at, :] = tile_low.T
            delta[h, :, across(c)] = colsum(
                tile_low[64:128, :].astype(F32)
                * att_t[HEAD * h : HEAD * h + HEAD, across(c)].astype(F32)
            )
        return (carry[0] + in_gain, carry[1] + in_shift, carry[2] + colsum(low.astype(F32)))

    sums = lax.fori_loop(0, chunks, back_middle, (zero_row, zero_row, zero_row))
    vg[2:3, :] = sums[0]
    vg[9:10, :] = sums[1]
    vg[8:9, :] = sums[2]
    a_three()
    b_two()

    def dkv(h, slot):
        return gp.at[rows(slot * keys, keys), tile_at(h)]

    def dk_core(h):
        return [
            remote(dkv(h, slot), rk1.at[h, t], kv_s.at[h, t], kv_r.at[h, t], me, j1)
            for t, slot in enumerate((j1, j3))
        ]

    def dk_x(h):
        return remote(dkv(h, j2), rk2.at[h], kv_s.at[h, 2], kv_r.at[h, 2], me, j2)

    def dk_two(h):
        for copy in dk_core(h):
            both(copy)
        for t, slot in enumerate((j, j2)):
            part = dkv(h, slot)
            part[...] = (part[...].astype(F32) + rk1[h, t].astype(F32)).astype(BF)
        dk_x(h).start()

    def dk_three(h):
        both(dk_x(h))
        qnat[h, 0:keys, :] = (dkv(h, j)[...].astype(F32) + rk2[h].astype(F32)).astype(BF)

    def back_head(h, carry):
        tile = kv[h].reshape(4 * keys, 128)
        total = None
        for c in range(tokens // qa):
            cut = slice(c * qa, (c + 1) * qa)
            powers = prob[h, :, cut]
            slopes = nn(tile, qt[h, :, cut]) - delta[h, :, cut]
            ds = (powers.astype(F32) * slopes).astype(BF)
            part = nn(ds, qnat[h, cut, :]) + nn(powers, datn[h, cut, :])
            prob[h, :, cut] = ds
            total = part if total is None else total + part
        gp[0 : 4 * keys, tile_at(h)] = total.astype(BF)
        for copy in dk_core(h):
            copy.start()

        @pl.when(h == 3)
        def _():
            a_four()
            bl_three()

        @pl.when(h >= 1)
        def _():
            dk_two(h - 1)

        return carry

    lax.fori_loop(0, HEADS, back_head, 0)

    dq_t = att_t

    def back_query(h, carry):
        for c in range(tokens // qa):
            cut = slice(c * qa, (c + 1) * qa)
            dq_t[rows(h * HEAD, HEAD), cut] = (
                nn(kvt[h, 0:64, :], prob[h, :, cut]) * HEAD**-0.5
            ).astype(BF)
        return carry

    lax.fori_loop(0, 2, back_query, 0)
    dk_two(HEADS - 1)
    bh_three()
    lax.fori_loop(2, HEADS, back_query, 0)
    bl_four()

    dq = dy

    def flip(c, total):
        low = dq_t[:, across(c)].T
        dq[rows(c * QC, QC), :] = low
        return total + colsum(low.astype(F32))

    vg[4:5, :] = lax.fori_loop(0, chunks, flip, zero_row)
    value = nn(dq_t[...], abf[...]).astype(BF)
    other = nn(dbr_t[...], att_n[...]).astype(BF)

    def folded(v, i):
        part = v[:, rb * i : rb * i + rb].reshape(4, 80, rb)
        return [
            part[:, 0:32],
            part[:, 32:64],
            jnp.concatenate([part[:, 64:80], jnp.zeros((4, 16, rb), BF)], axis=1),
        ]

    for i in range(n):
        gm[:, place_of(i), :, 0 : 3 * rb] = jnp.concatenate(folded(value, i), axis=2)
        gm[:, place_of(i), :, mo : mo + 3 * rb] = jnp.concatenate(folded(other, i), axis=2)
    m_one()
    tap_sums(0, 2)
    m_two()
    for h in range(HEADS):
        dk_three(h)

    dm = jnp.concatenate([qnat[h, 0:keys, :] for h in range(HEADS)], axis=1)
    dm_sum = colsum(dm.astype(F32))
    vg[7:8, :] = jnp.concatenate(
        [dm_sum[:, 128 * h + 64 : 128 * h + 128] for h in range(HEADS)], axis=1
    )
    kept = jnp.concatenate([a3[t, 0:keys, :] for t in range(3)], axis=1)[:, 0:D]
    dv, in_gain, in_shift = norm_back(kept, gain(1), nn(dm, wmt[...]))
    vg[1:2, :] = in_gain
    vg[6:7, :] = in_shift
    dred = dv.astype(BF)
    vg[5:6, :] = colsum(dred.astype(F32))
    dred_t = dred.T
    for dd in range(4):
        value = nn(dred_t, pat[dd]).astype(BF)
        count = n // 4
        for ii in range(count):
            i = dd * count + ii
            gt[:, place_of(i), :, 0 : 4 * rb] = value[
                :, 4 * rb * ii : 4 * rb * (ii + 1)
            ].reshape(4, 80, 4 * rb)
    value = nn(dm.T, memin[...]).astype(BF)
    value = jnp.concatenate(
        [value[128 * h : 128 * h + 64] for h in range(HEADS)]
        + [value[128 * h + 64 : 128 * h + 128] for h in range(HEADS)],
        axis=0,
    ).reshape(4, 2, 80, D)
    for i in range(n):
        gt[:, place_of(i), :, 4 * rb : 6 * rb] = jnp.concatenate(
            [value[:, v, :, rb * i : rb * i + rb] for v in range(2)], axis=2
        )
    t_one()

    t_two()

    for dd in range(4):
        back = nn(dred, wrt[dd])
        back = jnp.concatenate([back, jnp.zeros((keys, 64), F32)], axis=1)
        for i in range(band // 2):
            start = (2 * i + dd // 2) * side + dd % 2
            for t in range(3):
                a3[t, pl.ds(start, half, stride=2), :] = back[
                    i * half : (i + 1) * half, 128 * t : 128 * t + 128
                ]

    def back_first(c, carry):
        at = rows(c * QC, QC)
        e = nn(dq[at, :], wqt[...]) + jnp.concatenate([a3[t, at, :] for t in range(3)], axis=1)[:, 0:D]
        value, in_gain, in_shift = norm_back(x_s[at, :].astype(F32), gain(0), e)
        bn[at, :] = (mid[at, :] + value).astype(BF)
        return (carry[0] + in_gain, carry[1] + in_shift)

    sums = lax.fori_loop(0, chunks, back_first, (zero_row, zero_row))
    token_out = pltpu.make_async_copy(bn, tgrad_ref, loc.at[12])
    token_out.start()
    vg[0:1, :] = sums[0]
    vg[3:4, :] = sums[1]
    m_three()
    tap_sums(2, FF // 128)
    for i in range(n):
        sv[place_of(i), :, 0 : 4 * rb] = hg[:, 4 * rb * i : 4 * rb * (i + 1)].astype(BF)
        sv[place_of(i), :, 4 * rb : 5 * rb] = vg[:, rb * i : rb * i + rb].astype(BF)

    def v_out(k, peer, source):
        remote(sv.at[spot(peer)], rv1.at[k], gx_s.at[26], gx_r.at[26], peer, j).start()

    peers(v_out)
    tl_three(0)
    tl_three(1)
    bh_four()
    m_four()
    part = rv1.at[pl.ds(1, n - 1)]
    both(remote(part, part, gx_s.at[26], gx_r.at[26], beside, j))
    rv2[j] = lax.fori_loop(
        1, n, lambda k, total: total + rv1[k].astype(F32), sv[here].astype(F32)
    ).astype(BF)

    def v_seq(t, slot, other):
        ref = rv2.at[slot]
        return remote(ref, ref, gx_s.at[30 + t], gx_r.at[30 + t], me, other)

    for t, other in enumerate((j1, j2, j3)):
        v_seq(t, j, other).start()
    th_four()
    a_five()
    bl_five()
    bh_five()
    squares = jnp.sum(own_a[:, 0 : 4 * rb] * own_a[:, 0 : 4 * rb])
    squares += jnp.sum(own_b[:, 0 : 4 * rb] * own_b[:, 0 : 4 * rb])
    th_five()
    m_five()
    for at in (0, mo):
        full = own_m[:, at : at + 2 * rb]
        rest = own_m[0:16, at + 2 * rb : at + 3 * rb]
        squares += jnp.sum(full * full) + jnp.sum(rest * rest)
    tl_five()
    squares += jnp.sum(own_t[:, 0 : 6 * rb] * own_t[:, 0 : 6 * rb])
    for t, other in enumerate((j1, j2, j3)):
        v_seq(t, other, other).wait_send()
        v_seq(t, other, other).wait_recv()
    own_v = (rv2[0].astype(F32) + rv2[1].astype(F32)) + (rv2[2].astype(F32) + rv2[3].astype(F32))
    own_s[80:96, 0:vl] = own_v
    first_band = (j == 0).astype(jnp.int32).astype(F32)
    squares += first_band * jnp.sum(own_v[0:11, 0 : 5 * rb] * own_v[0:11, 0 : 5 * rb])

    nrm[4 * me + j] = jnp.full((1, 128), squares, F32)
    own_out_copy = pltpu.make_async_copy(own_s, own_ref, loc.at[13])
    own_out_copy.start()

    def send_norm(k, carry):
        mine = 4 * me + j
        to = lax.rem(mine + k, 4 * n)
        remote(
            nrm.at[mine], nrm.at[mine], nd_s.at[0], nd_r.at[0], lax.div(to, 4), lax.rem(to, 4)
        ).start()
        return carry

    lax.fori_loop(1, 4 * n, send_norm, 0)
    part = nrm.at[pl.ds(0, 4 * n - 1)]
    both(remote(part, part, nd_s.at[0], nd_r.at[0], beside, j))
    nrm[4 * n] = lax.fori_loop(1, 4 * n, lambda k, total: total + nrm[k], nrm[0])
    norm_out = pltpu.make_async_copy(nrm.at[4 * n], norm_ref, loc.at[14])
    norm_out.start()

    wait_out()
    own_out.wait()
    token_out.wait()
    own_out_copy.wait()
    norm_out.wait()


def update_kernel(rb, tl, al, mo, rates, decays, *refs):
    own_hbm, total_hbm, outt_hbm, tg_hbm = refs[0:4]
    in_hbm = refs[4:31]
    out_hbm, tok_hbm, norm_hbm = refs[31:34]
    new_hbm = refs[34:61]
    own_ref, total_ref, out_v, tok_v, norm_v = refs[61:66]
    in_v, new_v = refs[66:75], refs[75:84]
    in_sem, out_sem = refs[84:86]
    own_load, total_load, out_load, tok_load = [
        pltpu.make_async_copy(src, dst, in_sem.at[9 + at])
        for at, (src, dst) in enumerate(
            ((own_hbm, own_ref), (total_hbm, total_ref), (outt_hbm, out_v), (tg_hbm, tok_v))
        )
    ]
    own_load.start()
    total_load.start()
    for at in range(9):
        for part in range(3):
            pltpu.make_async_copy(in_hbm[at + 9 * part], in_v[at].at[part], in_sem.at[at]).start()
    out_load.start()
    tok_load.start()
    norm_store, out_store, tok_store = [
        pltpu.make_async_copy(src, dst, out_sem.at[9 + at])
        for at, (src, dst) in enumerate(((norm_v, norm_hbm), (out_v, out_hbm), (tok_v, tok_hbm)))
    ]
    own_load.wait()
    total_load.wait()
    total = total_ref[...]
    norm = jnp.sqrt(total)
    norm_v[...] = norm
    norm_store.start()
    clip = jnp.minimum(1.0, MAX_NORM / (norm + 1e-06))[:, 0:1]
    turned_t = own_ref[0:80, 0:tl].T
    turned_a = own_ref[0:80, tl : tl + al].T
    turned_b = own_ref[0:80, tl + al :].T
    turned_q, turned_o = [
        jnp.concatenate(
            [
                own_ref[96:128, at : at + rb],
                own_ref[96:128, at + rb : at + 2 * rb],
                own_ref[96:112, at + 2 * rb : at + 3 * rb],
            ],
            axis=0,
        ).T
        for at in (0, mo)
    ]
    grads = (
        turned_q,
        turned_t[0 : 4 * rb],
        jnp.concatenate([turned_t[(4 + v) * rb : (5 + v) * rb] for v in range(2)], axis=1),
        turned_o,
        jnp.concatenate([turned_b[v * rb : (v + 1) * rb] for v in range(4)], axis=1),
        turned_a[0 : 4 * rb],
        own_ref[80:83, 4 * rb : 5 * rb],
        own_ref[83:91, 4 * rb : 5 * rb],
        own_ref[80:91, 0 : 4 * rb],
    )
    for at in range(9):
        pltpu.make_async_copy(in_v[at], in_v[at], in_sem.at[at]).wait()
        clipped = clip * grads[at]
        weight = in_v[at][0]
        first = BETA_ONE * in_v[at][1] + (1.0 - BETA_ONE) * clipped
        second = BETA_TWO * in_v[at][2] + (1.0 - BETA_TWO) * clipped * clipped
        direction = (
            first
            / (1.0 - BETA_ONE**STEP)
            / (jnp.sqrt(second / (1.0 - BETA_TWO**STEP)) + ADAM_EPS)
        )
        new_v[at][0] = weight - rates[at] * (direction + decays[at] * weight)
        new_v[at][1] = first
        new_v[at][2] = second
        for part in range(3):
            pltpu.make_async_copy(
                new_v[at].at[part], new_hbm[at + 9 * part], out_sem.at[at]
            ).start()
    out_load.wait()
    out_store.start()
    tok_load.wait()
    tok_store.start()
    for at in range(9):
        pltpu.make_async_copy(new_v[at], new_v[at], out_sem.at[at]).wait()
    for store in (norm_store, out_store, tok_store):
        store.wait()


def on_device(n, *args):
    tokens, buckets, cotangent = args[0:3]
    weights, firsts, seconds = args[3:12], args[12:21], args[21:30]
    band, side, width = tokens.shape[1:4]
    count = band * side
    keys = count // 4
    rb = weights[0].shape[0]
    piece = cotangent.shape[3]
    wide = up(9 * rb, 128)
    tl = up(6 * rb, 128)
    al = up(4 * rb, 128)
    bl = up(4 * rb, 128)
    ml = up(6 * rb, 128)
    h = n // 2
    vl = up(5 * rb, 128)
    total = tl + al + bl
    qa = count if n <= 8 else 128
    turned = piece % 128 == 0
    block = (n, D, piece) if turned else (n, piece, D)
    vm = pltpu.VMEM
    dma = pltpu.SemaphoreType.DMA
    def landing(height, lanes, cut, direct):
        rest = height - cut
        count = n if direct else h
        shapes = (
            (2, n, height, lanes),
            (n, cut, lanes),
            (0 if direct else h, cut, lanes),
            (count, cut, lanes),
            (0 if direct else 2, h, rest, lanes),
            (2, count, rest, lanes),
            (rest, lanes),
        )
        return [vm(shape if 0 not in shape else (8, 128), BF) for shape in shapes]

    scratch = [
        vm((count, D), BF),
        *[vm(weights[at].shape, F32) for at in range(9)],
        vm((n, 16, vl), BF),
        vm((4, n, 80, tl), BF),
        vm((4, n, 32, ml), BF),
        vm((4, n, 80, wide), BF),
        vm((16, D), F32),
        vm((16, FF), F32),
        vm((D, D), BF),
        vm((D, D), BF),
        vm((2 * D, D), BF),
        vm((2 * D, D), BF),
        vm((4, D, D), BF),
        vm((FF, D), BF),
        vm((D, FF), BF),
        vm((3, count, 128), F32),
        vm((count, D), BF),
        vm((4, keys, D), BF),
        vm((keys, D), BF),
        vm((HEADS, 4, keys, 128), BF),
        vm((HEADS, 128, 4 * keys), BF),
        vm((HEADS, count, 128), BF),
        vm((HEADS, 128, count), BF),
        vm((HEADS, 4 * keys, count), BF),
        vm((D, count), BF),
        vm((count, D), BF),
        vm((HEADS, 1, count), F32),
        vm((HEADS, 1, count), F32),
        vm((count, D), F32),
        vm((count, D), BF),
        vm((count + 2 * side, FF), BF),
        vm((2, side, FF), BF),
        vm((count + 2 * side, FF), BF),
        vm((count, FF), BF),
        vm(block, BF),
        vm(block if turned else (8, 128), BF),
        vm((D, count), BF),
        vm((count, D), BF),
        vm((2, side, FF), BF),
        vm((HEADS, count, 128), BF),
        vm((HEADS, 2, keys, 128), BF),
        vm((HEADS, keys, 128), BF),
        vm((16, FF), F32),
        vm((16, D), F32),
        vm((128, total), F32),
        vm((4, n, 80, bl), BF),
        *landing(80, al, 80, False),
        *landing(80, bl, 32, False),
        *landing(80, tl, CUT, True),
        *landing(32, ml, 32, False),
        vm((n, 16, vl), BF),
        vm((n, 16, vl), BF),
        vm((4, 16, vl), BF),
        vm((4 * n + 1, 1, 128), F32),
        vm((side, 2 * side), BF),
        vm((side, 2 * side), BF),
        vm((2 * side, side), BF),
        dma((15,)),
        dma((n,)),
        dma((2, h)),
        *[dma((36,)) for _ in range(2)],
        *[dma((1,)) for _ in range(4)],
        *[dma((HEADS, 3)) for _ in range(2)],
        *[dma((4,)) for _ in range(2)],
        *[dma((1,)) for _ in range(2)],
    ]
    anywhere = pl.BlockSpec(memory_space=pl.ANY)
    out_t, token_grad, own, total_squares = pl.pallas_call(
        functools.partial(block_kernel, n, side, band, qa),
        out_shape=(
            jax.ShapeDtypeStruct(block, BF),
            jax.ShapeDtypeStruct((count, D), BF),
            jax.ShapeDtypeStruct((128, total), F32),
            jax.ShapeDtypeStruct((1, 128), F32),
        ),
        in_specs=[pl.BlockSpec(memory_space=pltpu.SMEM)] + [anywhere] * 11,
        out_specs=(anywhere,) * 4,
        scratch_shapes=scratch,
        compiler_params=pltpu.CompilerParams(
            collective_id=0, has_side_effects=True, vmem_limit_bytes=VMEM_LIMIT
        ),
    )(
        buckets,
        tokens.reshape(count, width),
        jnp.swapaxes(cotangent, 3, 4).reshape(block) if turned else cotangent.reshape(block),
        *weights,
    )
    rates = (
        D ** (-0.5),
        (4 * D) ** (-0.5),
        D ** (-0.5),
        OUT_FAN ** (-0.5),
        D ** (-0.5),
        FF ** (-0.5),
        GAIN_RATE,
        VECTOR_RATE,
        VECTOR_RATE,
    )
    decays = (DECAY_RATE,) * 6 + (0.0,) * 3
    shapes = tuple(jax.ShapeDtypeStruct(w.shape, F32) for w in weights)
    results = pl.pallas_call(
        functools.partial(
            update_kernel, rb, tl, al, 128 if ml > 128 else 3 * rb, rates, decays
        ),
        out_shape=(
            jax.ShapeDtypeStruct(block, BF),
            jax.ShapeDtypeStruct((count, D), BF),
            jax.ShapeDtypeStruct((1, 128), F32),
        )
        + shapes * 3,
        in_specs=[anywhere] * 31,
        out_specs=(anywhere,) * 30,
        scratch_shapes=[
            vm((128, total), F32),
            vm((1, 128), F32),
            vm(block, BF),
            vm((count, D), BF),
            vm((1, 128), F32),
            *[vm((3, *w.shape), F32) for w in weights * 2],
            dma((13,)),
            dma((12,)),
        ],
    )(own, total_squares, out_t, token_grad, *weights, *firsts, *seconds)
    if turned:
        block_output = jnp.swapaxes(results[0].reshape(n, 1, 1, width, piece), 3, 4)
    else:
        block_output = results[0].reshape(n, 1, 1, piece, width)
    return (
        block_output,
        results[1].reshape(1, band, side, width),
        results[2][0, 0],
        *results[3:],
    )


def solution(mesh):
    matrix = (P("dp", "seq"),) * 6 + (P(None, "dp"),) * 3
    return jax.shard_map(
        functools.partial(on_device, mesh.shape["dp"]),
        mesh=mesh,
        in_specs=(
            P("dp", "seq", None, None),
            P("dp"),
            P(None, "seq", "dp", None, None),
            *(matrix * 3),
        ),
        out_specs=(
            P(None, "seq", "dp", None, None),
            P("dp", "seq", None, None),
            P(),
            *(matrix * 3),
        ),
        check_vma=False,
    )
```

```python
import functools

import jax
import jax.numpy as jnp
from jax import lax
from jax.experimental import pallas as pl
from jax.experimental.pallas import tpu as pltpu
from jax.sharding import PartitionSpec as P

D = 320
HEADS = 5
HEAD = 64
FF = 1280
STEP = 10
OUT_FAN = 5

NORM_EPS = 1e-06
MAX_NORM = 1.0
BETA_ONE = 0.9
BETA_TWO = 0.95
ADAM_EPS = 1e-08
DECAY_RATE = 0.01
VECTOR_RATE = 0.3
GAIN_RATE = 0.8
MASKED = -1e30

BF = jnp.bfloat16
F32 = jnp.float32
MESH = pl.DeviceIdType.MESH
QC = 512
GATHER_CUT = 32
CUT = 48
VMEM_LIMIT = 63 * 1024 * 1024


def nn(a, b):
    return lax.dot_general(a, b, (((1,), (0,)), ((), ())), preferred_element_type=F32)


def nt(a, b):
    return lax.dot_general(a, b, (((1,), (1,)), ((), ())), preferred_element_type=F32)


def up(n, m):
    return (n + m - 1) // m * m


def norm_parts(v):
    centered = v - jnp.mean(v, axis=-1, keepdims=True)
    rstd = lax.rsqrt(jnp.mean(centered * centered, axis=-1, keepdims=True) + NORM_EPS)
    return centered * rstd, rstd


def norm_back(v, gain, e):
    vhat, rstd = norm_parts(v)
    u = e * gain
    dv = rstd * (
        u
        - jnp.mean(u, axis=-1, keepdims=True)
        - vhat * jnp.mean(u * vhat, axis=-1, keepdims=True)
    )
    return dv, jnp.sum(e * vhat, axis=0, keepdims=True), jnp.sum(e, axis=0, keepdims=True)


def colsum(v):
    return jnp.sum(v, axis=0, keepdims=True)


def rows(start, size):
    return pl.ds(pl.multiple_of(start, 16), size)


def block_kernel(
    n,
    side,
    band,
    qa,
    bucket_ref,
    tok_ref,
    cot_ref,
    wq_ref,
    wr_ref,
    wm_ref,
    wo_ref,
    w1_ref,
    w2_ref,
    gains_ref,
    biases_ref,
    hidden_ref,
    out_ref,
    tgrad_ref,
    own_ref,
    norm_ref,
    x_s,
    fq,
    fr,
    fm,
    fo,
    f1,
    f2,
    fg,
    fb,
    fh,
    gvec,
    gt,
    gm,
    gf,
    vp,
    hp,
    wqt,
    wot,
    wop,
    wmt,
    wrt,
    w1t,
    w2t,
    a3,
    abf,
    pat,
    memin,
    kv,
    kvt,
    qnat,
    qt,
    prob,
    att_t,
    att_n,
    rtot,
    delta,
    mid,
    bn,
    hidp,
    hidh,
    act,
    gp,
    out_t,
    dy_in,
    dy_t,
    dy,
    dzh,
    datn,
    rk1,
    rk2,
    hg,
    vg,
    own_s,
    sb,
    ra0,
    ra1,
    ra2,
    ra3,
    ra4,
    ra5,
    ra6,
    rb0,
    rb1,
    rb2,
    rb3,
    rb4,
    rb5,
    rb6,
    rt0,
    rt1,
    rt2,
    rt3,
    rt4,
    rt5,
    rt6,
    rm0,
    rm1,
    rm2,
    rm3,
    rm4,
    rm5,
    rm6,
    sv,
    rv1,
    rv2,
    nrm,
    shift_f,
    shift_b,
    shift_m,
    loc,
    tl_r,
    th_r,
    gx_s,
    gx_r,
    co_s,
    co_r,
    ou_s,
    ou_r,
    kv_s,
    kv_r,
    ha_s,
    ha_r,
    nd_s,
    nd_r,
):
    me = lax.axis_index("dp")
    j = lax.axis_index("seq")
    y0 = lax.rem(me, 2)
    y1 = 1 - y0
    z0 = lax.div(me, 2)
    beside = me + 1 - 2 * y0
    zn = n // 2
    here = y0 * zn + z0

    def place_of(i):
        return i % 2 * zn + i // 2

    def spot(i):
        return lax.rem(i, 2) * zn + lax.div(i, 2)

    j1 = j + 1 - 2 * lax.rem(j, 2)
    j2 = lax.rem(j + 2, 4)
    j3 = 3 - j
    tokens = band * side
    chunks = tokens // QC
    deep = band if qa == tokens else 4
    pairs = 2 if qa == tokens else 1
    rb = wq_ref.shape[0]
    piece = tokens // n
    keys = kv.shape[2]
    turned = cot_ref.shape[1] == D
    tl = gt.shape[3]
    fl = gf.shape[3]
    vl = gvec.shape[2]
    al = up(4 * rb, 128)
    bl = sb.shape[3]
    ml = gm.shape[3]
    mo = 128 if ml > 128 else 3 * rb

    def remote(src, dst, ss, rs, dp, seq):
        return pltpu.make_async_remote_copy(
            src_ref=src,
            dst_ref=dst,
            send_sem=ss,
            recv_sem=rs,
            device_id=(dp, seq),
            device_id_type=MESH,
        )

    def both(copy):
        copy.wait_send()
        copy.wait_recv()

    def peers(body):
        def step(k, carry):
            body(k, lax.rem(me + k, n), lax.rem(me + n - k, n))
            return carry

        lax.fori_loop(1, n, step, 0)

    def z_peers(body):
        def step(k, carry):
            body(k, lax.rem(me + 2 * k, n), lax.rem(z0 + k, zn), lax.rem(z0 + zn - k, zn))
            return carry

        lax.fori_loop(1, zn, step, 0)

    loads = [
        pltpu.make_async_copy(src, dst, loc.at[at])
        for at, (src, dst) in enumerate(
            (
                (gains_ref, fg),
                (biases_ref, fb),
                (hidden_ref, fh),
                (wr_ref, fr),
                (wm_ref, fm),
                (wq_ref, fq),
                (wo_ref, fo),
                (w1_ref, f1),
                (w2_ref, f2),
                (tok_ref, x_s),
            )
        )
    ]
    for copy in loads:
        copy.start()
    def incoming(i):
        return dy_in.at[i] if turned else dy.at[rows(i * piece, piece)]

    own_cot = pltpu.make_async_copy(cot_ref.at[me], incoming(me), loc.at[10])
    own_cot.start()

    barrier = pltpu.get_barrier_semaphore()

    def greet(k, carry):
        to = lax.rem(4 * me + j + k, 4 * n)
        pl.semaphore_signal(
            barrier, inc=1, device_id=(lax.div(to, 4), lax.rem(to, 4)), device_id_type=MESH
        )
        return carry

    lax.fori_loop(1, 4 * n, greet, 0)

    for copy in loads[:5]:
        copy.wait()
    hidden16 = jnp.concatenate([fh[...], jnp.zeros((5, 4 * rb), F32)], axis=0)
    small16 = jnp.concatenate([fg[...], fb[...], jnp.zeros((5, rb), F32)], axis=0)
    gvec[here] = jnp.concatenate(
        [hidden16, small16, jnp.zeros((16, vl - 5 * rb), F32)], axis=1
    ).astype(BF)
    wm_t = fm[...].T
    gt[j, here] = jnp.concatenate(
        [fr[...].T, wm_t[0:80], wm_t[80:160], jnp.zeros((80, tl - 6 * rb), F32)], axis=1
    ).astype(BF)

    def group(at, one_of, all_but_one, each):
        def start():
            def send(peer):
                ref = one_of(here)
                remote(ref, ref, gx_s.at[14 + at], gx_r.at[14 + at], peer, j).start()

            each(send)

        def wait():
            both(remote(all_but_one, all_but_one, gx_s.at[14 + at], gx_r.at[14 + at], beside, j))

        return start, wait

    def each_peer(send):
        peers(lambda k, peer, source: send(peer))

    def each_z(send):
        z_peers(lambda k, peer, to, source: send(peer))

    def over_dp(at, buf, rows_of):
        return group(
            at, lambda i: buf.at[i, rows_of], buf.at[pl.ds(0, n - 1), rows_of], each_peer
        )

    def over_z(at, buf, rows_of):
        return group(
            at, lambda i: buf.at[i, rows_of], buf.at[pl.ds(0, zn - 1), rows_of], each_z
        )

    def swap(at, mine, theirs, dp, seq):
        def start():
            remote(mine, mine, gx_s.at[at], gx_r.at[at], dp, seq).start()

        def wait():
            remote(mine, mine, gx_s.at[at], gx_r.at[at], dp, seq).wait_send()
            remote(theirs, theirs, gx_s.at[at], gx_r.at[at], dp, seq).wait_recv()

        return start, wait

    def over_y(at, buf, rows_of):
        mine = buf.at[pl.ds(y0 * zn, zn), rows_of]
        theirs = buf.at[pl.ds(y1 * zn, zn), rows_of]
        return swap(at, mine, theirs, beside, j)

    lower = slice(0, GATHER_CUT)
    upper = slice(GATHER_CUT, 80)
    every = slice(0, 16)
    v_dp, v_dp_wait = over_dp(0, gvec, every)

    def t_low(i):
        return gt.at[j, i, lower]

    def t_low_copy(k, i, peer):
        return remote(t_low(i), t_low(i), gx_s.at[15], tl_r.at[k], peer, j)

    def t_low_on(i):
        remote(t_low(i), t_low(i), gx_s.at[0], gx_r.at[0], me, j2).start()

    def t_low_start():
        t_low_on(here)
        peers(lambda k, peer, source: t_low_copy(k, here, peer).start())

    def t_low_forward():
        def body(k, peer, source):
            t_low_copy(k, spot(source), peer).wait_recv()
            t_low_on(spot(source))

        peers(body)

    def t_low_wait():
        part = gt.at[j, pl.ds(0, n - 1), lower]
        remote(part, part, gx_s.at[15], tl_r.at[0], beside, j).wait_send()
        both(remote(gt.at[j, :, lower], gt.at[j2, :, lower], gx_s.at[0], gx_r.at[0], me, j2))

    t_x0, t_x0_wait = swap(1, gt.at[j, here, upper], gt.at[j2, here, upper], me, j2)

    def t_high(slot, t):
        def ref(i):
            return gt.at[slot, i, upper]

        def copy(k, i, peer):
            return remote(ref(i), ref(i), gx_s.at[16 + t], th_r.at[t, k], peer, j)

        def on(i):
            remote(ref(i), ref(i), gx_s.at[2 + t], gx_r.at[2 + t], beside, j).start()

        def start():
            z_peers(lambda k, peer, to, source: copy(k, here, peer).start())
            on(here)

        def forward():
            def body(k, peer, to, source):
                copy(k, y0 * zn + source, peer).wait_recv()
                on(y0 * zn + source)

            z_peers(body)

        def wait():
            part = gt.at[slot, pl.ds(0, zn - 1), upper]
            remote(part, part, gx_s.at[16 + t], th_r.at[t, 0], beside, j).wait_send()
            mine = gt.at[slot, pl.ds(y0 * zn, zn), upper]
            theirs = gt.at[slot, pl.ds(y1 * zn, zn), upper]
            both(remote(mine, theirs, gx_s.at[2 + t], gx_r.at[2 + t], beside, j))

        return start, forward, wait

    t_za, t_za_forward, t_ya_wait = t_high(j, 0)
    t_zb, t_zb_forward, t_yb_wait = t_high(j2, 1)
    t_ca, t_ca_wait = swap(4, gt.at[j], gt.at[j1], me, j1)
    t_cb, t_cb_wait = swap(5, gt.at[j2], gt.at[j3], me, j1)
    wq_block = gm.at[:, :, :, 0:128]
    m_dp, m_dp_wait = over_dp(4, wq_block.at[j], slice(0, 32))
    m_x, m_x_wait = swap(6, wq_block.at[j], wq_block.at[j2], me, j2)
    m_ca, m_ca_wait = swap(7, wq_block.at[j], wq_block.at[j1], me, j1)
    m_cb, m_cb_wait = swap(8, wq_block.at[j2], wq_block.at[j3], me, j1)
    f_x0, f_x0_wait = swap(9, gf.at[j, here], gf.at[j2, here], me, j2)
    fl_za, fl_za_wait = over_z(5, gf.at[j], lower)
    fl_zb, fl_zb_wait = over_z(6, gf.at[j2], lower)
    fh_a, fh_a_wait = over_dp(7, gf.at[j], upper)
    fh_b, fh_b_wait = over_dp(8, gf.at[j2], upper)
    fl_ya, fl_ya_wait = over_y(10, gf.at[j], lower)
    fl_yb, fl_yb_wait = over_y(11, gf.at[j2], lower)
    fl_ca, fl_ca_wait = swap(12, gf.at[j, :, lower], gf.at[j1, :, lower], me, j1)
    fl_cb, fl_cb_wait = swap(13, gf.at[j2, :, lower], gf.at[j3, :, lower], me, j1)
    fh_ca, fh_ca_wait = swap(34, gf.at[j, :, upper], gf.at[j1, :, upper], me, j1)
    fh_cb, fh_cb_wait = swap(35, gf.at[j2, :, upper], gf.at[j3, :, upper], me, j1)

    pl.semaphore_wait(barrier, 4 * n - 1)
    t_x0()
    t_za()
    t_low_start()

    for copy in loads[5:9]:
        copy.wait()
    wq_t = fq[...].T
    gm[j, here, :, 0:128] = jnp.concatenate(
        [
            wq_t[0:32],
            wq_t[32:64],
            jnp.concatenate([wq_t[64:80], jnp.zeros((16, rb), F32)], axis=0),
            jnp.zeros((32, 128 - 3 * rb), F32),
        ],
        axis=1,
    ).astype(BF)
    w1_t = f1[...].T
    gf[j, here] = jnp.concatenate(
        [f2[...].T]
        + [w1_t[80 * v : 80 * v + 80] for v in range(4)]
        + [fo[...].T, jnp.zeros((80, fl - 9 * rb), F32)],
        axis=1,
    ).astype(BF)
    t_x0_wait()
    t_zb()
    v_dp()

    t_low_forward()
    m_dp()
    f_x0()
    t_za_forward()
    t_zb_forward()
    f_x0_wait()
    fl_za()
    fl_zb()
    v_dp_wait()
    hp[...] = jnp.concatenate([gvec[place_of(i), :, 0 : 4 * rb] for i in range(n)], axis=1).astype(F32)
    vp[...] = jnp.concatenate(
        [gvec[place_of(i), :, 4 * rb : 5 * rb] for i in range(n)], axis=1
    ).astype(F32)

    def gain(k):
        return vp[k : k + 1, :]

    def shift(k):
        return vp[3 + k : 4 + k, :]

    loads[9].wait()

    def norm_one(c, carry):
        at = rows(c * QC, QC)
        vhat, _ = norm_parts(x_s[at, :].astype(F32))
        low = (vhat * gain(0) + shift(0)).astype(BF)
        abf[at, :] = low
        wide = jnp.concatenate([low.astype(F32), jnp.zeros((QC, 64), F32)], axis=1)
        for t in range(3):
            a3[t, at, :] = wide[:, 128 * t : 128 * t + 128]
        return carry

    lax.fori_loop(0, chunks, norm_one, 0, unroll=pairs)
    half = side // 2
    for dd in range(4):
        for i in range(band // 2):
            start = (2 * i + dd // 2) * side + dd % 2
            cut = jnp.concatenate(
                [a3[t, pl.ds(start, half, stride=2), :] for t in range(3)], axis=1
            )
            pat[dd, i * half : (i + 1) * half, :] = cut[:, 0:D].astype(BF)

    bucket = bucket_ref[0]
    k_row = lax.broadcasted_iota(jnp.int32, (4 * keys, 128), 0)
    k_lane = lax.broadcasted_iota(jnp.int32, (4 * keys, 128), 1)
    k_id = (lax.div(k_row, half) >= half // 2).astype(jnp.int32) * 2 + (
        lax.rem(k_row, half) >= half // 2
    ).astype(jnp.int32)
    off = (k_id != k_lane).astype(jnp.int32) * bucket * (k_lane < 4).astype(jnp.int32)
    kmask = datn.at[0]
    qmask = dy_t.at[0:128]
    kmask[...] = (off.astype(F32) * MASKED).astype(BF)
    q_row = lax.broadcasted_iota(jnp.int32, (128, tokens), 0)
    place = lax.broadcasted_iota(jnp.int32, (128, tokens), 1)
    q_id = (lax.div(place, side) + j * band >= half).astype(jnp.int32) * 2 + (
        lax.rem(place, side) >= half
    ).astype(jnp.int32)
    qmask[...] = (q_id == q_row).astype(F32).astype(BF)
    col = lax.broadcasted_iota(jnp.int32, (side, side), 0)
    ok_l = (col > 0).astype(jnp.int32) * (1 - bucket * (col == half).astype(jnp.int32))
    ok_r = (col < side - 1).astype(jnp.int32) * (
        1 - bucket * (col == half - 1).astype(jnp.int32)
    )
    lane = lax.broadcasted_iota(jnp.int32, (side, side), 1)
    from_l = (ok_l * (lane == col - 1).astype(jnp.int32)).astype(F32).astype(BF)
    from_r = (ok_r * (lane == col + 1).astype(jnp.int32)).astype(F32).astype(BF)
    shift_f[...] = jnp.concatenate([from_l, from_r], axis=1)
    shift_b[...] = jnp.concatenate([from_r, from_l], axis=1)
    shift_m[...] = jnp.concatenate([from_r, from_l], axis=0)
    top_ok = (
        (j > 0).astype(jnp.int32) * (1 - bucket * (j * band == half).astype(jnp.int32))
    ).astype(F32)
    low_ok = (
        (j < 3).astype(jnp.int32) * (1 - bucket * ((j + 1) * band == half).astype(jnp.int32))
    ).astype(F32)

    t_ya_wait()
    t_yb_wait()
    t_low_wait()
    t_ca()
    t_cb()
    m_dp_wait()
    m_x()
    t_ca_wait()
    t_cb_wait()

    fh_a()
    fh_b()

    for s in range(4):
        span = slice(80 * s, 80 * s + 80)

        def lanes(lo, hi, over):
            return jnp.concatenate([gt[s, place_of(i), :, lo:hi] for i in over], axis=1)

        for dd in range(4):
            wrt[dd, span, :] = lanes(0, 4 * rb, range(dd * n // 4, (dd + 1) * n // 4))
        for v in range(2):
            wop[160 * s + 80 * v : 160 * s + 80 * v + 80, :] = lanes(
                (4 + v) * rb, (5 + v) * rb, range(n)
            )
    for h in range(HEADS):
        wmt[128 * h : 128 * h + 64, :] = wop[HEAD * h : HEAD * h + HEAD, :]
        wmt[128 * h + 64 : 128 * h + 128, :] = wop[D + HEAD * h : D + HEAD * h + HEAD, :]

    red = shift(2) + nt(pat[0], wrt[0])
    for dd in range(1, 4):
        red = red + nt(pat[dd], wrt[dd])
    wide_red = jnp.concatenate([red, jnp.zeros((keys, 64), F32)], axis=1)
    for t in range(3):
        a3[t, 0:keys, :] = wide_red[:, 128 * t : 128 * t + 128]
    vhat, _ = norm_parts(red)
    low = (vhat * gain(1) + shift(3)).astype(BF)
    memin[...] = low
    zero64 = jnp.zeros((1, HEAD), F32)
    value_shift = jnp.concatenate(
        [
            part
            for h in range(HEADS)
            for part in (zero64, shift(4)[:, HEAD * h : HEAD * h + HEAD])
        ],
        axis=1,
    )
    memory = (nt(low, wmt[...]) + value_shift).astype(BF)
    for h in range(HEADS):
        kv[h, j] = memory[:, 128 * h : 128 * h + 128]

    def kv_copy(h, slot, t, other):
        return remote(
            kv.at[h, slot], kv.at[h, slot], kv_s.at[h, t], kv_r.at[h, t], me, other
        )

    def kv_send(h, carry):
        kv_copy(h, j, 0, j2).start()
        kv_copy(h, j, 1, j1).start()
        return carry

    lax.fori_loop(0, 2, kv_send, 0)

    m_x_wait()
    m_ca()
    m_cb()
    wqp = wop
    m_ca_wait()
    m_cb_wait()
    for s in range(4):
        at = 80 * s
        wqt[at : at + 32, :] = jnp.concatenate([gm[s, place_of(i), :, 0:rb] for i in range(n)], axis=1)
        wqt[at + 32 : at + 64, :] = jnp.concatenate(
            [gm[s, place_of(i), :, rb : 2 * rb] for i in range(n)], axis=1
        )
        wqt[at + 64 : at + 80, :] = jnp.concatenate(
            [gm[s, place_of(i), 0:16, 2 * rb : 3 * rb] for i in range(n)], axis=1
        )
    for h in range(HEADS):
        wqp[128 * h : 128 * h + 64, :] = wqt[HEAD * h : HEAD * h + HEAD, :]
        wqp[128 * h + 64 : 128 * h + 128, :] = jnp.zeros((64, D), BF)

    query_shift = jnp.concatenate(
        [
            part
            for h in range(HEADS)
            for part in (shift(1)[:, HEAD * h : HEAD * h + HEAD], zero64)
        ],
        axis=1,
    )

    def across(c):
        return pl.ds(pl.multiple_of(c * QC, QC), QC)

    def queries(c, carry):
        at = rows(c * QC, QC)
        q = (nt(abf[at, :], wqp[...]) + query_shift).astype(BF) * jnp.asarray(HEAD**-0.5, BF)
        for h in range(HEADS):
            tile = q[:, 128 * h : 128 * h + 128]
            qnat[h, at, :] = tile
            qt[h, :, across(c)] = tile.T
        return carry

    lax.fori_loop(0, chunks, queries, 0, unroll=pairs)
    lax.fori_loop(2, HEADS, kv_send, 0)

    def send_cot(k, peer, source):
        remote(cot_ref.at[peer], incoming(me), co_s.at[0], co_r.at[0], peer, j).start()

    def wait_cot():
        part = cot_ref.at[pl.ds(0, n - 1)]
        both(remote(part, part, co_s.at[0], co_r.at[0], beside, j))

    def kv_forward(h):
        kv_copy(h, j2, 0, j2).wait_recv()
        kv_copy(h, j2, 2, j1).start()

    fl_za_wait()
    fl_zb_wait()
    fl_ya()
    fl_yb()
    kv_forward(0)

    def attend(h, carry):
        kv_copy(h, j, 0, j2).wait_send()
        kv_copy(h, j, 1, j1).wait_send()
        kv_copy(h, j2, 2, j1).wait_send()
        kv_copy(h, j1, 1, j1).wait_recv()
        kv_copy(h, j3, 2, j1).wait_recv()
        tile = kv[h].reshape(4 * keys, 128)
        kvt[h] = tile.T
        left = jnp.concatenate([tile, kmask[...]], axis=1)
        values = jnp.concatenate([kvt[h, 64:128, :], jnp.ones((16, 4 * keys), BF)], axis=0)
        for c in range(tokens // qa):
            cut = slice(c * qa, (c + 1) * qa)
            scores = nn(left, jnp.concatenate([qt[h, :, cut], qmask[:, cut]], axis=0))
            if c == 0:

                @pl.when(h < HEADS - 1)
                def _():
                    kv_forward(h + 1)

                @pl.when(h == 3)
                def _():
                    peers(send_cot)

                @pl.when(h == HEADS - 2)
                def _():
                    fl_ya_wait()
                    fl_yb_wait()
                    fl_ca()
                    fl_cb()

                @pl.when(h == HEADS - 1)
                def _():
                    fh_a_wait()
                    fh_b_wait()
                    fh_ca()
                    fh_cb()

            largest = jnp.max(scores, axis=0, keepdims=True)
            powers = jnp.exp(scores - largest).astype(BF)
            prob[h, :, cut] = powers
            got = nn(values, powers)
            scale = 1.0 / got[64:65, :]
            rtot[h, :, cut] = scale
            att_t[rows(h * HEAD, HEAD), cut] = (got[0:64, :] * scale).astype(BF)
        return carry

    lax.fori_loop(0, HEADS, attend, 0)

    fl_ca_wait()
    fl_cb_wait()

    def unpack_rows(part, lo, hi):
        for s in range(4):
            span = slice(80 * s + lo, 80 * s + hi)

            def lanes(at, width):
                return jnp.concatenate(
                    [gf[s, place_of(i), part, at : at + width] for i in range(n)], axis=1
                )

            w2t[span, :] = lanes(0, 4 * rb)
            for v in range(4):
                at = 320 * s + 80 * v
                w1t[at + lo : at + hi, :] = lanes((4 + v) * rb, rb)
            wot[span, :] = lanes(8 * rb, rb)

    unpack_rows(lower, 0, GATHER_CUT)
    fh_ca_wait()
    fh_cb_wait()
    unpack_rows(upper, GATHER_CUT, 80)
    wop_full = wot[...].T
    for h in range(HEADS):
        wop[128 * h : 128 * h + 64, :] = jnp.zeros((64, D), BF)
        wop[128 * h + 64 : 128 * h + 128, :] = wop_full[HEAD * h : HEAD * h + HEAD, :]

    def middle(c, carry):
        at = rows(c * QC, QC)
        att = att_t[:, across(c)].T
        att_n[at, :] = att
        value = x_s[at, :].astype(F32) + nt(att, wot[...]) + shift(5)
        mid[at, :] = value
        vhat, _ = norm_parts(value)
        low = (vhat * gain(2) + shift(6)).astype(BF)
        bn[at, :] = low
        return carry

    lax.fori_loop(0, chunks, middle, 0, unroll=pairs)

    edge = tokens - side

    def hidden_of(value):
        return (nt(value, w1t[...]) + hp[9:10, :]).astype(BF)

    ends = hidden_of(jnp.concatenate([bn[0:side, :], bn[edge:tokens, :]], axis=0))
    hidp[side : 2 * side, :] = ends[0:side]
    hidp[tokens : tokens + side, :] = ends[side : 2 * side]
    above = lax.rem(j + 3, 4)
    below = lax.rem(j + 1, 4)

    def rim_up(buf, halo, at):
        return remote(buf.at[pl.ds(side, side)], halo.at[1], ha_s.at[at], ha_r.at[at], me, above)

    def rim_down(buf, halo, at):
        return remote(
            buf.at[pl.ds(tokens, side)], halo.at[0], ha_s.at[at + 1], ha_r.at[at + 1], me, below
        )

    def rim_send(buf, halo, at):
        @pl.when(j > 0)
        def _():
            rim_up(buf, halo, at).start()

        @pl.when(j < 3)
        def _():
            rim_down(buf, halo, at).start()

    def rim_wait(buf, halo, at):
        @pl.when(j > 0)
        def _():
            rim_up(buf, halo, at).wait_send()
            rim_down(buf, halo, at).wait_recv()

        @pl.when(j < 3)
        def _():
            rim_down(buf, halo, at).wait_send()
            rim_up(buf, halo, at).wait_recv()

        for t, (to, ok) in enumerate(((0, top_ok), (tokens + side, low_ok))):
            seen = jnp.full((side, FF), ok, F32) > 0.5
            buf[to : to + side, :] = jnp.where(seen, halo[t].astype(F32), 0.0).astype(BF)

    rim_send(hidp, hidh, 0)

    inner = (tokens - 2 * side) // 2

    def inner_hidden(c, carry):
        start = side + c * inner
        hidp[rows(start + side, inner), :] = hidden_of(bn[rows(start, inner), :])
        return carry

    lax.fori_loop(0, 2, inner_hidden, 0, unroll=pairs)

    def tile_at(t):
        return pl.ds(pl.multiple_of(t * 128, 128), 128)

    def taps_of(lanes):
        return [hp[k : k + 1, lanes] for k in range(9)]

    def conv_over(lo, hi, step, tiles):
        def conv_tile(t, carry):
            lanes = tile_at(t)
            taps = taps_of(lanes)
            base = hp[10:11, lanes]

            def row(at, inner):
                r = lo + at * step
                around = [hidp[rows((r + a) * side, side), lanes].astype(F32) for a in range(3)]
                parts = [
                    taps[b] * around[0] + taps[3 + b] * around[1] + taps[6 + b] * around[2]
                    for b in range(3)
                ]
                moved = jnp.concatenate([parts[0].astype(BF), parts[2].astype(BF)], axis=0)
                z = base + parts[1] + nn(shift_f[...], moved)
                root = z * (0.5**0.5)
                cdf = 0.5 + 0.5 * lax.erf(root)
                slope = (z * 0.3989422804014327) * jnp.exp2(root * root * -1.4426950408889634)
                act[rows((r + 1) * side, side), lanes] = (z * cdf).astype(BF)
                gp[rows(r * side, side), lanes] = (cdf + slope).astype(BF)
                return inner

            lax.fori_loop(0, (hi - lo) // step, row, 0, unroll=True)
            return carry

        lax.fori_loop(0, FF // 128, conv_tile, 0, unroll=tiles)

    conv_over(1, band - 1, 1, 1)
    rim_wait(hidp, hidh, 0)
    conv_over(0, 2 * (band - 1), band - 1, 5)

    def out_chunk(c, carry):
        at = rows(c * QC, QC)
        value = mid[at, :] + nt(act[rows(side + c * QC, QC), :], w2t[...]) + shift(7)
        for p in range(QC // piece):
            part = value[p * piece : (p + 1) * piece, :]
            out_t[c * (QC // piece) + p] = (part.T if turned else part).astype(BF)
        return carry

    lax.fori_loop(0, chunks, out_chunk, 0, unroll=pairs)

    def send_out(k, peer, source):
        remote(out_t.at[peer], out_ref.at[me], ou_s.at[0], ou_r.at[0], peer, j).start()

    def wait_out():
        part = out_t.at[pl.ds(0, n - 1)]
        both(remote(part, part, ou_s.at[0], ou_r.at[0], beside, j))

    peers(send_out)
    own_out = pltpu.make_async_copy(out_t.at[me], out_ref.at[me], loc.at[11])
    own_out.start()

    own_cot.wait()
    wait_cot()
    for i in range(n):
        if turned:
            dy_t[:, i * piece : (i + 1) * piece] = dy_in[i]
            dy[i * piece : (i + 1) * piece, :] = dy_in[i].T
    if not turned:
        dy_t[...] = dy[...].T
    vg[...] = jnp.zeros(vg.shape, F32)
    vg[10:11, :] = colsum(dy[...].astype(F32))

    def scatter(sems, s, cut, direct, bufs, own):
        top = s.shape[2]
        r1, xl, yl, dl, yh, dh, xh = bufs
        low, high = slice(0, cut), slice(cut, top)
        slots = (j, j2)
        count = n if direct else zn
        mine = pl.ds(y0 * zn, zn)
        theirs = pl.ds(y1 * zn, zn)

        def copy(src, dst, t, dp, seq):
            at = sems[t]
            return remote(src, dst, gx_s.at[at], gx_r.at[at], dp, seq)

        def core():
            return [copy(s.at[slot], r1.at[t], t, me, j1) for t, slot in enumerate((j1, j3))]

        def low_x():
            return copy(s.at[j2, :, low], xl, 2, me, j2)

        def low_y():
            return copy(s.at[j, theirs, low], yl, 3, beside, j)

        def high_y():
            return [
                copy(s.at[slot, theirs, high], yh.at[t], 4 + t, beside, j)
                for t, slot in enumerate(slots)
            ]

        def high_x():
            return copy(s.at[j2, here, high], xh, 6, me, j2)

        def out(slot, rows_of, land, t):
            def send(k, peer, to):
                copy(s.at[slot, to, rows_of], land.at[k], t, peer, j).start()

            if direct:
                peers(lambda k, peer, source: send(k, peer, spot(peer)))
            else:
                z_peers(lambda k, peer, to, source: send(k, peer, y0 * zn + to))

        def landed(slot, rows_of, land, t):
            part = land.at[pl.ds(1, count - 1)]
            both(copy(part, part, t, beside, j))
            return lax.fori_loop(
                1,
                count,
                lambda k, v: v + land[k].astype(F32),
                s[slot, here, rows_of].astype(F32),
            )

        def add(slot, start, rows_of, extra):
            def body(i, carry):
                s[slot, start + i, rows_of] = (
                    s[slot, start + i, rows_of].astype(F32) + extra[i].astype(F32)
                ).astype(BF)
                return carry

            lax.fori_loop(0, extra.shape[0], body, 0)

        def one():
            for c in core():
                c.start()

        def two():
            for c in core():
                both(c)
            for t, slot in enumerate(slots):
                add(slot, 0, slice(0, top), r1.at[t])
            if cut < top:
                if direct:
                    for t, slot in enumerate(slots):
                        out(slot, high, dh.at[t], 4 + t)
                else:
                    for c in high_y():
                        c.start()
            if cut > 0:
                low_x().start()

        def low_three():
            both(low_x())
            add(j, 0, low, xl)
            if direct:
                out(j, low, dl, 3)
            else:
                low_y().start()

        def high_three():
            for c in high_y():
                both(c)
            for t, slot in enumerate(slots):
                add(slot, y0 * zn, high, yh.at[t])
                out(slot, high, dh.at[t], 7 + t)

        def low_four():
            both(low_y())
            add(j, y0 * zn, low, yl)
            out(j, low, dl, 9)

        def high_four():
            first = 4 if direct else 7
            own[high, :] = landed(j, high, dh.at[0], first)
            s[j2, here, high] = landed(j2, high, dh.at[1], first + 1).astype(BF)
            high_x().start()

        def low_five():
            own[low, :] = landed(j, low, dl, 3 if direct else 9)

        def high_five():
            both(high_x())
            own[high, :] = own[high, :] + xh[...].astype(F32)

        return one, two, low_three, low_four, low_five, high_three, high_four, high_five

    own_t = own_s.at[0:80, 0:tl]
    own_a = own_s.at[0:80, tl : tl + al]
    own_b = own_s.at[0:80, tl + al : tl + al + bl]
    own_m = own_s.at[96:128, 0:ml]
    a_one, a_two, a_three, a_four, a_five, _, _, _ = scatter(
        (0, 1, 2, 3, 0, 0, 0, 0, 0, 4), gf.at[:, :, :, 0:al], 80, False, (ra0, ra1, ra2, ra3, ra4, ra5, ra6), own_a
    )
    b_one, b_two, bl_three, bl_four, bl_five, bh_three, bh_four, bh_five = scatter(
        (5, 6, 27, 28, 7, 8, 9, 36, 37, 29), sb, 32, False, (rb0, rb1, rb2, rb3, rb4, rb5, rb6), own_b
    )
    m_one, m_two, m_three, m_four, m_five, _, _, _ = scatter(
        (12, 13, 14, 15, 0, 0, 0, 0, 0, 33), gm, 32, False, (rm0, rm1, rm2, rm3, rm4, rm5, rm6), own_m
    )
    below_cut = slice(0, CUT)
    above_cut = slice(CUT, 80)

    def t_core(t, slot, to, rows_of):
        return remote(
            gt.at[slot, :, rows_of], rt0.at[to, :, rows_of], gx_s.at[16 + t], gx_r.at[16 + t], me, j1
        )

    def t_cores():
        return (
            t_core(0, j3, 1, below_cut),
            t_core(1, j1, 0, above_cut),
            t_core(2, j3, 1, above_cut),
            t_core(3, j1, 0, below_cut),
        )

    def t_add(slot, start, count, rows_of, extra):
        def body(i, carry):
            gt[slot, start + i, rows_of] = (
                gt[slot, start + i, rows_of].astype(F32) + extra[start + i, rows_of].astype(F32)
            ).astype(BF)
            return carry

        lax.fori_loop(0, count, body, 0)

    def t_half(t):
        part = pl.ds((y1 if t == 0 else y0) * zn, zn)
        return remote(
            gt.at[j2, part, below_cut], rt1.at[part], gx_s.at[20 + t], gx_r.at[20 + t], me, j2
        )

    def t_dp(slot, i, rows_of, land, sem, k, peer):
        remote(
            gt.at[slot, i, rows_of], land.at[k], gx_s.at[sem], gx_r.at[sem], peer, j
        ).start()

    def t_landed(slot, rows_of, land, sem):
        part = land.at[pl.ds(1, n - 1)]
        both(remote(part, part, gx_s.at[sem], gx_r.at[sem], beside, j))
        return lax.fori_loop(
            1, n, lambda k, v: v + land[k].astype(F32), gt[slot, here, rows_of].astype(F32)
        )

    def t_one():
        for c in t_cores():
            c.start()

    def t_two():
        cores = t_cores()
        both(cores[0])
        t_add(j2, 0, n, below_cut, rt0.at[1])
        t_half(0).start()
        t_half(1).start()
        both(cores[1])
        both(cores[2])
        for t, slot in enumerate((j, j2)):
            t_add(slot, 0, n, above_cut, rt0.at[t])
            peers(
                lambda k, peer, source: t_dp(
                    slot, spot(peer), above_cut, rt5.at[t], 38 - 15 * t, k, peer
                )
            )
        both(cores[3])
        t_add(j, 0, n, below_cut, rt0.at[0])

    def tl_three(t):
        both(t_half(t))
        start = (y1 if t == 0 else y0) * zn

        def body(i, carry):
            at = start + i
            gt[j, at, below_cut] = (gt[j, at, below_cut].astype(F32) + rt1[at].astype(F32)).astype(BF)
            return carry

        lax.fori_loop(0, zn, body, 0)

        def send(i, carry):
            k = 2 * i + (1 if t == 0 else 2)
            peer = lax.rem(me + k, n)
            t_dp(j, spot(peer), below_cut, rt3, 24, k, peer)
            return carry

        lax.fori_loop(0, zn if t == 0 else zn - 1, send, 0)

    def th_x():
        return remote(gt.at[j2, here, above_cut], rt6, gx_s.at[25], gx_r.at[25], me, j2)

    def th_four():
        own_t[above_cut, :] = t_landed(j, above_cut, rt5.at[0], 38)
        gt[j2, here, above_cut] = t_landed(j2, above_cut, rt5.at[1], 23).astype(BF)
        th_x().start()

    def tl_five():
        own_t[below_cut, :] = t_landed(j, below_cut, rt3, 24)

    def th_five():
        both(th_x())
        own_t[above_cut, :] = own_t[above_cut, :] + rt6[...].astype(F32)


    per = 640 // (4 * rb)
    for b in range(2):
        value = nn(dy_t[...], act[side : side + tokens, 640 * b : 640 * b + 640]).astype(BF)
        for ii in range(per):
            i = b * per + ii
            gf[:, place_of(i), :, 0 : 4 * rb] = value[
                :, 4 * rb * ii : 4 * rb * (ii + 1)
            ].reshape(4, 80, 4 * rb)

    a_one()

    def slope_of(at):
        return nn(dy[at, :], w2t[...])

    dz = act
    for at in (0, edge):
        dz[side + at : 2 * side + at, :] = (
            slope_of(slice(at, at + side)) * gp[at : at + side, :].astype(F32)
        ).astype(BF)
    rim_send(dz, dzh, 2)

    def inner_slope(c, carry):
        at = rows(side + c * inner, inner)
        dz[rows(2 * side + c * inner, inner), :] = (
            slope_of(at) * gp[at, :].astype(F32)
        ).astype(BF)
        return carry

    lax.fori_loop(0, 2, inner_slope, 0, unroll=pairs)

    a_two()

    dhid = gp

    def back_over(lo, hi, step, tiles):
        def back_tile(t, carry):
            lanes = tile_at(t)
            taps = taps_of(lanes)

            def row(at, inner):
                r = lo + at * step
                around = [dz[rows((r + a) * side, side), lanes].astype(F32) for a in range(3)]
                parts = [
                    taps[b] * around[2] + taps[3 + b] * around[1] + taps[6 + b] * around[0]
                    for b in range(3)
                ]
                both_ways = jnp.concatenate([parts[0].astype(BF), parts[2].astype(BF)], axis=0)
                low = (parts[1] + nn(shift_b[...], both_ways)).astype(BF)
                dhid[rows(r * side, side), lanes] = low
                return inner

            lax.fori_loop(0, (hi - lo) // step, row, 0, unroll=True)
            return carry

        lax.fori_loop(0, FF // 128, back_tile, 0, unroll=tiles)

    back_over(1, band - 1, 1, 1)
    rim_wait(dz, dzh, 2)
    back_over(0, 2 * (band - 1), band - 1, 5)

    def fold(v):
        return jnp.sum(v.reshape(-1, 8, 128), axis=0)

    def tap_sums(lo, hi):
        def tile(t, carry):
            lanes = tile_at(t)

            def row(r, sums):
                low = dz[rows((r + 1) * side, side), lanes]
                here_f = low.astype(F32)
                sides = nn(shift_m[...], low)
                moved = [sides[0:side], here_f, sides[side : 2 * side]]
                found = []
                for a in range(3):
                    source = hidp[rows((r + a) * side, side), lanes].astype(F32)
                    for b in range(3):
                        found.append(fold(moved[b] * source))
                found.append(fold(here_f))
                return tuple(s + f for s, f in zip(sums, found))

            sums = lax.fori_loop(
                0, band, row, tuple(jnp.zeros((8, 128), F32) for _ in range(10)), unroll=deep
            )
            hg[:, lanes] = jnp.concatenate(
                [colsum(s) for s in sums[0:9]]
                + [hg[9:10, lanes], colsum(sums[9]), jnp.zeros((5, 128), F32)],
                axis=0,
            )
            return carry

        lax.fori_loop(lo, hi, tile, 0)

    bn_t = jnp.concatenate([bn[...].T, jnp.ones((16, tokens), BF)], axis=0)
    for b in range(2):
        found = nn(bn_t, dhid[:, 640 * b : 640 * b + 640])
        hg[9:10, 640 * b : 640 * b + 640] = found[D : D + 1]
        value = found[0:D].T.astype(BF).reshape(2, 4, 80, D)
        for i in range(n):
            sb[2 * b : 2 * b + 2, place_of(i), :, 0 : 4 * rb] = jnp.concatenate(
                [value[:, v, :, rb * i : rb * i + rb] for v in range(4)], axis=2
            )

    b_one()

    zero_row = jnp.zeros((1, D), F32)
    dbr = bn
    dbr_t = dy_t

    def back_middle(c, carry):
        at = rows(c * QC, QC)
        value, in_gain, in_shift = norm_back(mid[at, :], gain(2), nn(dhid[at, :], w1t[...]))
        value = value + dy[at, :].astype(F32)
        mid[at, :] = value
        low = value.astype(BF)
        dbr[at, :] = low
        dbr_t[:, across(c)] = low.T
        spread = nt(wop[...], low)
        for h in range(HEADS):
            tile = spread[128 * h : 128 * h + 128, :] * rtot[h, :, across(c)]
            tile_low = tile.astype(BF)
            qt[h, :, across(c)] = tile_low
            datn[h, at, :] = tile_low.T
            delta[h, :, across(c)] = colsum(
                tile_low[64:128, :].astype(F32)
                * att_t[HEAD * h : HEAD * h + HEAD, across(c)].astype(F32)
            )
        return (carry[0] + in_gain, carry[1] + in_shift, carry[2] + colsum(low.astype(F32)))

    sums = lax.fori_loop(0, chunks, back_middle, (zero_row, zero_row, zero_row), unroll=pairs)
    vg[2:3, :] = sums[0]
    vg[9:10, :] = sums[1]
    vg[8:9, :] = sums[2]
    a_three()
    b_two()

    def dkv(h, slot):
        return gp.at[rows(slot * keys, keys), tile_at(h)]

    def dk_core(h):
        return [
            remote(dkv(h, slot), rk1.at[h, t], kv_s.at[h, t], kv_r.at[h, t], me, j1)
            for t, slot in enumerate((j1, j3))
        ]

    def dk_x(h):
        return remote(dkv(h, j2), rk2.at[h], kv_s.at[h, 2], kv_r.at[h, 2], me, j2)

    def dk_two(h):
        for copy in dk_core(h):
            both(copy)
        for t, slot in enumerate((j, j2)):
            part = dkv(h, slot)
            part[...] = (part[...].astype(F32) + rk1[h, t].astype(F32)).astype(BF)
        dk_x(h).start()

    def dk_three(h):
        both(dk_x(h))
        qnat[h, 0:keys, :] = (dkv(h, j)[...].astype(F32) + rk2[h].astype(F32)).astype(BF)

    def back_head(h, carry):
        tile = kv[h].reshape(4 * keys, 128)
        total = None
        for c in range(tokens // qa):
            cut = slice(c * qa, (c + 1) * qa)
            powers = prob[h, :, cut]
            slopes = nn(tile, qt[h, :, cut]) - delta[h, :, cut]
            ds = (powers.astype(F32) * slopes).astype(BF)
            part = nn(ds, qnat[h, cut, :]) + nn(powers, datn[h, cut, :])
            prob[h, :, cut] = ds
            total = part if total is None else total + part
        gp[0 : 4 * keys, tile_at(h)] = total.astype(BF)
        for copy in dk_core(h):
            copy.start()

        @pl.when(h == 3)
        def _():
            a_four()
            bl_three()

        @pl.when(h >= 1)
        def _():
            dk_two(h - 1)

        return carry

    lax.fori_loop(0, HEADS, back_head, 0)

    dq_t = att_t

    def back_query(h, carry):
        for c in range(tokens // qa):
            cut = slice(c * qa, (c + 1) * qa)
            dq_t[rows(h * HEAD, HEAD), cut] = (
                nn(kvt[h, 0:64, :], prob[h, :, cut]) * HEAD**-0.5
            ).astype(BF)
        return carry

    lax.fori_loop(0, 2, back_query, 0)
    dk_two(HEADS - 1)
    bh_three()
    lax.fori_loop(2, HEADS, back_query, 0)
    bl_four()

    dq = dy

    def flip(c, total):
        low = dq_t[:, across(c)].T
        dq[rows(c * QC, QC), :] = low
        return total + colsum(low.astype(F32))

    vg[4:5, :] = lax.fori_loop(0, chunks, flip, zero_row, unroll=pairs)
    value = nn(dq_t[...], abf[...]).astype(BF)
    other = nn(dbr_t[...], att_n[...]).astype(BF)

    def folded(v, i):
        part = v[:, rb * i : rb * i + rb].reshape(4, 80, rb)
        return [
            part[:, 0:32],
            part[:, 32:64],
            jnp.concatenate([part[:, 64:80], jnp.zeros((4, 16, rb), BF)], axis=1),
        ]

    for i in range(n):
        gm[:, place_of(i), :, 0 : 3 * rb] = jnp.concatenate(folded(value, i), axis=2)
        gm[:, place_of(i), :, mo : mo + 3 * rb] = jnp.concatenate(folded(other, i), axis=2)
    m_one()
    tap_sums(0, 2)
    m_two()
    for h in range(HEADS):
        dk_three(h)

    dm = jnp.concatenate([qnat[h, 0:keys, :] for h in range(HEADS)], axis=1)
    dm_sum = colsum(dm.astype(F32))
    vg[7:8, :] = jnp.concatenate(
        [dm_sum[:, 128 * h + 64 : 128 * h + 128] for h in range(HEADS)], axis=1
    )
    kept = jnp.concatenate([a3[t, 0:keys, :] for t in range(3)], axis=1)[:, 0:D]
    dv, in_gain, in_shift = norm_back(kept, gain(1), nn(dm, wmt[...]))
    vg[1:2, :] = in_gain
    vg[6:7, :] = in_shift
    dred = dv.astype(BF)
    vg[5:6, :] = colsum(dred.astype(F32))
    dred_t = dred.T
    for dd in range(4):
        value = nn(dred_t, pat[dd]).astype(BF)
        count = n // 4
        for ii in range(count):
            i = dd * count + ii
            gt[:, place_of(i), :, 0 : 4 * rb] = value[
                :, 4 * rb * ii : 4 * rb * (ii + 1)
            ].reshape(4, 80, 4 * rb)
    value = nn(dm.T, memin[...]).astype(BF)
    value = jnp.concatenate(
        [value[128 * h : 128 * h + 64] for h in range(HEADS)]
        + [value[128 * h + 64 : 128 * h + 128] for h in range(HEADS)],
        axis=0,
    ).reshape(4, 2, 80, D)
    for i in range(n):
        gt[:, place_of(i), :, 4 * rb : 6 * rb] = jnp.concatenate(
            [value[:, v, :, rb * i : rb * i + rb] for v in range(2)], axis=2
        )
    t_one()

    t_two()

    for dd in range(4):
        back = nn(dred, wrt[dd])
        back = jnp.concatenate([back, jnp.zeros((keys, 64), F32)], axis=1)
        for i in range(band // 2):
            start = (2 * i + dd // 2) * side + dd % 2
            for t in range(3):
                a3[t, pl.ds(start, half, stride=2), :] = back[
                    i * half : (i + 1) * half, 128 * t : 128 * t + 128
                ]

    def back_first(c, carry):
        at = rows(c * QC, QC)
        e = nn(dq[at, :], wqt[...]) + jnp.concatenate([a3[t, at, :] for t in range(3)], axis=1)[:, 0:D]
        value, in_gain, in_shift = norm_back(x_s[at, :].astype(F32), gain(0), e)
        bn[at, :] = (mid[at, :] + value).astype(BF)
        return (carry[0] + in_gain, carry[1] + in_shift)

    sums = lax.fori_loop(0, chunks, back_first, (zero_row, zero_row), unroll=pairs)
    token_out = pltpu.make_async_copy(bn, tgrad_ref, loc.at[12])
    token_out.start()
    vg[0:1, :] = sums[0]
    vg[3:4, :] = sums[1]
    m_three()
    tap_sums(2, FF // 128)
    for i in range(n):
        sv[place_of(i), :, 0 : 4 * rb] = hg[:, 4 * rb * i : 4 * rb * (i + 1)].astype(BF)
        sv[place_of(i), :, 4 * rb : 5 * rb] = vg[:, rb * i : rb * i + rb].astype(BF)

    def v_out(k, peer, source):
        remote(sv.at[spot(peer)], rv1.at[k], gx_s.at[26], gx_r.at[26], peer, j).start()

    peers(v_out)
    tl_three(0)
    tl_three(1)
    bh_four()
    m_four()
    part = rv1.at[pl.ds(1, n - 1)]
    both(remote(part, part, gx_s.at[26], gx_r.at[26], beside, j))
    rv2[j] = lax.fori_loop(
        1, n, lambda k, total: total + rv1[k].astype(F32), sv[here].astype(F32)
    ).astype(BF)

    def v_seq(t, slot, other):
        ref = rv2.at[slot]
        return remote(ref, ref, gx_s.at[30 + t], gx_r.at[30 + t], me, other)

    for t, other in enumerate((j1, j2, j3)):
        v_seq(t, j, other).start()
    th_four()
    a_five()
    bl_five()
    bh_five()
    squares = jnp.sum(own_a[:, 0 : 4 * rb] * own_a[:, 0 : 4 * rb])
    squares += jnp.sum(own_b[:, 0 : 4 * rb] * own_b[:, 0 : 4 * rb])
    th_five()
    m_five()
    for at in (0, mo):
        full = own_m[:, at : at + 2 * rb]
        rest = own_m[0:16, at + 2 * rb : at + 3 * rb]
        squares += jnp.sum(full * full) + jnp.sum(rest * rest)
    tl_five()
    squares += jnp.sum(own_t[:, 0 : 6 * rb] * own_t[:, 0 : 6 * rb])
    for t, other in enumerate((j1, j2, j3)):
        v_seq(t, other, other).wait_send()
        v_seq(t, other, other).wait_recv()
    own_v = (rv2[0].astype(F32) + rv2[1].astype(F32)) + (rv2[2].astype(F32) + rv2[3].astype(F32))
    own_s[80:96, 0:vl] = own_v
    first_band = (j == 0).astype(jnp.int32).astype(F32)
    squares += first_band * jnp.sum(own_v[0:11, 0 : 5 * rb] * own_v[0:11, 0 : 5 * rb])

    nrm[4 * me + j] = jnp.full((1, 128), squares, F32)
    own_out_copy = pltpu.make_async_copy(own_s, own_ref, loc.at[13])
    own_out_copy.start()

    def send_norm(k, carry):
        mine = 4 * me + j
        to = lax.rem(mine + k, 4 * n)
        remote(
            nrm.at[mine], nrm.at[mine], nd_s.at[0], nd_r.at[0], lax.div(to, 4), lax.rem(to, 4)
        ).start()
        return carry

    lax.fori_loop(1, 4 * n, send_norm, 0)
    part = nrm.at[pl.ds(0, 4 * n - 1)]
    both(remote(part, part, nd_s.at[0], nd_r.at[0], beside, j))
    nrm[4 * n] = lax.fori_loop(1, 4 * n, lambda k, total: total + nrm[k], nrm[0])
    norm_out = pltpu.make_async_copy(nrm.at[4 * n], norm_ref, loc.at[14])
    norm_out.start()

    wait_out()
    own_out.wait()
    token_out.wait()
    own_out_copy.wait()
    norm_out.wait()


def update_kernel(rb, tl, al, mo, rates, decays, *refs):
    own_hbm, total_hbm, outt_hbm, tg_hbm = refs[0:4]
    in_hbm = refs[4:31]
    out_hbm, tok_hbm, norm_hbm = refs[31:34]
    new_hbm = refs[34:61]
    own_ref, total_ref, out_v, tok_v, norm_v = refs[61:66]
    in_v, new_v = refs[66:75], refs[75:84]
    in_sem, out_sem = refs[84:86]
    own_load, total_load, out_load, tok_load = [
        pltpu.make_async_copy(src, dst, in_sem.at[9 + at])
        for at, (src, dst) in enumerate(
            ((own_hbm, own_ref), (total_hbm, total_ref), (outt_hbm, out_v), (tg_hbm, tok_v))
        )
    ]
    own_load.start()
    total_load.start()
    for at in range(9):
        for part in range(3):
            pltpu.make_async_copy(in_hbm[at + 9 * part], in_v[at].at[part], in_sem.at[at]).start()
    out_load.start()
    tok_load.start()
    norm_store, out_store, tok_store = [
        pltpu.make_async_copy(src, dst, out_sem.at[9 + at])
        for at, (src, dst) in enumerate(((norm_v, norm_hbm), (out_v, out_hbm), (tok_v, tok_hbm)))
    ]
    own_load.wait()
    total_load.wait()
    total = total_ref[...]
    norm = jnp.sqrt(total)
    norm_v[...] = norm
    norm_store.start()
    clip = jnp.minimum(1.0, MAX_NORM / (norm + 1e-06))[:, 0:1]
    turned_t = own_ref[0:80, 0:tl].T
    turned_a = own_ref[0:80, tl : tl + al].T
    turned_b = own_ref[0:80, tl + al :].T
    turned_q, turned_o = [
        jnp.concatenate(
            [
                own_ref[96:128, at : at + rb],
                own_ref[96:128, at + rb : at + 2 * rb],
                own_ref[96:112, at + 2 * rb : at + 3 * rb],
            ],
            axis=0,
        ).T
        for at in (0, mo)
    ]
    grads = (
        turned_q,
        turned_t[0 : 4 * rb],
        jnp.concatenate([turned_t[(4 + v) * rb : (5 + v) * rb] for v in range(2)], axis=1),
        turned_o,
        jnp.concatenate([turned_b[v * rb : (v + 1) * rb] for v in range(4)], axis=1),
        turned_a[0 : 4 * rb],
        own_ref[80:83, 4 * rb : 5 * rb],
        own_ref[83:91, 4 * rb : 5 * rb],
        own_ref[80:91, 0 : 4 * rb],
    )
    for at in range(9):
        pltpu.make_async_copy(in_v[at], in_v[at], in_sem.at[at]).wait()
        clipped = clip * grads[at]
        weight = in_v[at][0]
        first = BETA_ONE * in_v[at][1] + (1.0 - BETA_ONE) * clipped
        second = BETA_TWO * in_v[at][2] + (1.0 - BETA_TWO) * clipped * clipped
        direction = (
            first
            / (1.0 - BETA_ONE**STEP)
            / (jnp.sqrt(second / (1.0 - BETA_TWO**STEP)) + ADAM_EPS)
        )
        new_v[at][0] = weight - rates[at] * (direction + decays[at] * weight)
        new_v[at][1] = first
        new_v[at][2] = second
        for part in range(3):
            pltpu.make_async_copy(
                new_v[at].at[part], new_hbm[at + 9 * part], out_sem.at[at]
            ).start()
    out_load.wait()
    out_store.start()
    tok_load.wait()
    tok_store.start()
    for at in range(9):
        pltpu.make_async_copy(new_v[at], new_v[at], out_sem.at[at]).wait()
    for store in (norm_store, out_store, tok_store):
        store.wait()


def on_device(n, *args):
    tokens, buckets, cotangent = args[0:3]
    weights, firsts, seconds = args[3:12], args[12:21], args[21:30]
    band, side, width = tokens.shape[1:4]
    count = band * side
    keys = count // 4
    rb = weights[0].shape[0]
    piece = cotangent.shape[3]
    wide = up(9 * rb, 128)
    tl = up(6 * rb, 128)
    al = up(4 * rb, 128)
    bl = up(4 * rb, 128)
    ml = up(6 * rb, 128)
    h = n // 2
    vl = up(5 * rb, 128)
    total = tl + al + bl
    qa = count if n <= 8 else 128
    turned = piece % 128 == 0
    block = (n, D, piece) if turned else (n, piece, D)
    vm = pltpu.VMEM
    dma = pltpu.SemaphoreType.DMA
    def landing(height, lanes, cut, direct):
        rest = height - cut
        count = n if direct else h
        shapes = (
            (2, n, height, lanes),
            (n, cut, lanes),
            (0 if direct else h, cut, lanes),
            (count, cut, lanes),
            (0 if direct else 2, h, rest, lanes),
            (2, count, rest, lanes),
            (rest, lanes),
        )
        return [vm(shape if 0 not in shape else (8, 128), BF) for shape in shapes]

    scratch = [
        vm((count, D), BF),
        *[vm(weights[at].shape, F32) for at in range(9)],
        vm((n, 16, vl), BF),
        vm((4, n, 80, tl), BF),
        vm((4, n, 32, ml), BF),
        vm((4, n, 80, wide), BF),
        vm((16, D), F32),
        vm((16, FF), F32),
        vm((D, D), BF),
        vm((D, D), BF),
        vm((2 * D, D), BF),
        vm((2 * D, D), BF),
        vm((4, D, D), BF),
        vm((FF, D), BF),
        vm((D, FF), BF),
        vm((3, count, 128), F32),
        vm((count, D), BF),
        vm((4, keys, D), BF),
        vm((keys, D), BF),
        vm((HEADS, 4, keys, 128), BF),
        vm((HEADS, 128, 4 * keys), BF),
        vm((HEADS, count, 128), BF),
        vm((HEADS, 128, count), BF),
        vm((HEADS, 4 * keys, count), BF),
        vm((D, count), BF),
        vm((count, D), BF),
        vm((HEADS, 1, count), F32),
        vm((HEADS, 1, count), F32),
        vm((count, D), F32),
        vm((count, D), BF),
        vm((count + 2 * side, FF), BF),
        vm((2, side, FF), BF),
        vm((count + 2 * side, FF), BF),
        vm((count, FF), BF),
        vm(block, BF),
        vm(block if turned else (8, 128), BF),
        vm((D, count), BF),
        vm((count, D), BF),
        vm((2, side, FF), BF),
        vm((HEADS, count, 128), BF),
        vm((HEADS, 2, keys, 128), BF),
        vm((HEADS, keys, 128), BF),
        vm((16, FF), F32),
        vm((16, D), F32),
        vm((128, total), F32),
        vm((4, n, 80, bl), BF),
        *landing(80, al, 80, False),
        *landing(80, bl, 32, False),
        *landing(80, tl, CUT, True),
        *landing(32, ml, 32, False),
        vm((n, 16, vl), BF),
        vm((n, 16, vl), BF),
        vm((4, 16, vl), BF),
        vm((4 * n + 1, 1, 128), F32),
        vm((side, 2 * side), BF),
        vm((side, 2 * side), BF),
        vm((2 * side, side), BF),
        dma((15,)),
        dma((n,)),
        dma((2, h)),
        *[dma((39,)) for _ in range(2)],
        *[dma((1,)) for _ in range(4)],
        *[dma((HEADS, 3)) for _ in range(2)],
        *[dma((4,)) for _ in range(2)],
        *[dma((1,)) for _ in range(2)],
    ]
    anywhere = pl.BlockSpec(memory_space=pl.ANY)
    out_t, token_grad, own, total_squares = pl.pallas_call(
        functools.partial(block_kernel, n, side, band, qa),
        out_shape=(
            jax.ShapeDtypeStruct(block, BF),
            jax.ShapeDtypeStruct((count, D), BF),
            jax.ShapeDtypeStruct((128, total), F32),
            jax.ShapeDtypeStruct((1, 128), F32),
        ),
        in_specs=[pl.BlockSpec(memory_space=pltpu.SMEM)] + [anywhere] * 11,
        out_specs=(anywhere,) * 4,
        scratch_shapes=scratch,
        compiler_params=pltpu.CompilerParams(
            collective_id=0, has_side_effects=True, vmem_limit_bytes=VMEM_LIMIT
        ),
    )(
        buckets,
        tokens.reshape(count, width),
        jnp.swapaxes(cotangent, 3, 4).reshape(block) if turned else cotangent.reshape(block),
        *weights,
    )
    rates = (
        D ** (-0.5),
        (4 * D) ** (-0.5),
        D ** (-0.5),
        OUT_FAN ** (-0.5),
        D ** (-0.5),
        FF ** (-0.5),
        GAIN_RATE,
        VECTOR_RATE,
        VECTOR_RATE,
    )
    decays = (DECAY_RATE,) * 6 + (0.0,) * 3
    shapes = tuple(jax.ShapeDtypeStruct(w.shape, F32) for w in weights)
    results = pl.pallas_call(
        functools.partial(
            update_kernel, rb, tl, al, 128 if ml > 128 else 3 * rb, rates, decays
        ),
        out_shape=(
            jax.ShapeDtypeStruct(block, BF),
            jax.ShapeDtypeStruct((count, D), BF),
            jax.ShapeDtypeStruct((1, 128), F32),
        )
        + shapes * 3,
        in_specs=[anywhere] * 31,
        out_specs=(anywhere,) * 30,
        scratch_shapes=[
            vm((128, total), F32),
            vm((1, 128), F32),
            vm(block, BF),
            vm((count, D), BF),
            vm((1, 128), F32),
            *[vm((3, *w.shape), F32) for w in weights * 2],
            dma((13,)),
            dma((12,)),
        ],
    )(own, total_squares, out_t, token_grad, *weights, *firsts, *seconds)
    if turned:
        block_output = jnp.swapaxes(results[0].reshape(n, 1, 1, width, piece), 3, 4)
    else:
        block_output = results[0].reshape(n, 1, 1, piece, width)
    return (
        block_output,
        results[1].reshape(1, band, side, width),
        results[2][0, 0],
        *results[3:],
    )


def solution(mesh):
    matrix = (P("dp", "seq"),) * 6 + (P(None, "dp"),) * 3
    return jax.shard_map(
        functools.partial(on_device, mesh.shape["dp"]),
        mesh=mesh,
        in_specs=(
            P("dp", "seq", None, None),
            P("dp"),
            P(None, "seq", "dp", None, None),
            *(matrix * 3),
        ),
        out_specs=(
            P(None, "seq", "dp", None, None),
            P("dp", "seq", None, None),
            P(),
            *(matrix * 3),
        ),
        check_vma=False,
    )
```

```python
import functools

import jax
import jax.numpy as jnp
from jax import lax
from jax.experimental import pallas as pl
from jax.experimental.pallas import tpu as pltpu
from jax.sharding import PartitionSpec as P

D = 320
HEADS = 5
HEAD = 64
FF = 1280
STEP = 10
OUT_FAN = 5

NORM_EPS = 1e-06
MAX_NORM = 1.0
BETA_ONE = 0.9
BETA_TWO = 0.95
ADAM_EPS = 1e-08
DECAY_RATE = 0.01
VECTOR_RATE = 0.3
GAIN_RATE = 0.8
MASKED = -1e30

BF = jnp.bfloat16
F32 = jnp.float32
MESH = pl.DeviceIdType.MESH
QC = 512
GATHER_CUT = 32
CUT = 48
VMEM_LIMIT = 63 * 1024 * 1024


def nn(a, b):
    return lax.dot_general(a, b, (((1,), (0,)), ((), ())), preferred_element_type=F32)


def nt(a, b):
    return lax.dot_general(a, b, (((1,), (1,)), ((), ())), preferred_element_type=F32)


def up(n, m):
    return (n + m - 1) // m * m


def norm_parts(v):
    centered = v - jnp.mean(v, axis=-1, keepdims=True)
    rstd = lax.rsqrt(jnp.mean(centered * centered, axis=-1, keepdims=True) + NORM_EPS)
    return centered * rstd, rstd


def norm_back(v, gain, e):
    vhat, rstd = norm_parts(v)
    u = e * gain
    dv = rstd * (
        u
        - jnp.mean(u, axis=-1, keepdims=True)
        - vhat * jnp.mean(u * vhat, axis=-1, keepdims=True)
    )
    return dv, jnp.sum(e * vhat, axis=0, keepdims=True), jnp.sum(e, axis=0, keepdims=True)


def colsum(v):
    return jnp.sum(v, axis=0, keepdims=True)


def rows(start, size):
    return pl.ds(pl.multiple_of(start, 16), size)


def block_kernel(
    n,
    side,
    band,
    qa,
    bucket_ref,
    tok_ref,
    cot_ref,
    wq_ref,
    wr_ref,
    wm_ref,
    wo_ref,
    w1_ref,
    w2_ref,
    gains_ref,
    biases_ref,
    hidden_ref,
    out_ref,
    tgrad_ref,
    own_ref,
    norm_ref,
    x_s,
    fq,
    fr,
    fm,
    fo,
    f1,
    f2,
    fg,
    fb,
    fh,
    gvec,
    gt,
    gm,
    gf,
    vp,
    hp,
    wqt,
    wot,
    wop,
    wmt,
    wrt,
    w1t,
    w2t,
    a3,
    abf,
    pat,
    memin,
    kv,
    kvt,
    qnat,
    qt,
    prob,
    att_t,
    att_n,
    rtot,
    delta,
    mid,
    bn,
    hidp,
    hidh,
    act,
    gp,
    out_t,
    dy_in,
    dy_t,
    dy,
    dzh,
    datn,
    rk1,
    rk2,
    hg,
    vg,
    own_s,
    sb,
    ra0,
    ra1,
    ra2,
    ra3,
    ra4,
    ra5,
    ra6,
    rb0,
    rb1,
    rb2,
    rb3,
    rb4,
    rb5,
    rb6,
    rt0,
    rt1,
    rt2,
    rt3,
    rt4,
    rt5,
    rt6,
    rm0,
    rm1,
    rm2,
    rm3,
    rm4,
    rm5,
    rm6,
    sv,
    rv1,
    rv2,
    nrm,
    shift_f,
    shift_b,
    shift_m,
    loc,
    tl_r,
    th_r,
    gx_s,
    gx_r,
    co_s,
    co_r,
    ou_s,
    ou_r,
    kv_s,
    kv_r,
    ha_s,
    ha_r,
    nd_s,
    nd_r,
):
    me = lax.axis_index("dp")
    j = lax.axis_index("seq")
    y0 = lax.rem(me, 2)
    y1 = 1 - y0
    z0 = lax.div(me, 2)
    beside = me + 1 - 2 * y0
    zn = n // 2
    here = y0 * zn + z0

    def place_of(i):
        return i % 2 * zn + i // 2

    def spot(i):
        return lax.rem(i, 2) * zn + lax.div(i, 2)

    j1 = j + 1 - 2 * lax.rem(j, 2)
    j2 = lax.rem(j + 2, 4)
    j3 = 3 - j
    tokens = band * side
    chunks = tokens // QC
    deep = band if qa == tokens else 4
    pairs = 2 if qa == tokens else 1
    rb = wq_ref.shape[0]
    piece = tokens // n
    keys = kv.shape[2]
    turned = cot_ref.shape[1] == D
    tl = gt.shape[3]
    fl = gf.shape[3]
    vl = gvec.shape[2]
    al = up(4 * rb, 128)
    bl = sb.shape[3]
    ml = gm.shape[3]
    mo = 128 if ml > 128 else 3 * rb

    def remote(src, dst, ss, rs, dp, seq):
        return pltpu.make_async_remote_copy(
            src_ref=src,
            dst_ref=dst,
            send_sem=ss,
            recv_sem=rs,
            device_id=(dp, seq),
            device_id_type=MESH,
        )

    def both(copy):
        copy.wait_send()
        copy.wait_recv()

    def peers(body):
        def step(k, carry):
            body(k, lax.rem(me + k, n), lax.rem(me + n - k, n))
            return carry

        lax.fori_loop(1, n, step, 0)

    def z_peers(body):
        def step(k, carry):
            body(k, lax.rem(me + 2 * k, n), lax.rem(z0 + k, zn), lax.rem(z0 + zn - k, zn))
            return carry

        lax.fori_loop(1, zn, step, 0)

    loads = [
        pltpu.make_async_copy(src, dst, loc.at[at])
        for at, (src, dst) in enumerate(
            (
                (gains_ref, fg),
                (biases_ref, fb),
                (hidden_ref, fh),
                (wr_ref, fr),
                (wm_ref, fm),
                (wq_ref, fq),
                (wo_ref, fo),
                (w1_ref, f1),
                (w2_ref, f2),
                (tok_ref, x_s),
            )
        )
    ]
    for copy in loads:
        copy.start()
    def incoming(i):
        return dy_in.at[i] if turned else dy.at[rows(i * piece, piece)]

    own_cot = pltpu.make_async_copy(cot_ref.at[me], incoming(me), loc.at[10])
    own_cot.start()

    barrier = pltpu.get_barrier_semaphore()

    def greet(k, carry):
        to = lax.rem(4 * me + j + k, 4 * n)
        pl.semaphore_signal(
            barrier, inc=1, device_id=(lax.div(to, 4), lax.rem(to, 4)), device_id_type=MESH
        )
        return carry

    lax.fori_loop(1, 4 * n, greet, 0)

    for copy in loads[:5]:
        copy.wait()
    hidden16 = jnp.concatenate([fh[...], jnp.zeros((5, 4 * rb), F32)], axis=0)
    small16 = jnp.concatenate([fg[...], fb[...], jnp.zeros((5, rb), F32)], axis=0)
    gvec[here] = jnp.concatenate(
        [hidden16, small16, jnp.zeros((16, vl - 5 * rb), F32)], axis=1
    ).astype(BF)
    wm_t = fm[...].T
    gt[j, here] = jnp.concatenate(
        [fr[...].T, wm_t[0:80], wm_t[80:160], jnp.zeros((80, tl - 6 * rb), F32)], axis=1
    ).astype(BF)

    def group(at, one_of, all_but_one, each):
        def start():
            def send(peer):
                ref = one_of(here)
                remote(ref, ref, gx_s.at[14 + at], gx_r.at[14 + at], peer, j).start()

            each(send)

        def wait():
            both(remote(all_but_one, all_but_one, gx_s.at[14 + at], gx_r.at[14 + at], beside, j))

        return start, wait

    def each_peer(send):
        peers(lambda k, peer, source: send(peer))

    def each_z(send):
        z_peers(lambda k, peer, to, source: send(peer))

    def over_dp(at, buf, rows_of):
        return group(
            at, lambda i: buf.at[i, rows_of], buf.at[pl.ds(0, n - 1), rows_of], each_peer
        )

    def over_z(at, buf, rows_of):
        return group(
            at, lambda i: buf.at[i, rows_of], buf.at[pl.ds(0, zn - 1), rows_of], each_z
        )

    def swap(at, mine, theirs, dp, seq):
        def start():
            remote(mine, mine, gx_s.at[at], gx_r.at[at], dp, seq).start()

        def wait():
            remote(mine, mine, gx_s.at[at], gx_r.at[at], dp, seq).wait_send()
            remote(theirs, theirs, gx_s.at[at], gx_r.at[at], dp, seq).wait_recv()

        return start, wait

    def over_y(at, buf, rows_of):
        mine = buf.at[pl.ds(y0 * zn, zn), rows_of]
        theirs = buf.at[pl.ds(y1 * zn, zn), rows_of]
        return swap(at, mine, theirs, beside, j)

    lower = slice(0, GATHER_CUT)
    upper = slice(GATHER_CUT, 80)
    every = slice(0, 16)
    v_dp, v_dp_wait = over_dp(0, gvec, every)

    def t_low(i):
        return gt.at[j, i, lower]

    def t_low_copy(k, i, peer):
        return remote(t_low(i), t_low(i), gx_s.at[15], tl_r.at[k], peer, j)

    def t_low_on(i):
        remote(t_low(i), t_low(i), gx_s.at[0], gx_r.at[0], me, j2).start()

    def t_low_start():
        t_low_on(here)
        peers(lambda k, peer, source: t_low_copy(k, here, peer).start())

    def t_low_forward():
        def body(k, peer, source):
            t_low_copy(k, spot(source), peer).wait_recv()
            t_low_on(spot(source))

        peers(body)

    def t_low_wait():
        part = gt.at[j, pl.ds(0, n - 1), lower]
        remote(part, part, gx_s.at[15], tl_r.at[0], beside, j).wait_send()
        both(remote(gt.at[j, :, lower], gt.at[j2, :, lower], gx_s.at[0], gx_r.at[0], me, j2))

    t_x0, t_x0_wait = swap(1, gt.at[j, here, upper], gt.at[j2, here, upper], me, j2)

    def t_high(slot, t):
        def ref(i):
            return gt.at[slot, i, upper]

        def copy(k, i, peer):
            return remote(ref(i), ref(i), gx_s.at[16 + t], th_r.at[t, k], peer, j)

        def on(i):
            remote(ref(i), ref(i), gx_s.at[2 + t], gx_r.at[2 + t], beside, j).start()

        def start():
            z_peers(lambda k, peer, to, source: copy(k, here, peer).start())
            on(here)

        def forward():
            def body(k, peer, to, source):
                copy(k, y0 * zn + source, peer).wait_recv()
                on(y0 * zn + source)

            z_peers(body)

        def wait():
            part = gt.at[slot, pl.ds(0, zn - 1), upper]
            remote(part, part, gx_s.at[16 + t], th_r.at[t, 0], beside, j).wait_send()
            mine = gt.at[slot, pl.ds(y0 * zn, zn), upper]
            theirs = gt.at[slot, pl.ds(y1 * zn, zn), upper]
            both(remote(mine, theirs, gx_s.at[2 + t], gx_r.at[2 + t], beside, j))

        return start, forward, wait

    t_za, t_za_forward, t_ya_wait = t_high(j, 0)
    t_zb, t_zb_forward, t_yb_wait = t_high(j2, 1)
    t_ca, t_ca_wait = swap(4, gt.at[j], gt.at[j1], me, j1)
    t_cb, t_cb_wait = swap(5, gt.at[j2], gt.at[j3], me, j1)
    wq_block = gm.at[:, :, :, 0:128]
    m_dp, m_dp_wait = over_dp(4, wq_block.at[j], slice(0, 32))
    m_x, m_x_wait = swap(6, wq_block.at[j], wq_block.at[j2], me, j2)
    m_ca, m_ca_wait = swap(7, wq_block.at[j], wq_block.at[j1], me, j1)
    m_cb, m_cb_wait = swap(8, wq_block.at[j2], wq_block.at[j3], me, j1)
    f_x0, f_x0_wait = swap(9, gf.at[j, here], gf.at[j2, here], me, j2)
    fl_za, fl_za_wait = over_z(5, gf.at[j], lower)
    fl_zb, fl_zb_wait = over_z(6, gf.at[j2], lower)
    fh_a, fh_a_wait = over_dp(7, gf.at[j], upper)
    fh_b, fh_b_wait = over_dp(8, gf.at[j2], upper)
    fl_ya, fl_ya_wait = over_y(10, gf.at[j], lower)
    fl_yb, fl_yb_wait = over_y(11, gf.at[j2], lower)
    fl_ca, fl_ca_wait = swap(12, gf.at[j, :, lower], gf.at[j1, :, lower], me, j1)
    fl_cb, fl_cb_wait = swap(13, gf.at[j2, :, lower], gf.at[j3, :, lower], me, j1)
    fh_ca, fh_ca_wait = swap(34, gf.at[j, :, upper], gf.at[j1, :, upper], me, j1)
    fh_cb, fh_cb_wait = swap(35, gf.at[j2, :, upper], gf.at[j3, :, upper], me, j1)

    pl.semaphore_wait(barrier, 4 * n - 1)
    t_x0()
    t_za()
    t_low_start()

    for copy in loads[5:9]:
        copy.wait()
    wq_t = fq[...].T
    gm[j, here, :, 0:128] = jnp.concatenate(
        [
            wq_t[0:32],
            wq_t[32:64],
            jnp.concatenate([wq_t[64:80], jnp.zeros((16, rb), F32)], axis=0),
            jnp.zeros((32, 128 - 3 * rb), F32),
        ],
        axis=1,
    ).astype(BF)
    w1_t = f1[...].T
    gf[j, here] = jnp.concatenate(
        [f2[...].T]
        + [w1_t[80 * v : 80 * v + 80] for v in range(4)]
        + [fo[...].T, jnp.zeros((80, fl - 9 * rb), F32)],
        axis=1,
    ).astype(BF)
    t_x0_wait()
    t_zb()
    v_dp()

    t_low_forward()
    m_dp()
    f_x0()
    t_za_forward()
    t_zb_forward()
    f_x0_wait()
    fl_za()
    fl_zb()
    v_dp_wait()
    hp[...] = jnp.concatenate([gvec[place_of(i), :, 0 : 4 * rb] for i in range(n)], axis=1).astype(F32)
    vp[...] = jnp.concatenate(
        [gvec[place_of(i), :, 4 * rb : 5 * rb] for i in range(n)], axis=1
    ).astype(F32)

    def gain(k):
        return vp[k : k + 1, :]

    def shift(k):
        return vp[3 + k : 4 + k, :]

    loads[9].wait()

    def norm_one(c, carry):
        at = rows(c * QC, QC)
        vhat, _ = norm_parts(x_s[at, :].astype(F32))
        low = (vhat * gain(0) + shift(0)).astype(BF)
        abf[at, :] = low
        wide = jnp.concatenate([low.astype(F32), jnp.zeros((QC, 64), F32)], axis=1)
        for t in range(3):
            a3[t, at, :] = wide[:, 128 * t : 128 * t + 128]
        return carry

    lax.fori_loop(0, chunks, norm_one, 0, unroll=pairs)
    half = side // 2
    for dd in range(4):
        for i in range(band // 2):
            start = (2 * i + dd // 2) * side + dd % 2
            cut = jnp.concatenate(
                [a3[t, pl.ds(start, half, stride=2), :] for t in range(3)], axis=1
            )
            pat[dd, i * half : (i + 1) * half, :] = cut[:, 0:D].astype(BF)

    bucket = bucket_ref[0]
    k_row = lax.broadcasted_iota(jnp.int32, (4 * keys, 128), 0)
    k_lane = lax.broadcasted_iota(jnp.int32, (4 * keys, 128), 1)
    k_id = (lax.div(k_row, half) >= half // 2).astype(jnp.int32) * 2 + (
        lax.rem(k_row, half) >= half // 2
    ).astype(jnp.int32)
    off = (k_id != k_lane).astype(jnp.int32) * bucket * (k_lane < 4).astype(jnp.int32)
    kmask = datn.at[0]
    qmask = dy_t.at[0:128]
    kmask[...] = (off.astype(F32) * MASKED).astype(BF)
    q_row = lax.broadcasted_iota(jnp.int32, (128, tokens), 0)
    place = lax.broadcasted_iota(jnp.int32, (128, tokens), 1)
    q_id = (lax.div(place, side) + j * band >= half).astype(jnp.int32) * 2 + (
        lax.rem(place, side) >= half
    ).astype(jnp.int32)
    qmask[...] = (q_id == q_row).astype(F32).astype(BF)
    col = lax.broadcasted_iota(jnp.int32, (side, side), 0)
    ok_l = (col > 0).astype(jnp.int32) * (1 - bucket * (col == half).astype(jnp.int32))
    ok_r = (col < side - 1).astype(jnp.int32) * (
        1 - bucket * (col == half - 1).astype(jnp.int32)
    )
    lane = lax.broadcasted_iota(jnp.int32, (side, side), 1)
    from_l = (ok_l * (lane == col - 1).astype(jnp.int32)).astype(F32).astype(BF)
    from_r = (ok_r * (lane == col + 1).astype(jnp.int32)).astype(F32).astype(BF)
    shift_f[...] = jnp.concatenate([from_l, from_r], axis=1)
    shift_b[...] = jnp.concatenate([from_r, from_l], axis=1)
    shift_m[...] = jnp.concatenate([from_r, from_l], axis=0)
    top_ok = (
        (j > 0).astype(jnp.int32) * (1 - bucket * (j * band == half).astype(jnp.int32))
    ).astype(F32)
    low_ok = (
        (j < 3).astype(jnp.int32) * (1 - bucket * ((j + 1) * band == half).astype(jnp.int32))
    ).astype(F32)

    t_ya_wait()
    t_yb_wait()
    t_low_wait()
    t_ca()
    t_cb()
    m_dp_wait()
    m_x()
    t_ca_wait()
    t_cb_wait()

    fh_a()
    fh_b()

    for s in range(4):
        span = slice(80 * s, 80 * s + 80)

        def lanes(lo, hi, over):
            return jnp.concatenate([gt[s, place_of(i), :, lo:hi] for i in over], axis=1)

        for dd in range(4):
            wrt[dd, span, :] = lanes(0, 4 * rb, range(dd * n // 4, (dd + 1) * n // 4))
        for v in range(2):
            wop[160 * s + 80 * v : 160 * s + 80 * v + 80, :] = lanes(
                (4 + v) * rb, (5 + v) * rb, range(n)
            )
    for h in range(HEADS):
        wmt[128 * h : 128 * h + 64, :] = wop[HEAD * h : HEAD * h + HEAD, :]
        wmt[128 * h + 64 : 128 * h + 128, :] = wop[D + HEAD * h : D + HEAD * h + HEAD, :]

    red = shift(2) + nt(pat[0], wrt[0])
    for dd in range(1, 4):
        red = red + nt(pat[dd], wrt[dd])
    wide_red = jnp.concatenate([red, jnp.zeros((keys, 64), F32)], axis=1)
    for t in range(3):
        a3[t, 0:keys, :] = wide_red[:, 128 * t : 128 * t + 128]
    vhat, _ = norm_parts(red)
    low = (vhat * gain(1) + shift(3)).astype(BF)
    memin[...] = low
    zero64 = jnp.zeros((1, HEAD), F32)
    value_shift = jnp.concatenate(
        [
            part
            for h in range(HEADS)
            for part in (zero64, shift(4)[:, HEAD * h : HEAD * h + HEAD])
        ],
        axis=1,
    )
    memory = (nt(low, wmt[...]) + value_shift).astype(BF)
    for h in range(HEADS):
        kv[h, j] = memory[:, 128 * h : 128 * h + 128]

    def kv_copy(h, slot, t, other):
        return remote(
            kv.at[h, slot], kv.at[h, slot], kv_s.at[h, t], kv_r.at[h, t], me, other
        )

    def kv_send(h, carry):
        kv_copy(h, j, 0, j2).start()
        kv_copy(h, j, 1, j1).start()
        return carry

    lax.fori_loop(0, 2, kv_send, 0)

    m_x_wait()
    m_ca()
    m_cb()
    wqp = wop
    m_ca_wait()
    m_cb_wait()
    for s in range(4):
        at = 80 * s
        wqt[at : at + 32, :] = jnp.concatenate([gm[s, place_of(i), :, 0:rb] for i in range(n)], axis=1)
        wqt[at + 32 : at + 64, :] = jnp.concatenate(
            [gm[s, place_of(i), :, rb : 2 * rb] for i in range(n)], axis=1
        )
        wqt[at + 64 : at + 80, :] = jnp.concatenate(
            [gm[s, place_of(i), 0:16, 2 * rb : 3 * rb] for i in range(n)], axis=1
        )
    for h in range(HEADS):
        wqp[128 * h : 128 * h + 64, :] = wqt[HEAD * h : HEAD * h + HEAD, :]
        wqp[128 * h + 64 : 128 * h + 128, :] = jnp.zeros((64, D), BF)

    query_shift = jnp.concatenate(
        [
            part
            for h in range(HEADS)
            for part in (shift(1)[:, HEAD * h : HEAD * h + HEAD], zero64)
        ],
        axis=1,
    )

    def across(c):
        return pl.ds(pl.multiple_of(c * QC, QC), QC)

    def queries(c, carry):
        at = rows(c * QC, QC)
        q = (nt(abf[at, :], wqp[...]) + query_shift).astype(BF) * jnp.asarray(HEAD**-0.5, BF)
        for h in range(HEADS):
            tile = q[:, 128 * h : 128 * h + 128]
            qnat[h, at, :] = tile
            qt[h, :, across(c)] = tile.T
        return carry

    lax.fori_loop(0, chunks, queries, 0, unroll=pairs)
    lax.fori_loop(2, HEADS, kv_send, 0)

    def send_cot(k, peer, source):
        remote(cot_ref.at[peer], incoming(me), co_s.at[0], co_r.at[0], peer, j).start()

    def wait_cot():
        part = cot_ref.at[pl.ds(0, n - 1)]
        both(remote(part, part, co_s.at[0], co_r.at[0], beside, j))

    def kv_forward(h):
        kv_copy(h, j2, 0, j2).wait_recv()
        kv_copy(h, j2, 2, j1).start()

    fl_za_wait()
    fl_zb_wait()
    fl_ya()
    fl_yb()
    kv_forward(0)

    def attend(h, carry):
        kv_copy(h, j, 0, j2).wait_send()
        kv_copy(h, j, 1, j1).wait_send()
        kv_copy(h, j2, 2, j1).wait_send()
        kv_copy(h, j1, 1, j1).wait_recv()
        kv_copy(h, j3, 2, j1).wait_recv()
        tile = kv[h].reshape(4 * keys, 128)
        kvt[h] = tile.T
        left = jnp.concatenate([tile, kmask[...]], axis=1)
        values = jnp.concatenate([kvt[h, 64:128, :], jnp.ones((16, 4 * keys), BF)], axis=0)
        for c in range(tokens // qa):
            cut = slice(c * qa, (c + 1) * qa)
            scores = nn(left, jnp.concatenate([qt[h, :, cut], qmask[:, cut]], axis=0))
            if c == 0:

                @pl.when(h < HEADS - 1)
                def _():
                    kv_forward(h + 1)

                @pl.when(h == 3)
                def _():
                    peers(send_cot)

                @pl.when(h == HEADS - 2)
                def _():
                    fl_ya_wait()
                    fl_yb_wait()
                    fl_ca()
                    fl_cb()

                @pl.when(h == HEADS - 1)
                def _():
                    fh_a_wait()
                    fh_b_wait()
                    fh_ca()
                    fh_cb()

            largest = jnp.max(scores, axis=0, keepdims=True)
            powers = jnp.exp(scores - largest).astype(BF)
            prob[h, :, cut] = powers
            got = nn(values, powers)
            scale = 1.0 / got[64:65, :]
            rtot[h, :, cut] = scale
            att_t[rows(h * HEAD, HEAD), cut] = (got[0:64, :] * scale).astype(BF)
        return carry

    lax.fori_loop(0, HEADS, attend, 0)

    fl_ca_wait()
    fl_cb_wait()

    def unpack_rows(part, lo, hi):
        for s in range(4):
            span = slice(80 * s + lo, 80 * s + hi)

            def lanes(at, width):
                return jnp.concatenate(
                    [gf[s, place_of(i), part, at : at + width] for i in range(n)], axis=1
                )

            w2t[span, :] = lanes(0, 4 * rb)
            for v in range(4):
                at = 320 * s + 80 * v
                w1t[at + lo : at + hi, :] = lanes((4 + v) * rb, rb)
            wot[span, :] = lanes(8 * rb, rb)

    unpack_rows(lower, 0, GATHER_CUT)
    fh_ca_wait()
    fh_cb_wait()
    unpack_rows(upper, GATHER_CUT, 80)
    wop_full = wot[...].T
    for h in range(HEADS):
        wop[128 * h : 128 * h + 64, :] = jnp.zeros((64, D), BF)
        wop[128 * h + 64 : 128 * h + 128, :] = wop_full[HEAD * h : HEAD * h + HEAD, :]

    def middle(c, carry):
        at = rows(c * QC, QC)
        att = att_t[:, across(c)].T
        att_n[at, :] = att
        value = x_s[at, :].astype(F32) + nt(att, wot[...]) + shift(5)
        mid[at, :] = value
        vhat, _ = norm_parts(value)
        low = (vhat * gain(2) + shift(6)).astype(BF)
        bn[at, :] = low
        return carry

    lax.fori_loop(0, chunks, middle, 0, unroll=pairs)

    edge = tokens - side

    def hidden_of(value):
        return (nt(value, w1t[...]) + hp[9:10, :]).astype(BF)

    ends = hidden_of(jnp.concatenate([bn[0:side, :], bn[edge:tokens, :]], axis=0))
    hidp[side : 2 * side, :] = ends[0:side]
    hidp[tokens : tokens + side, :] = ends[side : 2 * side]
    above = lax.rem(j + 3, 4)
    below = lax.rem(j + 1, 4)

    def rim_up(buf, halo, at):
        return remote(buf.at[pl.ds(side, side)], halo.at[1], ha_s.at[at], ha_r.at[at], me, above)

    def rim_down(buf, halo, at):
        return remote(
            buf.at[pl.ds(tokens, side)], halo.at[0], ha_s.at[at + 1], ha_r.at[at + 1], me, below
        )

    def rim_send(buf, halo, at):
        @pl.when(j > 0)
        def _():
            rim_up(buf, halo, at).start()

        @pl.when(j < 3)
        def _():
            rim_down(buf, halo, at).start()

    def rim_wait(buf, halo, at):
        @pl.when(j > 0)
        def _():
            rim_up(buf, halo, at).wait_send()
            rim_down(buf, halo, at).wait_recv()

        @pl.when(j < 3)
        def _():
            rim_down(buf, halo, at).wait_send()
            rim_up(buf, halo, at).wait_recv()

        for t, (to, ok) in enumerate(((0, top_ok), (tokens + side, low_ok))):
            seen = jnp.full((side, FF), ok, F32) > 0.5
            buf[to : to + side, :] = jnp.where(seen, halo[t].astype(F32), 0.0).astype(BF)

    rim_send(hidp, hidh, 0)

    inner = (tokens - 2 * side) // 2

    def inner_hidden(c, carry):
        start = side + c * inner
        hidp[rows(start + side, inner), :] = hidden_of(bn[rows(start, inner), :])
        return carry

    lax.fori_loop(0, 2, inner_hidden, 0, unroll=pairs)

    def tile_at(t):
        return pl.ds(pl.multiple_of(t * 128, 128), 128)

    def taps_of(lanes):
        return [hp[k : k + 1, lanes] for k in range(9)]

    def conv_over(lo, hi, step, tiles):
        def conv_tile(t, carry):
            lanes = tile_at(t)
            taps = taps_of(lanes)
            base = hp[10:11, lanes]

            def row(at, inner):
                r = lo + at * step
                around = [hidp[rows((r + a) * side, side), lanes].astype(F32) for a in range(3)]
                parts = [
                    taps[b] * around[0] + taps[3 + b] * around[1] + taps[6 + b] * around[2]
                    for b in range(3)
                ]
                moved = jnp.concatenate([parts[0].astype(BF), parts[2].astype(BF)], axis=0)
                z = base + parts[1] + nn(shift_f[...], moved)
                root = z * (0.5**0.5)
                cdf = 0.5 + 0.5 * lax.erf(root)
                slope = (z * 0.3989422804014327) * jnp.exp2(root * root * -1.4426950408889634)
                act[rows((r + 1) * side, side), lanes] = (z * cdf).astype(BF)
                gp[rows(r * side, side), lanes] = (cdf + slope).astype(BF)
                return inner

            lax.fori_loop(0, (hi - lo) // step, row, 0, unroll=True)
            return carry

        lax.fori_loop(0, FF // 128, conv_tile, 0, unroll=tiles)

    conv_over(1, band - 1, 1, 1)
    rim_wait(hidp, hidh, 0)
    conv_over(0, 2 * (band - 1), band - 1, 5)

    def out_chunk(c, carry):
        at = rows(c * QC, QC)
        value = mid[at, :] + nt(act[rows(side + c * QC, QC), :], w2t[...]) + shift(7)
        for p in range(QC // piece):
            part = value[p * piece : (p + 1) * piece, :]
            out_t[c * (QC // piece) + p] = (part.T if turned else part).astype(BF)
        return carry

    lax.fori_loop(0, chunks, out_chunk, 0, unroll=pairs)

    def send_out(k, peer, source):
        remote(out_t.at[peer], out_ref.at[me], ou_s.at[0], ou_r.at[0], peer, j).start()

    def wait_out():
        part = out_t.at[pl.ds(0, n - 1)]
        both(remote(part, part, ou_s.at[0], ou_r.at[0], beside, j))

    peers(send_out)
    own_out = pltpu.make_async_copy(out_t.at[me], out_ref.at[me], loc.at[11])
    own_out.start()

    own_cot.wait()
    wait_cot()
    for i in range(n):
        if turned:
            dy_t[:, i * piece : (i + 1) * piece] = dy_in[i]
            dy[i * piece : (i + 1) * piece, :] = dy_in[i].T
    if not turned:
        dy_t[...] = dy[...].T
    vg[...] = jnp.zeros(vg.shape, F32)
    vg[10:11, :] = colsum(dy[...].astype(F32))

    def scatter(sems, s, cut, direct, bufs, own):
        top = s.shape[2]
        r1, xl, yl, dl, yh, dh, xh = bufs
        low, high = slice(0, cut), slice(cut, top)
        slots = (j, j2)
        count = n if direct else zn
        mine = pl.ds(y0 * zn, zn)
        theirs = pl.ds(y1 * zn, zn)

        def copy(src, dst, t, dp, seq):
            at = sems[t]
            return remote(src, dst, gx_s.at[at], gx_r.at[at], dp, seq)

        def core():
            return [copy(s.at[slot], r1.at[t], t, me, j1) for t, slot in enumerate((j1, j3))]

        def low_x():
            return copy(s.at[j2, :, low], xl, 2, me, j2)

        def low_y():
            return copy(s.at[j, theirs, low], yl, 3, beside, j)

        def high_y():
            return [
                copy(s.at[slot, theirs, high], yh.at[t], 4 + t, beside, j)
                for t, slot in enumerate(slots)
            ]

        def high_x():
            return copy(s.at[j2, here, high], xh, 6, me, j2)

        def out(slot, rows_of, land, t):
            def send(k, peer, to):
                copy(s.at[slot, to, rows_of], land.at[k], t, peer, j).start()

            if direct:
                peers(lambda k, peer, source: send(k, peer, spot(peer)))
            else:
                z_peers(lambda k, peer, to, source: send(k, peer, y0 * zn + to))

        def landed(slot, rows_of, land, t):
            part = land.at[pl.ds(1, count - 1)]
            both(copy(part, part, t, beside, j))
            return lax.fori_loop(
                1,
                count,
                lambda k, v: v + land[k].astype(F32),
                s[slot, here, rows_of].astype(F32),
            )

        def add(slot, start, rows_of, extra):
            def body(i, carry):
                s[slot, start + i, rows_of] = (
                    s[slot, start + i, rows_of].astype(F32) + extra[i].astype(F32)
                ).astype(BF)
                return carry

            lax.fori_loop(0, extra.shape[0], body, 0)

        def one():
            for c in core():
                c.start()

        def two():
            for c in core():
                both(c)
            for t, slot in enumerate(slots):
                add(slot, 0, slice(0, top), r1.at[t])
            if cut < top:
                if direct:
                    for t, slot in enumerate(slots):
                        out(slot, high, dh.at[t], 4 + t)
                else:
                    for c in high_y():
                        c.start()
            if cut > 0:
                low_x().start()

        def low_three():
            both(low_x())
            add(j, 0, low, xl)
            if direct:
                out(j, low, dl, 3)
            else:
                low_y().start()

        def high_three():
            for c in high_y():
                both(c)
            for t, slot in enumerate(slots):
                add(slot, y0 * zn, high, yh.at[t])
                out(slot, high, dh.at[t], 7 + t)

        def low_four():
            both(low_y())
            add(j, y0 * zn, low, yl)
            out(j, low, dl, 9)

        def high_four():
            first = 4 if direct else 7
            own[high, :] = landed(j, high, dh.at[0], first)
            s[j2, here, high] = landed(j2, high, dh.at[1], first + 1).astype(BF)
            high_x().start()

        def low_five():
            own[low, :] = landed(j, low, dl, 3 if direct else 9)

        def high_five():
            both(high_x())
            own[high, :] = own[high, :] + xh[...].astype(F32)

        return one, two, low_three, low_four, low_five, high_three, high_four, high_five

    own_t = own_s.at[0:80, 0:tl]
    own_a = own_s.at[0:80, tl : tl + al]
    own_b = own_s.at[0:80, tl + al : tl + al + bl]
    own_m = own_s.at[96:128, 0:ml]
    a_one, a_two, a_three, a_four, a_five, _, _, _ = scatter(
        (0, 1, 2, 3, 0, 0, 0, 0, 0, 4), gf.at[:, :, :, 0:al], 80, False, (ra0, ra1, ra2, ra3, ra4, ra5, ra6), own_a
    )
    b_one, b_two, bl_three, bl_four, bl_five, bh_three, bh_four, bh_five = scatter(
        (5, 6, 27, 28, 7, 8, 9, 36, 37, 29), sb, 32, False, (rb0, rb1, rb2, rb3, rb4, rb5, rb6), own_b
    )
    m_one, m_two, m_three, m_four, m_five, _, _, _ = scatter(
        (12, 13, 14, 15, 0, 0, 0, 0, 0, 33), gm, 32, False, (rm0, rm1, rm2, rm3, rm4, rm5, rm6), own_m
    )
    below_cut = slice(0, CUT)
    above_cut = slice(CUT, 80)

    def t_core(t, slot, to, rows_of):
        return remote(
            gt.at[slot, :, rows_of], rt0.at[to, :, rows_of], gx_s.at[16 + t], gx_r.at[16 + t], me, j1
        )

    def t_cores():
        return (
            t_core(0, j3, 1, below_cut),
            t_core(1, j1, 0, above_cut),
            t_core(2, j3, 1, above_cut),
            t_core(3, j1, 0, below_cut),
        )

    def t_add(slot, start, count, rows_of, extra):
        def body(i, carry):
            gt[slot, start + i, rows_of] = (
                gt[slot, start + i, rows_of].astype(F32) + extra[start + i, rows_of].astype(F32)
            ).astype(BF)
            return carry

        lax.fori_loop(0, count, body, 0)

    def t_half(t):
        part = pl.ds((y1 if t == 0 else y0) * zn, zn)
        return remote(
            gt.at[j2, part, below_cut], rt1.at[part], gx_s.at[20 + t], gx_r.at[20 + t], me, j2
        )

    def t_dp(slot, i, rows_of, land, sem, k, peer):
        remote(
            gt.at[slot, i, rows_of], land.at[k], gx_s.at[sem], gx_r.at[sem], peer, j
        ).start()

    def t_landed(slot, rows_of, land, sem):
        part = land.at[pl.ds(1, n - 1)]
        both(remote(part, part, gx_s.at[sem], gx_r.at[sem], beside, j))
        return lax.fori_loop(
            1, n, lambda k, v: v + land[k].astype(F32), gt[slot, here, rows_of].astype(F32)
        )

    def t_one():
        for c in t_cores():
            c.start()

    def t_two():
        cores = t_cores()
        both(cores[0])
        t_add(j2, 0, n, below_cut, rt0.at[1])
        t_half(0).start()
        t_half(1).start()
        both(cores[1])
        both(cores[2])
        for t, slot in enumerate((j, j2)):
            t_add(slot, 0, n, above_cut, rt0.at[t])
            peers(
                lambda k, peer, source: t_dp(
                    slot, spot(peer), above_cut, rt5.at[t], 38 - 15 * t, k, peer
                )
            )
        both(cores[3])
        t_add(j, 0, n, below_cut, rt0.at[0])

    def tl_three(t):
        both(t_half(t))
        start = (y1 if t == 0 else y0) * zn

        def body(i, carry):
            at = start + i
            gt[j, at, below_cut] = (gt[j, at, below_cut].astype(F32) + rt1[at].astype(F32)).astype(BF)
            return carry

        lax.fori_loop(0, zn, body, 0)

        def send(i, carry):
            k = 2 * i + (1 if t == 0 else 2)
            peer = lax.rem(me + k, n)
            t_dp(j, spot(peer), below_cut, rt3, 24, k, peer)
            return carry

        lax.fori_loop(0, zn if t == 0 else zn - 1, send, 0)

    def th_x():
        return remote(gt.at[j2, here, above_cut], rt6, gx_s.at[25], gx_r.at[25], me, j2)

    def th_four():
        own_t[above_cut, :] = t_landed(j, above_cut, rt5.at[0], 38)
        gt[j2, here, above_cut] = t_landed(j2, above_cut, rt5.at[1], 23).astype(BF)
        th_x().start()

    def tl_five():
        own_t[below_cut, :] = t_landed(j, below_cut, rt3, 24)

    def th_five():
        both(th_x())
        own_t[above_cut, :] = own_t[above_cut, :] + rt6[...].astype(F32)


    per = 640 // (4 * rb)
    for b in range(2):
        value = nn(dy_t[...], act[side : side + tokens, 640 * b : 640 * b + 640]).astype(BF)
        for ii in range(per):
            i = b * per + ii
            gf[:, place_of(i), :, 0 : 4 * rb] = value[
                :, 4 * rb * ii : 4 * rb * (ii + 1)
            ].reshape(4, 80, 4 * rb)

    a_one()

    def slope_of(at):
        return nn(dy[at, :], w2t[...])

    dz = act
    for at in (0, edge):
        dz[side + at : 2 * side + at, :] = (
            slope_of(slice(at, at + side)) * gp[at : at + side, :].astype(F32)
        ).astype(BF)
    rim_send(dz, dzh, 2)

    def inner_slope(c, carry):
        at = rows(side + c * inner, inner)
        dz[rows(2 * side + c * inner, inner), :] = (
            slope_of(at) * gp[at, :].astype(F32)
        ).astype(BF)
        return carry

    lax.fori_loop(0, 2, inner_slope, 0, unroll=pairs)

    a_two()

    dhid = gp

    def back_over(lo, hi, step, tiles):
        def back_tile(t, carry):
            lanes = tile_at(t)
            taps = taps_of(lanes)

            def row(at, inner):
                r = lo + at * step
                around = [dz[rows((r + a) * side, side), lanes].astype(F32) for a in range(3)]
                parts = [
                    taps[b] * around[2] + taps[3 + b] * around[1] + taps[6 + b] * around[0]
                    for b in range(3)
                ]
                both_ways = jnp.concatenate([parts[0].astype(BF), parts[2].astype(BF)], axis=0)
                low = (parts[1] + nn(shift_b[...], both_ways)).astype(BF)
                dhid[rows(r * side, side), lanes] = low
                return inner

            lax.fori_loop(0, (hi - lo) // step, row, 0, unroll=True)
            return carry

        lax.fori_loop(0, FF // 128, back_tile, 0, unroll=tiles)

    back_over(1, band - 1, 1, 1)
    rim_wait(dz, dzh, 2)
    back_over(0, 2 * (band - 1), band - 1, 5)

    def fold(v):
        return jnp.sum(v.reshape(-1, 8, 128), axis=0)

    def tap_sums(lo, hi):
        def tile(t, carry):
            lanes = tile_at(t)

            def row(r, sums):
                low = dz[rows((r + 1) * side, side), lanes]
                here_f = low.astype(F32)
                sides = nn(shift_m[...], low)
                moved = [sides[0:side], here_f, sides[side : 2 * side]]
                found = []
                for a in range(3):
                    source = hidp[rows((r + a) * side, side), lanes].astype(F32)
                    for b in range(3):
                        found.append(fold(moved[b] * source))
                found.append(fold(here_f))
                return tuple(s + f for s, f in zip(sums, found))

            sums = lax.fori_loop(
                0, band, row, tuple(jnp.zeros((8, 128), F32) for _ in range(10)), unroll=deep
            )
            hg[:, lanes] = jnp.concatenate(
                [colsum(s) for s in sums[0:9]]
                + [hg[9:10, lanes], colsum(sums[9]), jnp.zeros((5, 128), F32)],
                axis=0,
            )
            return carry

        lax.fori_loop(lo, hi, tile, 0)

    bn_t = jnp.concatenate([bn[...].T, jnp.ones((16, tokens), BF)], axis=0)
    for b in range(2):
        found = nn(bn_t, dhid[:, 640 * b : 640 * b + 640])
        hg[9:10, 640 * b : 640 * b + 640] = found[D : D + 1]
        value = found[0:D].T.astype(BF).reshape(2, 4, 80, D)
        for i in range(n):
            sb[2 * b : 2 * b + 2, place_of(i), :, 0 : 4 * rb] = jnp.concatenate(
                [value[:, v, :, rb * i : rb * i + rb] for v in range(4)], axis=2
            )

    b_one()

    zero_row = jnp.zeros((1, D), F32)
    dbr = bn
    dbr_t = dy_t

    def back_middle(c, carry):
        at = rows(c * QC, QC)
        value, in_gain, in_shift = norm_back(mid[at, :], gain(2), nn(dhid[at, :], w1t[...]))
        value = value + dy[at, :].astype(F32)
        mid[at, :] = value
        low = value.astype(BF)
        dbr[at, :] = low
        dbr_t[:, across(c)] = low.T
        spread = nt(wop[...], low)
        for h in range(HEADS):
            tile = spread[128 * h : 128 * h + 128, :] * rtot[h, :, across(c)]
            tile_low = tile.astype(BF)
            qt[h, :, across(c)] = tile_low
            datn[h, at, :] = tile_low.T
            delta[h, :, across(c)] = colsum(
                tile_low[64:128, :].astype(F32)
                * att_t[HEAD * h : HEAD * h + HEAD, across(c)].astype(F32)
            )
        return (carry[0] + in_gain, carry[1] + in_shift, carry[2] + colsum(low.astype(F32)))

    sums = lax.fori_loop(0, chunks, back_middle, (zero_row, zero_row, zero_row), unroll=pairs)
    vg[2:3, :] = sums[0]
    vg[9:10, :] = sums[1]
    vg[8:9, :] = sums[2]
    a_three()
    b_two()

    def dkv(h, slot):
        return gp.at[rows(slot * keys, keys), tile_at(h)]

    def dk_core(h):
        return [
            remote(dkv(h, slot), rk1.at[h, t], kv_s.at[h, t], kv_r.at[h, t], me, j1)
            for t, slot in enumerate((j1, j3))
        ]

    def dk_x(h):
        return remote(dkv(h, j2), rk2.at[h], kv_s.at[h, 2], kv_r.at[h, 2], me, j2)

    def dk_two(h):
        for copy in dk_core(h):
            both(copy)
        for t, slot in enumerate((j, j2)):
            part = dkv(h, slot)
            part[...] = (part[...].astype(F32) + rk1[h, t].astype(F32)).astype(BF)
        dk_x(h).start()

    def dk_three(h):
        both(dk_x(h))
        qnat[h, 0:keys, :] = (dkv(h, j)[...].astype(F32) + rk2[h].astype(F32)).astype(BF)

    def back_head(h, carry):
        tile = kv[h].reshape(4 * keys, 128)
        total = None
        for c in range(tokens // qa):
            cut = slice(c * qa, (c + 1) * qa)
            powers = prob[h, :, cut]
            slopes = nn(tile, qt[h, :, cut]) - delta[h, :, cut]
            ds = (powers.astype(F32) * slopes).astype(BF)
            part = nn(ds, qnat[h, cut, :]) + nn(powers, datn[h, cut, :])
            prob[h, :, cut] = ds
            total = part if total is None else total + part
        gp[0 : 4 * keys, tile_at(h)] = total.astype(BF)
        for copy in dk_core(h):
            copy.start()

        @pl.when(h == 3)
        def _():
            a_four()
            bl_three()

        @pl.when(h >= 1)
        def _():
            dk_two(h - 1)

        return carry

    lax.fori_loop(0, HEADS, back_head, 0)

    dq_t = att_t

    def back_query(h, carry):
        for c in range(tokens // qa):
            cut = slice(c * qa, (c + 1) * qa)
            dq_t[rows(h * HEAD, HEAD), cut] = (
                nn(kvt[h, 0:64, :], prob[h, :, cut]) * HEAD**-0.5
            ).astype(BF)
        return carry

    lax.fori_loop(0, 2, back_query, 0, unroll=pairs)
    dk_two(HEADS - 1)
    bh_three()
    lax.fori_loop(2, HEADS, back_query, 0, unroll=3 if pairs > 1 else 1)
    bl_four()

    dq = dy

    def flip(c, total):
        low = dq_t[:, across(c)].T
        dq[rows(c * QC, QC), :] = low
        return total + colsum(low.astype(F32))

    vg[4:5, :] = lax.fori_loop(0, chunks, flip, zero_row, unroll=pairs)
    value = nn(dq_t[...], abf[...]).astype(BF)
    other = nn(dbr_t[...], att_n[...]).astype(BF)

    def folded(v, i):
        part = v[:, rb * i : rb * i + rb].reshape(4, 80, rb)
        return [
            part[:, 0:32],
            part[:, 32:64],
            jnp.concatenate([part[:, 64:80], jnp.zeros((4, 16, rb), BF)], axis=1),
        ]

    for i in range(n):
        gm[:, place_of(i), :, 0 : 3 * rb] = jnp.concatenate(folded(value, i), axis=2)
        gm[:, place_of(i), :, mo : mo + 3 * rb] = jnp.concatenate(folded(other, i), axis=2)
    m_one()
    tap_sums(0, 2)
    m_two()
    for h in range(HEADS):
        dk_three(h)

    dm = jnp.concatenate([qnat[h, 0:keys, :] for h in range(HEADS)], axis=1)
    dm_sum = colsum(dm.astype(F32))
    vg[7:8, :] = jnp.concatenate(
        [dm_sum[:, 128 * h + 64 : 128 * h + 128] for h in range(HEADS)], axis=1
    )
    kept = jnp.concatenate([a3[t, 0:keys, :] for t in range(3)], axis=1)[:, 0:D]
    dv, in_gain, in_shift = norm_back(kept, gain(1), nn(dm, wmt[...]))
    vg[1:2, :] = in_gain
    vg[6:7, :] = in_shift
    dred = dv.astype(BF)
    vg[5:6, :] = colsum(dred.astype(F32))
    dred_t = dred.T
    for dd in range(4):
        value = nn(dred_t, pat[dd]).astype(BF)
        count = n // 4
        for ii in range(count):
            i = dd * count + ii
            gt[:, place_of(i), :, 0 : 4 * rb] = value[
                :, 4 * rb * ii : 4 * rb * (ii + 1)
            ].reshape(4, 80, 4 * rb)
    value = nn(dm.T, memin[...]).astype(BF)
    value = jnp.concatenate(
        [value[128 * h : 128 * h + 64] for h in range(HEADS)]
        + [value[128 * h + 64 : 128 * h + 128] for h in range(HEADS)],
        axis=0,
    ).reshape(4, 2, 80, D)
    for i in range(n):
        gt[:, place_of(i), :, 4 * rb : 6 * rb] = jnp.concatenate(
            [value[:, v, :, rb * i : rb * i + rb] for v in range(2)], axis=2
        )
    t_one()

    t_two()

    for dd in range(4):
        back = nn(dred, wrt[dd])
        back = jnp.concatenate([back, jnp.zeros((keys, 64), F32)], axis=1)
        for i in range(band // 2):
            start = (2 * i + dd // 2) * side + dd % 2
            for t in range(3):
                a3[t, pl.ds(start, half, stride=2), :] = back[
                    i * half : (i + 1) * half, 128 * t : 128 * t + 128
                ]

    def back_first(c, carry):
        at = rows(c * QC, QC)
        e = nn(dq[at, :], wqt[...]) + jnp.concatenate([a3[t, at, :] for t in range(3)], axis=1)[:, 0:D]
        value, in_gain, in_shift = norm_back(x_s[at, :].astype(F32), gain(0), e)
        bn[at, :] = (mid[at, :] + value).astype(BF)
        return (carry[0] + in_gain, carry[1] + in_shift)

    sums = lax.fori_loop(0, chunks, back_first, (zero_row, zero_row), unroll=pairs)
    token_out = pltpu.make_async_copy(bn, tgrad_ref, loc.at[12])
    token_out.start()
    vg[0:1, :] = sums[0]
    vg[3:4, :] = sums[1]
    m_three()
    tap_sums(2, FF // 128)
    for i in range(n):
        sv[place_of(i), :, 0 : 4 * rb] = hg[:, 4 * rb * i : 4 * rb * (i + 1)].astype(BF)
        sv[place_of(i), :, 4 * rb : 5 * rb] = vg[:, rb * i : rb * i + rb].astype(BF)

    def v_out(k, peer, source):
        remote(sv.at[spot(peer)], rv1.at[k], gx_s.at[26], gx_r.at[26], peer, j).start()

    peers(v_out)
    tl_three(0)
    tl_three(1)
    bh_four()
    m_four()
    part = rv1.at[pl.ds(1, n - 1)]
    both(remote(part, part, gx_s.at[26], gx_r.at[26], beside, j))
    rv2[j] = lax.fori_loop(
        1, n, lambda k, total: total + rv1[k].astype(F32), sv[here].astype(F32)
    ).astype(BF)

    def v_seq(t, slot, other):
        ref = rv2.at[slot]
        return remote(ref, ref, gx_s.at[30 + t], gx_r.at[30 + t], me, other)

    for t, other in enumerate((j1, j2, j3)):
        v_seq(t, j, other).start()
    th_four()
    a_five()
    bl_five()
    bh_five()
    squares = jnp.sum(own_a[:, 0 : 4 * rb] * own_a[:, 0 : 4 * rb])
    squares += jnp.sum(own_b[:, 0 : 4 * rb] * own_b[:, 0 : 4 * rb])
    th_five()
    m_five()
    for at in (0, mo):
        full = own_m[:, at : at + 2 * rb]
        rest = own_m[0:16, at + 2 * rb : at + 3 * rb]
        squares += jnp.sum(full * full) + jnp.sum(rest * rest)
    tl_five()
    squares += jnp.sum(own_t[:, 0 : 6 * rb] * own_t[:, 0 : 6 * rb])
    for t, other in enumerate((j1, j2, j3)):
        v_seq(t, other, other).wait_send()
        v_seq(t, other, other).wait_recv()
    own_v = (rv2[0].astype(F32) + rv2[1].astype(F32)) + (rv2[2].astype(F32) + rv2[3].astype(F32))
    own_s[80:96, 0:vl] = own_v
    first_band = (j == 0).astype(jnp.int32).astype(F32)
    squares += first_band * jnp.sum(own_v[0:11, 0 : 5 * rb] * own_v[0:11, 0 : 5 * rb])

    nrm[4 * me + j] = jnp.full((1, 128), squares, F32)
    own_out_copy = pltpu.make_async_copy(own_s, own_ref, loc.at[13])
    own_out_copy.start()

    def send_norm(k, carry):
        mine = 4 * me + j
        to = lax.rem(mine + k, 4 * n)
        remote(
            nrm.at[mine], nrm.at[mine], nd_s.at[0], nd_r.at[0], lax.div(to, 4), lax.rem(to, 4)
        ).start()
        return carry

    lax.fori_loop(1, 4 * n, send_norm, 0)
    part = nrm.at[pl.ds(0, 4 * n - 1)]
    both(remote(part, part, nd_s.at[0], nd_r.at[0], beside, j))
    nrm[4 * n] = lax.fori_loop(1, 4 * n, lambda k, total: total + nrm[k], nrm[0])
    norm_out = pltpu.make_async_copy(nrm.at[4 * n], norm_ref, loc.at[14])
    norm_out.start()

    wait_out()
    own_out.wait()
    token_out.wait()
    own_out_copy.wait()
    norm_out.wait()


def update_kernel(rb, tl, al, mo, rates, decays, *refs):
    own_hbm, total_hbm, outt_hbm, tg_hbm = refs[0:4]
    in_hbm = refs[4:31]
    out_hbm, tok_hbm, norm_hbm = refs[31:34]
    new_hbm = refs[34:61]
    own_ref, total_ref, out_v, tok_v, norm_v = refs[61:66]
    in_v, new_v = refs[66:75], refs[75:84]
    in_sem, out_sem = refs[84:86]
    own_load, total_load, out_load, tok_load = [
        pltpu.make_async_copy(src, dst, in_sem.at[9 + at])
        for at, (src, dst) in enumerate(
            ((own_hbm, own_ref), (total_hbm, total_ref), (outt_hbm, out_v), (tg_hbm, tok_v))
        )
    ]
    own_load.start()
    total_load.start()
    for at in range(9):
        for part in range(3):
            pltpu.make_async_copy(in_hbm[at + 9 * part], in_v[at].at[part], in_sem.at[at]).start()
    out_load.start()
    tok_load.start()
    norm_store, out_store, tok_store = [
        pltpu.make_async_copy(src, dst, out_sem.at[9 + at])
        for at, (src, dst) in enumerate(((norm_v, norm_hbm), (out_v, out_hbm), (tok_v, tok_hbm)))
    ]
    own_load.wait()
    total_load.wait()
    total = total_ref[...]
    norm = jnp.sqrt(total)
    norm_v[...] = norm
    norm_store.start()
    clip = jnp.minimum(1.0, MAX_NORM / (norm + 1e-06))[:, 0:1]
    turned_t = own_ref[0:80, 0:tl].T
    turned_a = own_ref[0:80, tl : tl + al].T
    turned_b = own_ref[0:80, tl + al :].T
    turned_q, turned_o = [
        jnp.concatenate(
            [
                own_ref[96:128, at : at + rb],
                own_ref[96:128, at + rb : at + 2 * rb],
                own_ref[96:112, at + 2 * rb : at + 3 * rb],
            ],
            axis=0,
        ).T
        for at in (0, mo)
    ]
    grads = (
        turned_q,
        turned_t[0 : 4 * rb],
        jnp.concatenate([turned_t[(4 + v) * rb : (5 + v) * rb] for v in range(2)], axis=1),
        turned_o,
        jnp.concatenate([turned_b[v * rb : (v + 1) * rb] for v in range(4)], axis=1),
        turned_a[0 : 4 * rb],
        own_ref[80:83, 4 * rb : 5 * rb],
        own_ref[83:91, 4 * rb : 5 * rb],
        own_ref[80:91, 0 : 4 * rb],
    )
    for at in range(9):
        if at == 2:
            out_load.wait()
            out_store.start()
            tok_load.wait()
            tok_store.start()
        pltpu.make_async_copy(in_v[at], in_v[at], in_sem.at[at]).wait()
        clipped = clip * grads[at]
        weight = in_v[at][0]
        first = BETA_ONE * in_v[at][1] + (1.0 - BETA_ONE) * clipped
        second = BETA_TWO * in_v[at][2] + (1.0 - BETA_TWO) * clipped * clipped
        direction = (
            first
            / (1.0 - BETA_ONE**STEP)
            / (jnp.sqrt(second / (1.0 - BETA_TWO**STEP)) + ADAM_EPS)
        )
        new_v[at][0] = weight - rates[at] * (direction + decays[at] * weight)
        new_v[at][1] = first
        new_v[at][2] = second
        for part in range(3):
            pltpu.make_async_copy(
                new_v[at].at[part], new_hbm[at + 9 * part], out_sem.at[at]
            ).start()
    for at in range(9):
        pltpu.make_async_copy(new_v[at], new_v[at], out_sem.at[at]).wait()
    for store in (norm_store, out_store, tok_store):
        store.wait()


def on_device(n, *args):
    tokens, buckets, cotangent = args[0:3]
    weights, firsts, seconds = args[3:12], args[12:21], args[21:30]
    band, side, width = tokens.shape[1:4]
    count = band * side
    keys = count // 4
    rb = weights[0].shape[0]
    piece = cotangent.shape[3]
    wide = up(9 * rb, 128)
    tl = up(6 * rb, 128)
    al = up(4 * rb, 128)
    bl = up(4 * rb, 128)
    ml = up(6 * rb, 128)
    h = n // 2
    vl = up(5 * rb, 128)
    total = tl + al + bl
    qa = count if n <= 8 else 128
    turned = piece % 128 == 0
    block = (n, D, piece) if turned else (n, piece, D)
    vm = pltpu.VMEM
    dma = pltpu.SemaphoreType.DMA
    def landing(height, lanes, cut, direct):
        rest = height - cut
        count = n if direct else h
        shapes = (
            (2, n, height, lanes),
            (n, cut, lanes),
            (0 if direct else h, cut, lanes),
            (count, cut, lanes),
            (0 if direct else 2, h, rest, lanes),
            (2, count, rest, lanes),
            (rest, lanes),
        )
        return [vm(shape if 0 not in shape else (8, 128), BF) for shape in shapes]

    scratch = [
        vm((count, D), BF),
        *[vm(weights[at].shape, F32) for at in range(9)],
        vm((n, 16, vl), BF),
        vm((4, n, 80, tl), BF),
        vm((4, n, 32, ml), BF),
        vm((4, n, 80, wide), BF),
        vm((16, D), F32),
        vm((16, FF), F32),
        vm((D, D), BF),
        vm((D, D), BF),
        vm((2 * D, D), BF),
        vm((2 * D, D), BF),
        vm((4, D, D), BF),
        vm((FF, D), BF),
        vm((D, FF), BF),
        vm((3, count, 128), F32),
        vm((count, D), BF),
        vm((4, keys, D), BF),
        vm((keys, D), BF),
        vm((HEADS, 4, keys, 128), BF),
        vm((HEADS, 128, 4 * keys), BF),
        vm((HEADS, count, 128), BF),
        vm((HEADS, 128, count), BF),
        vm((HEADS, 4 * keys, count), BF),
        vm((D, count), BF),
        vm((count, D), BF),
        vm((HEADS, 1, count), F32),
        vm((HEADS, 1, count), F32),
        vm((count, D), F32),
        vm((count, D), BF),
        vm((count + 2 * side, FF), BF),
        vm((2, side, FF), BF),
        vm((count + 2 * side, FF), BF),
        vm((count, FF), BF),
        vm(block, BF),
        vm(block if turned else (8, 128), BF),
        vm((D, count), BF),
        vm((count, D), BF),
        vm((2, side, FF), BF),
        vm((HEADS, count, 128), BF),
        vm((HEADS, 2, keys, 128), BF),
        vm((HEADS, keys, 128), BF),
        vm((16, FF), F32),
        vm((16, D), F32),
        vm((128, total), F32),
        vm((4, n, 80, bl), BF),
        *landing(80, al, 80, False),
        *landing(80, bl, 32, False),
        *landing(80, tl, CUT, True),
        *landing(32, ml, 32, False),
        vm((n, 16, vl), BF),
        vm((n, 16, vl), BF),
        vm((4, 16, vl), BF),
        vm((4 * n + 1, 1, 128), F32),
        vm((side, 2 * side), BF),
        vm((side, 2 * side), BF),
        vm((2 * side, side), BF),
        dma((15,)),
        dma((n,)),
        dma((2, h)),
        *[dma((39,)) for _ in range(2)],
        *[dma((1,)) for _ in range(4)],
        *[dma((HEADS, 3)) for _ in range(2)],
        *[dma((4,)) for _ in range(2)],
        *[dma((1,)) for _ in range(2)],
    ]
    anywhere = pl.BlockSpec(memory_space=pl.ANY)
    out_t, token_grad, own, total_squares = pl.pallas_call(
        functools.partial(block_kernel, n, side, band, qa),
        out_shape=(
            jax.ShapeDtypeStruct(block, BF),
            jax.ShapeDtypeStruct((count, D), BF),
            jax.ShapeDtypeStruct((128, total), F32),
            jax.ShapeDtypeStruct((1, 128), F32),
        ),
        in_specs=[pl.BlockSpec(memory_space=pltpu.SMEM)] + [anywhere] * 11,
        out_specs=(anywhere,) * 4,
        scratch_shapes=scratch,
        compiler_params=pltpu.CompilerParams(
            collective_id=0, has_side_effects=True, vmem_limit_bytes=VMEM_LIMIT
        ),
    )(
        buckets,
        tokens.reshape(count, width),
        jnp.swapaxes(cotangent, 3, 4).reshape(block) if turned else cotangent.reshape(block),
        *weights,
    )
    rates = (
        D ** (-0.5),
        (4 * D) ** (-0.5),
        D ** (-0.5),
        OUT_FAN ** (-0.5),
        D ** (-0.5),
        FF ** (-0.5),
        GAIN_RATE,
        VECTOR_RATE,
        VECTOR_RATE,
    )
    decays = (DECAY_RATE,) * 6 + (0.0,) * 3
    shapes = tuple(jax.ShapeDtypeStruct(w.shape, F32) for w in weights)
    results = pl.pallas_call(
        functools.partial(
            update_kernel, rb, tl, al, 128 if ml > 128 else 3 * rb, rates, decays
        ),
        out_shape=(
            jax.ShapeDtypeStruct(block, BF),
            jax.ShapeDtypeStruct((count, D), BF),
            jax.ShapeDtypeStruct((1, 128), F32),
        )
        + shapes * 3,
        in_specs=[anywhere] * 31,
        out_specs=(anywhere,) * 30,
        scratch_shapes=[
            vm((128, total), F32),
            vm((1, 128), F32),
            vm(block, BF),
            vm((count, D), BF),
            vm((1, 128), F32),
            *[vm((3, *w.shape), F32) for w in weights * 2],
            dma((13,)),
            dma((12,)),
        ],
    )(own, total_squares, out_t, token_grad, *weights, *firsts, *seconds)
    if turned:
        block_output = jnp.swapaxes(results[0].reshape(n, 1, 1, width, piece), 3, 4)
    else:
        block_output = results[0].reshape(n, 1, 1, piece, width)
    return (
        block_output,
        results[1].reshape(1, band, side, width),
        results[2][0, 0],
        *results[3:],
    )


def solution(mesh):
    matrix = (P("dp", "seq"),) * 6 + (P(None, "dp"),) * 3
    return jax.shard_map(
        functools.partial(on_device, mesh.shape["dp"]),
        mesh=mesh,
        in_specs=(
            P("dp", "seq", None, None),
            P("dp"),
            P(None, "seq", "dp", None, None),
            *(matrix * 3),
        ),
        out_specs=(
            P(None, "seq", "dp", None, None),
            P("dp", "seq", None, None),
            P(),
            *(matrix * 3),
        ),
        check_vma=False,
    )
```

```python
import functools

import jax
import jax.numpy as jnp
from jax import lax
from jax.experimental import pallas as pl
from jax.experimental.pallas import tpu as pltpu
from jax.sharding import PartitionSpec as P

D = 320
HEADS = 5
HEAD = 64
FF = 1280
STEP = 10
OUT_FAN = 5

NORM_EPS = 1e-06
MAX_NORM = 1.0
BETA_ONE = 0.9
BETA_TWO = 0.95
ADAM_EPS = 1e-08
DECAY_RATE = 0.01
VECTOR_RATE = 0.3
GAIN_RATE = 0.8
MASKED = -1e30

BF = jnp.bfloat16
F32 = jnp.float32
MESH = pl.DeviceIdType.MESH
QC = 512
GATHER_CUT = 32
CUT = 48
VMEM_LIMIT = 63 * 1024 * 1024


def nn(a, b):
    return lax.dot_general(a, b, (((1,), (0,)), ((), ())), preferred_element_type=F32)


def nt(a, b):
    return lax.dot_general(a, b, (((1,), (1,)), ((), ())), preferred_element_type=F32)


def up(n, m):
    return (n + m - 1) // m * m


def norm_parts(v):
    centered = v - jnp.mean(v, axis=-1, keepdims=True)
    rstd = lax.rsqrt(jnp.mean(centered * centered, axis=-1, keepdims=True) + NORM_EPS)
    return centered * rstd, rstd


def norm_back(v, gain, e):
    vhat, rstd = norm_parts(v)
    u = e * gain
    dv = rstd * (
        u
        - jnp.mean(u, axis=-1, keepdims=True)
        - vhat * jnp.mean(u * vhat, axis=-1, keepdims=True)
    )
    return dv, jnp.sum(e * vhat, axis=0, keepdims=True), jnp.sum(e, axis=0, keepdims=True)


def colsum(v):
    return jnp.sum(v, axis=0, keepdims=True)


def rows(start, size):
    return pl.ds(pl.multiple_of(start, 16), size)


def block_kernel(
    n,
    side,
    band,
    qa,
    bucket_ref,
    tok_ref,
    cot_ref,
    wq_ref,
    wr_ref,
    wm_ref,
    wo_ref,
    w1_ref,
    w2_ref,
    gains_ref,
    biases_ref,
    hidden_ref,
    out_ref,
    tgrad_ref,
    own_ref,
    norm_ref,
    x_s,
    fq,
    fr,
    fm,
    fo,
    f1,
    f2,
    fg,
    fb,
    fh,
    gvec,
    gt,
    gm,
    gf,
    vp,
    hp,
    wqt,
    wot,
    wop,
    wmt,
    wrt,
    w1t,
    w2t,
    a3,
    abf,
    pat,
    memin,
    kv,
    kvt,
    qnat,
    qt,
    prob,
    att_t,
    att_n,
    rtot,
    delta,
    mid,
    bn,
    hidp,
    hidh,
    act,
    gp,
    out_t,
    dy_in,
    dy_t,
    dy,
    dzh,
    datn,
    rk1,
    rk2,
    hg,
    vg,
    own_s,
    sb,
    ra0,
    ra1,
    ra2,
    ra3,
    ra4,
    ra5,
    ra6,
    rb0,
    rb1,
    rb2,
    rb3,
    rb4,
    rb5,
    rb6,
    rt0,
    rt1,
    rt2,
    rt3,
    rt4,
    rt5,
    rt6,
    rm0,
    rm1,
    rm2,
    rm3,
    rm4,
    rm5,
    rm6,
    sv,
    rv1,
    rv2,
    nrm,
    shift_f,
    shift_b,
    shift_m,
    loc,
    tl_r,
    th_r,
    gx_s,
    gx_r,
    co_s,
    co_r,
    ou_s,
    ou_r,
    kv_s,
    kv_r,
    ha_s,
    ha_r,
    nd_s,
    nd_r,
):
    me = lax.axis_index("dp")
    j = lax.axis_index("seq")
    y0 = lax.rem(me, 2)
    y1 = 1 - y0
    z0 = lax.div(me, 2)
    beside = me + 1 - 2 * y0
    zn = n // 2
    here = y0 * zn + z0

    def place_of(i):
        return i % 2 * zn + i // 2

    def spot(i):
        return lax.rem(i, 2) * zn + lax.div(i, 2)

    j1 = j + 1 - 2 * lax.rem(j, 2)
    j2 = lax.rem(j + 2, 4)
    j3 = 3 - j
    tokens = band * side
    chunks = tokens // QC
    deep = band if qa == tokens else 4
    pairs = 2 if qa == tokens else 1
    flat = 4 * n - 1 if qa == tokens else 1
    rb = wq_ref.shape[0]
    piece = tokens // n
    keys = kv.shape[2]
    turned = cot_ref.shape[1] == D
    tl = gt.shape[3]
    fl = gf.shape[3]
    vl = gvec.shape[2]
    al = up(4 * rb, 128)
    bl = sb.shape[3]
    ml = gm.shape[3]
    mo = 128 if ml > 128 else 3 * rb

    def remote(src, dst, ss, rs, dp, seq):
        return pltpu.make_async_remote_copy(
            src_ref=src,
            dst_ref=dst,
            send_sem=ss,
            recv_sem=rs,
            device_id=(dp, seq),
            device_id_type=MESH,
        )

    def both(copy):
        copy.wait_send()
        copy.wait_recv()

    def peers(body):
        def step(k, carry):
            body(k, lax.rem(me + k, n), lax.rem(me + n - k, n))
            return carry

        lax.fori_loop(1, n, step, 0)

    def z_peers(body):
        def step(k, carry):
            body(k, lax.rem(me + 2 * k, n), lax.rem(z0 + k, zn), lax.rem(z0 + zn - k, zn))
            return carry

        lax.fori_loop(1, zn, step, 0)

    loads = [
        pltpu.make_async_copy(src, dst, loc.at[at])
        for at, (src, dst) in enumerate(
            (
                (gains_ref, fg),
                (biases_ref, fb),
                (hidden_ref, fh),
                (wr_ref, fr),
                (wm_ref, fm),
                (wq_ref, fq),
                (wo_ref, fo),
                (w1_ref, f1),
                (w2_ref, f2),
                (tok_ref, x_s),
            )
        )
    ]
    for copy in loads:
        copy.start()
    def incoming(i):
        return dy_in.at[i] if turned else dy.at[rows(i * piece, piece)]

    own_cot = pltpu.make_async_copy(cot_ref.at[me], incoming(me), loc.at[10])
    own_cot.start()

    barrier = pltpu.get_barrier_semaphore()

    def greet(k, carry):
        to = lax.rem(4 * me + j + k, 4 * n)
        pl.semaphore_signal(
            barrier, inc=1, device_id=(lax.div(to, 4), lax.rem(to, 4)), device_id_type=MESH
        )
        return carry

    lax.fori_loop(1, 4 * n, greet, 0, unroll=flat)

    for copy in loads[:5]:
        copy.wait()
    hidden16 = jnp.concatenate([fh[...], jnp.zeros((5, 4 * rb), F32)], axis=0)
    small16 = jnp.concatenate([fg[...], fb[...], jnp.zeros((5, rb), F32)], axis=0)
    gvec[here] = jnp.concatenate(
        [hidden16, small16, jnp.zeros((16, vl - 5 * rb), F32)], axis=1
    ).astype(BF)
    wm_t = fm[...].T
    gt[j, here] = jnp.concatenate(
        [fr[...].T, wm_t[0:80], wm_t[80:160], jnp.zeros((80, tl - 6 * rb), F32)], axis=1
    ).astype(BF)

    def group(at, one_of, all_but_one, each):
        def start():
            def send(peer):
                ref = one_of(here)
                remote(ref, ref, gx_s.at[14 + at], gx_r.at[14 + at], peer, j).start()

            each(send)

        def wait():
            both(remote(all_but_one, all_but_one, gx_s.at[14 + at], gx_r.at[14 + at], beside, j))

        return start, wait

    def each_peer(send):
        peers(lambda k, peer, source: send(peer))

    def each_z(send):
        z_peers(lambda k, peer, to, source: send(peer))

    def over_dp(at, buf, rows_of):
        return group(
            at, lambda i: buf.at[i, rows_of], buf.at[pl.ds(0, n - 1), rows_of], each_peer
        )

    def over_z(at, buf, rows_of):
        return group(
            at, lambda i: buf.at[i, rows_of], buf.at[pl.ds(0, zn - 1), rows_of], each_z
        )

    def swap(at, mine, theirs, dp, seq):
        def start():
            remote(mine, mine, gx_s.at[at], gx_r.at[at], dp, seq).start()

        def wait():
            remote(mine, mine, gx_s.at[at], gx_r.at[at], dp, seq).wait_send()
            remote(theirs, theirs, gx_s.at[at], gx_r.at[at], dp, seq).wait_recv()

        return start, wait

    def over_y(at, buf, rows_of):
        mine = buf.at[pl.ds(y0 * zn, zn), rows_of]
        theirs = buf.at[pl.ds(y1 * zn, zn), rows_of]
        return swap(at, mine, theirs, beside, j)

    lower = slice(0, GATHER_CUT)
    upper = slice(GATHER_CUT, 80)
    every = slice(0, 16)
    v_dp, v_dp_wait = over_dp(0, gvec, every)

    def t_low(i):
        return gt.at[j, i, lower]

    def t_low_copy(k, i, peer):
        return remote(t_low(i), t_low(i), gx_s.at[15], tl_r.at[k], peer, j)

    def t_low_on(i):
        remote(t_low(i), t_low(i), gx_s.at[0], gx_r.at[0], me, j2).start()

    def t_low_start():
        t_low_on(here)
        peers(lambda k, peer, source: t_low_copy(k, here, peer).start())

    def t_low_forward():
        def body(k, peer, source):
            t_low_copy(k, spot(source), peer).wait_recv()
            t_low_on(spot(source))

        peers(body)

    def t_low_wait():
        part = gt.at[j, pl.ds(0, n - 1), lower]
        remote(part, part, gx_s.at[15], tl_r.at[0], beside, j).wait_send()
        both(remote(gt.at[j, :, lower], gt.at[j2, :, lower], gx_s.at[0], gx_r.at[0], me, j2))

    t_x0, t_x0_wait = swap(1, gt.at[j, here, upper], gt.at[j2, here, upper], me, j2)

    def t_high(slot, t):
        def ref(i):
            return gt.at[slot, i, upper]

        def copy(k, i, peer):
            return remote(ref(i), ref(i), gx_s.at[16 + t], th_r.at[t, k], peer, j)

        def on(i):
            remote(ref(i), ref(i), gx_s.at[2 + t], gx_r.at[2 + t], beside, j).start()

        def start():
            z_peers(lambda k, peer, to, source: copy(k, here, peer).start())
            on(here)

        def forward():
            def body(k, peer, to, source):
                copy(k, y0 * zn + source, peer).wait_recv()
                on(y0 * zn + source)

            z_peers(body)

        def wait():
            part = gt.at[slot, pl.ds(0, zn - 1), upper]
            remote(part, part, gx_s.at[16 + t], th_r.at[t, 0], beside, j).wait_send()
            mine = gt.at[slot, pl.ds(y0 * zn, zn), upper]
            theirs = gt.at[slot, pl.ds(y1 * zn, zn), upper]
            both(remote(mine, theirs, gx_s.at[2 + t], gx_r.at[2 + t], beside, j))

        return start, forward, wait

    t_za, t_za_forward, t_ya_wait = t_high(j, 0)
    t_zb, t_zb_forward, t_yb_wait = t_high(j2, 1)
    t_ca, t_ca_wait = swap(4, gt.at[j], gt.at[j1], me, j1)
    t_cb, t_cb_wait = swap(5, gt.at[j2], gt.at[j3], me, j1)
    wq_block = gm.at[:, :, :, 0:128]
    m_dp, m_dp_wait = over_dp(4, wq_block.at[j], slice(0, 32))
    m_x, m_x_wait = swap(6, wq_block.at[j], wq_block.at[j2], me, j2)
    m_ca, m_ca_wait = swap(7, wq_block.at[j], wq_block.at[j1], me, j1)
    m_cb, m_cb_wait = swap(8, wq_block.at[j2], wq_block.at[j3], me, j1)
    f_x0, f_x0_wait = swap(9, gf.at[j, here], gf.at[j2, here], me, j2)
    fl_za, fl_za_wait = over_z(5, gf.at[j], lower)
    fl_zb, fl_zb_wait = over_z(6, gf.at[j2], lower)
    fh_a, fh_a_wait = over_dp(7, gf.at[j], upper)
    fh_b, fh_b_wait = over_dp(8, gf.at[j2], upper)
    fl_ya, fl_ya_wait = over_y(10, gf.at[j], lower)
    fl_yb, fl_yb_wait = over_y(11, gf.at[j2], lower)
    fl_ca, fl_ca_wait = swap(12, gf.at[j, :, lower], gf.at[j1, :, lower], me, j1)
    fl_cb, fl_cb_wait = swap(13, gf.at[j2, :, lower], gf.at[j3, :, lower], me, j1)
    fh_ca, fh_ca_wait = swap(34, gf.at[j, :, upper], gf.at[j1, :, upper], me, j1)
    fh_cb, fh_cb_wait = swap(35, gf.at[j2, :, upper], gf.at[j3, :, upper], me, j1)

    pl.semaphore_wait(barrier, 4 * n - 1)
    t_x0()
    t_za()
    t_low_start()

    for copy in loads[5:9]:
        copy.wait()
    wq_t = fq[...].T
    gm[j, here, :, 0:128] = jnp.concatenate(
        [
            wq_t[0:32],
            wq_t[32:64],
            jnp.concatenate([wq_t[64:80], jnp.zeros((16, rb), F32)], axis=0),
            jnp.zeros((32, 128 - 3 * rb), F32),
        ],
        axis=1,
    ).astype(BF)
    w1_t = f1[...].T
    gf[j, here] = jnp.concatenate(
        [f2[...].T]
        + [w1_t[80 * v : 80 * v + 80] for v in range(4)]
        + [fo[...].T, jnp.zeros((80, fl - 9 * rb), F32)],
        axis=1,
    ).astype(BF)
    t_x0_wait()
    t_zb()
    v_dp()

    t_low_forward()
    m_dp()
    f_x0()
    t_za_forward()
    t_zb_forward()
    f_x0_wait()
    fl_za()
    fl_zb()
    v_dp_wait()
    hp[...] = jnp.concatenate([gvec[place_of(i), :, 0 : 4 * rb] for i in range(n)], axis=1).astype(F32)
    vp[...] = jnp.concatenate(
        [gvec[place_of(i), :, 4 * rb : 5 * rb] for i in range(n)], axis=1
    ).astype(F32)

    def gain(k):
        return vp[k : k + 1, :]

    def shift(k):
        return vp[3 + k : 4 + k, :]

    loads[9].wait()

    def norm_one(c, carry):
        at = rows(c * QC, QC)
        vhat, _ = norm_parts(x_s[at, :].astype(F32))
        low = (vhat * gain(0) + shift(0)).astype(BF)
        abf[at, :] = low
        wide = jnp.concatenate([low.astype(F32), jnp.zeros((QC, 64), F32)], axis=1)
        for t in range(3):
            a3[t, at, :] = wide[:, 128 * t : 128 * t + 128]
        return carry

    lax.fori_loop(0, chunks, norm_one, 0, unroll=pairs)
    half = side // 2
    for dd in range(4):
        for i in range(band // 2):
            start = (2 * i + dd // 2) * side + dd % 2
            cut = jnp.concatenate(
                [a3[t, pl.ds(start, half, stride=2), :] for t in range(3)], axis=1
            )
            pat[dd, i * half : (i + 1) * half, :] = cut[:, 0:D].astype(BF)

    bucket = bucket_ref[0]
    k_row = lax.broadcasted_iota(jnp.int32, (4 * keys, 128), 0)
    k_lane = lax.broadcasted_iota(jnp.int32, (4 * keys, 128), 1)
    k_id = (lax.div(k_row, half) >= half // 2).astype(jnp.int32) * 2 + (
        lax.rem(k_row, half) >= half // 2
    ).astype(jnp.int32)
    off = (k_id != k_lane).astype(jnp.int32) * bucket * (k_lane < 4).astype(jnp.int32)
    kmask = datn.at[0]
    qmask = dy_t.at[0:128]
    kmask[...] = (off.astype(F32) * MASKED).astype(BF)
    q_row = lax.broadcasted_iota(jnp.int32, (128, tokens), 0)
    place = lax.broadcasted_iota(jnp.int32, (128, tokens), 1)
    q_id = (lax.div(place, side) + j * band >= half).astype(jnp.int32) * 2 + (
        lax.rem(place, side) >= half
    ).astype(jnp.int32)
    qmask[...] = (q_id == q_row).astype(F32).astype(BF)
    col = lax.broadcasted_iota(jnp.int32, (side, side), 0)
    ok_l = (col > 0).astype(jnp.int32) * (1 - bucket * (col == half).astype(jnp.int32))
    ok_r = (col < side - 1).astype(jnp.int32) * (
        1 - bucket * (col == half - 1).astype(jnp.int32)
    )
    lane = lax.broadcasted_iota(jnp.int32, (side, side), 1)
    from_l = (ok_l * (lane == col - 1).astype(jnp.int32)).astype(F32).astype(BF)
    from_r = (ok_r * (lane == col + 1).astype(jnp.int32)).astype(F32).astype(BF)
    shift_f[...] = jnp.concatenate([from_l, from_r], axis=1)
    shift_b[...] = jnp.concatenate([from_r, from_l], axis=1)
    shift_m[...] = jnp.concatenate([from_r, from_l], axis=0)
    top_ok = (
        (j > 0).astype(jnp.int32) * (1 - bucket * (j * band == half).astype(jnp.int32))
    ).astype(F32)
    low_ok = (
        (j < 3).astype(jnp.int32) * (1 - bucket * ((j + 1) * band == half).astype(jnp.int32))
    ).astype(F32)

    t_ya_wait()
    t_yb_wait()
    t_low_wait()
    t_ca()
    t_cb()
    m_dp_wait()
    m_x()
    t_ca_wait()
    t_cb_wait()

    fh_a()
    fh_b()

    for s in range(4):
        span = slice(80 * s, 80 * s + 80)

        def lanes(lo, hi, over):
            return jnp.concatenate([gt[s, place_of(i), :, lo:hi] for i in over], axis=1)

        for dd in range(4):
            wrt[dd, span, :] = lanes(0, 4 * rb, range(dd * n // 4, (dd + 1) * n // 4))
        for v in range(2):
            wop[160 * s + 80 * v : 160 * s + 80 * v + 80, :] = lanes(
                (4 + v) * rb, (5 + v) * rb, range(n)
            )
    for h in range(HEADS):
        wmt[128 * h : 128 * h + 64, :] = wop[HEAD * h : HEAD * h + HEAD, :]
        wmt[128 * h + 64 : 128 * h + 128, :] = wop[D + HEAD * h : D + HEAD * h + HEAD, :]

    red = shift(2) + nt(pat[0], wrt[0])
    for dd in range(1, 4):
        red = red + nt(pat[dd], wrt[dd])
    wide_red = jnp.concatenate([red, jnp.zeros((keys, 64), F32)], axis=1)
    for t in range(3):
        a3[t, 0:keys, :] = wide_red[:, 128 * t : 128 * t + 128]
    vhat, _ = norm_parts(red)
    low = (vhat * gain(1) + shift(3)).astype(BF)
    memin[...] = low
    zero64 = jnp.zeros((1, HEAD), F32)
    value_shift = jnp.concatenate(
        [
            part
            for h in range(HEADS)
            for part in (zero64, shift(4)[:, HEAD * h : HEAD * h + HEAD])
        ],
        axis=1,
    )
    memory = (nt(low, wmt[...]) + value_shift).astype(BF)
    for h in range(HEADS):
        kv[h, j] = memory[:, 128 * h : 128 * h + 128]

    def kv_copy(h, slot, t, other):
        return remote(
            kv.at[h, slot], kv.at[h, slot], kv_s.at[h, t], kv_r.at[h, t], me, other
        )

    def kv_send(h, carry):
        kv_copy(h, j, 0, j2).start()
        kv_copy(h, j, 1, j1).start()
        return carry

    lax.fori_loop(0, 2, kv_send, 0)

    m_x_wait()
    m_ca()
    m_cb()
    wqp = wop
    m_ca_wait()
    m_cb_wait()
    for s in range(4):
        at = 80 * s
        wqt[at : at + 32, :] = jnp.concatenate([gm[s, place_of(i), :, 0:rb] for i in range(n)], axis=1)
        wqt[at + 32 : at + 64, :] = jnp.concatenate(
            [gm[s, place_of(i), :, rb : 2 * rb] for i in range(n)], axis=1
        )
        wqt[at + 64 : at + 80, :] = jnp.concatenate(
            [gm[s, place_of(i), 0:16, 2 * rb : 3 * rb] for i in range(n)], axis=1
        )
    for h in range(HEADS):
        wqp[128 * h : 128 * h + 64, :] = wqt[HEAD * h : HEAD * h + HEAD, :]
        wqp[128 * h + 64 : 128 * h + 128, :] = jnp.zeros((64, D), BF)

    query_shift = jnp.concatenate(
        [
            part
            for h in range(HEADS)
            for part in (shift(1)[:, HEAD * h : HEAD * h + HEAD], zero64)
        ],
        axis=1,
    )

    def across(c):
        return pl.ds(pl.multiple_of(c * QC, QC), QC)

    def queries(c, carry):
        at = rows(c * QC, QC)
        q = (nt(abf[at, :], wqp[...]) + query_shift).astype(BF) * jnp.asarray(HEAD**-0.5, BF)
        for h in range(HEADS):
            tile = q[:, 128 * h : 128 * h + 128]
            qnat[h, at, :] = tile
            qt[h, :, across(c)] = tile.T
        return carry

    lax.fori_loop(0, chunks, queries, 0, unroll=pairs)
    lax.fori_loop(2, HEADS, kv_send, 0)

    def send_cot(k, peer, source):
        remote(cot_ref.at[peer], incoming(me), co_s.at[0], co_r.at[0], peer, j).start()

    def wait_cot():
        part = cot_ref.at[pl.ds(0, n - 1)]
        both(remote(part, part, co_s.at[0], co_r.at[0], beside, j))

    def kv_forward(h):
        kv_copy(h, j2, 0, j2).wait_recv()
        kv_copy(h, j2, 2, j1).start()

    fl_za_wait()
    fl_zb_wait()
    fl_ya()
    fl_yb()
    kv_forward(0)

    def attend(h, carry):
        kv_copy(h, j, 0, j2).wait_send()
        kv_copy(h, j, 1, j1).wait_send()
        kv_copy(h, j2, 2, j1).wait_send()
        kv_copy(h, j1, 1, j1).wait_recv()
        kv_copy(h, j3, 2, j1).wait_recv()
        tile = kv[h].reshape(4 * keys, 128)
        kvt[h] = tile.T
        left = jnp.concatenate([tile, kmask[...]], axis=1)
        values = jnp.concatenate([kvt[h, 64:128, :], jnp.ones((16, 4 * keys), BF)], axis=0)
        for c in range(tokens // qa):
            cut = slice(c * qa, (c + 1) * qa)
            scores = nn(left, jnp.concatenate([qt[h, :, cut], qmask[:, cut]], axis=0))
            if c == 0:

                @pl.when(h < HEADS - 1)
                def _():
                    kv_forward(h + 1)

                @pl.when(h == 3)
                def _():
                    peers(send_cot)

                @pl.when(h == HEADS - 2)
                def _():
                    fl_ya_wait()
                    fl_yb_wait()
                    fl_ca()
                    fl_cb()

                @pl.when(h == HEADS - 1)
                def _():
                    fh_a_wait()
                    fh_b_wait()
                    fh_ca()
                    fh_cb()

            largest = jnp.max(scores, axis=0, keepdims=True)
            powers = jnp.exp(scores - largest).astype(BF)
            prob[h, :, cut] = powers
            got = nn(values, powers)
            scale = 1.0 / got[64:65, :]
            rtot[h, :, cut] = scale
            att_t[rows(h * HEAD, HEAD), cut] = (got[0:64, :] * scale).astype(BF)
        return carry

    lax.fori_loop(0, HEADS, attend, 0)

    fl_ca_wait()
    fl_cb_wait()

    def unpack_rows(part, lo, hi):
        for s in range(4):
            span = slice(80 * s + lo, 80 * s + hi)

            def lanes(at, width):
                return jnp.concatenate(
                    [gf[s, place_of(i), part, at : at + width] for i in range(n)], axis=1
                )

            w2t[span, :] = lanes(0, 4 * rb)
            for v in range(4):
                at = 320 * s + 80 * v
                w1t[at + lo : at + hi, :] = lanes((4 + v) * rb, rb)
            wot[span, :] = lanes(8 * rb, rb)

    unpack_rows(lower, 0, GATHER_CUT)
    fh_ca_wait()
    fh_cb_wait()
    unpack_rows(upper, GATHER_CUT, 80)
    wop_full = wot[...].T
    for h in range(HEADS):
        wop[128 * h : 128 * h + 64, :] = jnp.zeros((64, D), BF)
        wop[128 * h + 64 : 128 * h + 128, :] = wop_full[HEAD * h : HEAD * h + HEAD, :]

    def middle(c, carry):
        at = rows(c * QC, QC)
        att = att_t[:, across(c)].T
        att_n[at, :] = att
        value = x_s[at, :].astype(F32) + nt(att, wot[...]) + shift(5)
        mid[at, :] = value
        vhat, _ = norm_parts(value)
        low = (vhat * gain(2) + shift(6)).astype(BF)
        bn[at, :] = low
        return carry

    lax.fori_loop(0, chunks, middle, 0, unroll=pairs)

    edge = tokens - side

    def hidden_of(value):
        return (nt(value, w1t[...]) + hp[9:10, :]).astype(BF)

    ends = hidden_of(jnp.concatenate([bn[0:side, :], bn[edge:tokens, :]], axis=0))
    hidp[side : 2 * side, :] = ends[0:side]
    hidp[tokens : tokens + side, :] = ends[side : 2 * side]
    above = lax.rem(j + 3, 4)
    below = lax.rem(j + 1, 4)

    def rim_up(buf, halo, at):
        return remote(buf.at[pl.ds(side, side)], halo.at[1], ha_s.at[at], ha_r.at[at], me, above)

    def rim_down(buf, halo, at):
        return remote(
            buf.at[pl.ds(tokens, side)], halo.at[0], ha_s.at[at + 1], ha_r.at[at + 1], me, below
        )

    def rim_send(buf, halo, at):
        @pl.when(j > 0)
        def _():
            rim_up(buf, halo, at).start()

        @pl.when(j < 3)
        def _():
            rim_down(buf, halo, at).start()

    def rim_wait(buf, halo, at):
        @pl.when(j > 0)
        def _():
            rim_up(buf, halo, at).wait_send()
            rim_down(buf, halo, at).wait_recv()

        @pl.when(j < 3)
        def _():
            rim_down(buf, halo, at).wait_send()
            rim_up(buf, halo, at).wait_recv()

        for t, (to, ok) in enumerate(((0, top_ok), (tokens + side, low_ok))):
            seen = jnp.full((side, FF), ok, F32) > 0.5
            buf[to : to + side, :] = jnp.where(seen, halo[t].astype(F32), 0.0).astype(BF)

    rim_send(hidp, hidh, 0)

    inner = (tokens - 2 * side) // 2

    def inner_hidden(c, carry):
        start = side + c * inner
        hidp[rows(start + side, inner), :] = hidden_of(bn[rows(start, inner), :])
        return carry

    lax.fori_loop(0, 2, inner_hidden, 0, unroll=pairs)

    def tile_at(t):
        return pl.ds(pl.multiple_of(t * 128, 128), 128)

    def taps_of(lanes):
        return [hp[k : k + 1, lanes] for k in range(9)]

    def conv_over(lo, hi, step, tiles):
        def conv_tile(t, carry):
            lanes = tile_at(t)
            taps = taps_of(lanes)
            base = hp[10:11, lanes]

            def row(at, inner):
                r = lo + at * step
                around = [hidp[rows((r + a) * side, side), lanes].astype(F32) for a in range(3)]
                parts = [
                    taps[b] * around[0] + taps[3 + b] * around[1] + taps[6 + b] * around[2]
                    for b in range(3)
                ]
                moved = jnp.concatenate([parts[0].astype(BF), parts[2].astype(BF)], axis=0)
                z = base + parts[1] + nn(shift_f[...], moved)
                root = z * (0.5**0.5)
                cdf = 0.5 + 0.5 * lax.erf(root)
                slope = (z * 0.3989422804014327) * jnp.exp2(root * root * -1.4426950408889634)
                act[rows((r + 1) * side, side), lanes] = (z * cdf).astype(BF)
                gp[rows(r * side, side), lanes] = (cdf + slope).astype(BF)
                return inner

            lax.fori_loop(0, (hi - lo) // step, row, 0, unroll=True)
            return carry

        lax.fori_loop(0, FF // 128, conv_tile, 0, unroll=tiles)

    conv_over(1, band - 1, 1, 1)
    rim_wait(hidp, hidh, 0)
    conv_over(0, 2 * (band - 1), band - 1, 5)

    def out_chunk(c, carry):
        at = rows(c * QC, QC)
        value = mid[at, :] + nt(act[rows(side + c * QC, QC), :], w2t[...]) + shift(7)
        for p in range(QC // piece):
            part = value[p * piece : (p + 1) * piece, :]
            out_t[c * (QC // piece) + p] = (part.T if turned else part).astype(BF)
        return carry

    lax.fori_loop(0, chunks, out_chunk, 0, unroll=pairs)

    def send_out(k, peer, source):
        remote(out_t.at[peer], out_ref.at[me], ou_s.at[0], ou_r.at[0], peer, j).start()

    def wait_out():
        part = out_t.at[pl.ds(0, n - 1)]
        both(remote(part, part, ou_s.at[0], ou_r.at[0], beside, j))

    peers(send_out)
    own_out = pltpu.make_async_copy(out_t.at[me], out_ref.at[me], loc.at[11])
    own_out.start()

    own_cot.wait()
    wait_cot()
    for i in range(n):
        if turned:
            dy_t[:, i * piece : (i + 1) * piece] = dy_in[i]
            dy[i * piece : (i + 1) * piece, :] = dy_in[i].T
    if not turned:
        dy_t[...] = dy[...].T
    vg[...] = jnp.zeros(vg.shape, F32)
    vg[10:11, :] = colsum(dy[...].astype(F32))

    def scatter(sems, s, cut, direct, bufs, own):
        top = s.shape[2]
        r1, xl, yl, dl, yh, dh, xh = bufs
        low, high = slice(0, cut), slice(cut, top)
        slots = (j, j2)
        count = n if direct else zn
        mine = pl.ds(y0 * zn, zn)
        theirs = pl.ds(y1 * zn, zn)

        def copy(src, dst, t, dp, seq):
            at = sems[t]
            return remote(src, dst, gx_s.at[at], gx_r.at[at], dp, seq)

        def core():
            return [copy(s.at[slot], r1.at[t], t, me, j1) for t, slot in enumerate((j1, j3))]

        def low_x():
            return copy(s.at[j2, :, low], xl, 2, me, j2)

        def low_y():
            return copy(s.at[j, theirs, low], yl, 3, beside, j)

        def high_y():
            return [
                copy(s.at[slot, theirs, high], yh.at[t], 4 + t, beside, j)
                for t, slot in enumerate(slots)
            ]

        def high_x():
            return copy(s.at[j2, here, high], xh, 6, me, j2)

        def out(slot, rows_of, land, t):
            def send(k, peer, to):
                copy(s.at[slot, to, rows_of], land.at[k], t, peer, j).start()

            if direct:
                peers(lambda k, peer, source: send(k, peer, spot(peer)))
            else:
                z_peers(lambda k, peer, to, source: send(k, peer, y0 * zn + to))

        def landed(slot, rows_of, land, t):
            part = land.at[pl.ds(1, count - 1)]
            both(copy(part, part, t, beside, j))
            return lax.fori_loop(
                1,
                count,
                lambda k, v: v + land[k].astype(F32),
                s[slot, here, rows_of].astype(F32),
            )

        def add(slot, start, rows_of, extra):
            def body(i, carry):
                s[slot, start + i, rows_of] = (
                    s[slot, start + i, rows_of].astype(F32) + extra[i].astype(F32)
                ).astype(BF)
                return carry

            lax.fori_loop(0, extra.shape[0], body, 0)

        def one():
            for c in core():
                c.start()

        def two():
            for c in core():
                both(c)
            for t, slot in enumerate(slots):
                add(slot, 0, slice(0, top), r1.at[t])
            if cut < top:
                if direct:
                    for t, slot in enumerate(slots):
                        out(slot, high, dh.at[t], 4 + t)
                else:
                    for c in high_y():
                        c.start()
            if cut > 0:
                low_x().start()

        def low_three():
            both(low_x())
            add(j, 0, low, xl)
            if direct:
                out(j, low, dl, 3)
            else:
                low_y().start()

        def high_three():
            for c in high_y():
                both(c)
            for t, slot in enumerate(slots):
                add(slot, y0 * zn, high, yh.at[t])
                out(slot, high, dh.at[t], 7 + t)

        def low_four():
            both(low_y())
            add(j, y0 * zn, low, yl)
            out(j, low, dl, 9)

        def high_four():
            first = 4 if direct else 7
            own[high, :] = landed(j, high, dh.at[0], first)
            s[j2, here, high] = landed(j2, high, dh.at[1], first + 1).astype(BF)
            high_x().start()

        def low_five():
            own[low, :] = landed(j, low, dl, 3 if direct else 9)

        def high_five():
            both(high_x())
            own[high, :] = own[high, :] + xh[...].astype(F32)

        return one, two, low_three, low_four, low_five, high_three, high_four, high_five

    own_t = own_s.at[0:80, 0:tl]
    own_a = own_s.at[0:80, tl : tl + al]
    own_b = own_s.at[0:80, tl + al : tl + al + bl]
    own_m = own_s.at[96:128, 0:ml]
    a_one, a_two, a_three, a_four, a_five, _, _, _ = scatter(
        (0, 1, 2, 3, 0, 0, 0, 0, 0, 4), gf.at[:, :, :, 0:al], 80, False, (ra0, ra1, ra2, ra3, ra4, ra5, ra6), own_a
    )
    b_one, b_two, bl_three, bl_four, bl_five, bh_three, bh_four, bh_five = scatter(
        (5, 6, 27, 28, 7, 8, 9, 36, 37, 29), sb, 32, False, (rb0, rb1, rb2, rb3, rb4, rb5, rb6), own_b
    )
    m_one, m_two, m_three, m_four, m_five, _, _, _ = scatter(
        (12, 13, 14, 15, 0, 0, 0, 0, 0, 33), gm, 32, False, (rm0, rm1, rm2, rm3, rm4, rm5, rm6), own_m
    )
    below_cut = slice(0, CUT)
    above_cut = slice(CUT, 80)

    def t_core(t, slot, to, rows_of):
        return remote(
            gt.at[slot, :, rows_of], rt0.at[to, :, rows_of], gx_s.at[16 + t], gx_r.at[16 + t], me, j1
        )

    def t_cores():
        return (
            t_core(0, j3, 1, below_cut),
            t_core(1, j1, 0, above_cut),
            t_core(2, j3, 1, above_cut),
            t_core(3, j1, 0, below_cut),
        )

    def t_add(slot, start, count, rows_of, extra):
        def body(i, carry):
            gt[slot, start + i, rows_of] = (
                gt[slot, start + i, rows_of].astype(F32) + extra[start + i, rows_of].astype(F32)
            ).astype(BF)
            return carry

        lax.fori_loop(0, count, body, 0)

    def t_half(t):
        part = pl.ds((y1 if t == 0 else y0) * zn, zn)
        return remote(
            gt.at[j2, part, below_cut], rt1.at[part], gx_s.at[20 + t], gx_r.at[20 + t], me, j2
        )

    def t_dp(slot, i, rows_of, land, sem, k, peer):
        remote(
            gt.at[slot, i, rows_of], land.at[k], gx_s.at[sem], gx_r.at[sem], peer, j
        ).start()

    def t_landed(slot, rows_of, land, sem):
        part = land.at[pl.ds(1, n - 1)]
        both(remote(part, part, gx_s.at[sem], gx_r.at[sem], beside, j))
        return lax.fori_loop(
            1, n, lambda k, v: v + land[k].astype(F32), gt[slot, here, rows_of].astype(F32)
        )

    def t_one():
        for c in t_cores():
            c.start()

    def t_two():
        cores = t_cores()
        both(cores[0])
        t_add(j2, 0, n, below_cut, rt0.at[1])
        t_half(0).start()
        t_half(1).start()
        both(cores[1])
        both(cores[2])
        for t, slot in enumerate((j, j2)):
            t_add(slot, 0, n, above_cut, rt0.at[t])
            peers(
                lambda k, peer, source: t_dp(
                    slot, spot(peer), above_cut, rt5.at[t], 38 - 15 * t, k, peer
                )
            )
        both(cores[3])
        t_add(j, 0, n, below_cut, rt0.at[0])

    def tl_three(t):
        both(t_half(t))
        start = (y1 if t == 0 else y0) * zn

        def body(i, carry):
            at = start + i
            gt[j, at, below_cut] = (gt[j, at, below_cut].astype(F32) + rt1[at].astype(F32)).astype(BF)
            return carry

        lax.fori_loop(0, zn, body, 0)

        def send(i, carry):
            k = 2 * i + (1 if t == 0 else 2)
            peer = lax.rem(me + k, n)
            t_dp(j, spot(peer), below_cut, rt3, 24, k, peer)
            return carry

        lax.fori_loop(0, zn if t == 0 else zn - 1, send, 0)

    def th_x():
        return remote(gt.at[j2, here, above_cut], rt6, gx_s.at[25], gx_r.at[25], me, j2)

    def th_four():
        own_t[above_cut, :] = t_landed(j, above_cut, rt5.at[0], 38)
        gt[j2, here, above_cut] = t_landed(j2, above_cut, rt5.at[1], 23).astype(BF)
        th_x().start()

    def tl_five():
        own_t[below_cut, :] = t_landed(j, below_cut, rt3, 24)

    def th_five():
        both(th_x())
        own_t[above_cut, :] = own_t[above_cut, :] + rt6[...].astype(F32)


    per = 640 // (4 * rb)
    for b in range(2):
        value = nn(dy_t[...], act[side : side + tokens, 640 * b : 640 * b + 640]).astype(BF)
        for ii in range(per):
            i = b * per + ii
            gf[:, place_of(i), :, 0 : 4 * rb] = value[
                :, 4 * rb * ii : 4 * rb * (ii + 1)
            ].reshape(4, 80, 4 * rb)

    a_one()

    def slope_of(at):
        return nn(dy[at, :], w2t[...])

    dz = act
    for at in (0, edge):
        dz[side + at : 2 * side + at, :] = (
            slope_of(slice(at, at + side)) * gp[at : at + side, :].astype(F32)
        ).astype(BF)
    rim_send(dz, dzh, 2)

    def inner_slope(c, carry):
        at = rows(side + c * inner, inner)
        dz[rows(2 * side + c * inner, inner), :] = (
            slope_of(at) * gp[at, :].astype(F32)
        ).astype(BF)
        return carry

    lax.fori_loop(0, 2, inner_slope, 0, unroll=pairs)

    a_two()

    dhid = gp

    def back_over(lo, hi, step, tiles):
        def back_tile(t, carry):
            lanes = tile_at(t)
            taps = taps_of(lanes)

            def row(at, inner):
                r = lo + at * step
                around = [dz[rows((r + a) * side, side), lanes].astype(F32) for a in range(3)]
                parts = [
                    taps[b] * around[2] + taps[3 + b] * around[1] + taps[6 + b] * around[0]
                    for b in range(3)
                ]
                both_ways = jnp.concatenate([parts[0].astype(BF), parts[2].astype(BF)], axis=0)
                low = (parts[1] + nn(shift_b[...], both_ways)).astype(BF)
                dhid[rows(r * side, side), lanes] = low
                return inner

            lax.fori_loop(0, (hi - lo) // step, row, 0, unroll=True)
            return carry

        lax.fori_loop(0, FF // 128, back_tile, 0, unroll=tiles)

    back_over(1, band - 1, 1, 1)
    rim_wait(dz, dzh, 2)
    back_over(0, 2 * (band - 1), band - 1, 5)

    def fold(v):
        return jnp.sum(v.reshape(-1, 8, 128), axis=0)

    def tap_sums(lo, hi):
        def tile(t, carry):
            lanes = tile_at(t)

            def row(r, sums):
                low = dz[rows((r + 1) * side, side), lanes]
                here_f = low.astype(F32)
                sides = nn(shift_m[...], low)
                moved = [sides[0:side], here_f, sides[side : 2 * side]]
                found = []
                for a in range(3):
                    source = hidp[rows((r + a) * side, side), lanes].astype(F32)
                    for b in range(3):
                        found.append(fold(moved[b] * source))
                found.append(fold(here_f))
                return tuple(s + f for s, f in zip(sums, found))

            sums = lax.fori_loop(
                0, band, row, tuple(jnp.zeros((8, 128), F32) for _ in range(10)), unroll=deep
            )
            hg[:, lanes] = jnp.concatenate(
                [colsum(s) for s in sums[0:9]]
                + [hg[9:10, lanes], colsum(sums[9]), jnp.zeros((5, 128), F32)],
                axis=0,
            )
            return carry

        lax.fori_loop(lo, hi, tile, 0)

    bn_t = jnp.concatenate([bn[...].T, jnp.ones((16, tokens), BF)], axis=0)
    for b in range(2):
        found = nn(bn_t, dhid[:, 640 * b : 640 * b + 640])
        hg[9:10, 640 * b : 640 * b + 640] = found[D : D + 1]
        value = found[0:D].T.astype(BF).reshape(2, 4, 80, D)
        for i in range(n):
            sb[2 * b : 2 * b + 2, place_of(i), :, 0 : 4 * rb] = jnp.concatenate(
                [value[:, v, :, rb * i : rb * i + rb] for v in range(4)], axis=2
            )

    b_one()

    zero_row = jnp.zeros((1, D), F32)
    dbr = bn
    dbr_t = dy_t

    def back_middle(c, carry):
        at = rows(c * QC, QC)
        value, in_gain, in_shift = norm_back(mid[at, :], gain(2), nn(dhid[at, :], w1t[...]))
        value = value + dy[at, :].astype(F32)
        mid[at, :] = value
        low = value.astype(BF)
        dbr[at, :] = low
        dbr_t[:, across(c)] = low.T
        spread = nt(wop[...], low)
        for h in range(HEADS):
            tile = spread[128 * h : 128 * h + 128, :] * rtot[h, :, across(c)]
            tile_low = tile.astype(BF)
            qt[h, :, across(c)] = tile_low
            datn[h, at, :] = tile_low.T
            delta[h, :, across(c)] = colsum(
                tile_low[64:128, :].astype(F32)
                * att_t[HEAD * h : HEAD * h + HEAD, across(c)].astype(F32)
            )
        return (carry[0] + in_gain, carry[1] + in_shift, carry[2] + colsum(low.astype(F32)))

    sums = lax.fori_loop(0, chunks, back_middle, (zero_row, zero_row, zero_row), unroll=pairs)
    vg[2:3, :] = sums[0]
    vg[9:10, :] = sums[1]
    vg[8:9, :] = sums[2]
    a_three()
    b_two()

    def dkv(h, slot):
        return gp.at[rows(slot * keys, keys), tile_at(h)]

    def dk_core(h):
        return [
            remote(dkv(h, slot), rk1.at[h, t], kv_s.at[h, t], kv_r.at[h, t], me, j1)
            for t, slot in enumerate((j1, j3))
        ]

    def dk_x(h):
        return remote(dkv(h, j2), rk2.at[h], kv_s.at[h, 2], kv_r.at[h, 2], me, j2)

    def dk_two(h):
        for copy in dk_core(h):
            both(copy)
        for t, slot in enumerate((j, j2)):
            part = dkv(h, slot)
            part[...] = (part[...].astype(F32) + rk1[h, t].astype(F32)).astype(BF)
        dk_x(h).start()

    def dk_three(h):
        both(dk_x(h))
        qnat[h, 0:keys, :] = (dkv(h, j)[...].astype(F32) + rk2[h].astype(F32)).astype(BF)

    def back_head(h, carry):
        tile = kv[h].reshape(4 * keys, 128)
        total = None
        for c in range(tokens // qa):
            cut = slice(c * qa, (c + 1) * qa)
            powers = prob[h, :, cut]
            slopes = nn(tile, qt[h, :, cut]) - delta[h, :, cut]
            ds = (powers.astype(F32) * slopes).astype(BF)
            part = nn(ds, qnat[h, cut, :]) + nn(powers, datn[h, cut, :])
            prob[h, :, cut] = ds
            total = part if total is None else total + part
        gp[0 : 4 * keys, tile_at(h)] = total.astype(BF)
        for copy in dk_core(h):
            copy.start()

        @pl.when(h == 3)
        def _():
            a_four()
            bl_three()

        @pl.when(h >= 1)
        def _():
            dk_two(h - 1)

        return carry

    lax.fori_loop(0, HEADS, back_head, 0)

    dq_t = att_t

    def back_query(h, carry):
        for c in range(tokens // qa):
            cut = slice(c * qa, (c + 1) * qa)
            dq_t[rows(h * HEAD, HEAD), cut] = (
                nn(kvt[h, 0:64, :], prob[h, :, cut]) * HEAD**-0.5
            ).astype(BF)
        return carry

    lax.fori_loop(0, 2, back_query, 0, unroll=pairs)
    dk_two(HEADS - 1)
    bh_three()
    lax.fori_loop(2, HEADS, back_query, 0, unroll=3 if pairs > 1 else 1)
    bl_four()

    dq = dy

    def flip(c, total):
        low = dq_t[:, across(c)].T
        dq[rows(c * QC, QC), :] = low
        return total + colsum(low.astype(F32))

    vg[4:5, :] = lax.fori_loop(0, chunks, flip, zero_row, unroll=pairs)
    value = nn(dq_t[...], abf[...]).astype(BF)
    other = nn(dbr_t[...], att_n[...]).astype(BF)

    def folded(v, i):
        part = v[:, rb * i : rb * i + rb].reshape(4, 80, rb)
        return [
            part[:, 0:32],
            part[:, 32:64],
            jnp.concatenate([part[:, 64:80], jnp.zeros((4, 16, rb), BF)], axis=1),
        ]

    for i in range(n):
        gm[:, place_of(i), :, 0 : 3 * rb] = jnp.concatenate(folded(value, i), axis=2)
        gm[:, place_of(i), :, mo : mo + 3 * rb] = jnp.concatenate(folded(other, i), axis=2)
    m_one()
    tap_sums(0, 2)
    m_two()
    for h in range(HEADS):
        dk_three(h)

    dm = jnp.concatenate([qnat[h, 0:keys, :] for h in range(HEADS)], axis=1)
    dm_sum = colsum(dm.astype(F32))
    vg[7:8, :] = jnp.concatenate(
        [dm_sum[:, 128 * h + 64 : 128 * h + 128] for h in range(HEADS)], axis=1
    )
    kept = jnp.concatenate([a3[t, 0:keys, :] for t in range(3)], axis=1)[:, 0:D]
    dv, in_gain, in_shift = norm_back(kept, gain(1), nn(dm, wmt[...]))
    vg[1:2, :] = in_gain
    vg[6:7, :] = in_shift
    dred = dv.astype(BF)
    vg[5:6, :] = colsum(dred.astype(F32))
    dred_t = dred.T
    for dd in range(4):
        value = nn(dred_t, pat[dd]).astype(BF)
        count = n // 4
        for ii in range(count):
            i = dd * count + ii
            gt[:, place_of(i), :, 0 : 4 * rb] = value[
                :, 4 * rb * ii : 4 * rb * (ii + 1)
            ].reshape(4, 80, 4 * rb)
    value = nn(dm.T, memin[...]).astype(BF)
    value = jnp.concatenate(
        [value[128 * h : 128 * h + 64] for h in range(HEADS)]
        + [value[128 * h + 64 : 128 * h + 128] for h in range(HEADS)],
        axis=0,
    ).reshape(4, 2, 80, D)
    for i in range(n):
        gt[:, place_of(i), :, 4 * rb : 6 * rb] = jnp.concatenate(
            [value[:, v, :, rb * i : rb * i + rb] for v in range(2)], axis=2
        )
    t_one()

    t_two()

    for dd in range(4):
        back = nn(dred, wrt[dd])
        back = jnp.concatenate([back, jnp.zeros((keys, 64), F32)], axis=1)
        for i in range(band // 2):
            start = (2 * i + dd // 2) * side + dd % 2
            for t in range(3):
                a3[t, pl.ds(start, half, stride=2), :] = back[
                    i * half : (i + 1) * half, 128 * t : 128 * t + 128
                ]

    def back_first(c, carry):
        at = rows(c * QC, QC)
        e = nn(dq[at, :], wqt[...]) + jnp.concatenate([a3[t, at, :] for t in range(3)], axis=1)[:, 0:D]
        value, in_gain, in_shift = norm_back(x_s[at, :].astype(F32), gain(0), e)
        bn[at, :] = (mid[at, :] + value).astype(BF)
        return (carry[0] + in_gain, carry[1] + in_shift)

    sums = lax.fori_loop(0, chunks, back_first, (zero_row, zero_row), unroll=pairs)
    token_out = pltpu.make_async_copy(bn, tgrad_ref, loc.at[12])
    token_out.start()
    vg[0:1, :] = sums[0]
    vg[3:4, :] = sums[1]
    m_three()
    tap_sums(2, FF // 128)
    for i in range(n):
        sv[place_of(i), :, 0 : 4 * rb] = hg[:, 4 * rb * i : 4 * rb * (i + 1)].astype(BF)
        sv[place_of(i), :, 4 * rb : 5 * rb] = vg[:, rb * i : rb * i + rb].astype(BF)

    def v_out(k, peer, source):
        remote(sv.at[spot(peer)], rv1.at[k], gx_s.at[26], gx_r.at[26], peer, j).start()

    peers(v_out)
    tl_three(0)
    tl_three(1)
    bh_four()
    m_four()
    part = rv1.at[pl.ds(1, n - 1)]
    both(remote(part, part, gx_s.at[26], gx_r.at[26], beside, j))
    rv2[j] = lax.fori_loop(
        1, n, lambda k, total: total + rv1[k].astype(F32), sv[here].astype(F32)
    ).astype(BF)

    def v_seq(t, slot, other):
        ref = rv2.at[slot]
        return remote(ref, ref, gx_s.at[30 + t], gx_r.at[30 + t], me, other)

    for t, other in enumerate((j1, j2, j3)):
        v_seq(t, j, other).start()
    th_four()
    a_five()
    bl_five()
    bh_five()
    squares = jnp.sum(own_a[:, 0 : 4 * rb] * own_a[:, 0 : 4 * rb])
    squares += jnp.sum(own_b[:, 0 : 4 * rb] * own_b[:, 0 : 4 * rb])
    th_five()
    m_five()
    for at in (0, mo):
        full = own_m[:, at : at + 2 * rb]
        rest = own_m[0:16, at + 2 * rb : at + 3 * rb]
        squares += jnp.sum(full * full) + jnp.sum(rest * rest)
    tl_five()
    squares += jnp.sum(own_t[:, 0 : 6 * rb] * own_t[:, 0 : 6 * rb])
    for t, other in enumerate((j1, j2, j3)):
        v_seq(t, other, other).wait_send()
        v_seq(t, other, other).wait_recv()
    own_v = (rv2[0].astype(F32) + rv2[1].astype(F32)) + (rv2[2].astype(F32) + rv2[3].astype(F32))
    own_s[80:96, 0:vl] = own_v
    first_band = (j == 0).astype(jnp.int32).astype(F32)
    squares += first_band * jnp.sum(own_v[0:11, 0 : 5 * rb] * own_v[0:11, 0 : 5 * rb])

    nrm[4 * me + j] = jnp.full((1, 128), squares, F32)
    own_out_copy = pltpu.make_async_copy(own_s, own_ref, loc.at[13])
    own_out_copy.start()

    def send_norm(k, carry):
        mine = 4 * me + j
        to = lax.rem(mine + k, 4 * n)
        remote(
            nrm.at[mine], nrm.at[mine], nd_s.at[0], nd_r.at[0], lax.div(to, 4), lax.rem(to, 4)
        ).start()
        return carry

    lax.fori_loop(1, 4 * n, send_norm, 0, unroll=flat)
    part = nrm.at[pl.ds(0, 4 * n - 1)]
    both(remote(part, part, nd_s.at[0], nd_r.at[0], beside, j))
    nrm[4 * n] = lax.fori_loop(
        1, 4 * n, lambda k, total: total + nrm[k], nrm[0], unroll=flat
    )
    norm_out = pltpu.make_async_copy(nrm.at[4 * n], norm_ref, loc.at[14])
    norm_out.start()

    wait_out()
    own_out.wait()
    token_out.wait()
    own_out_copy.wait()
    norm_out.wait()


def update_kernel(rb, tl, al, mo, rates, decays, *refs):
    own_hbm, total_hbm, outt_hbm, tg_hbm = refs[0:4]
    in_hbm = refs[4:31]
    out_hbm, tok_hbm, norm_hbm = refs[31:34]
    new_hbm = refs[34:61]
    own_ref, total_ref, out_v, tok_v, norm_v = refs[61:66]
    in_v, new_v = refs[66:75], refs[75:84]
    in_sem, out_sem = refs[84:86]
    own_load, total_load, out_load, tok_load = [
        pltpu.make_async_copy(src, dst, in_sem.at[9 + at])
        for at, (src, dst) in enumerate(
            ((own_hbm, own_ref), (total_hbm, total_ref), (outt_hbm, out_v), (tg_hbm, tok_v))
        )
    ]
    own_load.start()
    total_load.start()
    for at in range(9):
        for part in range(3):
            pltpu.make_async_copy(in_hbm[at + 9 * part], in_v[at].at[part], in_sem.at[at]).start()
    out_load.start()
    tok_load.start()
    norm_store, out_store, tok_store = [
        pltpu.make_async_copy(src, dst, out_sem.at[9 + at])
        for at, (src, dst) in enumerate(((norm_v, norm_hbm), (out_v, out_hbm), (tok_v, tok_hbm)))
    ]
    own_load.wait()
    total_load.wait()
    total = total_ref[...]
    norm = jnp.sqrt(total)
    norm_v[...] = norm
    norm_store.start()
    clip = jnp.minimum(1.0, MAX_NORM / (norm + 1e-06))[:, 0:1]
    turned_t = own_ref[0:80, 0:tl].T
    turned_a = own_ref[0:80, tl : tl + al].T
    turned_b = own_ref[0:80, tl + al :].T
    turned_q, turned_o = [
        jnp.concatenate(
            [
                own_ref[96:128, at : at + rb],
                own_ref[96:128, at + rb : at + 2 * rb],
                own_ref[96:112, at + 2 * rb : at + 3 * rb],
            ],
            axis=0,
        ).T
        for at in (0, mo)
    ]
    grads = (
        turned_q,
        turned_t[0 : 4 * rb],
        jnp.concatenate([turned_t[(4 + v) * rb : (5 + v) * rb] for v in range(2)], axis=1),
        turned_o,
        jnp.concatenate([turned_b[v * rb : (v + 1) * rb] for v in range(4)], axis=1),
        turned_a[0 : 4 * rb],
        own_ref[80:83, 4 * rb : 5 * rb],
        own_ref[83:91, 4 * rb : 5 * rb],
        own_ref[80:91, 0 : 4 * rb],
    )
    for at in range(9):
        if at == 2:
            out_load.wait()
            out_store.start()
            tok_load.wait()
            tok_store.start()
        pltpu.make_async_copy(in_v[at], in_v[at], in_sem.at[at]).wait()
        clipped = clip * grads[at]
        weight = in_v[at][0]
        first = BETA_ONE * in_v[at][1] + (1.0 - BETA_ONE) * clipped
        second = BETA_TWO * in_v[at][2] + (1.0 - BETA_TWO) * clipped * clipped
        direction = (
            first
            / (1.0 - BETA_ONE**STEP)
            / (jnp.sqrt(second / (1.0 - BETA_TWO**STEP)) + ADAM_EPS)
        )
        new_v[at][0] = weight - rates[at] * (direction + decays[at] * weight)
        new_v[at][1] = first
        new_v[at][2] = second
        for part in range(3):
            pltpu.make_async_copy(
                new_v[at].at[part], new_hbm[at + 9 * part], out_sem.at[at]
            ).start()
    for at in range(9):
        pltpu.make_async_copy(new_v[at], new_v[at], out_sem.at[at]).wait()
    for store in (norm_store, out_store, tok_store):
        store.wait()


def on_device(n, *args):
    tokens, buckets, cotangent = args[0:3]
    weights, firsts, seconds = args[3:12], args[12:21], args[21:30]
    band, side, width = tokens.shape[1:4]
    count = band * side
    keys = count // 4
    rb = weights[0].shape[0]
    piece = cotangent.shape[3]
    wide = up(9 * rb, 128)
    tl = up(6 * rb, 128)
    al = up(4 * rb, 128)
    bl = up(4 * rb, 128)
    ml = up(6 * rb, 128)
    h = n // 2
    vl = up(5 * rb, 128)
    total = tl + al + bl
    qa = count if n <= 8 else 128
    turned = piece % 128 == 0
    block = (n, D, piece) if turned else (n, piece, D)
    vm = pltpu.VMEM
    dma = pltpu.SemaphoreType.DMA
    def landing(height, lanes, cut, direct):
        rest = height - cut
        count = n if direct else h
        shapes = (
            (2, n, height, lanes),
            (n, cut, lanes),
            (0 if direct else h, cut, lanes),
            (count, cut, lanes),
            (0 if direct else 2, h, rest, lanes),
            (2, count, rest, lanes),
            (rest, lanes),
        )
        return [vm(shape if 0 not in shape else (8, 128), BF) for shape in shapes]

    scratch = [
        vm((count, D), BF),
        *[vm(weights[at].shape, F32) for at in range(9)],
        vm((n, 16, vl), BF),
        vm((4, n, 80, tl), BF),
        vm((4, n, 32, ml), BF),
        vm((4, n, 80, wide), BF),
        vm((16, D), F32),
        vm((16, FF), F32),
        vm((D, D), BF),
        vm((D, D), BF),
        vm((2 * D, D), BF),
        vm((2 * D, D), BF),
        vm((4, D, D), BF),
        vm((FF, D), BF),
        vm((D, FF), BF),
        vm((3, count, 128), F32),
        vm((count, D), BF),
        vm((4, keys, D), BF),
        vm((keys, D), BF),
        vm((HEADS, 4, keys, 128), BF),
        vm((HEADS, 128, 4 * keys), BF),
        vm((HEADS, count, 128), BF),
        vm((HEADS, 128, count), BF),
        vm((HEADS, 4 * keys, count), BF),
        vm((D, count), BF),
        vm((count, D), BF),
        vm((HEADS, 1, count), F32),
        vm((HEADS, 1, count), F32),
        vm((count, D), F32),
        vm((count, D), BF),
        vm((count + 2 * side, FF), BF),
        vm((2, side, FF), BF),
        vm((count + 2 * side, FF), BF),
        vm((count, FF), BF),
        vm(block, BF),
        vm(block if turned else (8, 128), BF),
        vm((D, count), BF),
        vm((count, D), BF),
        vm((2, side, FF), BF),
        vm((HEADS, count, 128), BF),
        vm((HEADS, 2, keys, 128), BF),
        vm((HEADS, keys, 128), BF),
        vm((16, FF), F32),
        vm((16, D), F32),
        vm((128, total), F32),
        vm((4, n, 80, bl), BF),
        *landing(80, al, 80, False),
        *landing(80, bl, 32, False),
        *landing(80, tl, CUT, True),
        *landing(32, ml, 32, False),
        vm((n, 16, vl), BF),
        vm((n, 16, vl), BF),
        vm((4, 16, vl), BF),
        vm((4 * n + 1, 1, 128), F32),
        vm((side, 2 * side), BF),
        vm((side, 2 * side), BF),
        vm((2 * side, side), BF),
        dma((15,)),
        dma((n,)),
        dma((2, h)),
        *[dma((39,)) for _ in range(2)],
        *[dma((1,)) for _ in range(4)],
        *[dma((HEADS, 3)) for _ in range(2)],
        *[dma((4,)) for _ in range(2)],
        *[dma((1,)) for _ in range(2)],
    ]
    anywhere = pl.BlockSpec(memory_space=pl.ANY)
    out_t, token_grad, own, total_squares = pl.pallas_call(
        functools.partial(block_kernel, n, side, band, qa),
        out_shape=(
            jax.ShapeDtypeStruct(block, BF),
            jax.ShapeDtypeStruct((count, D), BF),
            jax.ShapeDtypeStruct((128, total), F32),
            jax.ShapeDtypeStruct((1, 128), F32),
        ),
        in_specs=[pl.BlockSpec(memory_space=pltpu.SMEM)] + [anywhere] * 11,
        out_specs=(anywhere,) * 4,
        scratch_shapes=scratch,
        compiler_params=pltpu.CompilerParams(
            collective_id=0, has_side_effects=True, vmem_limit_bytes=VMEM_LIMIT
        ),
    )(
        buckets,
        tokens.reshape(count, width),
        jnp.swapaxes(cotangent, 3, 4).reshape(block) if turned else cotangent.reshape(block),
        *weights,
    )
    rates = (
        D ** (-0.5),
        (4 * D) ** (-0.5),
        D ** (-0.5),
        OUT_FAN ** (-0.5),
        D ** (-0.5),
        FF ** (-0.5),
        GAIN_RATE,
        VECTOR_RATE,
        VECTOR_RATE,
    )
    decays = (DECAY_RATE,) * 6 + (0.0,) * 3
    shapes = tuple(jax.ShapeDtypeStruct(w.shape, F32) for w in weights)
    results = pl.pallas_call(
        functools.partial(
            update_kernel, rb, tl, al, 128 if ml > 128 else 3 * rb, rates, decays
        ),
        out_shape=(
            jax.ShapeDtypeStruct(block, BF),
            jax.ShapeDtypeStruct((count, D), BF),
            jax.ShapeDtypeStruct((1, 128), F32),
        )
        + shapes * 3,
        in_specs=[anywhere] * 31,
        out_specs=(anywhere,) * 30,
        scratch_shapes=[
            vm((128, total), F32),
            vm((1, 128), F32),
            vm(block, BF),
            vm((count, D), BF),
            vm((1, 128), F32),
            *[vm((3, *w.shape), F32) for w in weights * 2],
            dma((13,)),
            dma((12,)),
        ],
    )(own, total_squares, out_t, token_grad, *weights, *firsts, *seconds)
    if turned:
        block_output = jnp.swapaxes(results[0].reshape(n, 1, 1, width, piece), 3, 4)
    else:
        block_output = results[0].reshape(n, 1, 1, piece, width)
    return (
        block_output,
        results[1].reshape(1, band, side, width),
        results[2][0, 0],
        *results[3:],
    )


def solution(mesh):
    matrix = (P("dp", "seq"),) * 6 + (P(None, "dp"),) * 3
    return jax.shard_map(
        functools.partial(on_device, mesh.shape["dp"]),
        mesh=mesh,
        in_specs=(
            P("dp", "seq", None, None),
            P("dp"),
            P(None, "seq", "dp", None, None),
            *(matrix * 3),
        ),
        out_specs=(
            P(None, "seq", "dp", None, None),
            P("dp", "seq", None, None),
            P(),
            *(matrix * 3),
        ),
        check_vma=False,
    )
```
